32 devices in a mesh: dp: 8 (over z, y), owner: 4 (over x, core).
Axes of the slice: x: 2, y: 2, z: 4, core: 2. Of those that a mesh axis runs over, the one named last changes fastest.
Arguments:
- images: bfloat16 [768, 7, 7, 2048], P(('dp', 'owner')), may hold values from -6 to 6
- valid_count: int32 [32], P(('dp', 'owner')), may hold values from 1 to 24, as said below
- labels: int32 [768], P(('dp', 'owner')), may hold values from 0 to 999
- loss_weight: int32 [768], P(('dp', 'owner')), may hold values from 1 to 4
- w_reduce: float32 [2, 512, 2048], P(None, 'owner', 'dp'), may hold values from -0.125 to 0.125
- w_spatial: float32 [2, 512, 4608], P(None, 'owner', 'dp'), may hold values from -0.09375 to 0.09375
- w_expand: float32 [2, 512, 2048], P(None, 'owner', 'dp'), may hold values from -0.25 to 0.25
- mom_reduce: float32 [2, 512, 2048], P(None, 'owner', 'dp'), may hold values from -0.001953125 to 0.001953125
- mom_spatial: float32 [2, 512, 4608], P(None, 'owner', 'dp'), may hold values from -0.001953125 to 0.001953125
- mom_expand: float32 [2, 512, 2048], P(None, 'owner', 'dp'), may hold values from -0.001953125 to 0.001953125
- head: float32 [1000, 2048], P('owner', 'dp'), may hold values from -0.5 to 0.5
- head_m: float32 [1000, 2048], P('owner', 'dp'), may hold values from -0.00048828125 to 0.00048828125
- head_v: float32 [1000, 2048], P('owner', 'dp'), may hold values from 4.6875e-10 to 1.875e-09
- norm_params: float32 [2, 2, 3072], replicated, may hold values from -1.5 to 1.5
- norm_m: float32 [2, 2, 3072], replicated, may hold values from -0.0012207031 to 0.0012207031
- norm_v: float32 [2, 2, 3072], replicated, may hold values from 3.8146974e-09 to 1.5894573e-08
- head_bias: float32 [1000], replicated, may hold values from -1.75 to 1.75
- bias_m: float32 [1000], replicated, may hold values from -0.0009765625 to 0.0009765625
- bias_v: float32 [1000], replicated, may hold values from 2.2135416e-09 to 8.854166e-09
Outputs:
- loss_sum: float32 [], replicated
- weight_total: float32 [], replicated
- new_reduce: float32 [2, 512, 2048], P(None, 'owner', 'dp')
- new_spatial: float32 [2, 512, 4608], P(None, 'owner', 'dp')
- new_expand: float32 [2, 512, 2048], P(None, 'owner', 'dp')
- new_mom_reduce: float32 [2, 512, 2048], P(None, 'owner', 'dp')
- new_mom_spatial: float32 [2, 512, 4608], P(None, 'owner', 'dp')
- new_mom_expand: float32 [2, 512, 2048], P(None, 'owner', 'dp')
- new_head: float32 [1000, 2048], P('owner', 'dp')
- new_head_m: float32 [1000, 2048], P('owner', 'dp')
- new_head_v: float32 [1000, 2048], P('owner', 'dp')
- new_norm: float32 [2, 2, 3072], replicated
- new_norm_m: float32 [2, 2, 3072], replicated
- new_norm_v: float32 [2, 2, 3072], replicated
- new_bias: float32 [1000], replicated
- new_bias_m: float32 [1000], replicated
- new_bias_v: float32 [1000], replicated
The draws below stay inside these ranges and needn't reach their ends.
Inputs may be any that keep to these rules, and one draw needn't show every extreme that they name: The first valid_count[d] of device block d's 24 image slots are real images, the others padding.
All inputs are finite; a program needn't handle non-finite values.
Results may differ from the reference program's by a relative error of at most 0.025.
Values may be sent and summed in bfloat16 or wider, within the bound.
No kernel may reach another device: no remote copies, remote signals or barrier semaphores. Data moves between devices by JAX's collectives and lax.ppermute only.
A program may use at most 256 MiB of HBM per device.

```python
import math
import jax
import jax.numpy as jnp
from jax import lax

WIDE = 2048
NARROW = 512
CLASSES = 1000
SIDE = 7
LAYERS = 2
NS_STEPS = 5
STEP = 10
IMG_DEV = 24
SHARDS = 32
IMAGES = 768


def draw_valid_count(key, part):
    key = jax.random.fold_in(key, 11)
    device_index = jnp.arange(SHARDS, dtype=jnp.int32)
    rising = 1 + (IMG_DEV - 1) * device_index // max(SHARDS - 1, 1)
    jitter = jax.random.randint(key, (SHARDS,), -1, 2, dtype=jnp.int32)
    counts = jnp.clip(rising + jitter, 1, IMG_DEV)
    return counts.at[SHARDS - 1].set(IMG_DEV)


def draw_norm_params(key, part):
    key = jax.random.fold_in(key, 23)
    gain_key, bias_key = jax.random.split(key)
    shape = (LAYERS, 2 * NARROW + WIDE)
    gains = 1.0 + 0.1 * jax.random.normal(gain_key, shape, jnp.float32)
    biases = 0.3 * jax.random.normal(bias_key, shape, jnp.float32)
    return jnp.stack([jnp.clip(gains, 0.5, 1.5), jnp.clip(biases, -1.5, 1.5)])


def plant(entries, own_key, smallest, largest):
    dims = entries.shape
    spot = [jax.random.randint(jax.random.fold_in(own_key, axis), (), 0, dims[axis]) for axis in range(len(dims))]
    entries = entries.at[tuple(spot)].set(smallest)
    longest = dims.index(max(dims))
    spot[longest] = (spot[longest] + 1) % dims[longest]
    return entries.at[tuple(spot)].set(largest)


def level_of(own_key, shape, shards, least, top_value):
    factor_of, own = 1.0, jax.random.fold_in(own_key, 6)
    for dim, parts in shards:
        steps = jnp.exp(jax.random.uniform(jax.random.fold_in(own, dim), (parts,), jnp.float32, least / len(shards), top_value / len(shards)))
        factor_of = factor_of * jnp.repeat(steps, shape[dim] // parts).reshape([-1 if axis == dim else 1 for axis in range(len(shape))])
    return factor_of


def scatter_about(stream_key, extent, width, reach, cuts=(), kind=jnp.bfloat16):
    values = jax.random.normal(stream_key, extent, jnp.float32) * width
    if len(cuts) > 0:
        values = level_of(stream_key, extent, cuts, -0.22, 0.18) * values
    return jnp.clip(values, min=-reach, max=reach).astype(kind)


def setup_inputs(seed: int = 0) -> dict:
    seeds = jax.random.split(jax.random.key(seed), 20)
    images = scatter_about(seeds[0], (IMAGES, SIDE, SIDE, WIDE), 1.0, 6.0, ((0, 32),))
    valid_count = draw_valid_count(jax.random.fold_in(seeds[19], 71), 0)
    labels = plant(jax.random.randint(seeds[2], (IMAGES,), 0, CLASSES), jax.random.fold_in(seeds[2], 1), 0, CLASSES - 1).astype(jnp.int32)
    loss_weight = plant(jax.random.randint(seeds[3], (IMAGES,), 1, 5), jax.random.fold_in(seeds[3], 1), 1, 4).astype(jnp.int32)
    w_reduce = scatter_about(seeds[4], (LAYERS, NARROW, WIDE), WIDE ** -0.5, 0.125, ((1, 4), (2, 8)), jnp.float32)
    w_spatial = scatter_about(seeds[5], (LAYERS, NARROW, 9 * NARROW), (9 * NARROW) ** -0.5, 0.09375, ((1, 4), (2, 8)), jnp.float32)
    w_expand = scatter_about(seeds[6], (LAYERS, NARROW, WIDE), NARROW ** -0.5, 0.25, ((1, 4), (2, 8)), jnp.float32)
    mom_reduce = scatter_about(seeds[7], (LAYERS, NARROW, WIDE), (0.45 * (WIDE * IMAGES) ** -0.5), 0.001953125, ((1, 4), (2, 8)), jnp.float32)
    mom_spatial = scatter_about(seeds[8], (LAYERS, NARROW, 9 * NARROW), (0.45 * (WIDE * IMAGES) ** -0.5), 0.001953125, ((1, 4), (2, 8)), jnp.float32)
    mom_expand = scatter_about(seeds[9], (LAYERS, NARROW, WIDE), (0.45 * (WIDE * IMAGES) ** -0.5), 0.001953125, ((1, 4), (2, 8)), jnp.float32)
    head = scatter_about(seeds[10], (CLASSES, WIDE), (4.0 * WIDE ** -0.5), 0.5, ((0, 4), (1, 8)), jnp.float32)
    head_m = scatter_about(seeds[11], (CLASSES, WIDE), (0.066 * (IMAGES * CLASSES) ** -0.5), 0.00048828125, ((0, 4), (1, 8)), jnp.float32)
    head_v = jnp.clip(jnp.exp(math.log(1.8749999330935907e-09) - 1.3862944 * jax.random.uniform(seeds[12], (CLASSES, WIDE), jnp.float32) ** level_of(seeds[12], (CLASSES, WIDE), ((0, 4), (1, 8)), -0.2, 0.2)), 4.687499832733977e-10, 1.8749999330935907e-09)
    norm_params = draw_norm_params(jax.random.fold_in(seeds[19], 71), 0)
    norm_m = scatter_about(seeds[14], (2, LAYERS, 2 * NARROW + WIDE), (0.28 * (WIDE * IMAGES) ** -0.5), 0.0012207031, (), jnp.float32)
    norm_v = jnp.clip(jnp.exp(jax.random.uniform(seeds[15], (2, LAYERS, 2 * NARROW + WIDE), jnp.float32, math.log(3.814697446813398e-09), math.log(1.5894572769070692e-08))), 3.814697446813398e-09, 1.5894572769070692e-08)
    head_bias = scatter_about(seeds[16], (CLASSES,), 0.3, 1.75, (), jnp.float32)
    bias_m = scatter_about(seeds[17], (CLASSES,), (0.14 * (IMAGES * CLASSES) ** -0.5), 0.0009765625, (), jnp.float32)
    bias_v = jnp.clip(jnp.exp(jax.random.uniform(seeds[18], (CLASSES,), jnp.float32, math.log(2.2135415722601692e-09), math.log(8.854166289040677e-09))), 2.2135415722601692e-09, 8.854166289040677e-09)
    return dict(images=images, valid_count=valid_count, labels=labels, loss_weight=loss_weight, w_reduce=w_reduce, w_spatial=w_spatial, w_expand=w_expand, mom_reduce=mom_reduce, mom_spatial=mom_spatial, mom_expand=mom_expand, head=head, head_m=head_m, head_v=head_v, norm_params=norm_params, norm_m=norm_m, norm_v=norm_v, head_bias=head_bias, bias_m=bias_m, bias_v=bias_v)


EPS = 1e-05
NS_A = 3.4445
NS_B = -4.775
NS_C = 2.0315
MOMENTUM = 0.9
LR_MATRIX = 0.5
DECAY_MATRIX = 0.01
BETA_ONE = 0.9
BETA_TWO = 0.999
ADAM_EPS = 1e-08
LR_HEAD = 0.2
DECAY_HEAD = 0.01
LR_VECTOR = 0.4

@jax.custom_vjp
def low(v):
    return lax.optimization_barrier(v.astype(jnp.bfloat16)).astype(jnp.float32)

@jax.custom_vjp
def low_back(v):
    return v

def low_keep(v):
    return (low(v), None)

def low_pass(kept, grad):
    return (grad,)

def back_keep(v):
    return (v, None)

def back_low(kept, grad):
    return (low(grad),)
low.defvjp(low_keep, low_pass)
low_back.defvjp(back_keep, back_low)

def matmul(left, right):
    return jnp.dot(left, right, precision=lax.Precision.HIGHEST, preferred_element_type=jnp.float32)

def columns(values, count_img):
    chans = values.shape[1]
    grid = values.reshape(count_img, SIDE, SIDE, chans)
    padded = jnp.pad(grid, ((0, 0), (1, 1), (1, 1), (0, 0)))
    pieces = [padded[:, offset // 3:offset // 3 + SIDE, offset % 3:offset % 3 + SIDE, :] for offset in range(9)]
    return jnp.concatenate(pieces, axis=3).reshape(count_img * SIDE * SIDE, 9 * chans)

def batch_norm(hidden, norm_gain, norm_bias, mask_pix, total_count):
    centre = lax.optimization_barrier(jnp.sum(hidden * mask_pix, axis=0)) / total_count
    spread = lax.optimization_barrier(jnp.sum(hidden * hidden * mask_pix, axis=0)) / total_count - centre * centre
    return (hidden - centre) * lax.rsqrt(spread + EPS) * norm_gain + norm_bias

def forward(weights, images, mask_pix, weight_img, onehot):
    w_reduce, w_spatial, w_expand, head, norm_params, head_bias = weights
    count_img = images.shape[0]
    total_count = jnp.sum(mask_pix)
    current = images.reshape(count_img * SIDE * SIDE, WIDE)
    for layer in range(LAYERS):
        gains = norm_params[0, layer]
        biases = norm_params[1, layer]
        first_h = low_back(matmul(low(current), low(w_reduce[layer]).T))
        first_a = jax.nn.silu(batch_norm(first_h, gains[:NARROW], biases[:NARROW], mask_pix, total_count))
        second_h = low_back(matmul(columns(low(first_a), count_img), low(w_spatial[layer]).T))
        second_a = jax.nn.silu(batch_norm(second_h, gains[NARROW:2 * NARROW], biases[NARROW:2 * NARROW], mask_pix, total_count))
        third_h = low_back(matmul(low(second_a), low(w_expand[layer])))
        current = jax.nn.silu(current + batch_norm(third_h, gains[2 * NARROW:], biases[2 * NARROW:], mask_pix, total_count))
    pooled = lax.optimization_barrier(jnp.mean(current.reshape(count_img, SIDE * SIDE, WIDE), axis=1))
    logits = low_back(matmul(low(pooled), low(head).T)) + head_bias
    top_logit = lax.optimization_barrier(jnp.max(logits, axis=1, keepdims=True))
    log_total = jnp.log(lax.optimization_barrier(jnp.sum(jnp.exp(logits - top_logit), axis=1))) + top_logit[:, 0]
    picked = lax.optimization_barrier(jnp.sum(logits * onehot, axis=1))
    loss_sum = jnp.sum(weight_img * (log_total - picked))
    return (loss_sum / jnp.sum(weight_img), loss_sum)

def orthogonalize(moment):
    iterate = moment / (jnp.sqrt(jnp.sum(moment * moment)) + 1e-07)
    for sweep_index in range(NS_STEPS):
        gram = matmul(iterate, iterate.T)
        mixed = NS_B * gram + NS_C * matmul(gram, gram)
        iterate = NS_A * iterate + matmul(mixed, iterate)
    return iterate

def muon(weight, grad, moment):
    moment = MOMENTUM * moment + grad
    direction = jnp.stack([orthogonalize(moment[layer]) for layer in range(LAYERS)])
    return (weight * (1.0 - LR_MATRIX * DECAY_MATRIX) - LR_MATRIX * direction, moment)

def adamw(weight, grad, first, second, rate, decay):
    first = BETA_ONE * first + (1.0 - BETA_ONE) * grad
    second = BETA_TWO * second + (1.0 - BETA_TWO) * grad * grad
    first_hat = first / (1.0 - BETA_ONE ** STEP)
    second_hat = second / (1.0 - BETA_TWO ** STEP)
    weight = weight - rate * (first_hat / (jnp.sqrt(second_hat) + ADAM_EPS) + decay * weight)
    return (weight, first, second)

def reference(images, valid_count, labels, loss_weight, w_reduce, w_spatial, w_expand, mom_reduce, mom_spatial, mom_expand, head, head_m, head_v, norm_params, norm_m, norm_v, head_bias, bias_m, bias_v):
    image_index = jnp.arange(IMAGES, dtype=jnp.int32)
    valid = (image_index % IMG_DEV < valid_count[image_index // IMG_DEV]).astype(jnp.float32)
    mask_pix = jnp.repeat(valid, SIDE * SIDE)[:, None]
    weight_img = valid * loss_weight.astype(jnp.float32)
    onehot = (labels[:, None] == jnp.arange(CLASSES, dtype=jnp.int32)[None, :]).astype(jnp.float32)
    weights = (w_reduce, w_spatial, w_expand, head, norm_params, head_bias)
    loss_value, pullback, loss_sum = jax.vjp(lambda params: forward(params, images.astype(jnp.float32), mask_pix, weight_img, onehot), weights, has_aux=True)
    grads = pullback(jnp.ones_like(loss_value))[0]
    new_reduce, new_mom_reduce = muon(w_reduce, grads[0], mom_reduce)
    new_spatial, new_mom_spatial = muon(w_spatial, grads[1], mom_spatial)
    new_expand, new_mom_expand = muon(w_expand, grads[2], mom_expand)
    new_head, new_head_m, new_head_v = adamw(head, grads[3], head_m, head_v, LR_HEAD, DECAY_HEAD)
    new_norm, new_norm_m, new_norm_v = adamw(norm_params, grads[4], norm_m, norm_v, LR_VECTOR, 0.0)
    new_bias, new_bias_m, new_bias_v = adamw(head_bias, grads[5], bias_m, bias_v, LR_VECTOR, 0.0)
    return (loss_sum, jnp.sum(weight_img), new_reduce, new_spatial, new_expand, new_mom_reduce, new_mom_spatial, new_mom_expand, new_head, new_head_m, new_head_v, new_norm, new_norm_m, new_norm_v, new_bias, new_bias_m, new_bias_v)
```

```python
import math

import jax
import jax.numpy as jnp
from jax import lax
from jax.sharding import PartitionSpec as P

LAYERS = 2
NS_STEPS = 5
STEP = 10


AXES = ("dp", "owner")
EPS = 1e-05
NS_A = 3.4445
NS_B = -4.775
NS_C = 2.0315
MOMENTUM = 0.9
LR_MATRIX = 0.5
DECAY_MATRIX = 0.01
BETA_ONE = 0.9
BETA_TWO = 0.999
ADAM_EPS = 1e-08
LR_HEAD = 0.2
DECAY_HEAD = 0.01
LR_VECTOR = 0.4


def contract_rows(left, right):
    return lax.dot_general(
        left, right, (((0,), (0,)), ((), ())), preferred_element_type=jnp.float32
    )


def contract_cols(left, right):
    return lax.dot_general(
        left, right, (((1,), (1,)), ((), ())), preferred_element_type=jnp.float32
    )


def silu_slope(values):
    sigmoid_part = jax.nn.sigmoid(values)
    return sigmoid_part * (1.0 + values * (1.0 - sigmoid_part))


def columns(values, count_img, side):
    chans = values.shape[1]
    grid = values.reshape(count_img, side, side, chans)
    padded = jnp.pad(grid, ((0, 0), (1, 1), (1, 1), (0, 0)))
    pieces = [
        padded[:, offset // 3 : offset // 3 + side, offset % 3 : offset % 3 + side, :]
        for offset in range(9)
    ]
    return jnp.concatenate(pieces, axis=3).reshape(count_img * side * side, 9 * chans)


def columns_back(grad_patches, count_img, side, chans):
    grid = grad_patches.reshape(count_img, side, side, 9, chans)
    summed = jnp.zeros((count_img, side + 2, side + 2, chans), jnp.float32)
    for offset in range(9):
        row_shift = offset // 3
        col_shift = offset % 3
        summed = summed + jnp.pad(
            grid[:, :, :, offset, :],
            ((0, 0), (row_shift, 2 - row_shift), (col_shift, 2 - col_shift), (0, 0)),
        )
    return summed[:, 1 : side + 1, 1 : side + 1, :].reshape(count_img * side * side, chans)


def norm_forward(hidden, norm_gain, norm_bias, mask_pix):
    local_terms = (
        jnp.sum(hidden * mask_pix, axis=0),
        jnp.sum(hidden * hidden * mask_pix, axis=0),
        jnp.sum(mask_pix),
    )
    first_sum, square_sum, total_count = all_sum(local_terms)
    centre = first_sum / total_count
    spread = square_sum / total_count - centre * centre
    inverse = lax.rsqrt(spread + EPS)
    normed = (hidden - centre) * inverse
    return (normed * norm_gain + norm_bias, normed, inverse, total_count)


def norm_backward(grad_out, normed, inverse, norm_gain, mask_pix, total_count):
    bias_grad, gain_grad = all_sum(
        (jnp.sum(grad_out, axis=0), jnp.sum(grad_out * normed, axis=0))
    )
    grad_in = (
        norm_gain * inverse * (grad_out - mask_pix * (bias_grad + normed * gain_grad) / total_count)
    )
    return (grad_in, gain_grad, bias_grad)


def layer_forward(
    inputs, weight_one, weight_two, weight_three, norm_gain, norm_bias, mask_pix, count_img, side
):
    narrow = weight_one.shape[1]
    inputs_low = inputs.astype(jnp.bfloat16)
    reduced = jnp.dot(inputs_low, weight_one, preferred_element_type=jnp.float32)
    first_out, first_norm, first_inv, total_count = norm_forward(
        reduced, norm_gain[:narrow], norm_bias[:narrow], mask_pix
    )
    first_act = jax.nn.silu(first_out).astype(jnp.bfloat16)
    patches = columns(first_act, count_img, side)
    spatial = jnp.dot(patches, weight_two, preferred_element_type=jnp.float32)
    second_out, second_norm, second_inv, unused_one = norm_forward(
        spatial, norm_gain[narrow : 2 * narrow], norm_bias[narrow : 2 * narrow], mask_pix
    )
    second_act = jax.nn.silu(second_out).astype(jnp.bfloat16)
    expanded = contract_cols(second_act, weight_three)
    third_out, third_norm, third_inv, unused_two = norm_forward(
        expanded, norm_gain[2 * narrow :], norm_bias[2 * narrow :], mask_pix
    )
    summed = inputs + third_out
    kept = (
        inputs_low,
        first_out,
        first_norm,
        first_inv,
        patches,
        second_out,
        second_norm,
        second_inv,
        second_act,
        third_norm,
        third_inv,
        summed,
        total_count,
    )
    return (jax.nn.silu(summed), kept)


def layer_backward(
    grad_out, kept, weight_one, weight_two, weight_three, norm_gain, mask_pix, count_img, side
):
    (
        inputs_low,
        first_out,
        first_norm,
        first_inv,
        patches,
        second_out,
        second_norm,
        second_inv,
        second_act,
        third_norm,
        third_inv,
        summed,
        total_count,
    ) = kept
    narrow = weight_one.shape[1]
    grad_sum = grad_out * silu_slope(summed)
    grad_third, gain_three, bias_three = norm_backward(
        grad_sum, third_norm, third_inv, norm_gain[2 * narrow :], mask_pix, total_count
    )
    grad_third = grad_third.astype(jnp.bfloat16)
    grad_w_three = contract_rows(grad_third, second_act)
    grad_second = jnp.dot(grad_third, weight_three, preferred_element_type=jnp.float32) * silu_slope(second_out)
    grad_spatial, gain_two, bias_two = norm_backward(
        grad_second, second_norm, second_inv, norm_gain[narrow : 2 * narrow], mask_pix, total_count
    )
    grad_spatial = grad_spatial.astype(jnp.bfloat16)
    grad_w_two = contract_rows(patches, grad_spatial)
    grad_patches = contract_cols(grad_spatial, weight_two)
    grad_first = columns_back(grad_patches, count_img, side, narrow) * silu_slope(first_out)
    grad_reduced, gain_one, bias_one = norm_backward(
        grad_first, first_norm, first_inv, norm_gain[:narrow], mask_pix, total_count
    )
    grad_reduced = grad_reduced.astype(jnp.bfloat16)
    grad_w_one = contract_rows(inputs_low, grad_reduced)
    grad_in = contract_cols(grad_reduced, weight_one) + grad_sum
    gain_grads = jnp.concatenate([gain_one, gain_two, gain_three])
    bias_grads = jnp.concatenate([bias_one, bias_two, bias_three])
    return (grad_in, (grad_w_one, grad_w_two, grad_w_three), gain_grads, bias_grads)


def all_sum(parts):
    shapes = [part.shape for part in parts]
    sizes = [math.prod(shape) for shape in shapes]
    flat = jnp.concatenate([part.reshape(-1) for part in parts])
    total = flat.shape[0]
    rows = -(-total // 1024) * 8
    flat = jnp.pad(flat, (0, rows * 128 - total)).reshape(rows, 128)
    copies = jnp.broadcast_to(flat[None], (device_count(), rows, 128))
    summed = jnp.sum(lax.all_to_all(copies, AXES, 0, 0, tiled=True), axis=0).reshape(-1)
    out, start = [], 0
    for shape, size in zip(shapes, sizes):
        out.append(summed[start : start + size].reshape(shape))
        start += size
    return out


def device_count():
    return lax.axis_size("dp") * lax.axis_size("owner")


def my_index():
    return lax.axis_index("dp") * lax.axis_size("owner") + lax.axis_index("owner")


def swap(values, bit):
    count = device_count()
    return lax.ppermute(values, AXES, [(src, src ^ (1 << bit)) for src in range(count)])


def halving_sum(blocks, order):
    count, rows, lanes = blocks.shape
    left = list(range(count.bit_length() - 2, -1, -1))
    values = blocks
    for bit in order:
        place = left.index(bit)
        values = values.reshape(2**place, 2, -1, rows, lanes)
        own = (my_index() >> bit) & 1
        kept = lax.dynamic_index_in_dim(values, own, 1, keepdims=False)
        sent = lax.dynamic_index_in_dim(values, 1 - own, 1, keepdims=False)
        values = kept + swap(sent, bit)
        left.pop(place)
    return values.reshape(rows, lanes)


def rotated_halving(blocks, cuts):
    count = blocks.shape[0]
    bits = list(range(1, count.bit_length() - 1))
    out, start = [], 0
    for number, rows in enumerate(cuts):
        turn = number % len(bits)
        order = [0] + bits[turn:] + bits[:turn]
        out.append(halving_sum(blocks[:, start : start + rows], order))
        start += rows
    return jnp.concatenate(out, axis=0)


def pack(parts):
    return jnp.concatenate([part.T.astype(jnp.bfloat16) for part in parts], axis=0)


def spread(gathered, start, rows):
    piece = gathered[:, :, start : start + rows]
    return piece.transpose(0, 2, 1, 3).reshape(piece.shape[0] * rows, -1)


def unspread(grad, dp_size, owner_size):
    rows, lanes = grad.shape[0] // dp_size, grad.shape[1] // owner_size
    grad = grad.astype(jnp.bfloat16).reshape(dp_size, rows, owner_size, lanes)
    return grad.transpose(0, 2, 1, 3).reshape(dp_size * owner_size, rows, lanes)


def newton_schulz(moments):
    dp_size, owner_size = lax.axis_size("dp"), lax.axis_size("owner")
    owner = lax.axis_index("owner")
    cols = [moment.shape[0] for moment in moments]
    lanes = moments[0].shape[1]
    low = jnp.concatenate([moment.astype(jnp.bfloat16) for moment in moments], axis=0)
    all_rows = lax.all_gather(low, "owner")
    all_rows = all_rows.transpose(1, 0, 2).reshape(low.shape[0], owner_size * lanes)
    pieces, start = [], 0
    for size in cols:
        pieces.append(all_rows[start : start + size])
        start += size
    side = owner_size * lanes
    pairs = [(i, j) for i in range(owner_size) for j in range(i, owner_size)]
    packed = []
    for piece in pieces:
        gram = contract_rows(piece, piece)
        blocks = [gram[i * lanes : (i + 1) * lanes, j * lanes : (j + 1) * lanes] for i, j in pairs]
        packed.append(jnp.concatenate(blocks, axis=0))
    rows = packed[0].shape[0] // owner_size
    stack = jnp.stack(packed + [jnp.zeros_like(packed[0])] * (dp_size - len(packed)))
    mine = lax.dynamic_slice_in_dim(stack, owner * rows, rows, axis=1)
    bits = [bit for bit in range(device_count().bit_length() - 1) if (1 << bit) >= owner_size]
    values = mine
    for bit in bits:
        place = dp_size.bit_length() - 1 - (len(bits) - bits.index(bit))
        own = (my_index() >> bit) & 1
        values = values.reshape(-1, 2, rows, lanes)
        kept = lax.dynamic_index_in_dim(values, own, 1, keepdims=False)
        sent = lax.dynamic_index_in_dim(values, 1 - own, 1, keepdims=False)
        values = kept + swap(sent, bit)
    whole = lax.all_gather(values[0], "owner", tiled=True)
    blocks = {}
    for number, (i, j) in enumerate(pairs):
        block = whole[number * lanes : (number + 1) * lanes]
        blocks[i, j] = block
        if i != j:
            blocks[j, i] = block.T
    gram = jnp.concatenate(
        [jnp.concatenate([blocks[i, j] for j in range(owner_size)], axis=1) for i in range(owner_size)],
        axis=0,
    )
    dot = lambda left, right: jnp.dot(left, right, precision=lax.Precision.HIGHEST)
    eye = jnp.eye(side, dtype=jnp.float32)
    factor = 1.0 / (jnp.sqrt(jnp.trace(gram)) + 1e-07)
    gram = gram * (factor * factor)
    product = None
    for iteration in range(NS_STEPS):
        square = dot(gram, gram)
        poly = NS_A * eye + NS_B * gram + NS_C * square
        if iteration < NS_STEPS - 1:
            gram = dot(dot(gram, poly), poly)
        product = poly if product is None else dot(product, poly)
    product = (product * factor).astype(jnp.bfloat16)
    own_rows = lax.dynamic_slice_in_dim(product, owner * lanes, lanes, axis=0)
    copies = jnp.broadcast_to(own_rows[None], (dp_size,) + own_rows.shape)
    products = lax.all_to_all(copies, "dp", 0, 0, tiled=True)
    return [contract_cols(piece, products[number]) for number, piece in enumerate(pieces)]


def adamw(weight, grad, first, second, rate, decay):
    first = BETA_ONE * first + (1.0 - BETA_ONE) * grad
    second = BETA_TWO * second + (1.0 - BETA_TWO) * grad * grad
    first_hat = first / (1.0 - BETA_ONE**STEP)
    second_hat = second / (1.0 - BETA_TWO**STEP)
    weight = weight - rate * (first_hat / (jnp.sqrt(second_hat) + ADAM_EPS) + decay * weight)
    return (weight, first, second)


def per_device(
    images,
    valid_count,
    labels,
    loss_weight,
    w_reduce,
    w_spatial,
    w_expand,
    mom_reduce,
    mom_spatial,
    mom_expand,
    head,
    head_m,
    head_v,
    norm_params,
    norm_m,
    norm_v,
    head_bias,
    bias_m,
    bias_v,
):
    count_img = images.shape[0]
    side = images.shape[1]
    wide = images.shape[3]
    pixels = side * side
    dp_size, owner_size = lax.axis_size("dp"), lax.axis_size("owner")
    rows_of = (w_reduce.shape[2], w_spatial.shape[2], w_expand.shape[2])
    starts = (0, rows_of[0], rows_of[0] + rows_of[1])
    weight_one, weight_two, weight_three = ([], [], [])
    for layer in range(LAYERS):
        gathered = lax.all_gather(pack((w_reduce[layer], w_spatial[layer], w_expand[layer])), AXES)
        gathered = gathered.reshape((dp_size, owner_size) + gathered.shape[1:])
        for kind, stack in enumerate((weight_one, weight_two, weight_three)):
            stack.append(spread(gathered, starts[kind], rows_of[kind]))
    classes = head.shape[0]
    class_slots = -(-classes // 16) * 16
    slack = class_slots - classes
    head_low = jnp.pad(head.astype(jnp.bfloat16), ((0, slack), (0, 0)))
    head_all = lax.all_gather(head_low, AXES)
    head_all = head_all.reshape(dp_size, owner_size * class_slots, head.shape[1])
    head_full = head_all.transpose(1, 0, 2).reshape(owner_size * class_slots, wide)
    slot_bias = jnp.pad(
        head_bias.reshape(owner_size, classes), ((0, 0), (0, slack)), constant_values=-1e30
    ).reshape(-1)
    slot_labels = (labels // classes) * class_slots + labels % classes
    valid = (jnp.arange(count_img, dtype=jnp.int32) < valid_count[0]).astype(jnp.float32)
    mask_pix = jnp.repeat(valid, pixels)[:, None]
    current = images.reshape(count_img * pixels, wide).astype(jnp.float32)
    kept_layers = []
    for layer in range(LAYERS):
        current, kept = layer_forward(
            current,
            weight_one[layer],
            weight_two[layer],
            weight_three[layer],
            norm_params[0, layer],
            norm_params[1, layer],
            mask_pix,
            count_img,
            side,
        )
        kept_layers.append(kept)
    pooled = jnp.mean(current.reshape(count_img, pixels, wide), axis=1)
    pooled_low = pooled.astype(jnp.bfloat16)
    logits = contract_cols(pooled_low, head_full) + slot_bias
    top_logit = jnp.max(logits, axis=1, keepdims=True)
    log_total = jnp.log(jnp.sum(jnp.exp(logits - top_logit), axis=1, keepdims=True)) + top_logit
    onehot = (slot_labels[:, None] == jnp.arange(logits.shape[1], dtype=jnp.int32)[None, :]).astype(
        jnp.float32
    )
    weight_img = valid * loss_weight.astype(jnp.float32)
    local_loss = jnp.sum(weight_img * (log_total[:, 0] - jnp.sum(logits * onehot, axis=1)))
    residue = weight_img[:, None] * (jnp.exp(logits - log_total) - onehot)
    weight_total, loss_sum, bias_raw = all_sum(
        (jnp.sum(weight_img), local_loss, jnp.sum(residue, axis=0))
    )
    grad_bias = bias_raw.reshape(owner_size, class_slots)[:, :classes].reshape(-1) / weight_total
    grad_low = (residue / weight_total).astype(jnp.bfloat16)
    grad_head = contract_rows(grad_low, pooled_low)
    grad_pooled = jnp.dot(grad_low, head_full, preferred_element_type=jnp.float32)
    grad_current = jnp.repeat(grad_pooled / pixels, pixels, axis=0)
    grads_one, grads_two, grads_three, gain_rows, bias_rows = ([], [], [], [], [])
    for layer in reversed(range(LAYERS)):
        grad_current, weight_grads, gain_grads, bias_grads = layer_backward(
            grad_current,
            kept_layers[layer],
            weight_one[layer],
            weight_two[layer],
            weight_three[layer],
            norm_params[0, layer],
            mask_pix,
            count_img,
            side,
        )
        grads_one.insert(0, weight_grads[0])
        grads_two.insert(0, weight_grads[1])
        grads_three.insert(0, weight_grads[2])
        gain_rows.insert(0, gain_grads)
        bias_rows.insert(0, bias_grads)
    norm_grad = jnp.stack([jnp.stack(gain_rows), jnp.stack(bias_rows)])
    head_blocks = grad_head.astype(jnp.bfloat16).reshape(
        owner_size, class_slots, dp_size, head.shape[1]
    )
    head_blocks = head_blocks.transpose(2, 0, 1, 3).reshape(
        dp_size * owner_size, class_slots, head.shape[1]
    )
    lanes = w_reduce.shape[1]
    halves = head.shape[1] // lanes if head.shape[1] % lanes == 0 else 0
    sums = []
    for layer in range(LAYERS):
        blocks = jnp.concatenate(
            [
                unspread(grad, dp_size, owner_size)
                for grad in (grads_one[layer], grads_two[layer], grads_three[layer])
            ],
            axis=1,
        )
        if layer == 0:
            third = blocks.shape[1] // 48 * 16
            cuts = (third, third, blocks.shape[1] - 2 * third)
            sums.append(rotated_halving(blocks, cuts).astype(jnp.float32))
        elif halves:
            extra = [head_blocks[:, :, i * lanes : (i + 1) * lanes] for i in range(halves)]
            blocks = jnp.concatenate([blocks] + extra, axis=1)
            total = lax.psum_scatter(blocks, AXES, scatter_dimension=0).astype(jnp.float32)
            height = sum(rows_of)
            sums.append(total[:height])
            head_sum = jnp.concatenate(
                [
                    total[height + i * class_slots : height + i * class_slots + classes]
                    for i in range(halves)
                ],
                axis=1,
            )
        else:
            sums.append(lax.psum_scatter(blocks, AXES, scatter_dimension=0).astype(jnp.float32))
            head_sum = lax.psum_scatter(head_blocks, AXES, scatter_dimension=0)
            head_sum = head_sum.astype(jnp.float32)[:classes]
    olds = (mom_reduce, mom_spatial, mom_expand)
    moments_t = [
        MOMENTUM * olds[kind][layer].T + sums[layer][starts[kind] : starts[kind] + rows_of[kind]]
        for layer in range(LAYERS)
        for kind in range(3)
    ]
    directions_t = newton_schulz(moments_t)
    moments, directions = (
        [
            jnp.stack([values[layer * 3 + kind].T for layer in range(LAYERS)])
            for kind in range(3)
        ]
        for values in (moments_t, directions_t)
    )
    masters = (w_reduce, w_spatial, w_expand)
    updated = tuple(
        (
            master * (1.0 - LR_MATRIX * DECAY_MATRIX) - LR_MATRIX * direction
            for master, direction in zip(masters, directions)
        )
    )
    new_head, new_head_m, new_head_v = adamw(
        head, head_sum, head_m, head_v, LR_HEAD, DECAY_HEAD
    )
    new_norm, new_norm_m, new_norm_v = adamw(norm_params, norm_grad, norm_m, norm_v, LR_VECTOR, 0.0)
    new_bias, new_bias_m, new_bias_v = adamw(head_bias, grad_bias, bias_m, bias_v, LR_VECTOR, 0.0)
    return (
        loss_sum,
        weight_total,
        updated[0],
        updated[1],
        updated[2],
        moments[0],
        moments[1],
        moments[2],
        new_head,
        new_head_m,
        new_head_v,
        new_norm,
        new_norm_m,
        new_norm_v,
        new_bias,
        new_bias_m,
        new_bias_v,
    )


def solution(mesh):
    return jax.shard_map(
        per_device,
        mesh=mesh,
        in_specs=(
            P(("dp", "owner"), None, None, None),
            P(("dp", "owner")),
            P(("dp", "owner")),
            P(("dp", "owner")),
            P(None, "owner", "dp"),
            P(None, "owner", "dp"),
            P(None, "owner", "dp"),
            P(None, "owner", "dp"),
            P(None, "owner", "dp"),
            P(None, "owner", "dp"),
            P("owner", "dp"),
            P("owner", "dp"),
            P("owner", "dp"),
            P(),
            P(),
            P(),
            P(),
            P(),
            P(),
        ),
        out_specs=(
            P(),
            P(),
            P(None, "owner", "dp"),
            P(None, "owner", "dp"),
            P(None, "owner", "dp"),
            P(None, "owner", "dp"),
            P(None, "owner", "dp"),
            P(None, "owner", "dp"),
            P("owner", "dp"),
            P("owner", "dp"),
            P("owner", "dp"),
            P(),
            P(),
            P(),
            P(),
            P(),
            P(),
        ),
        check_vma=False,
    )
```

```python
import functools
import math

import jax
import jax.numpy as jnp
from jax import lax
from jax.experimental import pallas as pl
from jax.experimental.pallas import tpu as pltpu
from jax.sharding import PartitionSpec as P

LAYERS = 2
NS_STEPS = 5
STEP = 10

AXES = ("dp", "owner")
EPS = 1e-05
NS_A = 3.4445
NS_B = -4.775
NS_C = 2.0315
MOMENTUM = 0.9
LR_MATRIX = 0.5
DECAY_MATRIX = 0.01
BETA_ONE = 0.9
BETA_TWO = 0.999
ADAM_EPS = 1e-08
LR_HEAD = 0.2
DECAY_HEAD = 0.01
LR_VECTOR = 0.4
LANES = 128
SLOT = 8
F32 = jnp.float32
BF16 = jnp.bfloat16


def device_count():
    return lax.axis_size("dp") * lax.axis_size("owner")


def my_index():
    return lax.axis_index("dp") * lax.axis_size("owner") + lax.axis_index("owner")


def exchange(copies):
    return lax.all_to_all(copies, AXES, 0, 0, tiled=True)


def swap(values, bit):
    count = device_count()
    return lax.ppermute(values, AXES, [(src, src ^ (1 << bit)) for src in range(count)])


def halving_sum(blocks, left, order):
    count, rows, lanes = blocks.shape
    left = list(left)
    values = blocks
    for bit in order:
        place = left.index(bit)
        values = values.reshape(2**place, 2, -1, rows, lanes)
        own = (my_index() >> bit) & 1
        kept = lax.dynamic_index_in_dim(values, own, 1, keepdims=False)
        sent = lax.dynamic_index_in_dim(values, 1 - own, 1, keepdims=False)
        values = kept + swap(sent, bit)
        left.pop(place)
    return values.reshape(rows, lanes)


def bits_of(dp_size, owner_size):
    low = owner_size.bit_length() - 1
    high = dp_size.bit_length() - 1
    return list(range(low - 1, -1, -1)) + list(range(low + high - 1, low - 1, -1))


def sigmoid(values):
    return 1.0 / (1.0 + jnp.exp(-values))


def silu(values):
    return values * sigmoid(values)


def silu_slope(values):
    part = sigmoid(values)
    return part * (1.0 + values * (1.0 - part))


def total_of(parts_ref):
    return jnp.sum(parts_ref[...], axis=0)


def row_of(table, start, width):
    count = width // LANES
    return jnp.concatenate([table[start + i : start + i + 1, :] for i in range(count)], axis=1)


def send_rows(out_ref, rows):
    place = 0
    for row in rows:
        for i in range(row.shape[1] // LANES):
            piece = row[:, i * LANES : (i + 1) * LANES]
            out_ref[:, place, :] = jnp.broadcast_to(piece, (out_ref.shape[0], LANES))
            place += 1


def fold_rows(values):
    return jnp.sum(values.reshape(values.shape[0] // 8, 8, values.shape[1]), axis=0)


def norm_of(parts_ref, count, width):
    table = total_of(parts_ref)
    centre = row_of(table, 0, width) / count
    spread = row_of(table, width // LANES, width) / count - centre * centre
    return centre, lax.rsqrt(spread + EPS)


def keep_norm(stat_ref, centre, inverse):
    stat_ref[0:1, :] = centre
    stat_ref[1:2, :] = inverse


class Weights:
    def __init__(self, array, start, rows):
        self.array, self.start, self.rows = array, start, rows
        self.blocks, self.owners = array.shape[0], array.shape[1]
        self.depth = self.blocks * rows
        self.width = self.owners * LANES

    def scratch(self):
        return [
            pltpu.VMEM((self.depth, self.width), BF16),
            pltpu.SemaphoreType.DMA((self.blocks * self.owners,)),
        ]

    def copies(self, ref, buffer, sems):
        return [
            pltpu.make_async_copy(
                ref.at[d, o, pl.ds(self.start, self.rows)],
                buffer.at[pl.ds(d * self.rows, self.rows), pl.ds(o * LANES, LANES)],
                sems.at[d * self.owners + o],
            )
            for d in range(self.blocks)
            for o in range(self.owners)
        ]


def whole(shape):
    return pl.BlockSpec(shape, lambda *ids: (0,) * len(shape), pipeline_mode=pl.Buffered(1))


def strip(rows, width):
    return pl.BlockSpec((rows, width), lambda i: (i, 0))


ANYWHERE = pl.BlockSpec(memory_space=pl.ANY)
SCALAR = pl.BlockSpec(memory_space=pltpu.SMEM)


def launch(kernel, name, grid, operands, specs, outs, out_specs, scratch, flops):
    moved = sum(math.prod(a.shape) * a.dtype.itemsize for a in jax.tree.leaves((operands, outs)))
    return pl.pallas_call(
        kernel,
        name=name,
        grid=grid,
        in_specs=specs,
        out_specs=out_specs,
        out_shape=outs,
        scratch_shapes=scratch,
        cost_estimate=pl.CostEstimate(flops=flops, bytes_accessed=min(moved, 2**25), transcendentals=0),
        compiler_params=pltpu.CompilerParams(
            vmem_limit_bytes=60 * 2**20, dimension_semantics=("arbitrary",) * len(grid)
        ),
    )(*operands)


def out_of(shape, dtype):
    return jax.ShapeDtypeStruct(shape, dtype)


def block_rows(rows, parts):
    for count in range(parts, rows):
        if rows % count == 0 and (rows // count) % 16 == 0:
            return rows // count
    return rows


def dot_nn(left, right):
    return jnp.dot(left, right, preferred_element_type=F32)


def dot_nt(left, right):
    return lax.dot_general(left, right, (((1,), (1,)), ((), ())), preferred_element_type=F32)


def dot_tn(left, right):
    return lax.dot_general(left, right, (((0,), (0,)), ((), ())), preferred_element_type=F32)


def first_reduce(images, masks, weights, devices):
    rows, wide = images.shape
    narrow = weights.width
    strip_rows = block_rows(rows, 3)
    steps = rows // strip_rows

    def kernel(x_ref, mask_ref, w_ref, h_ref, send_ref, buffer, sems, sums):
        step = pl.program_id(0)

        @pl.when(step == 0)
        def _():
            copies = weights.copies(w_ref, buffer, sems)
            for copy in copies:
                copy.start()
            sums[...] = jnp.zeros_like(sums)
            for copy in copies:
                copy.wait()

        hidden = dot_nn(x_ref[...], buffer[...])
        h_ref[...] = hidden
        kept = hidden * mask_ref[:, 0:1]
        sums[0:8] += fold_rows(kept)
        sums[8:16] += fold_rows(kept * hidden)

        @pl.when(step == steps - 1)
        def _():
            send_rows(send_ref, [jnp.sum(sums[i * 8 : i * 8 + 8], axis=0, keepdims=True) for i in range(2)])

    send = (devices, 2 * narrow // LANES, LANES)
    return launch(
        kernel, "reduce_first", (steps,),
        (images, masks, weights.array),
        [strip(strip_rows, wide), strip(strip_rows, 2), ANYWHERE],
        (out_of((rows, narrow), F32), out_of(send, F32)),
        (strip(strip_rows, narrow), whole(send)),
        weights.scratch() + [pltpu.VMEM((16, narrow), F32)],
        2 * rows * wide * narrow,
    )


def store_shifted(shifted, place, values, zone, narrow):
    for offset in range(3):
        moved = values if offset == 1 else pltpu.roll(values, 1 if offset == 0 else zone - 1, 0)
        shifted[pl.ds(place, zone), offset * narrow : (offset + 1) * narrow] = moved.astype(BF16)


def clear_edges(shifted, rows, zone):
    edge = jnp.zeros((zone, shifted.shape[1]), BF16)
    shifted[0:zone] = edge
    shifted[zone + rows : 2 * zone + rows] = edge


def spatial_conv(hidden, parts, counts, norms, masks, weights, layer, zone, devices):
    rows, narrow = hidden.shape
    strip_rows = block_rows(rows, 3)
    steps = rows // strip_rows

    def kernel(
        h_ref, parts_ref, count_ref, norm_ref, mask_ref, w_ref,
        a_ref, out_ref, stat_ref, send_ref, buffer, sems, sums, shifted,
    ):
        step = pl.program_id(0)

        @pl.when(step == 0)
        def _():
            copies = weights.copies(w_ref, buffer, sems)
            for copy in copies:
                copy.start()
            sums[...] = jnp.zeros_like(sums)
            centre, inverse = norm_of(parts_ref, count_ref[0:1, 0:1], narrow)
            keep_norm(stat_ref, centre, inverse)
            gain = norm_ref[0, layer : layer + 1, 0:narrow]
            bias = norm_ref[1, layer : layer + 1, 0:narrow]
            clear_edges(shifted, rows, zone)

            def body(index, carry):
                start = pl.multiple_of(index * zone, zone)
                place = pl.ds(start, zone)
                value = silu((h_ref[place, :] - centre) * inverse * gain + bias) * mask_ref[place, 1:2]
                a_ref[place, :] = value.astype(BF16)
                store_shifted(shifted, pl.multiple_of(start + zone, zone), value, zone, narrow)
                return carry

            lax.fori_loop(0, rows // zone, body, 0)
            for copy in copies:
                copy.wait()

        base = step * strip_rows
        total = None
        for tap in range(3):
            piece = shifted[pl.ds(pl.multiple_of(base + tap * zone, 16), strip_rows), :]
            part = dot_nn(piece, buffer[tap * 3 * narrow : (tap + 1) * 3 * narrow])
            total = part if total is None else total + part
        out_ref[...] = total
        kept = total * mask_ref[pl.ds(pl.multiple_of(base, 16), strip_rows), 0:1]
        sums[0:8] += fold_rows(kept)
        sums[8:16] += fold_rows(kept * total)

        @pl.when(step == steps - 1)
        def _():
            send_rows(send_ref, [jnp.sum(sums[i * 8 : i * 8 + 8], axis=0, keepdims=True) for i in range(2)])

    send = (devices, 2 * narrow // LANES, LANES)
    return launch(
        kernel, "spatial_conv", (steps,),
        (hidden, parts, counts, norms, masks, weights.array),
        [whole(hidden.shape), whole(parts.shape), whole(counts.shape), whole(norms.shape), whole(masks.shape), ANYWHERE],
        (out_of((rows, narrow), BF16), out_of((rows, narrow), F32), out_of((8, narrow), F32), out_of(send, F32)),
        (whole((rows, narrow)), strip(strip_rows, narrow), whole((8, narrow)), whole(send)),
        weights.scratch() + [pltpu.VMEM((16, narrow), F32), pltpu.VMEM((rows + 2 * zone, 3 * narrow), BF16)],
        2 * rows * 9 * narrow * narrow,
    )


def expand(hidden, parts, counts, norms, masks, weights, layer, devices):
    rows, narrow = hidden.shape
    wide = weights.depth
    strip_rows = block_rows(rows, 4)
    steps = rows // strip_rows

    def kernel(
        h_ref, parts_ref, count_ref, norm_ref, mask_ref, w_ref,
        a_ref, out_ref, stat_ref, send_ref, buffer, sems, sums,
    ):
        step = pl.program_id(0)

        @pl.when(step == 0)
        def _():
            copies = weights.copies(w_ref, buffer, sems)
            for copy in copies:
                copy.start()
            sums[...] = jnp.zeros_like(sums)
            centre, inverse = norm_of(parts_ref, count_ref[0:1, 0:1], narrow)
            stat_ref[...] = jnp.zeros_like(stat_ref)
            keep_norm(stat_ref, centre, inverse)
            for copy in copies:
                copy.wait()

        gain = norm_ref[0, layer : layer + 1, narrow : 2 * narrow]
        bias = norm_ref[1, layer : layer + 1, narrow : 2 * narrow]
        value = silu((h_ref[...] - stat_ref[0:1]) * stat_ref[1:2] * gain + bias).astype(BF16)
        a_ref[...] = value
        total = dot_nt(value, buffer[...])
        out_ref[...] = total
        kept = total * mask_ref[:, 0:1]
        sums[0:8] += fold_rows(kept)
        sums[8:16] += fold_rows(kept * total)

        @pl.when(step == steps - 1)
        def _():
            send_rows(send_ref, [jnp.sum(sums[i * 8 : i * 8 + 8], axis=0, keepdims=True) for i in range(2)])

    send = (devices, 2 * wide // LANES, LANES)
    return launch(
        kernel, "expand", (steps,),
        (hidden, parts, counts, norms, masks, weights.array),
        [strip(strip_rows, narrow), whole(parts.shape), whole(counts.shape), whole(norms.shape), strip(strip_rows, 2), ANYWHERE],
        (out_of((rows, narrow), BF16), out_of((rows, wide), F32), out_of((8, narrow), F32), out_of(send, F32)),
        (strip(strip_rows, narrow), strip(strip_rows, wide), whole((8, narrow)), whole(send)),
        weights.scratch() + [pltpu.VMEM((16, wide), F32)],
        2 * rows * wide * narrow,
    )


def close_and_reduce(hidden, inputs, parts, counts, norms, masks, weights, layer, devices):
    rows, wide = hidden.shape
    narrow = weights.width
    strip_rows = block_rows(rows, 6)
    steps = rows // strip_rows

    def kernel(
        h_ref, x_ref, parts_ref, count_ref, norm_ref, mask_ref, w_ref,
        next_ref, low_ref, out_ref, stat_ref, send_ref, buffer, sems, sums,
    ):
        step = pl.program_id(0)

        @pl.when(step == 0)
        def _():
            copies = weights.copies(w_ref, buffer, sems)
            for copy in copies:
                copy.start()
            sums[...] = jnp.zeros_like(sums)
            centre, inverse = norm_of(parts_ref, count_ref[0:1, 0:1], wide)
            stat_ref[...] = jnp.zeros_like(stat_ref)
            keep_norm(stat_ref, centre, inverse)
            for copy in copies:
                copy.wait()

        gain = norm_ref[0, layer : layer + 1, 2 * narrow :]
        bias = norm_ref[1, layer : layer + 1, 2 * narrow :]
        normed = (h_ref[...] - stat_ref[0:1]) * stat_ref[1:2] * gain + bias
        value = silu(x_ref[...].astype(F32) + normed)
        next_ref[...] = value
        low = value.astype(BF16)
        low_ref[...] = low
        total = dot_nn(low, buffer[...])
        out_ref[...] = total
        kept = total * mask_ref[:, 0:1]
        sums[0:8] += fold_rows(kept)
        sums[8:16] += fold_rows(kept * total)

        @pl.when(step == steps - 1)
        def _():
            send_rows(send_ref, [jnp.sum(sums[i * 8 : i * 8 + 8], axis=0, keepdims=True) for i in range(2)])

    send = (devices, 2 * narrow // LANES, LANES)
    return launch(
        kernel, "close_and_reduce", (steps,),
        (hidden, inputs, parts, counts, norms, masks, weights.array),
        [strip(strip_rows, wide), strip(strip_rows, wide), whole(parts.shape), whole(counts.shape), whole(norms.shape), strip(strip_rows, 2), ANYWHERE],
        (out_of((rows, wide), F32), out_of((rows, wide), BF16), out_of((rows, narrow), F32), out_of((8, wide), F32), out_of(send, F32)),
        (strip(strip_rows, wide), strip(strip_rows, wide), strip(strip_rows, narrow), whole((8, wide)), whole(send)),
        weights.scratch() + [pltpu.VMEM((16, narrow), F32)],
        2 * rows * wide * narrow,
    )


def head_step(hidden, inputs, parts, counts, norms, masks, head_all, slot_bias, image_cols, layer, pixels, zone, devices):
    rows, wide = hidden.shape
    images = zone // SLOT
    dp_size, owners, slots, cols = head_all.shape
    classes = owners * slots
    steps = rows // zone
    count_rows = classes // LANES + 8
    tile = LANES

    def kernel(
        h_ref, x_ref, parts_ref, count_ref, norm_ref, mask_ref, head_ref, bias_ref, image_ref,
        ds_ref, stat_ref, send_ref, extra_ref, grad_ref, summed, pooled, sums,
    ):
        step = pl.program_id(0)
        gain = norm_ref[0, layer : layer + 1, norm_ref.shape[2] - wide :]
        bias = norm_ref[1, layer : layer + 1, norm_ref.shape[2] - wide :]

        @pl.when(step == 0)
        def _():
            sums[...] = jnp.zeros_like(sums)
            pooled[...] = jnp.zeros_like(pooled)
            centre, inverse = norm_of(parts_ref, count_ref[0:1, 0:1], wide)
            stat_ref[...] = jnp.zeros_like(stat_ref)
            keep_norm(stat_ref, centre, inverse)

        @pl.when(step < steps)
        def _():
            place = pl.ds(pl.multiple_of(step * zone, zone), zone)
            value = x_ref[...] + ((h_ref[...] - stat_ref[0:1]) * stat_ref[1:2] * gain + bias)
            summed[place, :] = value
            out = silu(value) * mask_ref[:, 1:2]
            pooled[...] += jnp.sum(out.reshape(images, SLOT, wide), axis=1)

        @pl.when(step == steps - 1)
        def _():
            low = (pooled[...] * (1.0 / pixels)).astype(BF16)
            columns = []
            for o in range(owners):
                logit = None
                for d in range(dp_size):
                    part = dot_nt(low[:, d * cols : (d + 1) * cols], head_ref[d, o])
                    logit = part if logit is None else logit + part
                columns.append(logit)
            logits = jnp.concatenate(columns, axis=1) + bias_ref[0:1, :]
            top = jnp.max(logits, axis=1, keepdims=True)
            shifted = jnp.exp(logits - top)
            mass = jnp.sum(shifted, axis=1, keepdims=True)
            log_total = jnp.log(mass) + top
            spots = lax.broadcasted_iota(jnp.int32, logits.shape, 1)
            onehot = (spots == image_ref[:, 0:1]).astype(F32)
            weight = image_ref[:, 1:2].astype(F32)
            picked = jnp.sum(logits * onehot, axis=1, keepdims=True)
            loss = jnp.sum(weight * (log_total - picked), axis=0, keepdims=True)
            residue = weight * (jnp.exp(logits - log_total) - onehot)
            send_rows(
                extra_ref,
                [jnp.sum(residue, axis=0, keepdims=True), jnp.broadcast_to(loss, (1, 8 * LANES))],
            )
            grad = (residue / count_ref[1:2, 0:1]).astype(BF16)
            for d in range(dp_size):
                back = None
                for o in range(owners):
                    mine = grad[:, o * slots : (o + 1) * slots]
                    part = dot_nn(mine, head_ref[d, o])
                    back = part if back is None else back + part
                    weight_part = dot_tn(mine, low[:, d * cols : (d + 1) * cols]).astype(BF16)
                    for i in range(grad_ref.shape[2]):
                        grad_ref[o, d, i] = weight_part[:, i * tile : (i + 1) * tile]
                pooled[:, d * cols : (d + 1) * cols] = back * (1.0 / pixels)

        @pl.when(step >= steps)
        def _():
            place = pl.ds(pl.multiple_of((step - steps) * zone, zone), zone)
            spread = jnp.broadcast_to(pooled[...][:, None, :], (images, SLOT, wide)).reshape(zone, wide)
            ds = spread * silu_slope(summed[place, :]) * mask_ref[:, 1:2]
            ds_ref[...] = ds
            normed = (h_ref[...] - stat_ref[0:1]) * stat_ref[1:2]
            sums[0:8] += fold_rows(ds)
            sums[8:16] += fold_rows(ds * normed)

        @pl.when(step == 2 * steps - 1)
        def _():
            send_rows(send_ref, [jnp.sum(sums[i * 8 : i * 8 + 8], axis=0, keepdims=True) for i in range(2)])

    send = (devices, 2 * wide // LANES, LANES)
    extra = (devices, count_rows, LANES)
    grads = (owners, dp_size, cols // tile, slots, tile)
    again = pl.BlockSpec((zone, wide), lambda i: (lax.rem(i, steps), 0))
    once = pl.BlockSpec((zone, wide), lambda i: (jnp.minimum(i, steps - 1), 0))
    later = pl.BlockSpec((zone, wide), lambda i: (jnp.maximum(i - steps, 0), 0))
    return launch(
        kernel, "head_step", (2 * steps,),
        (hidden, inputs, parts, counts, norms, masks, head_all, slot_bias, image_cols),
        [
            again, once, whole(parts.shape), whole(counts.shape), whole(norms.shape),
            pl.BlockSpec((zone, 2), lambda i: (lax.rem(i, steps), 0)),
            whole(head_all.shape), whole(slot_bias.shape), whole(image_cols.shape),
        ],
        (out_of((rows, wide), F32), out_of((8, wide), F32), out_of(send, F32), out_of(extra, F32), out_of(grads, BF16)),
        (later, whole((8, wide)), whole(send), whole(extra), whole(grads)),
        [pltpu.VMEM((rows, wide), F32), pltpu.VMEM((images, wide), F32), pltpu.VMEM((16, wide), F32)],
        6 * images * classes * wide,
    )


def back_norm(grad, normed, gain, inverse, mask, bias_sum, gain_sum, count):
    return gain * inverse * (grad - mask * (bias_sum + normed * gain_sum) / count)


def back_expand(ds, hidden, parts, stat_wide, counts, norms, masks, narrow_hidden, stat_narrow, weights, layer, devices):
    rows, wide = ds.shape
    narrow = weights.width
    strip_rows = block_rows(rows, 4)
    steps = rows // strip_rows

    def kernel(
        ds_ref, h_ref, parts_ref, stat_ref, count_ref, norm_ref, mask_ref, narrow_ref, narrow_stat, w_ref,
        low_ref, out_ref, send_ref, buffer, sems, sums, terms,
    ):
        step = pl.program_id(0)

        @pl.when(step == 0)
        def _():
            copies = weights.copies(w_ref, buffer, sems)
            for copy in copies:
                copy.start()
            sums[...] = jnp.zeros_like(sums)
            table = total_of(parts_ref)
            terms[0:1] = row_of(table, 0, wide)
            terms[1:2] = row_of(table, wide // LANES, wide)
            for copy in copies:
                copy.wait()

        gain = norm_ref[0, layer : layer + 1, 2 * narrow :]
        normed = (h_ref[...] - stat_ref[0:1]) * stat_ref[1:2]
        low = back_norm(
            ds_ref[...], normed, gain, stat_ref[1:2], mask_ref[:, 0:1], terms[0:1], terms[1:2], count_ref[0:1, 0:1]
        ).astype(BF16)
        low_ref[...] = low
        back = dot_nn(low, buffer[...])
        inner = (narrow_ref[...] - narrow_stat[0:1]) * narrow_stat[1:2]
        value = inner * norm_ref[0, layer : layer + 1, narrow : 2 * narrow] + norm_ref[1, layer : layer + 1, narrow : 2 * narrow]
        total = back * silu_slope(value)
        out_ref[...] = total
        sums[0:8] += fold_rows(total)
        sums[8:16] += fold_rows(total * inner)

        @pl.when(step == steps - 1)
        def _():
            send_rows(send_ref, [jnp.sum(sums[i * 8 : i * 8 + 8], axis=0, keepdims=True) for i in range(2)])

    send = (devices, 2 * narrow // LANES, LANES)
    return launch(
        kernel, "back_expand", (steps,),
        (ds, hidden, parts, stat_wide, counts, norms, masks, narrow_hidden, stat_narrow, weights.array),
        [
            strip(strip_rows, wide), strip(strip_rows, wide), whole(parts.shape), whole(stat_wide.shape), whole(counts.shape),
            whole(norms.shape), strip(strip_rows, 2), strip(strip_rows, narrow), whole(stat_narrow.shape), ANYWHERE,
        ],
        (out_of((rows, wide), BF16), out_of((rows, narrow), F32), out_of(send, F32)),
        (strip(strip_rows, wide), strip(strip_rows, narrow), whole(send)),
        weights.scratch() + [pltpu.VMEM((16, narrow), F32), pltpu.VMEM((8, wide), F32)],
        2 * rows * wide * narrow,
    )


def back_conv(dz, hidden, parts, stat_two, counts, norms, masks, first_hidden, stat_one, weights, layer, zone, devices):
    rows, narrow = dz.shape
    strip_rows = block_rows(rows, 3)
    steps = rows // strip_rows

    def kernel(
        dz_ref, h_ref, parts_ref, stat_ref, count_ref, norm_ref, mask_ref, first_ref, first_stat, w_ref,
        low_ref, out_ref, send_ref, buffer, sems, sums, shifted,
    ):
        step = pl.program_id(0)

        @pl.when(step == 0)
        def _():
            copies = weights.copies(w_ref, buffer, sems)
            for copy in copies:
                copy.start()
            sums[...] = jnp.zeros_like(sums)
            table = total_of(parts_ref)
            bias_sum = row_of(table, 0, narrow)
            gain_sum = row_of(table, narrow // LANES, narrow)
            centre, inverse = stat_ref[0:1], stat_ref[1:2]
            gain = norm_ref[0, layer : layer + 1, narrow : 2 * narrow]
            count = count_ref[0:1, 0:1]
            clear_edges(shifted, rows, zone)

            def body(index, carry):
                start = pl.multiple_of(index * zone, zone)
                place = pl.ds(start, zone)
                normed = (h_ref[place, :] - centre) * inverse
                value = back_norm(dz_ref[place, :], normed, gain, inverse, mask_ref[place, 0:1], bias_sum, gain_sum, count)
                low_ref[place, :] = value.astype(BF16)
                store_shifted(shifted, pl.multiple_of(start + zone, zone), value, zone, narrow)
                return carry

            lax.fori_loop(0, rows // zone, body, 0)
            for copy in copies:
                copy.wait()

        base = step * strip_rows
        total = None
        for tap_row in range(3):
            here = pl.ds(pl.multiple_of(base + (2 - tap_row) * zone, 16), strip_rows)
            for tap_col in range(3):
                tap = tap_row * 3 + tap_col
                piece = shifted[here, (2 - tap_col) * narrow : (3 - tap_col) * narrow]
                part = dot_nt(piece, buffer[tap * narrow : (tap + 1) * narrow])
                total = part if total is None else total + part
        place = pl.ds(pl.multiple_of(base, 16), strip_rows)
        inner = (first_ref[...] - first_stat[0:1]) * first_stat[1:2]
        value = inner * norm_ref[0, layer : layer + 1, 0:narrow] + norm_ref[1, layer : layer + 1, 0:narrow]
        total = total * silu_slope(value) * mask_ref[place, 1:2]
        out_ref[...] = total
        sums[0:8] += fold_rows(total)
        sums[8:16] += fold_rows(total * inner)

        @pl.when(step == steps - 1)
        def _():
            send_rows(send_ref, [jnp.sum(sums[i * 8 : i * 8 + 8], axis=0, keepdims=True) for i in range(2)])

    send = (devices, 2 * narrow // LANES, LANES)
    return launch(
        kernel, "back_conv", (steps,),
        (dz, hidden, parts, stat_two, counts, norms, masks, first_hidden, stat_one, weights.array),
        [
            whole(dz.shape), whole(hidden.shape), whole(parts.shape), whole(stat_two.shape), whole(counts.shape),
            whole(norms.shape), whole(masks.shape), strip(strip_rows, narrow), whole(stat_one.shape), ANYWHERE,
        ],
        (out_of((rows, narrow), BF16), out_of((rows, narrow), F32), out_of(send, F32)),
        (whole((rows, narrow)), strip(strip_rows, narrow), whole(send)),
        weights.scratch() + [pltpu.VMEM((16, narrow), F32), pltpu.VMEM((rows + 2 * zone, 3 * narrow), BF16)],
        2 * rows * 9 * narrow * narrow,
    )


def back_reduce(dz, first_hidden, parts, stat_one, counts, norms, masks, ds, hidden, inputs, stat_wide, weights, layer, devices):
    rows, narrow = dz.shape
    wide = ds.shape[1]
    strip_rows = block_rows(rows, 6)
    steps = rows // strip_rows
    below = layer - 1

    def kernel(
        dz_ref, first_ref, parts_ref, first_stat, count_ref, norm_ref, mask_ref, ds_ref, h_ref, x_ref, stat_ref, w_ref,
        low_ref, out_ref, send_ref, buffer, sems, sums, terms,
    ):
        step = pl.program_id(0)

        @pl.when(step == 0)
        def _():
            copies = weights.copies(w_ref, buffer, sems)
            for copy in copies:
                copy.start()
            sums[...] = jnp.zeros_like(sums)
            table = total_of(parts_ref)
            terms[0:1] = row_of(table, 0, narrow)
            terms[1:2] = row_of(table, narrow // LANES, narrow)
            for copy in copies:
                copy.wait()

        normed = (first_ref[...] - first_stat[0:1]) * first_stat[1:2]
        low = back_norm(
            dz_ref[...], normed, norm_ref[0, layer : layer + 1, 0:narrow], first_stat[1:2], mask_ref[:, 0:1],
            terms[0:1], terms[1:2], count_ref[0:1, 0:1],
        ).astype(BF16)
        low_ref[...] = low
        grad = dot_nt(low, buffer[...]) + ds_ref[...]
        inner = (h_ref[...] - stat_ref[0:1]) * stat_ref[1:2]
        value = inner * norm_ref[0, below : below + 1, 2 * narrow :] + norm_ref[1, below : below + 1, 2 * narrow :]
        total = grad * silu_slope(x_ref[...].astype(F32) + value)
        out_ref[...] = total
        sums[0:8] += fold_rows(total)
        sums[8:16] += fold_rows(total * inner)

        @pl.when(step == steps - 1)
        def _():
            send_rows(send_ref, [jnp.sum(sums[i * 8 : i * 8 + 8], axis=0, keepdims=True) for i in range(2)])

    send = (devices, 2 * wide // LANES, LANES)
    return launch(
        kernel, "back_reduce", (steps,),
        (dz, first_hidden, parts, stat_one, counts, norms, masks, ds, hidden, inputs, stat_wide, weights.array),
        [
            strip(strip_rows, narrow), strip(strip_rows, narrow), whole(parts.shape), whole(stat_one.shape), whole(counts.shape),
            whole(norms.shape), strip(strip_rows, 2), strip(strip_rows, wide), strip(strip_rows, wide), strip(strip_rows, wide),
            whole(stat_wide.shape), ANYWHERE,
        ],
        (out_of((rows, narrow), BF16), out_of((rows, wide), F32), out_of(send, F32)),
        (strip(strip_rows, narrow), strip(strip_rows, wide), whole(send)),
        weights.scratch() + [pltpu.VMEM((16, wide), F32), pltpu.VMEM((8, narrow), F32)],
        2 * rows * wide * narrow,
    )


def last_back(dz, first_hidden, parts, stat_one, counts, norms, masks, layer):
    rows, narrow = dz.shape
    strip_rows = block_rows(rows, 3)

    def kernel(dz_ref, first_ref, parts_ref, first_stat, count_ref, norm_ref, mask_ref, low_ref):
        table = total_of(parts_ref)
        normed = (first_ref[...] - first_stat[0:1]) * first_stat[1:2]
        low_ref[...] = back_norm(
            dz_ref[...], normed, norm_ref[0, layer : layer + 1, 0:narrow], first_stat[1:2], mask_ref[:, 0:1],
            row_of(table, 0, narrow), row_of(table, narrow // LANES, narrow), count_ref[0:1, 0:1],
        ).astype(BF16)

    return launch(
        kernel, "last_back", (rows // strip_rows,),
        (dz, first_hidden, parts, stat_one, counts, norms, masks),
        [
            strip(strip_rows, narrow), strip(strip_rows, narrow), whole(parts.shape), whole(stat_one.shape), whole(counts.shape),
            whole(norms.shape), strip(strip_rows, 2),
        ],
        out_of((rows, narrow), BF16),
        strip(strip_rows, narrow),
        [],
        rows * narrow,
    )


def weight_grad(left, right, owners):
    rows, depth = left.shape
    narrow = right.shape[1]
    tile = min(depth, 512)

    def kernel(left_ref, right_ref, out_ref):
        total = dot_tn(left_ref[...], right_ref[...]).astype(BF16)
        for o in range(owners):
            out_ref[o] = total[:, o * LANES : (o + 1) * LANES]

    return launch(
        kernel, "weight_grad", (depth // tile,),
        (left, right),
        [pl.BlockSpec((rows, tile), lambda i: (0, i)), whole(right.shape)],
        out_of((owners, depth, LANES), BF16),
        pl.BlockSpec((owners, tile, LANES), lambda i: (0, i, 0)),
        [],
        2 * rows * depth * narrow,
    )


def spatial_grad(act, right, owners, zone):
    rows, narrow = act.shape

    def kernel(act_ref, right_ref, out_ref, shifted):
        tap = pl.program_id(0)

        @pl.when(tap == 0)
        def _():
            clear_edges(shifted, rows, zone)

            def body(index, carry):
                start = pl.multiple_of(index * zone, zone)
                value = act_ref[pl.ds(start, zone), :].astype(F32)
                store_shifted(shifted, pl.multiple_of(start + zone, zone), value, zone, narrow)
                return carry

            lax.fori_loop(0, rows // zone, body, 0)

        for tap_col in range(3):
            piece = shifted[pl.ds(pl.multiple_of(tap * zone, zone), rows), tap_col * narrow : (tap_col + 1) * narrow]
            total = dot_tn(piece, right_ref[...]).astype(BF16)
            for o in range(owners):
                out_ref[o, tap_col * narrow : (tap_col + 1) * narrow] = total[:, o * LANES : (o + 1) * LANES]

    return launch(
        kernel, "spatial_grad", (3,),
        (act, right),
        [whole(act.shape), whole(right.shape)],
        out_of((owners, 9 * narrow, LANES), BF16),
        pl.BlockSpec((owners, 3 * narrow, LANES), lambda i: (0, i, 0)),
        [pltpu.VMEM((rows + 2 * zone, 3 * narrow), BF16)],
        2 * rows * 9 * narrow * narrow,
    )


def newton_schulz(moments):
    dp_size, owner_size = lax.axis_size("dp"), lax.axis_size("owner")
    owner = lax.axis_index("owner")
    cols = [moment.shape[0] for moment in moments]
    lanes = moments[0].shape[1]
    low = jnp.concatenate([moment.astype(jnp.bfloat16) for moment in moments], axis=0)
    all_rows = lax.all_gather(low, "owner")
    all_rows = all_rows.transpose(1, 0, 2).reshape(low.shape[0], owner_size * lanes)
    pieces, start = [], 0
    for size in cols:
        pieces.append(all_rows[start : start + size])
        start += size
    side = owner_size * lanes
    pairs = [(i, j) for i in range(owner_size) for j in range(i, owner_size)]
    packed = []
    for piece in pieces:
        gram = dot_tn(piece, piece)
        blocks = [gram[i * lanes : (i + 1) * lanes, j * lanes : (j + 1) * lanes] for i, j in pairs]
        packed.append(jnp.concatenate(blocks, axis=0))
    rows = packed[0].shape[0] // owner_size
    stack = jnp.stack(packed + [jnp.zeros_like(packed[0])] * (dp_size - len(packed)))
    mine = lax.dynamic_slice_in_dim(stack, owner * rows, rows, axis=1)
    bits = [bit for bit in range(device_count().bit_length() - 1) if (1 << bit) >= owner_size]
    values = mine
    for bit in bits:
        place = dp_size.bit_length() - 1 - (len(bits) - bits.index(bit))
        own = (my_index() >> bit) & 1
        values = values.reshape(-1, 2, rows, lanes)
        kept = lax.dynamic_index_in_dim(values, own, 1, keepdims=False)
        sent = lax.dynamic_index_in_dim(values, 1 - own, 1, keepdims=False)
        values = kept + swap(sent, bit)
    whole = lax.all_gather(values[0], "owner", tiled=True)
    blocks = {}
    for number, (i, j) in enumerate(pairs):
        block = whole[number * lanes : (number + 1) * lanes]
        blocks[i, j] = block
        if i != j:
            blocks[j, i] = block.T
    gram = jnp.concatenate(
        [jnp.concatenate([blocks[i, j] for j in range(owner_size)], axis=1) for i in range(owner_size)],
        axis=0,
    )
    dot = lambda left, right: jnp.dot(left, right, precision=lax.Precision.HIGHEST)
    eye = jnp.eye(side, dtype=jnp.float32)
    factor = 1.0 / (jnp.sqrt(jnp.trace(gram)) + 1e-07)
    gram = gram * (factor * factor)
    product = None
    for iteration in range(NS_STEPS):
        square = dot(gram, gram)
        poly = NS_A * eye + NS_B * gram + NS_C * square
        if iteration < NS_STEPS - 1:
            gram = dot(dot(gram, poly), poly)
        product = poly if product is None else dot(product, poly)
    product = (product * factor).astype(jnp.bfloat16)
    own_rows = lax.dynamic_slice_in_dim(product, owner * lanes, lanes, axis=0)
    copies = jnp.broadcast_to(own_rows[None], (dp_size,) + own_rows.shape)
    products = lax.all_to_all(copies, "dp", 0, 0, tiled=True)
    return [dot_nt(piece, products[number]) for number, piece in enumerate(pieces)]


def adamw(weight, grad, first, second, rate, decay):
    first = BETA_ONE * first + (1.0 - BETA_ONE) * grad
    second = BETA_TWO * second + (1.0 - BETA_TWO) * grad * grad
    first_hat = first / (1.0 - BETA_ONE**STEP)
    second_hat = second / (1.0 - BETA_TWO**STEP)
    weight = weight - rate * (first_hat / (jnp.sqrt(second_hat) + ADAM_EPS) + decay * weight)
    return (weight, first, second)


def per_device(
    images, valid_count, labels, loss_weight, w_reduce, w_spatial, w_expand, mom_reduce, mom_spatial, mom_expand,
    head, head_m, head_v, norm_params, norm_m, norm_v, head_bias, bias_m, bias_v,
):
    dp_size, owner_size = lax.axis_size("dp"), lax.axis_size("owner")
    devices = dp_size * owner_size
    count_img, side, _, wide = images.shape
    pixels = side * side
    narrow = w_reduce.shape[1] * owner_size
    zone = count_img * SLOT
    rows = side * zone

    valid = (jnp.arange(count_img, dtype=jnp.int32) < valid_count[0]).astype(jnp.int32)
    weight_img = valid * loss_weight
    tallies = jnp.stack([valid_count[0] * pixels, jnp.sum(weight_img)]).astype(F32)
    tallies = jnp.pad(tallies, (0, 6))[:, None]
    counts = jnp.sum(exchange(jnp.broadcast_to(tallies[None], (devices, 8, LANES))), axis=0)
    weight_total = counts[1, 0]

    rows_of = (w_reduce.shape[2], w_spatial.shape[2], w_expand.shape[2])
    starts = (0, rows_of[0], rows_of[0] + rows_of[1])
    mats = []
    for layer in range(LAYERS):
        parts = (w_reduce[layer], w_spatial[layer], w_expand[layer])
        packed = jnp.concatenate([part.T.astype(BF16) for part in parts], axis=0)
        gathered = lax.all_gather(packed, AXES).reshape(dp_size, owner_size, packed.shape[0], LANES)
        for kind in range(3):
            if dp_size <= 8:
                mats.append(Weights(gathered, starts[kind], rows_of[kind]))
            else:
                piece = gathered[:, :, starts[kind] : starts[kind] + rows_of[kind]]
                piece = piece.transpose(1, 0, 2, 3).reshape(1, owner_size, -1, LANES)
                mats.append(Weights(piece, 0, piece.shape[2]))
    classes = head.shape[0]
    slots = -(-classes // LANES) * LANES
    slack = slots - classes
    head_low = jnp.pad(head.astype(BF16), ((0, slack), (0, 0)))
    head_all = lax.all_gather(head_low, AXES).reshape(dp_size, owner_size, slots, head.shape[1])
    aligned = head.shape[1] % LANES == 0
    if not aligned:
        head_all = head_all.transpose(1, 2, 0, 3).reshape(1, owner_size, slots, wide)
    slot_bias = jnp.pad(head_bias.reshape(owner_size, classes), ((0, 0), (0, slack)), constant_values=-1e30)
    slot_bias = jnp.broadcast_to(slot_bias.reshape(1, -1), (8, owner_size * slots))
    slot_labels = (labels // classes) * slots + labels % classes
    image_cols = jnp.stack([slot_labels, weight_img], axis=1)

    in_map = (jnp.arange(SLOT) < side).astype(F32)
    pad_mask = jnp.broadcast_to(in_map, (side, count_img, SLOT))
    masks = jnp.stack([pad_mask * valid.astype(F32)[:, None], pad_mask], axis=-1).reshape(rows, 2)
    pixels_in = jnp.pad(images, ((0, 0), (0, 0), (0, SLOT - side), (0, 0))).transpose(1, 0, 2, 3).reshape(rows, wide)

    norms = norm_params
    h1, h2, h3, a1, a2, stat1, stat2, stat3 = ([None] * LAYERS for _ in range(8))
    inputs, inputs_low = [pixels_in] + [None] * (LAYERS - 1), [pixels_in] + [None] * (LAYERS - 1)
    h1[0], sums = first_reduce(pixels_in, masks, mats[0], devices)
    for layer in range(LAYERS):
        a1[layer], h2[layer], stat1[layer], sums = spatial_conv(
            h1[layer], exchange(sums), counts, norms, masks, mats[3 * layer + 1], layer, zone, devices
        )
        a2[layer], h3[layer], stat2[layer], sums = expand(
            h2[layer], exchange(sums), counts, norms, masks, mats[3 * layer + 2], layer, devices
        )
        if layer < LAYERS - 1:
            inputs[layer + 1], inputs_low[layer + 1], h1[layer + 1], stat3[layer], sums = close_and_reduce(
                h3[layer], inputs[layer], exchange(sums), counts, norms, masks, mats[3 * layer + 3], layer, devices
            )
    last = LAYERS - 1
    ds, stat3[last], sums, extra, grad_head = head_step(
        h3[last], inputs[last], exchange(sums), counts, norms, masks, head_all, slot_bias, image_cols, last, pixels, zone, devices
    )
    extra = jnp.sum(exchange(extra), axis=0)
    class_rows = owner_size * slots // LANES
    bias_raw = extra[:class_rows].reshape(owner_size, slots)[:, :classes].reshape(-1)
    loss_sum = extra[class_rows, 0]
    grad_bias = bias_raw / weight_total

    norm_sums, grads = ([], [])
    for layer in reversed(range(LAYERS)):
        parts3 = exchange(sums)
        dh3, dz2, sums = back_expand(
            ds, h3[layer], parts3, stat3[layer], counts, norms, masks, h2[layer], stat2[layer], mats[3 * layer + 2], layer, devices
        )
        grad_three = weight_grad(dh3, a2[layer], owner_size)
        parts2 = exchange(sums)
        dh2, dz1, sums = back_conv(
            dz2, h2[layer], parts2, stat2[layer], counts, norms, masks, h1[layer], stat1[layer], mats[3 * layer + 1], layer, zone, devices
        )
        grad_two = spatial_grad(a1[layer], dh2, owner_size, zone)
        parts1 = exchange(sums)
        if layer > 0:
            dh1, ds, sums = back_reduce(
                dz1, h1[layer], parts1, stat1[layer], counts, norms, masks, ds, h3[layer - 1], inputs[layer - 1], stat3[layer - 1],
                mats[3 * layer], layer, devices,
            )
        else:
            dh1 = last_back(dz1, h1[layer], parts1, stat1[layer], counts, norms, masks, layer)
        grad_one = weight_grad(inputs_low[layer], dh1, owner_size)
        grads.insert(0, (grad_one, grad_two, grad_three))
        norm_sums.insert(0, [jnp.sum(part, axis=0).reshape(2, -1) for part in (parts1, parts2, parts3)])
    norm_grad = jnp.stack(
        [jnp.stack([jnp.concatenate([part[kind] for part in norm_sums[layer]]) for layer in range(LAYERS)]) for kind in (1, 0)]
    )

    left = bits_of(dp_size, owner_size)
    sums_of = []
    for layer in range(LAYERS):
        blocks = [grad.reshape(devices, -1, LANES) for grad in grads[layer]]
        if layer == 0:
            bits = list(range(1, len(left)))
            pieces = []
            for number, block in enumerate(blocks):
                turn = number % len(bits)
                pieces.append(halving_sum(block, left, [0] + bits[turn:] + bits[:turn]))
            sums_of.append([piece.astype(F32) for piece in pieces])
            continue
        if aligned:
            head_blocks = grad_head.reshape(devices, -1, LANES)
        else:
            head_blocks = grad_head.reshape(owner_size, wide // LANES, slots, LANES // head.shape[1], head.shape[1])
            head_blocks = head_blocks.transpose(0, 1, 3, 2, 4).reshape(devices, slots, head.shape[1])
        height = sum(rows_of)
        if aligned:
            total = lax.psum_scatter(jnp.concatenate(blocks + [head_blocks], axis=1), ("owner", "dp"), scatter_dimension=0).astype(F32)
            head_sum = total[height:]
        else:
            total = lax.psum_scatter(jnp.concatenate(blocks, axis=1), ("owner", "dp"), scatter_dimension=0).astype(F32)
            head_sum = lax.psum_scatter(head_blocks, ("owner", "dp"), scatter_dimension=0).astype(F32)
        sums_of.append([total[starts[kind] : starts[kind] + rows_of[kind]] for kind in range(3)])
        head_sum = head_sum.reshape(-1, slots, head_sum.shape[-1])[:, :classes].transpose(1, 0, 2).reshape(classes, -1)

    olds = (mom_reduce, mom_spatial, mom_expand)
    moments_t = [MOMENTUM * olds[kind][layer].T + sums_of[layer][kind] for layer in range(LAYERS) for kind in range(3)]
    directions_t = newton_schulz(moments_t)
    moments, directions = (
        [jnp.stack([values[layer * 3 + kind].T for layer in range(LAYERS)]) for kind in range(3)]
        for values in (moments_t, directions_t)
    )
    masters = (w_reduce, w_spatial, w_expand)
    updated = tuple(
        (
            master * (1.0 - LR_MATRIX * DECAY_MATRIX) - LR_MATRIX * direction
            for master, direction in zip(masters, directions)
        )
    )
    new_head, new_head_m, new_head_v = adamw(head, head_sum, head_m, head_v, LR_HEAD, DECAY_HEAD)
    new_norm, new_norm_m, new_norm_v = adamw(norm_params, norm_grad, norm_m, norm_v, LR_VECTOR, 0.0)
    new_bias, new_bias_m, new_bias_v = adamw(head_bias, grad_bias, bias_m, bias_v, LR_VECTOR, 0.0)
    return (
        loss_sum,
        weight_total,
        updated[0],
        updated[1],
        updated[2],
        moments[0],
        moments[1],
        moments[2],
        new_head,
        new_head_m,
        new_head_v,
        new_norm,
        new_norm_m,
        new_norm_v,
        new_bias,
        new_bias_m,
        new_bias_v,
    )


def solution(mesh):
    return jax.shard_map(
        per_device,
        mesh=mesh,
        in_specs=(
            P(("dp", "owner"), None, None, None),
            P(("dp", "owner")),
            P(("dp", "owner")),
            P(("dp", "owner")),
            P(None, "owner", "dp"),
            P(None, "owner", "dp"),
            P(None, "owner", "dp"),
            P(None, "owner", "dp"),
            P(None, "owner", "dp"),
            P(None, "owner", "dp"),
            P("owner", "dp"),
            P("owner", "dp"),
            P("owner", "dp"),
            P(),
            P(),
            P(),
            P(),
            P(),
            P(),
        ),
        out_specs=(
            P(),
            P(),
            P(None, "owner", "dp"),
            P(None, "owner", "dp"),
            P(None, "owner", "dp"),
            P(None, "owner", "dp"),
            P(None, "owner", "dp"),
            P(None, "owner", "dp"),
            P("owner", "dp"),
            P("owner", "dp"),
            P("owner", "dp"),
            P(),
            P(),
            P(),
            P(),
            P(),
            P(),
        ),
        check_vma=False,
    )
```

```python
import functools
import math

import jax
import jax.numpy as jnp
from jax import lax
from jax.experimental import pallas as pl
from jax.experimental.pallas import tpu as pltpu
from jax.sharding import PartitionSpec as P

LAYERS = 2
NS_STEPS = 5
STEP = 10

AXES = ("dp", "owner")
EPS = 1e-05
NS_A = 3.4445
NS_B = -4.775
NS_C = 2.0315
MOMENTUM = 0.9
LR_MATRIX = 0.5
DECAY_MATRIX = 0.01
BETA_ONE = 0.9
BETA_TWO = 0.999
ADAM_EPS = 1e-08
LR_HEAD = 0.2
DECAY_HEAD = 0.01
LR_VECTOR = 0.4
LANES = 128
SLOT = 8
F32 = jnp.float32
BF16 = jnp.bfloat16


def device_count():
    return lax.axis_size("dp") * lax.axis_size("owner")


def my_index():
    return lax.axis_index("dp") * lax.axis_size("owner") + lax.axis_index("owner")


def exchange(copies):
    return lax.all_to_all(copies, AXES, 0, 0, tiled=True)


def swap(values, bit):
    count = device_count()
    return lax.ppermute(values, AXES, [(src, src ^ (1 << bit)) for src in range(count)])


def half_of(values, place, side):
    split = values.reshape((2**place, 2, -1) + values.shape[1:])
    picked = lax.dynamic_index_in_dim(split, side, 1, keepdims=False)
    return picked.reshape((-1,) + values.shape[1:])


class Flow:
    def __init__(self, pairs, left, order):
        self.left, self.order = [bit for bit in left if bit != order[0]], list(order[1:])
        self.kept = [kept for kept, _ in pairs]
        self.sent = [sent for _, sent in pairs]
        self.bit = order[0]
        self.values = self.got = None

    def send(self):
        self.got = [swap(sent, self.bit) for sent in self.sent]
        self.sent = None

    def add(self):
        if self.values is None:
            parts = [kept + got for kept, got in zip(self.kept, self.got)]
            self.values = parts[0] if len(parts) == 1 else jnp.concatenate(parts, axis=1)
        else:
            self.values = half_of(self.values, self.place, self.own) + self.got[0]
        self.got = None

    def split(self):
        if self.order:
            self.bit = self.order.pop(0)
            self.place = self.left.index(self.bit)
            self.left.pop(self.place)
            self.own = (my_index() >> self.bit) & 1
            self.sent = [half_of(self.values, self.place, 1 - self.own)]

    def turn(self):
        if self.got is not None:
            self.add()
            self.split()
        if self.sent is not None:
            self.send()

    def result(self):
        while self.got is not None or self.sent is not None:
            self.turn()
        return self.values[0] if self.values.shape[0] == 1 else self.values


def advance(ahead, flows):
    got = [flow.got for flow in flows]
    ahead, got = lax.optimization_barrier((ahead, got))
    for flow, values in zip(flows, got):
        flow.got = values
        if values is not None:
            flow.add()
            flow.split()
    ahead, sent = lax.optimization_barrier((ahead, [flow.sent for flow in flows]))
    for flow, values in zip(flows, sent):
        flow.sent = values
        if values is not None:
            flow.send()
    return ahead


def bits_of(dp_size, owner_size):
    low = owner_size.bit_length() - 1
    high = dp_size.bit_length() - 1
    return list(range(low - 1, -1, -1)) + list(range(low + high - 1, low - 1, -1))


def sigmoid(values):
    return 1.0 / (1.0 + jnp.exp(-values))


def silu(values):
    return values * sigmoid(values)


def silu_slope(values):
    part = sigmoid(values)
    return part * (1.0 + values * (1.0 - part))


def total_of(parts_ref):
    return jnp.sum(parts_ref[...], axis=0)


def row_of(table, start, width):
    count = width // LANES
    return jnp.concatenate([table[start + i : start + i + 1, :] for i in range(count)], axis=1)


def send_rows(out_ref, rows, place=0):
    for row in rows:
        for i in range(row.shape[1] // LANES):
            piece = row[:, i * LANES : (i + 1) * LANES]
            out_ref[:, place, :] = jnp.broadcast_to(piece, (out_ref.shape[0], LANES))
            place += 1


def fold_rows(values):
    return jnp.sum(values.reshape(values.shape[0] // 8, 8, values.shape[1]), axis=0)


def norm_of(parts_ref, count, width):
    table = total_of(parts_ref)
    centre = row_of(table, 0, width) / count
    spread = row_of(table, width // LANES, width) / count - centre * centre
    return centre, lax.rsqrt(spread + EPS)


def keep_norm(stat_ref, centre, inverse):
    stat_ref[0:1, :] = centre
    stat_ref[1:2, :] = inverse


class Weights:
    def __init__(self, operands, blocks, rows, dp_size, owners, masked):
        self.operands, self.blocks, self.rows, self.masked = operands, blocks, rows, masked
        self.owners = owners
        self.depth, self.width = dp_size * rows, owners * LANES

    def scratch(self):
        return [pltpu.VMEM((self.depth, self.width), BF16), pltpu.SemaphoreType.DMA((len(self.blocks),))]

    def copies(self, refs, buffer, sems):
        shift = self.owners.bit_length() - 1
        me = (lax.axis_index("dp") << shift) | lax.axis_index("owner") if self.masked else 0
        out = []
        for number, (operand, index, start, rows, device, offset) in enumerate(self.blocks):
            device = me ^ device
            base, lane = (device >> shift) * self.rows + offset, (device & (self.owners - 1)) * LANES
            if self.masked:
                base, lane = pl.multiple_of(base, 16), pl.multiple_of(lane, LANES)
            out.append(
                pltpu.make_async_copy(
                    refs[operand].at[index + (pl.ds(start, rows),)],
                    buffer.at[pl.ds(base, rows), pl.ds(lane, LANES)],
                    sems.at[number],
                )
            )
        return out


def gathered_weights(array, start, rows):
    dp_size, owners = array.shape[:2]
    blocks = [(0, (d, o), start, rows, d * owners + o, 0) for d in range(dp_size) for o in range(owners)]
    return Weights([array], blocks, rows, dp_size, owners, False)


def relative_weights(pieces, rows, dp_size, owners):
    operands, blocks = [], []
    for arrays, masks, start, height, offset in pieces:
        for array, names in zip(arrays, masks):
            for index, mask in enumerate(names):
                blocks.append((len(operands), (index,), start, height, mask, offset))
            operands.append(array)
    return Weights(operands, blocks, rows, dp_size, owners, True)


class Gather:
    def __init__(self, block, order):
        self.values, self.masks, self.order = block[None], [0], list(order)

    def send(self):
        self.bit = self.order.pop(0)
        self.got = swap(self.values, self.bit)

    def join(self):
        more = [mask ^ (1 << self.bit) for mask in self.masks]
        if self.order:
            self.values, self.masks = jnp.concatenate([self.values, self.got], axis=0), self.masks + more
        else:
            self.values, self.masks = [self.values, self.got], [self.masks, more]


def meet(flows):
    got = lax.optimization_barrier([flow.got for flow in flows])
    for flow, values in zip(flows, got):
        flow.got = values
        flow.join()


def whole(shape):
    return pl.BlockSpec(shape, lambda *ids: (0,) * len(shape), pipeline_mode=pl.Buffered(1))


def strip(rows, width):
    return pl.BlockSpec((rows, width), lambda i: (i, 0))


ANYWHERE = pl.BlockSpec(memory_space=pl.ANY)
SCALAR = pl.BlockSpec(memory_space=pltpu.SMEM)


def launch(kernel, name, grid, operands, specs, outs, out_specs, scratch, flops):
    arrays, flat_specs, groups = [], [], []
    for operand, spec in zip(operands, specs):
        group = operand.operands if isinstance(operand, Weights) else [operand]
        groups.append(len(group) if isinstance(operand, Weights) else 0)
        arrays += group
        flat_specs += [spec] * len(group)

    def grouped(*refs):
        refs, firsts = list(refs), []
        for count in groups:
            if count:
                firsts.append(tuple(refs[:count]))
                refs = refs[count:]
            else:
                firsts.append(refs.pop(0))
        kernel(*firsts, *refs)

    moved = sum(math.prod(a.shape) * a.dtype.itemsize for a in jax.tree.leaves((arrays, outs)))
    return pl.pallas_call(
        grouped,
        name=name,
        grid=grid,
        in_specs=flat_specs,
        out_specs=out_specs,
        out_shape=outs,
        scratch_shapes=scratch,
        cost_estimate=pl.CostEstimate(flops=flops, bytes_accessed=min(moved, 2**25), transcendentals=0),
        compiler_params=pltpu.CompilerParams(
            vmem_limit_bytes=60 * 2**20, dimension_semantics=("arbitrary",) * len(grid)
        ),
    )(*arrays)


def out_of(shape, dtype):
    return jax.ShapeDtypeStruct(shape, dtype)


def block_rows(rows, parts):
    for count in range(parts, rows):
        if rows % count == 0 and (rows // count) % 16 == 0:
            return rows // count
    return rows


def dot_nn(left, right):
    return jnp.dot(left, right, preferred_element_type=F32)


def dot_nt(left, right):
    return lax.dot_general(left, right, (((1,), (1,)), ((), ())), preferred_element_type=F32)


def dot_tn(left, right):
    return lax.dot_general(left, right, (((0,), (0,)), ((), ())), preferred_element_type=F32)


def store_halves(kept_ref, sent_ref, place, values):
    even = (lax.axis_index("owner") & 1) == 0
    for pair in range(len(values) // 2):
        first, second = values[2 * pair], values[2 * pair + 1]
        kept_ref[(pair,) + place] = jnp.where(even, first, second).astype(BF16)
        sent_ref[(pair,) + place] = jnp.where(even, second, first).astype(BF16)


def first_reduce(images, masks, weights, devices):
    rows, wide = images.shape
    narrow = weights.width
    strip_rows = block_rows(rows, 3)
    steps = rows // strip_rows

    def kernel(x_ref, mask_ref, w_ref, h_ref, send_ref, buffer, sems, sums):
        step = pl.program_id(0)

        @pl.when(step == 0)
        def _():
            copies = weights.copies(w_ref, buffer, sems)
            for copy in copies:
                copy.start()
            sums[...] = jnp.zeros_like(sums)
            for copy in copies:
                copy.wait()

        hidden = dot_nn(x_ref[...], buffer[...])
        h_ref[...] = hidden
        kept = hidden * mask_ref[:, 0:1]
        sums[0:8] += fold_rows(kept)
        sums[8:16] += fold_rows(kept * hidden)

        @pl.when(step == steps - 1)
        def _():
            send_rows(send_ref, [jnp.sum(sums[i * 8 : i * 8 + 8], axis=0, keepdims=True) for i in range(2)])

    send = (devices, 2 * narrow // LANES, LANES)
    return launch(
        kernel, "reduce_first", (steps,),
        (images, masks, weights),
        [strip(strip_rows, wide), strip(strip_rows, 2), ANYWHERE],
        (out_of((rows, narrow), F32), out_of(send, F32)),
        (strip(strip_rows, narrow), whole(send)),
        weights.scratch() + [pltpu.VMEM((16, narrow), F32)],
        2 * rows * wide * narrow,
    )


def store_shifted(shifted, place, values, zone, narrow):
    for offset in range(3):
        moved = values if offset == 1 else pltpu.roll(values, 1 if offset == 0 else zone - 1, 0)
        shifted[pl.ds(place, zone), offset * narrow : (offset + 1) * narrow] = moved.astype(BF16)


def clear_edges(shifted, rows, zone):
    edge = jnp.zeros((zone, shifted.shape[1]), BF16)
    shifted[0:zone] = edge
    shifted[zone + rows : 2 * zone + rows] = edge


def spatial_conv(hidden, parts, counts, norms, masks, weights, layer, zone, devices):
    rows, narrow = hidden.shape
    strip_rows = block_rows(rows, 3)
    steps = rows // strip_rows

    def kernel(
        h_ref, parts_ref, count_ref, norm_ref, mask_ref, w_ref,
        a_ref, out_ref, stat_ref, send_ref, buffer, sems, sums, shifted,
    ):
        step = pl.program_id(0)

        @pl.when(step == 0)
        def _():
            copies = weights.copies(w_ref, buffer, sems)
            for copy in copies:
                copy.start()
            sums[...] = jnp.zeros_like(sums)
            centre, inverse = norm_of(parts_ref, count_ref[0:1, 0:1], narrow)
            keep_norm(stat_ref, centre, inverse)
            gain = norm_ref[0, layer : layer + 1, 0:narrow]
            bias = norm_ref[1, layer : layer + 1, 0:narrow]
            clear_edges(shifted, rows, zone)

            def body(index, carry):
                start = pl.multiple_of(index * zone, zone)
                place = pl.ds(start, zone)
                value = silu((h_ref[place, :] - centre) * inverse * gain + bias) * mask_ref[place, 1:2]
                a_ref[place, :] = value.astype(BF16)
                store_shifted(shifted, pl.multiple_of(start + zone, zone), value, zone, narrow)
                return carry

            lax.fori_loop(0, rows // zone, body, 0)
            for copy in copies:
                copy.wait()

        base = step * strip_rows
        total = None
        for tap in range(3):
            piece = shifted[pl.ds(pl.multiple_of(base + tap * zone, 16), strip_rows), :]
            part = dot_nn(piece, buffer[tap * 3 * narrow : (tap + 1) * 3 * narrow])
            total = part if total is None else total + part
        out_ref[...] = total
        kept = total * mask_ref[pl.ds(pl.multiple_of(base, 16), strip_rows), 0:1]
        sums[0:8] += fold_rows(kept)
        sums[8:16] += fold_rows(kept * total)

        @pl.when(step == steps - 1)
        def _():
            send_rows(send_ref, [jnp.sum(sums[i * 8 : i * 8 + 8], axis=0, keepdims=True) for i in range(2)])

    send = (devices, 2 * narrow // LANES, LANES)
    return launch(
        kernel, "spatial_conv", (steps,),
        (hidden, parts, counts, norms, masks, weights),
        [whole(hidden.shape), whole(parts.shape), whole(counts.shape), whole(norms.shape), whole(masks.shape), ANYWHERE],
        (out_of((rows, narrow), BF16), out_of((rows, narrow), F32), out_of((8, narrow), F32), out_of(send, F32)),
        (whole((rows, narrow)), strip(strip_rows, narrow), whole((8, narrow)), whole(send)),
        weights.scratch() + [pltpu.VMEM((16, narrow), F32), pltpu.VMEM((rows + 2 * zone, 3 * narrow), BF16)],
        2 * rows * 9 * narrow * narrow,
    )


def expand(hidden, parts, counts, norms, masks, weights, layer, devices):
    rows, narrow = hidden.shape
    wide = weights.depth
    strip_rows = block_rows(rows, 4)
    steps = rows // strip_rows

    def kernel(
        h_ref, parts_ref, count_ref, norm_ref, mask_ref, w_ref,
        a_ref, out_ref, stat_ref, send_ref, buffer, sems, sums,
    ):
        step = pl.program_id(0)

        @pl.when(step == 0)
        def _():
            copies = weights.copies(w_ref, buffer, sems)
            for copy in copies:
                copy.start()
            sums[...] = jnp.zeros_like(sums)
            centre, inverse = norm_of(parts_ref, count_ref[0:1, 0:1], narrow)
            stat_ref[...] = jnp.zeros_like(stat_ref)
            keep_norm(stat_ref, centre, inverse)
            for copy in copies:
                copy.wait()

        gain = norm_ref[0, layer : layer + 1, narrow : 2 * narrow]
        bias = norm_ref[1, layer : layer + 1, narrow : 2 * narrow]
        value = silu((h_ref[...] - stat_ref[0:1]) * stat_ref[1:2] * gain + bias).astype(BF16)
        a_ref[...] = value
        total = dot_nt(value, buffer[...])
        out_ref[...] = total
        kept = total * mask_ref[:, 0:1]
        sums[0:8] += fold_rows(kept)
        sums[8:16] += fold_rows(kept * total)

        @pl.when(step == steps - 1)
        def _():
            send_rows(send_ref, [jnp.sum(sums[i * 8 : i * 8 + 8], axis=0, keepdims=True) for i in range(2)])

    send = (devices, 2 * wide // LANES, LANES)
    return launch(
        kernel, "expand", (steps,),
        (hidden, parts, counts, norms, masks, weights),
        [strip(strip_rows, narrow), whole(parts.shape), whole(counts.shape), whole(norms.shape), strip(strip_rows, 2), ANYWHERE],
        (out_of((rows, narrow), BF16), out_of((rows, wide), F32), out_of((8, narrow), F32), out_of(send, F32)),
        (strip(strip_rows, narrow), strip(strip_rows, wide), whole((8, narrow)), whole(send)),
        weights.scratch() + [pltpu.VMEM((16, wide), F32)],
        2 * rows * wide * narrow,
    )


def close_and_reduce(hidden, inputs, parts, counts, norms, masks, weights, layer, devices):
    rows, wide = hidden.shape
    narrow = weights.width
    strip_rows = block_rows(rows, 6)
    steps = rows // strip_rows

    def kernel(
        h_ref, x_ref, parts_ref, count_ref, norm_ref, mask_ref, w_ref,
        next_ref, low_ref, out_ref, stat_ref, send_ref, buffer, sems, sums,
    ):
        step = pl.program_id(0)

        @pl.when(step == 0)
        def _():
            copies = weights.copies(w_ref, buffer, sems)
            for copy in copies:
                copy.start()
            sums[...] = jnp.zeros_like(sums)
            centre, inverse = norm_of(parts_ref, count_ref[0:1, 0:1], wide)
            stat_ref[...] = jnp.zeros_like(stat_ref)
            keep_norm(stat_ref, centre, inverse)
            for copy in copies:
                copy.wait()

        gain = norm_ref[0, layer : layer + 1, 2 * narrow :]
        bias = norm_ref[1, layer : layer + 1, 2 * narrow :]
        normed = (h_ref[...] - stat_ref[0:1]) * stat_ref[1:2] * gain + bias
        value = silu(x_ref[...].astype(F32) + normed)
        next_ref[...] = value
        low = value.astype(BF16)
        low_ref[...] = low
        total = dot_nn(low, buffer[...])
        out_ref[...] = total
        kept = total * mask_ref[:, 0:1]
        sums[0:8] += fold_rows(kept)
        sums[8:16] += fold_rows(kept * total)

        @pl.when(step == steps - 1)
        def _():
            send_rows(send_ref, [jnp.sum(sums[i * 8 : i * 8 + 8], axis=0, keepdims=True) for i in range(2)])

    send = (devices, 2 * narrow // LANES, LANES)
    return launch(
        kernel, "close_and_reduce", (steps,),
        (hidden, inputs, parts, counts, norms, masks, weights),
        [strip(strip_rows, wide), strip(strip_rows, wide), whole(parts.shape), whole(counts.shape), whole(norms.shape), strip(strip_rows, 2), ANYWHERE],
        (out_of((rows, wide), F32), out_of((rows, wide), BF16), out_of((rows, narrow), F32), out_of((8, wide), F32), out_of(send, F32)),
        (strip(strip_rows, wide), strip(strip_rows, wide), strip(strip_rows, narrow), whole((8, wide)), whole(send)),
        weights.scratch() + [pltpu.VMEM((16, narrow), F32)],
        2 * rows * wide * narrow,
    )


def head_step(hidden, inputs, parts, counts, norms, masks, head_all, slot_bias, image_cols, layer, pixels, zone, devices):
    rows, wide = hidden.shape
    images = zone // SLOT
    dp_size, owners, slots, cols = head_all.shape
    classes = owners * slots
    steps = rows // zone
    count_rows = classes // LANES + 8
    tile = LANES

    def kernel(
        h_ref, x_ref, parts_ref, count_ref, norm_ref, mask_ref, head_ref, bias_ref, image_ref,
        ds_ref, stat_ref, send_ref, kept_ref, sent_ref, summed, pooled, sums,
    ):
        step = pl.program_id(0)
        gain = norm_ref[0, layer : layer + 1, norm_ref.shape[2] - wide :]
        bias = norm_ref[1, layer : layer + 1, norm_ref.shape[2] - wide :]

        @pl.when(step == 0)
        def _():
            sums[...] = jnp.zeros_like(sums)
            pooled[...] = jnp.zeros_like(pooled)
            centre, inverse = norm_of(parts_ref, count_ref[0:1, 0:1], wide)
            stat_ref[...] = jnp.zeros_like(stat_ref)
            keep_norm(stat_ref, centre, inverse)

        @pl.when(step < steps)
        def _():
            place = pl.ds(pl.multiple_of(step * zone, zone), zone)
            value = x_ref[...] + ((h_ref[...] - stat_ref[0:1]) * stat_ref[1:2] * gain + bias)
            summed[place, :] = value
            out = silu(value) * mask_ref[:, 1:2]
            pooled[...] += jnp.sum(out.reshape(images, SLOT, wide), axis=1)

        @pl.when(step == steps - 1)
        def _():
            low = (pooled[...] * (1.0 / pixels)).astype(BF16)
            columns = []
            for o in range(owners):
                logit = None
                for d in range(dp_size):
                    part = dot_nt(low[:, d * cols : (d + 1) * cols], head_ref[d, o])
                    logit = part if logit is None else logit + part
                columns.append(logit)
            logits = jnp.concatenate(columns, axis=1) + bias_ref[0:1, :]
            top = jnp.max(logits, axis=1, keepdims=True)
            shifted = jnp.exp(logits - top)
            mass = jnp.sum(shifted, axis=1, keepdims=True)
            log_total = jnp.log(mass) + top
            spots = lax.broadcasted_iota(jnp.int32, logits.shape, 1)
            onehot = (spots == image_ref[:, 0:1]).astype(F32)
            weight = image_ref[:, 1:2].astype(F32)
            picked = jnp.sum(logits * onehot, axis=1, keepdims=True)
            loss = jnp.sum(weight * (log_total - picked), axis=0, keepdims=True)
            residue = weight * (jnp.exp(logits - log_total) - onehot)
            send_rows(
                send_ref,
                [jnp.sum(residue, axis=0, keepdims=True), jnp.broadcast_to(loss, (1, 8 * LANES))],
                2 * wide // LANES,
            )
            grad = (residue / count_ref[1:2, 0:1]).astype(BF16)
            for d in range(dp_size):
                back, weight_parts = None, []
                for o in range(owners):
                    mine = grad[:, o * slots : (o + 1) * slots]
                    part = dot_nn(mine, head_ref[d, o])
                    back = part if back is None else back + part
                    weight_parts.append(dot_tn(mine, low[:, d * cols : (d + 1) * cols]))
                for i in range(kept_ref.shape[2]):
                    store_halves(kept_ref, sent_ref, (d, i), [part[:, i * tile : (i + 1) * tile] for part in weight_parts])
                pooled[:, d * cols : (d + 1) * cols] = back * (1.0 / pixels)

        @pl.when(step >= steps)
        def _():
            place = pl.ds(pl.multiple_of((step - steps) * zone, zone), zone)
            spread = jnp.broadcast_to(pooled[...][:, None, :], (images, SLOT, wide)).reshape(zone, wide)
            ds = spread * silu_slope(summed[place, :]) * mask_ref[:, 1:2]
            ds_ref[...] = ds
            normed = (h_ref[...] - stat_ref[0:1]) * stat_ref[1:2]
            sums[0:8] += fold_rows(ds)
            sums[8:16] += fold_rows(ds * normed)

        @pl.when(step == 2 * steps - 1)
        def _():
            send_rows(send_ref, [jnp.sum(sums[i * 8 : i * 8 + 8], axis=0, keepdims=True) for i in range(2)])

    send = (devices, 2 * wide // LANES + count_rows, LANES)
    grads = (owners // 2, dp_size, cols // tile, slots, tile)
    again = pl.BlockSpec((zone, wide), lambda i: (lax.rem(i, steps), 0))
    once = pl.BlockSpec((zone, wide), lambda i: (jnp.minimum(i, steps - 1), 0))
    later = pl.BlockSpec((zone, wide), lambda i: (jnp.maximum(i - steps, 0), 0))
    return launch(
        kernel, "head_step", (2 * steps,),
        (hidden, inputs, parts, counts, norms, masks, head_all, slot_bias, image_cols),
        [
            again, once, whole(parts.shape), whole(counts.shape), whole(norms.shape),
            pl.BlockSpec((zone, 2), lambda i: (lax.rem(i, steps), 0)),
            whole(head_all.shape), whole(slot_bias.shape), whole(image_cols.shape),
        ],
        (out_of((rows, wide), F32), out_of((8, wide), F32), out_of(send, F32), out_of(grads, BF16), out_of(grads, BF16)),
        (later, whole((8, wide)), whole(send), whole(grads), whole(grads)),
        [pltpu.VMEM((rows, wide), F32), pltpu.VMEM((images, wide), F32), pltpu.VMEM((16, wide), F32)],
        6 * images * classes * wide,
    )


def back_norm(grad, normed, gain, inverse, mask, bias_sum, gain_sum, count):
    return gain * inverse * (grad - mask * (bias_sum + normed * gain_sum) / count)


def back_expand(ds, hidden, parts, stat_wide, counts, norms, masks, narrow_hidden, stat_narrow, weights, layer, devices):
    rows, wide = ds.shape
    narrow = weights.width
    strip_rows = block_rows(rows, 4)
    steps = rows // strip_rows

    def kernel(
        ds_ref, h_ref, parts_ref, stat_ref, count_ref, norm_ref, mask_ref, narrow_ref, narrow_stat, w_ref,
        low_ref, out_ref, send_ref, buffer, sems, sums, terms,
    ):
        step = pl.program_id(0)

        @pl.when(step == 0)
        def _():
            copies = weights.copies(w_ref, buffer, sems)
            for copy in copies:
                copy.start()
            sums[...] = jnp.zeros_like(sums)
            table = total_of(parts_ref)
            terms[0:1] = row_of(table, 0, wide)
            terms[1:2] = row_of(table, wide // LANES, wide)
            for copy in copies:
                copy.wait()

        gain = norm_ref[0, layer : layer + 1, 2 * narrow :]
        normed = (h_ref[...] - stat_ref[0:1]) * stat_ref[1:2]
        low = back_norm(
            ds_ref[...], normed, gain, stat_ref[1:2], mask_ref[:, 0:1], terms[0:1], terms[1:2], count_ref[0:1, 0:1]
        ).astype(BF16)
        low_ref[...] = low
        back = dot_nn(low, buffer[...])
        inner = (narrow_ref[...] - narrow_stat[0:1]) * narrow_stat[1:2]
        value = inner * norm_ref[0, layer : layer + 1, narrow : 2 * narrow] + norm_ref[1, layer : layer + 1, narrow : 2 * narrow]
        total = back * silu_slope(value)
        out_ref[...] = total
        sums[0:8] += fold_rows(total)
        sums[8:16] += fold_rows(total * inner)

        @pl.when(step == steps - 1)
        def _():
            send_rows(send_ref, [jnp.sum(sums[i * 8 : i * 8 + 8], axis=0, keepdims=True) for i in range(2)])

    send = (devices, 2 * narrow // LANES, LANES)
    return launch(
        kernel, "back_expand", (steps,),
        (ds, hidden, parts, stat_wide, counts, norms, masks, narrow_hidden, stat_narrow, weights),
        [
            strip(strip_rows, wide), strip(strip_rows, wide), whole(parts.shape), whole(stat_wide.shape), whole(counts.shape),
            whole(norms.shape), strip(strip_rows, 2), strip(strip_rows, narrow), whole(stat_narrow.shape), ANYWHERE,
        ],
        (out_of((rows, wide), BF16), out_of((rows, narrow), F32), out_of(send, F32)),
        (strip(strip_rows, wide), strip(strip_rows, narrow), whole(send)),
        weights.scratch() + [pltpu.VMEM((16, narrow), F32), pltpu.VMEM((8, wide), F32)],
        2 * rows * wide * narrow,
    )


def back_conv(dz, hidden, parts, stat_two, counts, norms, masks, first_hidden, stat_one, weights, layer, zone, devices):
    rows, narrow = dz.shape
    strip_rows = block_rows(rows, 3)
    steps = rows // strip_rows

    def kernel(
        dz_ref, h_ref, parts_ref, stat_ref, count_ref, norm_ref, mask_ref, first_ref, first_stat, w_ref,
        low_ref, out_ref, send_ref, buffer, sems, sums, shifted,
    ):
        step = pl.program_id(0)

        @pl.when(step == 0)
        def _():
            copies = weights.copies(w_ref, buffer, sems)
            for copy in copies:
                copy.start()
            sums[...] = jnp.zeros_like(sums)
            table = total_of(parts_ref)
            bias_sum = row_of(table, 0, narrow)
            gain_sum = row_of(table, narrow // LANES, narrow)
            centre, inverse = stat_ref[0:1], stat_ref[1:2]
            gain = norm_ref[0, layer : layer + 1, narrow : 2 * narrow]
            count = count_ref[0:1, 0:1]
            clear_edges(shifted, rows, zone)

            def body(index, carry):
                start = pl.multiple_of(index * zone, zone)
                place = pl.ds(start, zone)
                normed = (h_ref[place, :] - centre) * inverse
                value = back_norm(dz_ref[place, :], normed, gain, inverse, mask_ref[place, 0:1], bias_sum, gain_sum, count)
                low_ref[place, :] = value.astype(BF16)
                store_shifted(shifted, pl.multiple_of(start + zone, zone), value, zone, narrow)
                return carry

            lax.fori_loop(0, rows // zone, body, 0)
            for copy in copies:
                copy.wait()

        base = step * strip_rows
        total = None
        for tap_row in range(3):
            here = pl.ds(pl.multiple_of(base + (2 - tap_row) * zone, 16), strip_rows)
            for tap_col in range(3):
                tap = tap_row * 3 + tap_col
                piece = shifted[here, (2 - tap_col) * narrow : (3 - tap_col) * narrow]
                part = dot_nt(piece, buffer[tap * narrow : (tap + 1) * narrow])
                total = part if total is None else total + part
        place = pl.ds(pl.multiple_of(base, 16), strip_rows)
        inner = (first_ref[...] - first_stat[0:1]) * first_stat[1:2]
        value = inner * norm_ref[0, layer : layer + 1, 0:narrow] + norm_ref[1, layer : layer + 1, 0:narrow]
        total = total * silu_slope(value) * mask_ref[place, 1:2]
        out_ref[...] = total
        sums[0:8] += fold_rows(total)
        sums[8:16] += fold_rows(total * inner)

        @pl.when(step == steps - 1)
        def _():
            send_rows(send_ref, [jnp.sum(sums[i * 8 : i * 8 + 8], axis=0, keepdims=True) for i in range(2)])

    send = (devices, 2 * narrow // LANES, LANES)
    return launch(
        kernel, "back_conv", (steps,),
        (dz, hidden, parts, stat_two, counts, norms, masks, first_hidden, stat_one, weights),
        [
            whole(dz.shape), whole(hidden.shape), whole(parts.shape), whole(stat_two.shape), whole(counts.shape),
            whole(norms.shape), whole(masks.shape), strip(strip_rows, narrow), whole(stat_one.shape), ANYWHERE,
        ],
        (out_of((rows, narrow), BF16), out_of((rows, narrow), F32), out_of(send, F32)),
        (whole((rows, narrow)), strip(strip_rows, narrow), whole(send)),
        weights.scratch() + [pltpu.VMEM((16, narrow), F32), pltpu.VMEM((rows + 2 * zone, 3 * narrow), BF16)],
        2 * rows * 9 * narrow * narrow,
    )


def back_reduce(dz, first_hidden, parts, stat_one, counts, norms, masks, ds, hidden, inputs, stat_wide, weights, layer, devices):
    rows, narrow = dz.shape
    wide = ds.shape[1]
    strip_rows = block_rows(rows, 6)
    steps = rows // strip_rows
    below = layer - 1

    def kernel(
        dz_ref, first_ref, parts_ref, first_stat, count_ref, norm_ref, mask_ref, ds_ref, h_ref, x_ref, stat_ref, w_ref,
        low_ref, out_ref, send_ref, buffer, sems, sums, terms,
    ):
        step = pl.program_id(0)

        @pl.when(step == 0)
        def _():
            copies = weights.copies(w_ref, buffer, sems)
            for copy in copies:
                copy.start()
            sums[...] = jnp.zeros_like(sums)
            table = total_of(parts_ref)
            terms[0:1] = row_of(table, 0, narrow)
            terms[1:2] = row_of(table, narrow // LANES, narrow)
            for copy in copies:
                copy.wait()

        normed = (first_ref[...] - first_stat[0:1]) * first_stat[1:2]
        low = back_norm(
            dz_ref[...], normed, norm_ref[0, layer : layer + 1, 0:narrow], first_stat[1:2], mask_ref[:, 0:1],
            terms[0:1], terms[1:2], count_ref[0:1, 0:1],
        ).astype(BF16)
        low_ref[...] = low
        grad = dot_nt(low, buffer[...]) + ds_ref[...]
        inner = (h_ref[...] - stat_ref[0:1]) * stat_ref[1:2]
        value = inner * norm_ref[0, below : below + 1, 2 * narrow :] + norm_ref[1, below : below + 1, 2 * narrow :]
        total = grad * silu_slope(x_ref[...].astype(F32) + value)
        out_ref[...] = total
        sums[0:8] += fold_rows(total)
        sums[8:16] += fold_rows(total * inner)

        @pl.when(step == steps - 1)
        def _():
            send_rows(send_ref, [jnp.sum(sums[i * 8 : i * 8 + 8], axis=0, keepdims=True) for i in range(2)])

    send = (devices, 2 * wide // LANES, LANES)
    return launch(
        kernel, "back_reduce", (steps,),
        (dz, first_hidden, parts, stat_one, counts, norms, masks, ds, hidden, inputs, stat_wide, weights),
        [
            strip(strip_rows, narrow), strip(strip_rows, narrow), whole(parts.shape), whole(stat_one.shape), whole(counts.shape),
            whole(norms.shape), strip(strip_rows, 2), strip(strip_rows, wide), strip(strip_rows, wide), strip(strip_rows, wide),
            whole(stat_wide.shape), ANYWHERE,
        ],
        (out_of((rows, narrow), BF16), out_of((rows, wide), F32), out_of(send, F32)),
        (strip(strip_rows, narrow), strip(strip_rows, wide), whole(send)),
        weights.scratch() + [pltpu.VMEM((16, wide), F32), pltpu.VMEM((8, narrow), F32)],
        2 * rows * wide * narrow,
    )


def last_back(dz, first_hidden, parts, stat_one, counts, norms, masks, layer):
    rows, narrow = dz.shape
    strip_rows = block_rows(rows, 3)

    def kernel(dz_ref, first_ref, parts_ref, first_stat, count_ref, norm_ref, mask_ref, low_ref):
        table = total_of(parts_ref)
        normed = (first_ref[...] - first_stat[0:1]) * first_stat[1:2]
        low_ref[...] = back_norm(
            dz_ref[...], normed, norm_ref[0, layer : layer + 1, 0:narrow], first_stat[1:2], mask_ref[:, 0:1],
            row_of(table, 0, narrow), row_of(table, narrow // LANES, narrow), count_ref[0:1, 0:1],
        ).astype(BF16)

    return launch(
        kernel, "last_back", (rows // strip_rows,),
        (dz, first_hidden, parts, stat_one, counts, norms, masks),
        [
            strip(strip_rows, narrow), strip(strip_rows, narrow), whole(parts.shape), whole(stat_one.shape), whole(counts.shape),
            whole(norms.shape), strip(strip_rows, 2),
        ],
        out_of((rows, narrow), BF16),
        strip(strip_rows, narrow),
        [],
        rows * narrow,
    )


def weight_grad(left, right, owners):
    rows, depth = left.shape
    narrow = right.shape[1]
    tile = min(depth, 512)

    def kernel(left_ref, right_ref, kept_ref, sent_ref):
        total = dot_tn(left_ref[...], right_ref[...])
        store_halves(kept_ref, sent_ref, (), [total[:, o * LANES : (o + 1) * LANES] for o in range(owners)])

    half = out_of((owners // 2, depth, LANES), BF16)
    half_spec = pl.BlockSpec((owners // 2, tile, LANES), lambda i: (0, i, 0))

    return launch(
        kernel, "weight_grad", (depth // tile,),
        (left, right),
        [pl.BlockSpec((rows, tile), lambda i: (0, i)), whole(right.shape)],
        (half, half),
        (half_spec, half_spec),
        [],
        2 * rows * depth * narrow,
    )


def spatial_grad(act, right, owners, zone):
    rows, narrow = act.shape

    def kernel(act_ref, right_ref, kept_ref, sent_ref, shifted):
        tap = pl.program_id(0)

        @pl.when(tap == 0)
        def _():
            clear_edges(shifted, rows, zone)

            def body(index, carry):
                start = pl.multiple_of(index * zone, zone)
                value = act_ref[pl.ds(start, zone), :].astype(F32)
                store_shifted(shifted, pl.multiple_of(start + zone, zone), value, zone, narrow)
                return carry

            lax.fori_loop(0, rows // zone, body, 0)

        for tap_col in range(3):
            piece = shifted[pl.ds(pl.multiple_of(tap * zone, zone), rows), tap_col * narrow : (tap_col + 1) * narrow]
            total = dot_tn(piece, right_ref[...])
            place = (slice(tap_col * narrow, (tap_col + 1) * narrow),)
            store_halves(kept_ref, sent_ref, place, [total[:, o * LANES : (o + 1) * LANES] for o in range(owners)])

    half = out_of((owners // 2, 9 * narrow, LANES), BF16)
    half_spec = pl.BlockSpec((owners // 2, 3 * narrow, LANES), lambda i: (0, i, 0))

    return launch(
        kernel, "spatial_grad", (3,),
        (act, right),
        [whole(act.shape), whole(right.shape)],
        (half, half),
        (half_spec, half_spec),
        [pltpu.VMEM((rows + 2 * zone, 3 * narrow), BF16)],
        2 * rows * 9 * narrow * narrow,
    )


def padded(values):
    return jnp.pad(values, ((0, -values.shape[0] % 16), (0, 0)))


def gather_rows(moments_t):
    low = [padded(moment.astype(BF16)) for moment in moments_t]
    starts = [sum(part.shape[0] for part in low[:i]) for i in range(len(low))]
    return lax.all_gather(jnp.concatenate(low, axis=0), "owner"), starts


def upper_pairs(owners):
    return [(i, j) for i in range(owners) for j in range(i, owners)]


def own_grams(gathered, starts, sizes):
    owners = gathered.shape[0]
    pairs = upper_pairs(owners)
    share = len(pairs) * LANES // owners

    def kernel(all_ref, out_ref, packed):
        for number, (start, size) in enumerate(zip(starts, sizes)):
            for place, (i, j) in enumerate(pairs):
                packed[place * LANES : (place + 1) * LANES] = dot_tn(
                    all_ref[i, start : start + size, :], all_ref[j, start : start + size, :]
                )
            own = pl.multiple_of(lax.axis_index("owner") * share, 8)
            out_ref[number] = packed[pl.ds(own, share), :]

    shape = (len(sizes), share, LANES)
    return launch(
        kernel, "own_grams", (1,), (gathered,), [whole(gathered.shape)], out_of(shape, F32), whole(shape),
        [pltpu.VMEM((len(pairs) * LANES, LANES), F32)], 2 * sum(sizes) * len(pairs) * LANES * LANES,
    )


def dp_bits():
    low = lax.axis_size("owner").bit_length() - 1
    return list(range(low, low + lax.axis_size("dp").bit_length() - 1))


def bit_of(bit):
    return (my_index() >> bit) & 1


def keep_half(values, bit):
    own = bit_of(bit)
    half = values.shape[0] // 2
    values = values.reshape((2, half) + values.shape[1:])
    kept = lax.dynamic_index_in_dim(values, own, 0, keepdims=False)
    sent = lax.dynamic_index_in_dim(values, 1 - own, 0, keepdims=False)
    return kept + swap(sent, bit)


def split_two(values):
    high = values.astype(BF16)
    return high, (values - high.astype(F32)).astype(BF16)


def dot_fine(left, right):
    return jnp.dot(left, right, precision=lax.Precision.HIGHEST, preferred_element_type=F32)


def dot_split(left, right):
    left_high, left_low = split_two(left)
    right_high, right_low = split_two(right)
    return dot_nn(left_high, right_high) + (dot_nn(left_high, right_low) + dot_nn(left_low, right_high))


def polynomial(packed, owners):
    side = owners * LANES
    pairs = upper_pairs(owners)

    def kernel(packed_ref, out_ref, gram, product):
        for place, (i, j) in enumerate(pairs):
            block = packed_ref[place * LANES : (place + 1) * LANES, :]
            gram[i * LANES : (i + 1) * LANES, j * LANES : (j + 1) * LANES] = block
            if i != j:
                gram[j * LANES : (j + 1) * LANES, i * LANES : (i + 1) * LANES] = block.T
        eye = (
            lax.broadcasted_iota(jnp.int32, (side, side), 0) == lax.broadcasted_iota(jnp.int32, (side, side), 1)
        ).astype(F32)
        trace = jnp.sum(jnp.sum(gram[...] * eye, axis=0, keepdims=True), axis=1, keepdims=True)
        factor = 1.0 / (jnp.sqrt(trace) + 1e-07)
        first = gram[...] * (factor * factor)
        poly = NS_A * eye + NS_B * first + NS_C * dot_fine(first, first)
        gram[...] = dot_fine(dot_fine(first, poly), poly)
        product[...] = poly * factor

        def body(index, carry):
            now = gram[...]
            poly = NS_A * eye + NS_B * now + NS_C * dot_split(now, now)
            gram[...] = dot_split(dot_split(now, poly), poly)
            product[...] = dot_split(product[...], poly)
            return carry

        lax.fori_loop(0, NS_STEPS - 2, body, 0)
        now = gram[...]
        poly = NS_A * eye + NS_B * now + NS_C * dot_split(now, now)
        own = pl.ds(pl.multiple_of(lax.axis_index("owner") * LANES, LANES), LANES)
        out_ref[...] = dot_split(product[own, :], poly).astype(BF16)

    return launch(
        kernel, "polynomial", (1,), (packed,), [whole(packed.shape)], out_of((LANES, side), BF16), whole((LANES, side)),
        [pltpu.VMEM((side, side), F32), pltpu.VMEM((side, side), F32)], 60 * 2 * side**3,
    )


def apply_polynomials(early, late, gathered, starts, products, masters):
    owners = gathered[0].shape[0]
    y_bit, z_bit = dp_bits()[:2]
    shift = lax.axis_size("owner").bit_length() - 1
    q_own, q_other, q_late = products
    kinds = len(masters)

    def kernel(own_ref, other_ref, late_ref, early_all, late_all, *refs):
        sources, outs = refs[:kinds], refs[kinds:]
        place = lax.axis_index("dp")
        my_y = (place >> (y_bit - shift)) & 1
        my_z = (place >> (z_bit - shift)) & 1

        def finish(layer, kind, poly, all_ref, start):
            size = sources[kind].shape[2]
            total = None
            for o in range(owners):
                part = dot_nt(poly[:, o * LANES : (o + 1) * LANES], all_ref[o, start : start + size, :])
                total = part if total is None else total + part
            outs[kind][layer] = sources[kind][layer] * (1.0 - LR_MATRIX * DECAY_MATRIX) - LR_MATRIX * total

        for number, (layer, kind) in enumerate(early):
            y, z = number // 2, number % 2
            turn = y ^ my_y
            poly = jnp.where(my_z == z, own_ref[turn].astype(F32), other_ref[turn].astype(F32)).astype(BF16)
            finish(layer, kind, poly, early_all, starts[0][number])
        for number, (layer, kind) in enumerate(late):
            finish(layer, kind, late_ref[number ^ my_y], late_all, starts[1][number])

    operands = (q_own, q_other, q_late, gathered[0], gathered[1]) + masters
    outs = tuple(out_of(master.shape, F32) for master in masters)
    return launch(
        kernel, "apply_polynomials", (1,), operands, [whole(a.shape) for a in operands], outs,
        tuple(whole(master.shape) for master in masters), [], 2**31,
    )


def newton_schulz(early, late, moments_t, masters):
    y_bit, z_bit, turn_bit = dp_bits()[:3]
    gathered, starts, grams = [], [], []
    for names in (early, late):
        both, begin = gather_rows([moments_t[name] for name in names])
        gathered.append(both)
        starts.append(begin)
        values = own_grams(both, begin, [moments_t[name].shape[0] for name in names])
        for bit in dp_bits():
            if values.shape[0] > 1:
                values = keep_half(values, bit)
            else:
                values = values + swap(values, bit)
        grams.append(values[0])
    on_late = bit_of(turn_bit) == 1
    mine = jnp.where(on_late, grams[1], grams[0])
    packed = lax.all_gather(mine, "owner", tiled=True)
    own = polynomial(packed, gathered[0].shape[0])
    other = swap(own, turn_bit)
    q_early = jnp.where(on_late, other, own)
    q_late = jnp.where(on_late, own, other)
    both = jnp.stack([q_early, q_late])
    pair = jnp.stack([both, swap(both, y_bit)])
    q_own, q_late = pair[:, 0], pair[:, 1]
    q_other = swap(q_own, z_bit)
    return apply_polynomials(early, late, gathered, starts, (q_own, q_other, q_late), masters)


def adamw(weight, grad, first, second, rate, decay):
    first = BETA_ONE * first + (1.0 - BETA_ONE) * grad
    second = BETA_TWO * second + (1.0 - BETA_TWO) * grad * grad
    first_hat = first / (1.0 - BETA_ONE**STEP)
    second_hat = second / (1.0 - BETA_TWO**STEP)
    weight = weight - rate * (first_hat / (jnp.sqrt(second_hat) + ADAM_EPS) + decay * weight)
    return (weight, first, second)


def per_device(
    images, valid_count, labels, loss_weight, w_reduce, w_spatial, w_expand, mom_reduce, mom_spatial, mom_expand,
    head, head_m, head_v, norm_params, norm_m, norm_v, head_bias, bias_m, bias_v,
):
    dp_size, owner_size = lax.axis_size("dp"), lax.axis_size("owner")
    devices = dp_size * owner_size
    count_img, side, _, wide = images.shape
    pixels = side * side
    narrow = w_reduce.shape[1] * owner_size
    zone = count_img * SLOT
    rows = side * zone

    valid = (jnp.arange(count_img, dtype=jnp.int32) < valid_count[0]).astype(jnp.int32)
    weight_img = valid * loss_weight
    tallies = jnp.stack([valid_count[0] * pixels, jnp.sum(weight_img)]).astype(F32)
    tallies = jnp.pad(tallies, (0, 6))[:, None]
    counts = jnp.sum(exchange(jnp.broadcast_to(tallies[None], (devices, 8, LANES))), axis=0)

    in_map = (jnp.arange(SLOT) < side).astype(F32)
    pad_mask = jnp.broadcast_to(in_map, (side, count_img, SLOT))
    masks = jnp.stack([pad_mask * valid.astype(F32)[:, None], pad_mask], axis=-1).reshape(rows, 2)
    pixels_in = jnp.pad(images, ((0, 0), (0, 0), (0, SLOT - side), (0, 0))).transpose(1, 0, 2, 3).reshape(rows, wide)

    rows_of = (w_reduce.shape[2], w_spatial.shape[2], w_expand.shape[2])
    starts = (0, rows_of[0], rows_of[0] + rows_of[1])
    packs = [
        [part.T.astype(BF16) for part in (w_reduce[layer], w_spatial[layer], w_expand[layer])] for layer in range(LAYERS)
    ]
    mats = []
    if dp_size == 8 and owner_size == 4:
        first = Gather(packs[0][0], (4, 3, 2, 1, 0))
        first.send()
        first.join()
        first.send()
        halves = [[part[: part.shape[0] // 2], part[part.shape[0] // 2 :]] for part in packs[0][1:]]
        sets = [jnp.concatenate([part[i] for part in halves], axis=0) for i in range(2)]
        first.got, sets = lax.optimization_barrier((first.got, sets))
        others = [Gather(sets[0], (4, 3, 1, 2, 0)), Gather(sets[1], (4, 2, 3, 1, 0))]
        first.join()
        first.send()
        for flow in others:
            flow.send()
        meet([first] + others)
        first.send()
        for flow in others:
            flow.send()
        meet([first] + others)
        first.values, pixels_in, masks, counts, packs[1] = lax.optimization_barrier(
            (first.values, pixels_in, masks, counts, packs[1])
        )
        first.send()
        for flow in others:
            flow.send()
        first.join()
        mats.append(relative_weights([(first.values, first.masks, 0, rows_of[0], 0)], rows_of[0], dp_size, owner_size))
        h1_first, sums = first_reduce(pixels_in, masks, mats[0], devices)
        got, h1_first = lax.optimization_barrier(([flow.got for flow in others], h1_first))
        for flow, values in zip(others, got):
            flow.got = values
            flow.join()
        for _ in range(2):
            for flow in others:
                flow.send()
            meet(others)
        tops = (rows_of[1] // 2, rows_of[2] // 2)
        for kind in (1, 2):
            pieces = [
                (others[i].values, others[i].masks, 0 if kind == 1 else tops[0], tops[kind - 1], i * tops[kind - 1])
                for i in range(2)
            ]
            mats.append(relative_weights(pieces, rows_of[kind], dp_size, owner_size))
    layers_done = len(mats) // 3
    for layer in range(layers_done, LAYERS):
        packed = jnp.concatenate(packs[layer], axis=0)
        gathered = lax.all_gather(packed, AXES).reshape(dp_size, owner_size, packed.shape[0], LANES)
        for kind in range(3):
            if dp_size <= 8:
                mats.append(gathered_weights(gathered, starts[kind], rows_of[kind]))
            else:
                piece = gathered[:, :, starts[kind] : starts[kind] + rows_of[kind]]
                piece = piece.transpose(1, 0, 2, 3).reshape(1, owner_size, -1, LANES)
                mats.append(gathered_weights(piece, 0, piece.shape[2]))
    classes = head.shape[0]
    slots = -(-classes // LANES) * LANES
    slack = slots - classes
    head_low = jnp.pad(head.astype(BF16), ((0, slack), (0, 0)))
    head_all = lax.all_gather(head_low, AXES).reshape(dp_size, owner_size, slots, head.shape[1])
    aligned = head.shape[1] % LANES == 0
    if not aligned:
        head_all = head_all.transpose(1, 2, 0, 3).reshape(1, owner_size, slots, wide)
    slot_bias = jnp.pad(head_bias.reshape(owner_size, classes), ((0, 0), (0, slack)), constant_values=-1e30)
    slot_bias = jnp.broadcast_to(slot_bias.reshape(1, -1), (8, owner_size * slots))
    slot_labels = (labels // classes) * slots + labels % classes
    image_cols = jnp.stack([slot_labels, weight_img], axis=1)

    weight_total = counts[1, 0]
    norms = norm_params
    h1, h2, h3, a1, a2, stat1, stat2, stat3 = ([None] * LAYERS for _ in range(8))
    inputs, inputs_low = [pixels_in] + [None] * (LAYERS - 1), [pixels_in] + [None] * (LAYERS - 1)
    if layers_done:
        h1[0] = h1_first
    else:
        h1[0], sums = first_reduce(pixels_in, masks, mats[0], devices)
    for layer in range(LAYERS):
        a1[layer], h2[layer], stat1[layer], sums = spatial_conv(
            h1[layer], exchange(sums), counts, norms, masks, mats[3 * layer + 1], layer, zone, devices
        )
        a2[layer], h3[layer], stat2[layer], sums = expand(
            h2[layer], exchange(sums), counts, norms, masks, mats[3 * layer + 2], layer, devices
        )
        if layer < LAYERS - 1:
            inputs[layer + 1], inputs_low[layer + 1], h1[layer + 1], stat3[layer], sums = close_and_reduce(
                h3[layer], inputs[layer], exchange(sums), counts, norms, masks, mats[3 * layer + 3], layer, devices
            )
    last = LAYERS - 1
    ds, stat3[last], sums, *head_halves = head_step(
        h3[last], inputs[last], exchange(sums), counts, norms, masks, head_all, slot_bias, image_cols, last, pixels, zone, devices
    )
    left = bits_of(dp_size, owner_size)
    rest = list(range(1, len(left)))
    turned = [[0] + rest[turn:] + rest[:turn] for turn in range(3)]
    if not aligned:
        width = head.shape[1]
        head_halves = [
            jnp.pad(
                half.reshape(owner_size // 2, wide // LANES, slots, LANES // width, width).transpose(0, 1, 3, 2, 4),
                ((0, 0),) * 4 + ((0, LANES - width),),
            )
            for half in head_halves
        ]
    blocked = lambda halves: tuple(half.reshape(devices // 2, -1, LANES) for half in halves)
    head_flow = Flow([blocked(head_halves)], left, turned[0])
    flows = [head_flow]
    norm_sums = []
    wide_rows = 2 * wide // LANES
    for layer in reversed(range(LAYERS)):
        parts3 = exchange(sums)
        if layer == last:
            extra = parts3
        parts3 = advance(parts3, flows)
        dh3, dz2, sums = back_expand(
            ds, h3[layer], parts3, stat3[layer], counts, norms, masks, h2[layer], stat2[layer], mats[3 * layer + 2], layer, devices
        )
        grad_three = blocked(weight_grad(dh3, a2[layer], owner_size))
        if layer == 0:
            three_flow = Flow([grad_three], left, turned[0])
            flows.append(three_flow)
        parts2 = exchange(sums)
        parts2 = advance(parts2, flows)
        dh2, dz1, sums = back_conv(
            dz2, h2[layer], parts2, stat2[layer], counts, norms, masks, h1[layer], stat1[layer], mats[3 * layer + 1], layer, zone, devices
        )
        grad_two = blocked(spatial_grad(a1[layer], dh2, owner_size, zone))
        if layer > 0:
            high_flow = Flow([grad_three, grad_two], left, turned[1])
            flows.append(high_flow)
        else:
            two_flow = Flow([grad_two], left, [0])
            flows.append(two_flow)
        parts1 = exchange(sums)
        parts1 = advance(parts1, flows)
        if layer > 0:
            dh1, ds, sums = back_reduce(
                dz1, h1[layer], parts1, stat1[layer], counts, norms, masks, ds, h3[layer - 1], inputs[layer - 1], stat3[layer - 1],
                mats[3 * layer], layer, devices,
            )
        else:
            dh1 = last_back(dz1, h1[layer], parts1, stat1[layer], counts, norms, masks, layer)
        grad_one = blocked(weight_grad(inputs_low[layer], dh1, owner_size))
        if layer > 0:
            one_flow = Flow([grad_one], left, turned[2])
            flows.append(one_flow)
        norm_sums.insert(0, [jnp.sum(part, axis=0).reshape(2, -1) for part in (parts1, parts2, parts3[:, :wide_rows])])
    norm_grad = jnp.stack(
        [jnp.stack([jnp.concatenate([part[kind] for part in norm_sums[layer]]) for layer in range(LAYERS)]) for kind in (1, 0)]
    )
    extra = jnp.sum(extra[:, wide_rows:], axis=0)
    class_rows = owner_size * slots // LANES
    bias_raw = extra[:class_rows].reshape(owner_size, slots)[:, :classes].reshape(-1)
    loss_sum = extra[class_rows, 0]
    grad_bias = bias_raw / weight_total
    last_flow = Flow([grad_one], left, [0])
    low_sums = jnp.concatenate([two_flow.result(), last_flow.result()], axis=1)
    remaining = [bit for bit in left if bit != 0]
    height = low_sums.shape[1]
    third = height // 3 // 16 * 16
    cuts = [0, third, 2 * third, height]
    thirds = []
    for i in range(3):
        order = turned[i][1:]
        piece = low_sums[:, cuts[i] : cuts[i + 1]]
        place = remaining.index(order[0])
        own = (my_index() >> order[0]) & 1
        thirds.append(Flow([(half_of(piece, place, own), half_of(piece, place, 1 - own))], remaining, order))
    high, low = LAYERS - 1, 0
    low_sums = jnp.concatenate([flow.result() for flow in thirds], axis=0)
    two_low, one_low = low_sums[: rows_of[1]], low_sums[rows_of[1] :]
    three_low, one_high = three_flow.result(), one_flow.result()
    three_high, two_high = jnp.split(high_flow.result(), [rows_of[2]])
    head_sum = head_flow.result().astype(F32).reshape(-1, slots, LANES)[:, :classes]
    head_sum = head_sum.transpose(1, 0, 2).reshape(classes, -1)[:, : head.shape[1]]

    olds = (mom_reduce, mom_spatial, mom_expand)
    moment = lambda layer, kind, total: MOMENTUM * olds[kind][layer].T + total.astype(F32)
    early = [(high, 2, three_high), (high, 1, two_high), (high, 0, one_high), (low, 2, three_low)]
    late = [(low, 1, two_low), (low, 0, one_low)]
    moments_t = {(layer, kind): moment(layer, kind, total) for layer, kind, total in early + late}
    updated = newton_schulz(
        [item[:2] for item in early], [item[:2] for item in late], moments_t, (w_reduce, w_spatial, w_expand)
    )
    moments = [jnp.stack([moments_t[layer, kind].T for layer in range(LAYERS)]) for kind in range(3)]
    new_head, new_head_m, new_head_v = adamw(head, head_sum, head_m, head_v, LR_HEAD, DECAY_HEAD)
    new_norm, new_norm_m, new_norm_v = adamw(norm_params, norm_grad, norm_m, norm_v, LR_VECTOR, 0.0)
    new_bias, new_bias_m, new_bias_v = adamw(head_bias, grad_bias, bias_m, bias_v, LR_VECTOR, 0.0)
    return (
        loss_sum,
        weight_total,
        updated[0],
        updated[1],
        updated[2],
        moments[0],
        moments[1],
        moments[2],
        new_head,
        new_head_m,
        new_head_v,
        new_norm,
        new_norm_m,
        new_norm_v,
        new_bias,
        new_bias_m,
        new_bias_v,
    )


def solution(mesh):
    return jax.shard_map(
        per_device,
        mesh=mesh,
        in_specs=(
            P(("dp", "owner"), None, None, None),
            P(("dp", "owner")),
            P(("dp", "owner")),
            P(("dp", "owner")),
            P(None, "owner", "dp"),
            P(None, "owner", "dp"),
            P(None, "owner", "dp"),
            P(None, "owner", "dp"),
            P(None, "owner", "dp"),
            P(None, "owner", "dp"),
            P("owner", "dp"),
            P("owner", "dp"),
            P("owner", "dp"),
            P(),
            P(),
            P(),
            P(),
            P(),
            P(),
        ),
        out_specs=(
            P(),
            P(),
            P(None, "owner", "dp"),
            P(None, "owner", "dp"),
            P(None, "owner", "dp"),
            P(None, "owner", "dp"),
            P(None, "owner", "dp"),
            P(None, "owner", "dp"),
            P("owner", "dp"),
            P("owner", "dp"),
            P("owner", "dp"),
            P(),
            P(),
            P(),
            P(),
            P(),
            P(),
        ),
        check_vma=False,
    )
```

```python
import functools
import math

import jax
import jax.numpy as jnp
from jax import lax
from jax.experimental import pallas as pl
from jax.experimental.pallas import tpu as pltpu
from jax.sharding import PartitionSpec as P

LAYERS = 2
NS_STEPS = 5
STEP = 10

AXES = ("dp", "owner")
EPS = 1e-05
NS_A = 3.4445
NS_B = -4.775
NS_C = 2.0315
MOMENTUM = 0.9
LR_MATRIX = 0.5
DECAY_MATRIX = 0.01
BETA_ONE = 0.9
BETA_TWO = 0.999
ADAM_EPS = 1e-08
LR_HEAD = 0.2
DECAY_HEAD = 0.01
LR_VECTOR = 0.4
LANES = 128
SLOT = 8
PATIENT = 280000
F32 = jnp.float32
BF16 = jnp.bfloat16


def device_count():
    return lax.axis_size("dp") * lax.axis_size("owner")


def my_index():
    return lax.axis_index("dp") * lax.axis_size("owner") + lax.axis_index("owner")


def exchange(copies):
    return lax.all_to_all(copies, AXES, 0, 0, tiled=True)


def swap(values, bit):
    count = device_count()
    return lax.ppermute(values, AXES, [(src, src ^ (1 << bit)) for src in range(count)])


def half_of(values, place, side):
    split = values.reshape((2**place, 2, -1) + values.shape[1:])
    picked = lax.dynamic_index_in_dim(split, side, 1, keepdims=False)
    return picked.reshape((-1,) + values.shape[1:])


class Flow:
    def __init__(self, pairs, left, order):
        self.left, self.order = [bit for bit in left if bit != order[0]], list(order[1:])
        self.kept = [kept for kept, _ in pairs]
        self.sent = [sent for _, sent in pairs]
        self.bit = order[0]
        self.values = self.got = None
        self.wait = 1

    def send(self):
        self.got = [swap(sent, self.bit) for sent in self.sent]
        self.wait = 2 if self.order is not None and self.values is not None and self.sent[0].size > PATIENT else 1
        self.sent = None

    def add(self):
        if self.values is None:
            parts = [kept + got for kept, got in zip(self.kept, self.got)]
            self.values = parts[0] if len(parts) == 1 else jnp.concatenate(parts, axis=1)
        else:
            self.values = half_of(self.values, self.place, self.own) + self.got[0]
        self.got = None

    def split(self):
        if self.order:
            self.bit = self.order.pop(0)
            self.place = self.left.index(self.bit)
            self.left.pop(self.place)
            self.own = (my_index() >> self.bit) & 1
            self.sent = [half_of(self.values, self.place, 1 - self.own)]

    def turn(self):
        if self.got is not None:
            self.add()
            self.split()
        if self.sent is not None:
            self.send()

    def result(self):
        while self.got is not None or self.sent is not None:
            self.turn()
        return self.values[0] if self.values.shape[0] == 1 else self.values


class Fork:
    def __init__(self, pair, left, first, orders):
        self.trunk, self.orders, self.branches = Flow([pair], left, [first]), orders, []
        self.wait = 1

    @property
    def parts(self):
        return self.branches or [self.trunk]

    def add(self):
        for part in self.parts:
            part.add()

    def split(self):
        if self.branches:
            for part in self.branches:
                part.split()
            return
        values, left, count = self.trunk.values, self.trunk.left, len(self.orders)
        step = values.shape[1] // count // 16 * 16
        for number, order in enumerate(self.orders):
            piece = values[:, number * step : (number + 1) * step if number < count - 1 else values.shape[1]]
            place = left.index(order[0])
            own = (my_index() >> order[0]) & 1
            self.branches.append(Flow([(half_of(piece, place, own), half_of(piece, place, 1 - own))], left, order))

    def send(self):
        for part in self.parts:
            if part.sent is not None:
                part.send()
        self.wait = max(part.wait for part in self.parts)

    @property
    def got(self):
        got = [part.got for part in self.parts]
        return None if all(values is None for values in got) else got

    @got.setter
    def got(self, values):
        for part, value in zip(self.parts, values or [None] * len(self.parts)):
            part.got = value

    @property
    def sent(self):
        sent = [part.sent for part in self.parts]
        return None if all(values is None for values in sent) else sent

    @sent.setter
    def sent(self, values):
        for part, value in zip(self.parts, values or [None] * len(self.parts)):
            part.sent = value

    def result(self):
        return jnp.concatenate([part.result() for part in self.branches], axis=0)


def advance(ahead, flows, eager=False):
    for flow in flows:
        flow.wait -= flow.got is not None
    moving = [flow for flow in flows if flow.got is not None and (eager or flow.wait <= 0)]
    ahead, got = lax.optimization_barrier((ahead, [flow.got for flow in moving]))
    for flow, values in zip(moving, got):
        flow.got = values
        flow.add()
        flow.split()
    moving = [flow for flow in flows if flow.sent is not None]
    ahead, sent = lax.optimization_barrier((ahead, [flow.sent for flow in moving]))
    for flow, values in zip(moving, sent):
        flow.sent = values
        flow.send()
    return ahead


def bits_of(dp_size, owner_size):
    low = owner_size.bit_length() - 1
    high = dp_size.bit_length() - 1
    return list(range(low - 1, -1, -1)) + list(range(low + high - 1, low - 1, -1))


def silu(values):
    half = 0.5 * values
    return half * jnp.tanh(half) + half


def silu_slope(values):
    half = 0.5 * values
    bend = jnp.tanh(half)
    return 0.5 * (1.0 + bend + half * (1.0 - bend * bend))


def total_of(parts_ref):
    return jnp.sum(parts_ref[...], axis=0)


def row_of(table, start, width):
    count = width // LANES
    return jnp.concatenate([table[start + i : start + i + 1, :] for i in range(count)], axis=1)


def send_rows(out_ref, rows, place=0):
    for row in rows:
        for i in range(row.shape[1] // LANES):
            piece = row[:, i * LANES : (i + 1) * LANES]
            out_ref[:, place, :] = jnp.broadcast_to(piece, (out_ref.shape[0], LANES))
            place += 1


def fold_rows(values):
    return jnp.sum(values.reshape(values.shape[0] // 8, 8, values.shape[1]), axis=0)


def norm_of(parts_ref, count, width):
    table = total_of(parts_ref)
    centre = row_of(table, 0, width) / count
    spread = row_of(table, width // LANES, width) / count - centre * centre
    return centre, lax.rsqrt(spread + EPS)


def keep_norm(stat_ref, centre, inverse, gain, bias):
    scale = inverse * gain
    rows = [centre, inverse, scale, bias - centre * scale]
    stat_ref[...] = jnp.concatenate(rows + [jnp.zeros_like(centre)] * 4, axis=0)


def normed_of(values, stat_ref):
    return values * stat_ref[2:3] + stat_ref[3:4]


def back_terms(terms, table, stat_ref, count, width):
    bias_sum, gain_sum = row_of(table, 0, width), row_of(table, width // LANES, width)
    centre, inverse, scale = stat_ref[0:1], stat_ref[1:2], stat_ref[2:3]
    terms[0:1] = scale * (bias_sum - centre * inverse * gain_sum) / count
    terms[1:2] = scale * inverse * gain_sum / count


def back_norm(grad, hidden, stat_ref, terms, mask):
    return grad * stat_ref[2:3] - mask * (terms[0:1] + hidden * terms[1:2])


def send_back_sums(send_ref, sums, stat_ref):
    bias_sum = jnp.sum(sums[0:8], axis=0, keepdims=True)
    cross = jnp.sum(sums[8:16], axis=0, keepdims=True)
    send_rows(send_ref, [bias_sum, (cross - stat_ref[0:1] * bias_sum) * stat_ref[1:2]])


class Weights:
    def __init__(self, operands, blocks, rows, dp_size, owners, masked):
        self.operands, self.blocks, self.rows, self.masked = operands, blocks, rows, masked
        self.owners = owners
        self.depth, self.width = dp_size * rows, owners * LANES

    def scratch(self):
        return [pltpu.VMEM((self.depth, self.width), BF16), pltpu.SemaphoreType.DMA((len(self.blocks),))]

    def copies(self, refs, buffer, sems):
        shift = self.owners.bit_length() - 1
        me = (lax.axis_index("dp") << shift) | lax.axis_index("owner") if self.masked else 0
        out = []
        for number, (operand, index, start, rows, device, offset) in enumerate(self.blocks):
            device = me ^ device
            base, lane = (device >> shift) * self.rows + offset, (device & (self.owners - 1)) * LANES
            if self.masked:
                base, lane = pl.multiple_of(base, 16), pl.multiple_of(lane, LANES)
            out.append(
                pltpu.make_async_copy(
                    refs[operand].at[index + (pl.ds(start, rows),)],
                    buffer.at[pl.ds(base, rows), pl.ds(lane, LANES)],
                    sems.at[number],
                )
            )
        return out


def gathered_weights(array, start, rows):
    dp_size, owners = array.shape[:2]
    blocks = [(0, (d, o), start, rows, d * owners + o, 0) for d in range(dp_size) for o in range(owners)]
    return Weights([array], blocks, rows, dp_size, owners, False)


def relative_weights(pieces, rows, dp_size, owners):
    operands, blocks = [], []
    for arrays, masks, start, height, offset in pieces:
        for array, names in zip(arrays, masks):
            for index, mask in enumerate(names):
                blocks.append((len(operands), (index,), start, height, mask, offset))
            operands.append(array)
    return Weights(operands, blocks, rows, dp_size, owners, True)


class Gather:
    def __init__(self, block, order):
        self.values, self.masks, self.order = block[None], [0], list(order)

    def send(self):
        self.bit = self.order.pop(0)
        self.got = swap(self.values, self.bit)

    def join(self):
        more = [mask ^ (1 << self.bit) for mask in self.masks]
        if self.order:
            self.values, self.masks = jnp.concatenate([self.values, self.got], axis=0), self.masks + more
        else:
            self.values, self.masks = [self.values, self.got], [self.masks, more]


def meet(flows):
    got = lax.optimization_barrier([flow.got for flow in flows])
    for flow, values in zip(flows, got):
        flow.got = values
        flow.join()


def whole(shape):
    return pl.BlockSpec(shape, lambda *ids: (0,) * len(shape), pipeline_mode=pl.Buffered(1))


def strip(rows, width):
    return pl.BlockSpec((rows, width), lambda i: (i, 0))


ANYWHERE = pl.BlockSpec(memory_space=pl.ANY)
SCALAR = pl.BlockSpec(memory_space=pltpu.SMEM)


def launch(kernel, name, grid, operands, specs, outs, out_specs, scratch, flops):
    arrays, flat_specs, groups = [], [], []
    for operand, spec in zip(operands, specs):
        group = operand.operands if isinstance(operand, Weights) else [operand]
        groups.append(len(group) if isinstance(operand, Weights) else 0)
        arrays += group
        flat_specs += [spec] * len(group)

    def grouped(*refs):
        refs, firsts = list(refs), []
        for count in groups:
            if count:
                firsts.append(tuple(refs[:count]))
                refs = refs[count:]
            else:
                firsts.append(refs.pop(0))
        kernel(*firsts, *refs)

    moved = sum(math.prod(a.shape) * a.dtype.itemsize for a in jax.tree.leaves((arrays, outs)))
    return pl.pallas_call(
        grouped,
        name=name,
        grid=grid,
        in_specs=flat_specs,
        out_specs=out_specs,
        out_shape=outs,
        scratch_shapes=scratch,
        cost_estimate=pl.CostEstimate(flops=flops, bytes_accessed=min(moved, 2**25), transcendentals=0),
        compiler_params=pltpu.CompilerParams(
            vmem_limit_bytes=60 * 2**20, dimension_semantics=("arbitrary",) * len(grid)
        ),
    )(*arrays)


def out_of(shape, dtype):
    return jax.ShapeDtypeStruct(shape, dtype)


def block_rows(rows, parts):
    for count in range(parts, rows):
        if rows % count == 0 and (rows // count) % 16 == 0:
            return rows // count
    return rows


def dot_nn(left, right):
    return jnp.dot(left, right, preferred_element_type=F32)


def dot_nt(left, right):
    return lax.dot_general(left, right, (((1,), (1,)), ((), ())), preferred_element_type=F32)


def dot_tn(left, right):
    return lax.dot_general(left, right, (((0,), (0,)), ((), ())), preferred_element_type=F32)


def store_halves(kept_ref, sent_ref, place, values):
    even = (lax.axis_index("owner") & 1) == 0
    for pair in range(len(values) // 2):
        first, second = values[2 * pair], values[2 * pair + 1]
        kept_ref[(pair,) + place] = jnp.where(even, first, second).astype(BF16)
        sent_ref[(pair,) + place] = jnp.where(even, second, first).astype(BF16)


def first_reduce(images, masks, tallies, weights, devices):
    rows, wide = images.shape
    narrow = weights.width
    strip_rows = block_rows(rows, 3)
    steps = rows // strip_rows

    def kernel(x_ref, mask_ref, tally_ref, w_ref, h_ref, send_ref, buffer, sems, sums):
        step = pl.program_id(0)

        @pl.when(step == 0)
        def _():
            copies = weights.copies(w_ref, buffer, sems)
            for copy in copies:
                copy.start()
            sums[...] = jnp.zeros_like(sums)
            for copy in copies:
                copy.wait()

        hidden = dot_nn(x_ref[...], buffer[...])
        h_ref[...] = hidden
        kept = hidden * mask_ref[:, 0:1]
        sums[0:8] += fold_rows(kept)
        sums[8:16] += fold_rows(kept * hidden)

        @pl.when(step == steps - 1)
        def _():
            send_rows(send_ref, [jnp.sum(sums[i * 8 : i * 8 + 8], axis=0, keepdims=True) for i in range(2)])
            send_ref[:, send_ref.shape[1] - 8 :, :] = jnp.broadcast_to(tally_ref[...][None], (devices, 8, LANES))

    send = (devices, 2 * narrow // LANES + 8, LANES)
    return launch(
        kernel, "reduce_first", (steps,),
        (images, masks, tallies, weights),
        [strip(strip_rows, wide), strip(strip_rows, 2), whole(tallies.shape), ANYWHERE],
        (out_of((rows, narrow), F32), out_of(send, F32)),
        (strip(strip_rows, narrow), whole(send)),
        weights.scratch() + [pltpu.VMEM((16, narrow), F32)],
        2 * rows * wide * narrow,
    )


def store_shifted(shifted, place, values, zone, narrow):
    for offset in range(3):
        moved = values if offset == 1 else pltpu.roll(values, 1 if offset == 0 else zone - 1, 0)
        shifted[pl.ds(place, zone), offset * narrow : (offset + 1) * narrow] = moved.astype(BF16)


def clear_edges(shifted, rows, zone):
    edge = jnp.zeros((zone, shifted.shape[1]), BF16)
    shifted[0:zone] = edge
    shifted[zone + rows : 2 * zone + rows] = edge


def spatial_conv(hidden, parts, counts, norms, masks, weights, layer, zone, devices):
    rows, narrow = hidden.shape
    strip_rows = block_rows(rows, 3)
    steps = rows // strip_rows

    def kernel(
        h_ref, parts_ref, count_ref, norm_ref, mask_ref, w_ref,
        a_ref, out_ref, stat_ref, send_ref, buffer, sems, sums, shifted,
    ):
        step = pl.program_id(0)

        @pl.when(step == 0)
        def _():
            copies = weights.copies(w_ref, buffer, sems)
            for copy in copies:
                copy.start()
            sums[...] = jnp.zeros_like(sums)
            centre, inverse = norm_of(parts_ref, count_ref[0:1, 0:1], narrow)
            keep_norm(stat_ref, centre, inverse, norm_ref[0, layer : layer + 1, 0:narrow], norm_ref[1, layer : layer + 1, 0:narrow])
            clear_edges(shifted, rows, zone)

            def body(index, carry):
                start = pl.multiple_of(index * zone, zone)
                place = pl.ds(start, zone)
                value = silu(normed_of(h_ref[place, :], stat_ref)) * mask_ref[place, 1:2]
                a_ref[place, :] = value.astype(BF16)
                store_shifted(shifted, pl.multiple_of(start + zone, zone), value, zone, narrow)
                return carry

            lax.fori_loop(0, rows // zone, body, 0)
            for copy in copies:
                copy.wait()

        base = step * strip_rows
        total = None
        for tap in range(3):
            piece = shifted[pl.ds(pl.multiple_of(base + tap * zone, 16), strip_rows), :]
            part = dot_nn(piece, buffer[tap * 3 * narrow : (tap + 1) * 3 * narrow])
            total = part if total is None else total + part
        out_ref[...] = total
        kept = total * mask_ref[pl.ds(pl.multiple_of(base, 16), strip_rows), 0:1]
        sums[0:8] += fold_rows(kept)
        sums[8:16] += fold_rows(kept * total)

        @pl.when(step == steps - 1)
        def _():
            send_rows(send_ref, [jnp.sum(sums[i * 8 : i * 8 + 8], axis=0, keepdims=True) for i in range(2)])

    send = (devices, 2 * narrow // LANES, LANES)
    return launch(
        kernel, "spatial_conv", (steps,),
        (hidden, parts, counts, norms, masks, weights),
        [whole(hidden.shape), whole(parts.shape), whole(counts.shape), whole(norms.shape), whole(masks.shape), ANYWHERE],
        (out_of((rows, narrow), BF16), out_of((rows, narrow), F32), out_of((8, narrow), F32), out_of(send, F32)),
        (whole((rows, narrow)), strip(strip_rows, narrow), whole((8, narrow)), whole(send)),
        weights.scratch() + [pltpu.VMEM((16, narrow), F32), pltpu.VMEM((rows + 2 * zone, 3 * narrow), BF16)],
        2 * rows * 9 * narrow * narrow,
    )


def expand(hidden, parts, counts, norms, masks, weights, layer, devices):
    rows, narrow = hidden.shape
    wide = weights.depth
    strip_rows = block_rows(rows, 4)
    steps = rows // strip_rows

    def kernel(
        h_ref, parts_ref, count_ref, norm_ref, mask_ref, w_ref,
        a_ref, out_ref, stat_ref, send_ref, buffer, sems, sums,
    ):
        step = pl.program_id(0)

        @pl.when(step == 0)
        def _():
            copies = weights.copies(w_ref, buffer, sems)
            for copy in copies:
                copy.start()
            sums[...] = jnp.zeros_like(sums)
            centre, inverse = norm_of(parts_ref, count_ref[0:1, 0:1], narrow)
            span = slice(narrow, 2 * narrow)
            keep_norm(stat_ref, centre, inverse, norm_ref[0, layer : layer + 1, span], norm_ref[1, layer : layer + 1, span])
            for copy in copies:
                copy.wait()

        value = silu(normed_of(h_ref[...], stat_ref)).astype(BF16)
        a_ref[...] = value
        total = dot_nt(value, buffer[...])
        out_ref[...] = total.astype(BF16)
        kept = total * mask_ref[:, 0:1]
        sums[0:8] += fold_rows(kept)
        sums[8:16] += fold_rows(kept * total)

        @pl.when(step == steps - 1)
        def _():
            send_rows(send_ref, [jnp.sum(sums[i * 8 : i * 8 + 8], axis=0, keepdims=True) for i in range(2)])

    send = (devices, 2 * wide // LANES, LANES)
    return launch(
        kernel, "expand", (steps,),
        (hidden, parts, counts, norms, masks, weights),
        [strip(strip_rows, narrow), whole(parts.shape), whole(counts.shape), whole(norms.shape), strip(strip_rows, 2), ANYWHERE],
        (out_of((rows, narrow), BF16), out_of((rows, wide), BF16), out_of((8, narrow), F32), out_of(send, F32)),
        (strip(strip_rows, narrow), strip(strip_rows, wide), whole((8, narrow)), whole(send)),
        weights.scratch() + [pltpu.VMEM((16, wide), F32)],
        2 * rows * wide * narrow,
    )


def close_and_reduce(hidden, inputs, parts, counts, norms, masks, weights, layer, devices):
    rows, wide = hidden.shape
    narrow = weights.width
    strip_rows = block_rows(rows, 6)
    steps = rows // strip_rows

    def kernel(
        h_ref, x_ref, parts_ref, count_ref, norm_ref, mask_ref, w_ref,
        low_ref, out_ref, stat_ref, send_ref, buffer, sems, sums,
    ):
        step = pl.program_id(0)

        @pl.when(step == 0)
        def _():
            copies = weights.copies(w_ref, buffer, sems)
            for copy in copies:
                copy.start()
            sums[...] = jnp.zeros_like(sums)
            centre, inverse = norm_of(parts_ref, count_ref[0:1, 0:1], wide)
            span = slice(2 * narrow, None)
            keep_norm(stat_ref, centre, inverse, norm_ref[0, layer : layer + 1, span], norm_ref[1, layer : layer + 1, span])
            for copy in copies:
                copy.wait()

        value = silu(x_ref[...].astype(F32) + normed_of(h_ref[...].astype(F32), stat_ref))
        low = value.astype(BF16)
        low_ref[...] = low
        total = dot_nn(low, buffer[...])
        out_ref[...] = total
        kept = total * mask_ref[:, 0:1]
        sums[0:8] += fold_rows(kept)
        sums[8:16] += fold_rows(kept * total)

        @pl.when(step == steps - 1)
        def _():
            send_rows(send_ref, [jnp.sum(sums[i * 8 : i * 8 + 8], axis=0, keepdims=True) for i in range(2)])

    send = (devices, 2 * narrow // LANES, LANES)
    return launch(
        kernel, "close_and_reduce", (steps,),
        (hidden, inputs, parts, counts, norms, masks, weights),
        [strip(strip_rows, wide), strip(strip_rows, wide), whole(parts.shape), whole(counts.shape), whole(norms.shape), strip(strip_rows, 2), ANYWHERE],
        (out_of((rows, wide), BF16), out_of((rows, narrow), F32), out_of((8, wide), F32), out_of(send, F32)),
        (strip(strip_rows, wide), strip(strip_rows, narrow), whole((8, wide)), whole(send)),
        weights.scratch() + [pltpu.VMEM((16, narrow), F32)],
        2 * rows * wide * narrow,
    )


def head_step(hidden, inputs, parts, counts, norms, masks, head_all, slot_bias, image_cols, layer, pixels, zone, devices):
    rows, wide = hidden.shape
    images = zone // SLOT
    dp_size, owners, slots, cols = head_all.shape
    classes = owners * slots
    steps = rows // zone
    count_rows = classes // LANES + 8
    tile = LANES

    def kernel(
        h_ref, x_ref, parts_ref, count_ref, norm_ref, mask_ref, head_ref, bias_ref, image_ref,
        ds_ref, stat_ref, send_ref, kept_ref, sent_ref, summed, kept, piled, pooled, sums,
    ):
        step = pl.program_id(0)
        @pl.when(step == 0)
        def _():
            sums[...] = jnp.zeros_like(sums)
            piled[...] = jnp.zeros_like(piled)
            centre, inverse = norm_of(parts_ref, count_ref[0:1, 0:1], wide)
            span = slice(norm_ref.shape[2] - wide, None)
            keep_norm(stat_ref, centre, inverse, norm_ref[0, layer : layer + 1, span], norm_ref[1, layer : layer + 1, span])

        @pl.when(step < steps)
        def _():
            place = pl.ds(pl.multiple_of(step * zone, zone), zone)
            hidden_here = h_ref[...]
            kept[place, :] = hidden_here
            value = x_ref[...].astype(F32) + normed_of(hidden_here.astype(F32), stat_ref)
            summed[place, :] = value
            out = silu(value) * mask_ref[:, 1:2]
            piled[...] += out

        @pl.when(step == steps - 1)
        def _():
            low = (jnp.sum(piled[...].reshape(images, SLOT, wide), axis=1) * (1.0 / pixels)).astype(BF16)
            flipped = None
            for d in range(dp_size):
                part = dot_nt(head_ref[d].reshape(classes, cols), low[:, d * cols : (d + 1) * cols])
                flipped = part if flipped is None else flipped + part
            logits = flipped.T + bias_ref[0:1, :]
            top = jnp.max(logits, axis=1, keepdims=True)
            shifted = jnp.exp(logits - top)
            mass = jnp.sum(shifted, axis=1, keepdims=True)
            log_total = jnp.log(mass) + top
            spots = lax.broadcasted_iota(jnp.int32, logits.shape, 1)
            onehot = (spots == image_ref[:, 0:1]).astype(F32)
            weight = image_ref[:, 1:2].astype(F32)
            picked = jnp.sum(logits * onehot, axis=1, keepdims=True)
            loss = jnp.sum(weight * (log_total - picked), axis=0, keepdims=True)
            residue = weight * (jnp.exp(logits - log_total) - onehot)
            send_rows(
                send_ref,
                [jnp.sum(residue, axis=0, keepdims=True), jnp.broadcast_to(loss, (1, 8 * LANES))],
                2 * wide // LANES,
            )
            exact = residue / count_ref[1:2, 0:1]
            grad, grad_flipped = exact.astype(BF16), exact.T.astype(BF16)
            for d in range(dp_size):
                back = dot_nn(grad, head_ref[d].reshape(classes, cols))
                weight_part = dot_nn(grad_flipped, low[:, d * cols : (d + 1) * cols])
                for i in range(kept_ref.shape[2]):
                    parts = [weight_part[o * slots : (o + 1) * slots, i * tile : (i + 1) * tile] for o in range(owners)]
                    store_halves(kept_ref, sent_ref, (d, i), parts)
                pooled[:, d * cols : (d + 1) * cols] = back * (1.0 / pixels)

        @pl.when(step >= steps)
        def _():
            place = pl.ds(pl.multiple_of((step - steps) * zone, zone), zone)
            spread = jnp.broadcast_to(pooled[...][:, None, :], (images, SLOT, wide)).reshape(zone, wide)
            ds = spread * silu_slope(summed[place, :]) * mask_ref[:, 1:2]
            ds_ref[...] = ds.astype(BF16)
            sums[0:8] += fold_rows(ds)
            sums[8:16] += fold_rows(ds * kept[place, :].astype(F32))

        @pl.when(step == 2 * steps - 1)
        def _():
            send_back_sums(send_ref, sums, stat_ref)

    send = (devices, 2 * wide // LANES + count_rows, LANES)
    grads = (owners // 2, dp_size, cols // tile, slots, tile)
    once = pl.BlockSpec((zone, wide), lambda i: (jnp.minimum(i, steps - 1), 0))
    later = pl.BlockSpec((zone, wide), lambda i: (jnp.maximum(i - steps, 0), 0))
    return launch(
        kernel, "head_step", (2 * steps,),
        (hidden, inputs, parts, counts, norms, masks, head_all, slot_bias, image_cols),
        [
            once, once, whole(parts.shape), whole(counts.shape), whole(norms.shape),
            pl.BlockSpec((zone, 2), lambda i: (lax.rem(i, steps), 0)),
            whole(head_all.shape), whole(slot_bias.shape), whole(image_cols.shape),
        ],
        (out_of((rows, wide), BF16), out_of((8, wide), F32), out_of(send, F32), out_of(grads, BF16), out_of(grads, BF16)),
        (later, whole((8, wide)), whole(send), whole(grads), whole(grads)),
        [pltpu.VMEM((rows, wide), F32), pltpu.VMEM((rows, wide), BF16), pltpu.VMEM((zone, wide), F32), pltpu.VMEM((images, wide), F32), pltpu.VMEM((16, wide), F32)],
        6 * images * classes * wide,
    )


def back_expand(ds, hidden, parts, stat_wide, counts, norms, masks, narrow_hidden, stat_narrow, weights, layer, devices):
    rows, wide = ds.shape
    narrow = weights.width
    strip_rows = block_rows(rows, 4)
    steps = rows // strip_rows

    def kernel(
        ds_ref, h_ref, parts_ref, stat_ref, count_ref, norm_ref, mask_ref, narrow_ref, narrow_stat, w_ref,
        low_ref, out_ref, send_ref, buffer, sems, sums, terms,
    ):
        step = pl.program_id(0)

        @pl.when(step == 0)
        def _():
            copies = weights.copies(w_ref, buffer, sems)
            for copy in copies:
                copy.start()
            sums[...] = jnp.zeros_like(sums)
            back_terms(terms, total_of(parts_ref), stat_ref, count_ref[0:1, 0:1], wide)
            for copy in copies:
                copy.wait()

        low = back_norm(ds_ref[...].astype(F32), h_ref[...].astype(F32), stat_ref, terms, mask_ref[:, 0:1]).astype(BF16)
        low_ref[...] = low
        total = dot_nn(low, buffer[...]) * silu_slope(normed_of(narrow_ref[...], narrow_stat))
        out_ref[...] = total
        sums[0:8] += fold_rows(total)
        sums[8:16] += fold_rows(total * narrow_ref[...])

        @pl.when(step == steps - 1)
        def _():
            send_back_sums(send_ref, sums, narrow_stat)

    send = (devices, 2 * narrow // LANES, LANES)
    return launch(
        kernel, "back_expand", (steps,),
        (ds, hidden, parts, stat_wide, counts, norms, masks, narrow_hidden, stat_narrow, weights),
        [
            strip(strip_rows, wide), strip(strip_rows, wide), whole(parts.shape), whole(stat_wide.shape), whole(counts.shape),
            whole(norms.shape), strip(strip_rows, 2), strip(strip_rows, narrow), whole(stat_narrow.shape), ANYWHERE,
        ],
        (out_of((rows, wide), BF16), out_of((rows, narrow), F32), out_of(send, F32)),
        (strip(strip_rows, wide), strip(strip_rows, narrow), whole(send)),
        weights.scratch() + [pltpu.VMEM((16, narrow), F32), pltpu.VMEM((8, wide), F32)],
        2 * rows * wide * narrow,
    )


def back_conv(dz, hidden, parts, stat_two, counts, norms, masks, first_hidden, stat_one, weights, layer, zone, devices):
    rows, narrow = dz.shape
    strip_rows = block_rows(rows, 3)
    steps = rows // strip_rows

    def kernel(
        dz_ref, h_ref, parts_ref, stat_ref, count_ref, norm_ref, mask_ref, first_ref, first_stat, w_ref,
        low_ref, out_ref, send_ref, buffer, sems, sums, terms, shifted,
    ):
        step = pl.program_id(0)

        @pl.when(step == 0)
        def _():
            copies = weights.copies(w_ref, buffer, sems)
            for copy in copies:
                copy.start()
            sums[...] = jnp.zeros_like(sums)
            back_terms(terms, total_of(parts_ref), stat_ref, count_ref[0:1, 0:1], narrow)
            clear_edges(shifted, rows, zone)

            def body(index, carry):
                start = pl.multiple_of(index * zone, zone)
                place = pl.ds(start, zone)
                value = back_norm(dz_ref[place, :], h_ref[place, :], stat_ref, terms, mask_ref[place, 0:1])
                low_ref[place, :] = value.astype(BF16)
                store_shifted(shifted, pl.multiple_of(start + zone, zone), value, zone, narrow)
                return carry

            lax.fori_loop(0, rows // zone, body, 0)
            for copy in copies:
                copy.wait()

        base = step * strip_rows
        total = None
        for tap_row in range(3):
            here = pl.ds(pl.multiple_of(base + (2 - tap_row) * zone, 16), strip_rows)
            for tap_col in range(3):
                tap = tap_row * 3 + tap_col
                piece = shifted[here, (2 - tap_col) * narrow : (3 - tap_col) * narrow]
                part = dot_nt(piece, buffer[tap * narrow : (tap + 1) * narrow])
                total = part if total is None else total + part
        place = pl.ds(pl.multiple_of(base, 16), strip_rows)
        total = total * silu_slope(normed_of(first_ref[...], first_stat)) * mask_ref[place, 1:2]
        out_ref[...] = total
        sums[0:8] += fold_rows(total)
        sums[8:16] += fold_rows(total * first_ref[...])

        @pl.when(step == steps - 1)
        def _():
            send_back_sums(send_ref, sums, first_stat)

    send = (devices, 2 * narrow // LANES, LANES)
    return launch(
        kernel, "back_conv", (steps,),
        (dz, hidden, parts, stat_two, counts, norms, masks, first_hidden, stat_one, weights),
        [
            whole(dz.shape), whole(hidden.shape), whole(parts.shape), whole(stat_two.shape), whole(counts.shape),
            whole(norms.shape), whole(masks.shape), strip(strip_rows, narrow), whole(stat_one.shape), ANYWHERE,
        ],
        (out_of((rows, narrow), BF16), out_of((rows, narrow), F32), out_of(send, F32)),
        (whole((rows, narrow)), strip(strip_rows, narrow), whole(send)),
        weights.scratch() + [pltpu.VMEM((16, narrow), F32), pltpu.VMEM((8, narrow), F32), pltpu.VMEM((rows + 2 * zone, 3 * narrow), BF16)],
        2 * rows * 9 * narrow * narrow,
    )


def back_reduce(dz, first_hidden, parts, stat_one, counts, norms, masks, ds, hidden, inputs, stat_wide, weights, layer, devices):
    rows, narrow = dz.shape
    wide = ds.shape[1]
    strip_rows = block_rows(rows, 6)
    steps = rows // strip_rows

    def kernel(
        dz_ref, first_ref, parts_ref, first_stat, count_ref, norm_ref, mask_ref, ds_ref, h_ref, x_ref, stat_ref, w_ref,
        low_ref, out_ref, send_ref, buffer, sems, sums, terms,
    ):
        step = pl.program_id(0)

        @pl.when(step == 0)
        def _():
            copies = weights.copies(w_ref, buffer, sems)
            for copy in copies:
                copy.start()
            sums[...] = jnp.zeros_like(sums)
            back_terms(terms, total_of(parts_ref), first_stat, count_ref[0:1, 0:1], narrow)
            for copy in copies:
                copy.wait()

        low = back_norm(dz_ref[...], first_ref[...], first_stat, terms, mask_ref[:, 0:1]).astype(BF16)
        low_ref[...] = low
        grad = dot_nt(low, buffer[...]) + ds_ref[...].astype(F32)
        hidden_here = h_ref[...].astype(F32)
        total = grad * silu_slope(x_ref[...].astype(F32) + normed_of(hidden_here, stat_ref))
        out_ref[...] = total.astype(BF16)
        sums[0:8] += fold_rows(total)
        sums[8:16] += fold_rows(total * hidden_here)

        @pl.when(step == steps - 1)
        def _():
            send_back_sums(send_ref, sums, stat_ref)

    send = (devices, 2 * wide // LANES, LANES)
    return launch(
        kernel, "back_reduce", (steps,),
        (dz, first_hidden, parts, stat_one, counts, norms, masks, ds, hidden, inputs, stat_wide, weights),
        [
            strip(strip_rows, narrow), strip(strip_rows, narrow), whole(parts.shape), whole(stat_one.shape), whole(counts.shape),
            whole(norms.shape), strip(strip_rows, 2), strip(strip_rows, wide), strip(strip_rows, wide), strip(strip_rows, wide),
            whole(stat_wide.shape), ANYWHERE,
        ],
        (out_of((rows, narrow), BF16), out_of((rows, wide), BF16), out_of(send, F32)),
        (strip(strip_rows, narrow), strip(strip_rows, wide), whole(send)),
        weights.scratch() + [pltpu.VMEM((16, wide), F32), pltpu.VMEM((8, narrow), F32)],
        2 * rows * wide * narrow,
    )


def last_back(dz, first_hidden, parts, stat_one, counts, masks):
    rows, narrow = dz.shape
    strip_rows = block_rows(rows, 3)

    def kernel(dz_ref, first_ref, parts_ref, first_stat, count_ref, mask_ref, low_ref, terms):
        @pl.when(pl.program_id(0) == 0)
        def _():
            back_terms(terms, total_of(parts_ref), first_stat, count_ref[0:1, 0:1], narrow)

        low_ref[...] = back_norm(dz_ref[...], first_ref[...], first_stat, terms, mask_ref[:, 0:1]).astype(BF16)

    return launch(
        kernel, "last_back", (rows // strip_rows,),
        (dz, first_hidden, parts, stat_one, counts, masks),
        [
            strip(strip_rows, narrow), strip(strip_rows, narrow), whole(parts.shape), whole(stat_one.shape), whole(counts.shape),
            strip(strip_rows, 2),
        ],
        out_of((rows, narrow), BF16),
        strip(strip_rows, narrow),
        [pltpu.VMEM((8, narrow), F32)],
        rows * narrow,
    )


def weight_grad(left, right, owners):
    rows, depth = left.shape
    narrow = right.shape[1]
    tile = min(depth, 512)

    def kernel(left_ref, right_ref, kept_ref, sent_ref):
        total = dot_tn(left_ref[...], right_ref[...])
        store_halves(kept_ref, sent_ref, (), [total[:, o * LANES : (o + 1) * LANES] for o in range(owners)])

    half = out_of((owners // 2, depth, LANES), BF16)
    half_spec = pl.BlockSpec((owners // 2, tile, LANES), lambda i: (0, i, 0))

    return launch(
        kernel, "weight_grad", (depth // tile,),
        (left, right),
        [pl.BlockSpec((rows, tile), lambda i: (0, i)), whole(right.shape)],
        (half, half),
        (half_spec, half_spec),
        [],
        2 * rows * depth * narrow,
    )


def spatial_grad(act, right, owners, zone):
    rows, narrow = act.shape

    def kernel(act_ref, right_ref, kept_ref, sent_ref, shifted):
        tap = pl.program_id(0)

        @pl.when(tap == 0)
        def _():
            clear_edges(shifted, rows, zone)

            def body(index, carry):
                start = pl.multiple_of(index * zone, zone)
                value = act_ref[pl.ds(start, zone), :].astype(F32)
                store_shifted(shifted, pl.multiple_of(start + zone, zone), value, zone, narrow)
                return carry

            lax.fori_loop(0, rows // zone, body, 0)

        for tap_col in range(3):
            piece = shifted[pl.ds(pl.multiple_of(tap * zone, zone), rows), tap_col * narrow : (tap_col + 1) * narrow]
            total = dot_tn(piece, right_ref[...])
            place = (slice(tap_col * narrow, (tap_col + 1) * narrow),)
            store_halves(kept_ref, sent_ref, place, [total[:, o * LANES : (o + 1) * LANES] for o in range(owners)])

    half = out_of((owners // 2, 9 * narrow, LANES), BF16)
    half_spec = pl.BlockSpec((owners // 2, 3 * narrow, LANES), lambda i: (0, i, 0))

    return launch(
        kernel, "spatial_grad", (3,),
        (act, right),
        [whole(act.shape), whole(right.shape)],
        (half, half),
        (half_spec, half_spec),
        [pltpu.VMEM((rows + 2 * zone, 3 * narrow), BF16)],
        2 * rows * 9 * narrow * narrow,
    )


def gather_rows(items, olds, flipped):
    sizes = [total.shape[0] for _, _, total in items]
    heights = [size + -size % 16 for size in sizes]
    starts = [sum(heights[:i]) for i in range(len(heights))]
    kinds = sorted({kind for _, kind, _ in items})

    def kernel(*refs):
        grads, sources, out_ref = refs[: len(items)], refs[len(items) : -1], refs[-1]
        for (layer, kind, _), grad, size, height, start in zip(items, grads, sizes, heights, starts):
            old = sources[kinds.index(kind)][layer]
            value = MOMENTUM * (old if flipped[kind] else old.T) + grad[...].astype(F32)
            if height > size:
                value = jnp.concatenate([value, jnp.zeros((height - size, LANES), F32)], axis=0)
            out_ref[start : start + height] = value.astype(BF16)

    operands = [total for _, _, total in items] + [olds[kind] for kind in kinds]
    shape = (sum(heights), LANES)
    low = launch(
        kernel, "momenta_low", (1,), operands, [whole(a.shape) for a in operands], out_of(shape, BF16), whole(shape), [],
        2**20,
    )
    return lax.all_gather(low, "owner"), starts


def new_momenta(items, olds, flipped):
    kinds = len(olds)

    def kernel(*refs):
        grads, sources, outs = refs[: len(items)], refs[len(items) : len(items) + kinds], refs[len(items) + kinds :]
        for (layer, kind, _), grad in zip(items, grads):
            value = grad[...].astype(F32)
            outs[kind][layer] = MOMENTUM * sources[kind][layer] + (value if flipped[kind] else value.T)

    operands = [total for _, _, total in items] + list(olds)
    return launch(
        kernel, "new_momenta", (1,), operands, [whole(a.shape) for a in operands],
        tuple(out_of(old.shape, F32) for old in olds), tuple(whole(old.shape) for old in olds), [], 2**20,
    )


def head_update(total, head, head_m, head_v, slots):
    classes, width = head.shape

    def kernel(total_ref, *refs):
        tiles = total_ref.shape[0] // slots
        grad = jnp.concatenate(
            [total_ref[i * slots : i * slots + slots, :].astype(F32)[:classes] for i in range(tiles)], axis=1
        )[:, :width]
        for out_ref, value in zip(refs[3:], adamw(refs[0][...], grad, refs[1][...], refs[2][...], LR_HEAD, DECAY_HEAD)):
            out_ref[...] = value

    operands = [total, head, head_m, head_v]
    return launch(
        kernel, "head_update", (1,), operands, [whole(a.shape) for a in operands],
        (out_of(head.shape, F32),) * 3, (whole(head.shape),) * 3, [], 2**20,
    )


def norm_update(parts, norms, norm_m, norm_v):
    layers, count = len(parts), len(parts[0])
    narrow = parts[0][0].shape[1] * LANES // 2
    widths = [narrow] * (count - 1) + [norms.shape[2] - narrow * (count - 1)]

    def kernel(*refs):
        tables, (p_ref, m_ref, v_ref), outs = refs[: layers * count], refs[layers * count : -3], refs[-3:]
        for layer in range(layers):
            begin = 0
            for number, width in enumerate(widths):
                table = total_of(tables[layer * count + number])
                span = slice(begin, begin + width)
                begin += width
                for row in range(2):
                    grad = row_of(table, (1 - row) * (width // LANES), width)
                    here = (row, slice(layer, layer + 1), span)
                    for out_ref, value in zip(outs, adamw(p_ref[here], grad, m_ref[here], v_ref[here], LR_VECTOR, 0.0)):
                        out_ref[here] = value

    operands = [part for group in parts for part in group] + [norms, norm_m, norm_v]
    return launch(
        kernel, "norm_update", (1,), operands, [whole(a.shape) for a in operands],
        (out_of(norms.shape, F32),) * 3, (whole(norms.shape),) * 3, [], 2**20,
    )


def upper_pairs(owners):
    return [(i, j) for i in range(owners) for j in range(i, owners)]


def own_grams(gathered, starts, sizes):
    owners = gathered.shape[0]
    pairs = upper_pairs(owners)
    share = len(pairs) * LANES // owners

    def kernel(all_ref, out_ref, packed):
        for number, (start, size) in enumerate(zip(starts, sizes)):
            for place, (i, j) in enumerate(pairs):
                packed[place * LANES : (place + 1) * LANES] = dot_tn(
                    all_ref[i, start : start + size, :], all_ref[j, start : start + size, :]
                )
            own = pl.multiple_of(lax.axis_index("owner") * share, 8)
            out_ref[number] = packed[pl.ds(own, share), :]

    shape = (len(sizes), share, LANES)
    return launch(
        kernel, "own_grams", (1,), (gathered,), [whole(gathered.shape)], out_of(shape, F32), whole(shape),
        [pltpu.VMEM((len(pairs) * LANES, LANES), F32)], 2 * sum(sizes) * len(pairs) * LANES * LANES,
    )


def dp_bits():
    low = lax.axis_size("owner").bit_length() - 1
    return list(range(low, low + lax.axis_size("dp").bit_length() - 1))


def bit_of(bit):
    return (my_index() >> bit) & 1


def split_two(values):
    high = values.astype(BF16)
    return high, (values - high.astype(F32)).astype(BF16)


def dot_fine(left, right):
    return jnp.dot(left, right, precision=lax.Precision.HIGHEST, preferred_element_type=F32)


def dot_split(left, right):
    left_high, left_low = split_two(left)
    right_high, right_low = split_two(right)
    return dot_nn(left_high, right_high) + (dot_nn(left_high, right_low) + dot_nn(left_low, right_high))


def polynomial(packed, owners):
    side = owners * LANES
    pairs = upper_pairs(owners)

    def kernel(packed_ref, out_ref, gram, product):
        for place, (i, j) in enumerate(pairs):
            block = packed_ref[place * LANES : (place + 1) * LANES, :]
            gram[i * LANES : (i + 1) * LANES, j * LANES : (j + 1) * LANES] = block
            if i != j:
                gram[j * LANES : (j + 1) * LANES, i * LANES : (i + 1) * LANES] = block.T
        eye = (
            lax.broadcasted_iota(jnp.int32, (side, side), 0) == lax.broadcasted_iota(jnp.int32, (side, side), 1)
        ).astype(F32)
        trace = jnp.sum(jnp.sum(gram[...] * eye, axis=0, keepdims=True), axis=1, keepdims=True)
        factor = 1.0 / (jnp.sqrt(trace) + 1e-07)
        first = gram[...] * (factor * factor)
        poly = NS_A * eye + NS_B * first + NS_C * dot_fine(first, first)
        gram[...] = dot_fine(dot_fine(first, poly), poly)
        product[...] = poly * factor

        def body(index, carry):
            now = gram[...]
            poly = NS_A * eye + NS_B * now + NS_C * dot_split(now, now)
            gram[...] = dot_split(dot_split(now, poly), poly)
            product[...] = dot_split(product[...], poly)
            return carry

        lax.fori_loop(0, NS_STEPS - 2, body, 0)
        now = gram[...]
        poly = NS_A * eye + NS_B * now + NS_C * dot_split(now, now)
        own = pl.ds(pl.multiple_of(lax.axis_index("owner") * LANES, LANES), LANES)
        out_ref[...] = dot_split(product[own, :], poly).astype(BF16)

    return launch(
        kernel, "polynomial", (1,), (packed,), [whole(packed.shape)], out_of((LANES, side), BF16), whole((LANES, side)),
        [pltpu.VMEM((side, side), F32), pltpu.VMEM((side, side), F32)], 60 * 2 * side**3,
    )


def apply_polynomials(early, late, gathered, starts, products, masters, flipped):
    owners = gathered[0].shape[0]
    y_bit, z_bit = dp_bits()[:2]
    shift = lax.axis_size("owner").bit_length() - 1
    q_own, q_other, q_late = products
    kinds = len(masters)

    def kernel(own_ref, other_ref, late_ref, early_all, late_all, *refs):
        sources, outs = refs[:kinds], refs[kinds:]
        place = lax.axis_index("dp")
        my_y = (place >> (y_bit - shift)) & 1
        my_z = (place >> (z_bit - shift)) & 1

        def finish(layer, kind, poly, all_ref, start):
            size = sources[kind].shape[1 if flipped[kind] else 2]
            total = None
            for o in range(owners):
                left, right = poly[:, o * LANES : (o + 1) * LANES], all_ref[o, start : start + size, :]
                part = dot_nt(right, left) if flipped[kind] else dot_nt(left, right)
                total = part if total is None else total + part
            outs[kind][layer] = sources[kind][layer] * (1.0 - LR_MATRIX * DECAY_MATRIX) - LR_MATRIX * total

        for number, (layer, kind, _) in enumerate(early):
            y, z = number // 2, number % 2
            turn = y ^ my_y
            poly = jnp.where(my_z == z, own_ref[turn].astype(F32), other_ref[turn].astype(F32)).astype(BF16)
            finish(layer, kind, poly, early_all, starts[0][number])
        for number, (layer, kind, _) in enumerate(late):
            finish(layer, kind, late_ref[number ^ my_y], late_all, starts[1][number])

    operands = (q_own, q_other, q_late, gathered[0], gathered[1]) + masters
    outs = tuple(out_of(master.shape, F32) for master in masters)
    return launch(
        kernel, "apply_polynomials", (1,), operands, [whole(a.shape) for a in operands], outs,
        tuple(whole(master.shape) for master in masters), [], 2**31,
    )


def newton_schulz(early, late, olds, masters, flipped):
    y_bit, z_bit, turn_bit = dp_bits()[:3]
    gathered, starts, grams = [], [], []
    for items in (early, late):
        both, begin = gather_rows(items, olds, flipped)
        both, grams = lax.optimization_barrier((both, grams))
        gathered.append(both)
        starts.append(begin)
        grams.append(own_grams(both, begin, [total.shape[0] for _, _, total in items]))
    on_late, moments = bit_of(turn_bit) == 1, None
    for bit in dp_bits():
        if bit == turn_bit:
            continue
        kept, sent = [], []
        for values in grams:
            whole_count = values.shape[0]
            if whole_count > 1:
                halves = values.reshape((2, whole_count // 2) + values.shape[1:])
                kept.append(lax.dynamic_index_in_dim(halves, bit_of(bit), 0, keepdims=False))
                sent.append(lax.dynamic_index_in_dim(halves, 1 - bit_of(bit), 0, keepdims=False))
            else:
                kept.append(values)
                sent.append(values)
        got = swap(jnp.concatenate(sent, axis=0), bit)
        if moments is None:
            moments = new_momenta(early + late, olds, flipped)
            got, moments = lax.optimization_barrier((got, moments))
        grams = [kept[0] + got[: kept[0].shape[0]], kept[1] + got[kept[0].shape[0] :]]
    got = swap(jnp.where(on_late, grams[0][0], grams[1][0]), turn_bit)
    mine = jnp.where(on_late, grams[1][0], grams[0][0]) + got
    packed = lax.all_gather(mine, "owner", tiled=True)
    own = polynomial(packed, gathered[0].shape[0])
    other = swap(own, turn_bit)
    q_early = jnp.where(on_late, other, own)
    q_late = jnp.where(on_late, own, other)
    both = jnp.stack([q_early, q_late])
    pair = jnp.stack([both, swap(both, y_bit)])
    q_own, q_late = pair[:, 0], pair[:, 1]
    q_other = swap(q_own, z_bit)
    return apply_polynomials(early, late, gathered, starts, (q_own, q_other, q_late), masters, flipped), moments


def adamw(weight, grad, first, second, rate, decay):
    first = BETA_ONE * first + (1.0 - BETA_ONE) * grad
    second = BETA_TWO * second + (1.0 - BETA_TWO) * grad * grad
    first_hat = first / (1.0 - BETA_ONE**STEP)
    second_hat = second / (1.0 - BETA_TWO**STEP)
    weight = weight - rate * (first_hat / (jnp.sqrt(second_hat) + ADAM_EPS) + decay * weight)
    return (weight, first, second)


def per_device(
    images, valid_count, labels, loss_weight, w_reduce, w_spatial, w_expand, mom_reduce, mom_spatial, mom_expand,
    head, head_m, head_v, norm_params, norm_m, norm_v, head_bias, bias_m, bias_v,
):
    dp_size, owner_size = lax.axis_size("dp"), lax.axis_size("owner")
    devices = dp_size * owner_size
    count_img, side, _, wide = images.shape
    pixels = side * side
    narrow = w_reduce.shape[1] * owner_size
    zone = count_img * SLOT
    rows = side * zone

    valid = (jnp.arange(count_img, dtype=jnp.int32) < valid_count[0]).astype(jnp.int32)
    weight_img = valid * loss_weight
    tallies = jnp.stack([valid_count[0] * pixels, jnp.sum(weight_img)]).astype(F32)
    tallies = jnp.pad(tallies, (0, 6))[:, None]
    tallies = jnp.broadcast_to(tallies, (8, LANES))

    in_map = (jnp.arange(SLOT) < side).astype(F32)
    pad_mask = jnp.broadcast_to(in_map, (side, count_img, SLOT))
    masks = jnp.stack([pad_mask * valid.astype(F32)[:, None], pad_mask], axis=-1).reshape(rows, 2)
    arrange = lambda maps: jnp.pad(maps, ((0, 0), (0, 0), (0, SLOT - side), (0, 0))).transpose(1, 0, 2, 3).reshape(rows, wide)

    rows_of = (w_reduce.shape[2], w_spatial.shape[2], w_expand.shape[2])
    starts = (0, rows_of[0], rows_of[0] + rows_of[1])
    packs = [
        [part.T.astype(BF16) for part in (w_reduce[layer], w_spatial[layer], w_expand[layer])] for layer in range(LAYERS)
    ]
    mats = []
    if dp_size == 8 and owner_size == 4 and LAYERS == 2:
        first = Gather(packs[0][0], (4, 3, 2, 1, 0))
        first.send()
        first.join()
        first.send()
        half = rows_of[1] // 2
        sets = [packs[0][1][:half], packs[0][1][half:]]
        packed = jnp.concatenate([packs[0][2], packs[1][0]], axis=0)
        third = lax.all_gather(packed, AXES).reshape(dp_size, owner_size, packed.shape[0], LANES)
        first.got, sets, images = lax.optimization_barrier((first.got, sets, images))
        pixels_in = arrange(images)
        others = [Gather(sets[0], (4, 3, 1, 2, 0)), Gather(sets[1], (4, 2, 3, 1, 0))]
        first.join()
        first.send()
        for flow in others:
            flow.send()
        meet([first] + others)
        first.send()
        for flow in others:
            flow.send()
        meet([first] + others)
        first.values, pixels_in, masks, tallies = lax.optimization_barrier((first.values, pixels_in, masks, tallies))
        first.send()
        for flow in others:
            flow.send()
        first.join()
        mats.append(relative_weights([(first.values, first.masks, 0, rows_of[0], 0)], rows_of[0], dp_size, owner_size))
        h1_first, sums = first_reduce(pixels_in, masks, tallies, mats[0], devices)
        got, h1_first, packs[1] = lax.optimization_barrier(([flow.got for flow in others], h1_first, packs[1]))
        for flow, values in zip(others, got):
            flow.got = values
            flow.join()
        for flow in others:
            flow.send()
        first_parts = exchange(sums)
        got, first_parts = lax.optimization_barrier(([flow.got for flow in others], first_parts))
        for flow, values in zip(others, got):
            flow.got = values
            flow.join()
            flow.send()
        meet(others)
        pieces = [(others[i].values, others[i].masks, 0, half, i * half) for i in range(2)]
        mats.append(relative_weights(pieces, rows_of[1], dp_size, owner_size))
        mats.append(gathered_weights(third, 0, rows_of[2]))
    layers_done = len(mats) // 3
    if layers_done:
        packed = jnp.concatenate(packs[1][1:], axis=0)
        gathered = lax.all_gather(packed, AXES).reshape(dp_size, owner_size, packed.shape[0], LANES)
        mats.append(gathered_weights(third, rows_of[2], rows_of[0]))
        mats.append(gathered_weights(gathered, 0, rows_of[1]))
        mats.append(gathered_weights(gathered, rows_of[1], rows_of[2]))
    else:
        for layer in range(LAYERS):
            packed = jnp.concatenate(packs[layer], axis=0)
            gathered = lax.all_gather(packed, AXES).reshape(dp_size, owner_size, packed.shape[0], LANES)
            for kind in range(3):
                piece = gathered[:, :, starts[kind] : starts[kind] + rows_of[kind]]
                piece = piece.transpose(1, 0, 2, 3).reshape(1, owner_size, -1, LANES)
                mats.append(gathered_weights(piece, 0, piece.shape[2]))
    classes = head.shape[0]
    slots = -(-classes // LANES) * LANES
    slack = slots - classes
    head_low = jnp.pad(head.astype(BF16), ((0, slack), (0, 0)))
    head_all = lax.all_gather(head_low, AXES).reshape(dp_size, owner_size, slots, head.shape[1])
    aligned = head.shape[1] % LANES == 0
    if not aligned:
        head_all = head_all.transpose(1, 2, 0, 3).reshape(1, owner_size, slots, wide)
    slot_bias = jnp.pad(head_bias.reshape(owner_size, classes), ((0, 0), (0, slack)), constant_values=-1e30)
    slot_bias = jnp.broadcast_to(slot_bias.reshape(1, -1), (8, owner_size * slots))
    slot_labels = (labels // classes) * slots + labels % classes
    image_cols = jnp.stack([slot_labels, weight_img], axis=1)

    norms = norm_params
    h1, h2, h3, a1, a2, stat1, stat2, stat3 = ([None] * LAYERS for _ in range(8))
    if not layers_done:
        pixels_in = arrange(images)
    inputs = [pixels_in] + [None] * (LAYERS - 1)
    if layers_done:
        h1[0] = h1_first
    else:
        h1[0], sums = first_reduce(pixels_in, masks, tallies, mats[0], devices)
    for layer in range(LAYERS):
        parts = first_parts if layer == 0 and layers_done else exchange(sums)
        if layer == 0:
            counts = jnp.sum(parts[:, parts.shape[1] - 8 :], axis=0)
            weight_total = counts[1, 0]
        a1[layer], h2[layer], stat1[layer], sums = spatial_conv(
            h1[layer], parts, counts, norms, masks, mats[3 * layer + 1], layer, zone, devices
        )
        a2[layer], h3[layer], stat2[layer], sums = expand(
            h2[layer], exchange(sums), counts, norms, masks, mats[3 * layer + 2], layer, devices
        )
        if layer < LAYERS - 1:
            inputs[layer + 1], h1[layer + 1], stat3[layer], sums = close_and_reduce(
                h3[layer], inputs[layer], exchange(sums), counts, norms, masks, mats[3 * layer + 3], layer, devices
            )
    last = LAYERS - 1
    ds, stat3[last], sums, *head_halves = head_step(
        h3[last], inputs[last], exchange(sums), counts, norms, masks, head_all, slot_bias, image_cols, last, pixels, zone, devices
    )
    left = bits_of(dp_size, owner_size)
    rest = list(range(1, len(left)))
    turned = [[0] + rest[turn:] + rest[:turn] for turn in range(3)]
    if not aligned:
        width = head.shape[1]
        head_halves = [
            jnp.pad(
                half.reshape(owner_size // 2, wide // LANES, slots, LANES // width, width).transpose(0, 1, 3, 2, 4),
                ((0, 0),) * 4 + ((0, LANES - width),),
            )
            for half in head_halves
        ]
    blocked = lambda halves: tuple(half.reshape(devices // 2, -1, LANES) for half in halves)
    head_flow = Flow([blocked(head_halves)], left, turned[0])
    flows = [head_flow]
    norm_sums, three_flow, two_flow = [], {}, {}
    wide_rows = 2 * wide // LANES
    for layer in reversed(range(LAYERS)):
        parts3 = exchange(sums)
        if layer == last:
            extra = parts3
        parts3 = advance(parts3, flows)
        dh3, dz2, sums = back_expand(
            ds, h3[layer], parts3, stat3[layer], counts, norms, masks, h2[layer], stat2[layer], mats[3 * layer + 2], layer, devices
        )
        sums = advance(sums, flows)
        grad_three = blocked(weight_grad(dh3, a2[layer], owner_size))
        three_flow[layer] = Flow([grad_three], left, turned[2] if layer > 0 else turned[0])
        flows.append(three_flow[layer])
        parts2 = exchange(sums)
        parts2 = advance(parts2, flows)
        dh2, dz1, sums = back_conv(
            dz2, h2[layer], parts2, stat2[layer], counts, norms, masks, h1[layer], stat1[layer], mats[3 * layer + 1], layer, zone, devices
        )
        sums = advance(sums, flows)
        grad_two = blocked(spatial_grad(a1[layer], dh2, owner_size, zone))
        two_flow[layer] = Fork(grad_two, left, 0, [turned[0 if layer > 0 else 2][1:], turned[1][1:]])
        flows.append(two_flow[layer])
        parts1 = exchange(sums)
        parts1 = advance(parts1, flows)
        if layer > 0:
            dh1, ds, sums = back_reduce(
                dz1, h1[layer], parts1, stat1[layer], counts, norms, masks, ds, h3[layer - 1], inputs[layer - 1], stat3[layer - 1],
                mats[3 * layer], layer, devices,
            )
            sums = advance(sums, flows)
        else:
            dh1 = last_back(dz1, h1[layer], parts1, stat1[layer], counts, masks)
            dh1 = advance(dh1, [two_flow[0]])
        grad_one = blocked(weight_grad(inputs[layer], dh1, owner_size))
        if layer > 0:
            one_flow = Flow([grad_one], left, turned[0])
            flows.append(one_flow)
        norm_sums.insert(0, (parts1, parts2, parts3))
    extra = jnp.sum(extra[:, wide_rows:], axis=0)
    class_rows = owner_size * slots // LANES
    bias_raw = extra[:class_rows].reshape(owner_size, slots)[:, :classes].reshape(-1)
    loss_sum = extra[class_rows, 0]
    grad_bias = bias_raw / weight_total
    last_flow = Flow([grad_one], left, turned[0])
    last_flow.sent = advance(last_flow.sent, flows, True)
    last_flow.send()
    flows.append(last_flow)
    rest_updates = [
        lambda: norm_update(norm_sums, norm_params, norm_m, norm_v),
        lambda: head_update(head_flow.result(), head, head_m, head_v, slots),
    ]
    updates = []
    while rest_updates or any(flow.got is not None for flow in flows):
        if rest_updates:
            updates.append(rest_updates.pop(0)())
        updates = advance(updates, flows, True)
    high, low = LAYERS - 1, 0
    one_low, one_high = last_flow.result(), one_flow.result()
    three_low, three_high = three_flow[low].result(), three_flow[high].result()
    two_low, two_high = two_flow[low].result(), two_flow[high].result()
    early = [(high, 2, three_high), (high, 1, two_high), (high, 0, one_high), (low, 2, three_low)]
    late = [(low, 1, two_low), (low, 0, one_low)]
    stored = lambda arrays: tuple(a if a.shape[2] % LANES == 0 else jnp.swapaxes(a, 1, 2) for a in arrays)
    results = newton_schulz(
        early, late, stored((mom_reduce, mom_spatial, mom_expand)), stored((w_reduce, w_spatial, w_expand)),
        [size % LANES != 0 for size in rows_of],
    )
    updated, moments = (
        [jnp.swapaxes(a, 1, 2) if size % LANES else a for a, size in zip(arrays, rows_of)] for arrays in results
    )
    (new_norm, new_norm_m, new_norm_v), (new_head, new_head_m, new_head_v) = updates
    new_bias, new_bias_m, new_bias_v = adamw(head_bias, grad_bias, bias_m, bias_v, LR_VECTOR, 0.0)
    return (
        loss_sum,
        weight_total,
        updated[0],
        updated[1],
        updated[2],
        moments[0],
        moments[1],
        moments[2],
        new_head,
        new_head_m,
        new_head_v,
        new_norm,
        new_norm_m,
        new_norm_v,
        new_bias,
        new_bias_m,
        new_bias_v,
    )


def solution(mesh):
    return jax.shard_map(
        per_device,
        mesh=mesh,
        in_specs=(
            P(("dp", "owner"), None, None, None),
            P(("dp", "owner")),
            P(("dp", "owner")),
            P(("dp", "owner")),
            P(None, "owner", "dp"),
            P(None, "owner", "dp"),
            P(None, "owner", "dp"),
            P(None, "owner", "dp"),
            P(None, "owner", "dp"),
            P(None, "owner", "dp"),
            P("owner", "dp"),
            P("owner", "dp"),
            P("owner", "dp"),
            P(),
            P(),
            P(),
            P(),
            P(),
            P(),
        ),
        out_specs=(
            P(),
            P(),
            P(None, "owner", "dp"),
            P(None, "owner", "dp"),
            P(None, "owner", "dp"),
            P(None, "owner", "dp"),
            P(None, "owner", "dp"),
            P(None, "owner", "dp"),
            P("owner", "dp"),
            P("owner", "dp"),
            P("owner", "dp"),
            P(),
            P(),
            P(),
            P(),
            P(),
            P(),
        ),
        check_vma=False,
    )
```

```python
import functools
import math

import jax
import jax.numpy as jnp
from jax import lax
from jax.experimental import pallas as pl
from jax.experimental.pallas import tpu as pltpu
from jax.sharding import PartitionSpec as P

LAYERS = 2
NS_STEPS = 5
STEP = 10

AXES = ("dp", "owner")
EPS = 1e-05
NS_A = 3.4445
NS_B = -4.775
NS_C = 2.0315
MOMENTUM = 0.9
LR_MATRIX = 0.5
DECAY_MATRIX = 0.01
BETA_ONE = 0.9
BETA_TWO = 0.999
ADAM_EPS = 1e-08
LR_HEAD = 0.2
DECAY_HEAD = 0.01
LR_VECTOR = 0.4
LANES = 128
SLOT = 8
PATIENT = 280000
F32 = jnp.float32
BF16 = jnp.bfloat16


def device_count():
    return lax.axis_size("dp") * lax.axis_size("owner")


def my_index():
    return lax.axis_index("dp") * lax.axis_size("owner") + lax.axis_index("owner")


def exchange(copies):
    return lax.all_to_all(copies, AXES, 0, 0, tiled=True)


def swap(values, bit):
    count = device_count()
    return lax.ppermute(values, AXES, [(src, src ^ (1 << bit)) for src in range(count)])


def half_of(values, place, side):
    split = values.reshape((2**place, 2, -1) + values.shape[1:])
    picked = lax.dynamic_index_in_dim(split, side, 1, keepdims=False)
    return picked.reshape((-1,) + values.shape[1:])


class Flow:
    def __init__(self, pairs, left, order):
        self.left, self.order = [bit for bit in left if bit != order[0]], list(order[1:])
        self.kept = [kept for kept, _ in pairs]
        self.sent = [sent for _, sent in pairs]
        self.bit = order[0]
        self.values = self.got = None
        self.wait = 1

    def send(self):
        self.got = [swap(sent, self.bit) for sent in self.sent]
        self.wait = 2 if self.order is not None and self.values is not None and self.sent[0].size > PATIENT else 1
        self.sent = None

    def add(self):
        if self.values is None:
            parts = [kept + got for kept, got in zip(self.kept, self.got)]
            self.values = parts[0] if len(parts) == 1 else jnp.concatenate(parts, axis=1)
        else:
            self.values = half_of(self.values, self.place, self.own) + self.got[0]
        self.got = None

    def split(self):
        if self.order:
            self.bit = self.order.pop(0)
            self.place = self.left.index(self.bit)
            self.left.pop(self.place)
            self.own = (my_index() >> self.bit) & 1
            self.sent = [half_of(self.values, self.place, 1 - self.own)]

    def turn(self):
        if self.got is not None:
            self.add()
            self.split()
        if self.sent is not None:
            self.send()

    def result(self):
        while self.got is not None or self.sent is not None:
            self.turn()
        return self.values[0] if self.values.shape[0] == 1 else self.values


class Fork:
    def __init__(self, pair, left, first, orders):
        self.trunk, self.orders, self.branches = Flow([pair], left, [first]), orders, []
        self.wait = 1

    @property
    def parts(self):
        return self.branches or [self.trunk]

    def add(self):
        for part in self.parts:
            part.add()

    def split(self):
        if self.branches:
            for part in self.branches:
                part.split()
            return
        values, left, count = self.trunk.values, self.trunk.left, len(self.orders)
        step = values.shape[1] // count // 16 * 16
        for number, order in enumerate(self.orders):
            piece = values[:, number * step : (number + 1) * step if number < count - 1 else values.shape[1]]
            place = left.index(order[0])
            own = (my_index() >> order[0]) & 1
            self.branches.append(Flow([(half_of(piece, place, own), half_of(piece, place, 1 - own))], left, order))

    def send(self):
        for part in self.parts:
            if part.sent is not None:
                part.send()
        self.wait = max(part.wait for part in self.parts)

    @property
    def got(self):
        got = [part.got for part in self.parts]
        return None if all(values is None for values in got) else got

    @got.setter
    def got(self, values):
        for part, value in zip(self.parts, values or [None] * len(self.parts)):
            part.got = value

    @property
    def sent(self):
        sent = [part.sent for part in self.parts]
        return None if all(values is None for values in sent) else sent

    @sent.setter
    def sent(self, values):
        for part, value in zip(self.parts, values or [None] * len(self.parts)):
            part.sent = value

    def result(self):
        return jnp.concatenate([part.result() for part in self.branches], axis=0)


def advance(ahead, flows, eager=False):
    for flow in flows:
        flow.wait -= flow.got is not None
    moving = [flow for flow in flows if flow.got is not None and (eager or flow.wait <= 0)]
    ahead, got = lax.optimization_barrier((ahead, [flow.got for flow in moving]))
    for flow, values in zip(moving, got):
        flow.got = values
        flow.add()
        flow.split()
    moving = [flow for flow in flows if flow.sent is not None]
    ahead, sent = lax.optimization_barrier((ahead, [flow.sent for flow in moving]))
    for flow, values in zip(moving, sent):
        flow.sent = values
        flow.send()
    return ahead


def bits_of(dp_size, owner_size):
    low = owner_size.bit_length() - 1
    high = dp_size.bit_length() - 1
    return list(range(low - 1, -1, -1)) + list(range(low + high - 1, low - 1, -1))


def silu(values):
    half = 0.5 * values
    return half * jnp.tanh(half) + half


def silu_slope(values):
    half = 0.5 * values
    bend = jnp.tanh(half)
    return 0.5 * (1.0 + bend + half * (1.0 - bend * bend))


def total_of(parts_ref):
    return jnp.sum(parts_ref[...].astype(F32), axis=0)


def row_of(table, start, width):
    count = width // LANES
    return jnp.concatenate([table[start + i : start + i + 1, :] for i in range(count)], axis=1)


def send_rows(out_ref, rows):
    pieces = [row[:, i * LANES : (i + 1) * LANES] for row in rows for i in range(row.shape[1] // LANES)]
    block = jnp.concatenate(pieces, axis=0).astype(out_ref.dtype)
    out_ref[...] = jnp.broadcast_to(block[None], (out_ref.shape[0],) + block.shape)


def fold_rows(values):
    return jnp.sum(values.reshape(values.shape[0] // 8, 8, values.shape[1]), axis=0)


def norm_of(parts_ref, count, width):
    table = total_of(parts_ref)
    centre = row_of(table, 0, width) / count
    spread = row_of(table, width // LANES, width) / count - centre * centre
    return centre, lax.rsqrt(spread + EPS)


def keep_norm(stat_ref, centre, inverse, gain, bias):
    scale = inverse * gain
    rows = [centre, inverse, scale, bias - centre * scale]
    stat_ref[...] = jnp.concatenate(rows + [jnp.zeros_like(centre)] * 4, axis=0)


def normed_of(values, stat_ref):
    return values * stat_ref[2:3] + stat_ref[3:4]


def back_terms(terms, table, stat_ref, count, width):
    bias_sum, gain_sum = row_of(table, 0, width), row_of(table, width // LANES, width)
    centre, inverse, scale = stat_ref[0:1], stat_ref[1:2], stat_ref[2:3]
    terms[0:1] = scale * (bias_sum - centre * inverse * gain_sum) / count
    terms[1:2] = scale * inverse * gain_sum / count


def back_norm(grad, hidden, stat_ref, terms, mask):
    return grad * stat_ref[2:3] - mask * (terms[0:1] + hidden * terms[1:2])


def send_back_sums(send_ref, sums, stat_ref, more=()):
    bias_sum = jnp.sum(sums[0:8], axis=0, keepdims=True)
    cross = jnp.sum(sums[8:16], axis=0, keepdims=True)
    send_rows(send_ref, [bias_sum, (cross - stat_ref[0:1] * bias_sum) * stat_ref[1:2], *more])


class Weights:
    def __init__(self, operands, blocks, rows, dp_size, owners, masked):
        self.operands, self.blocks, self.rows, self.masked = operands, blocks, rows, masked
        self.owners = owners
        self.depth, self.width = dp_size * rows, owners * LANES

    def scratch(self):
        return [pltpu.VMEM((self.depth, self.width), BF16), pltpu.SemaphoreType.DMA((len(self.blocks),))]

    def copies(self, refs, buffer, sems):
        shift = self.owners.bit_length() - 1
        me = (lax.axis_index("dp") << shift) | lax.axis_index("owner") if self.masked else 0
        out = []
        for number, (operand, index, start, rows, device, offset) in enumerate(self.blocks):
            device = me ^ device
            base, lane = (device >> shift) * self.rows + offset, (device & (self.owners - 1)) * LANES
            if self.masked:
                base, lane = pl.multiple_of(base, 16), pl.multiple_of(lane, LANES)
            out.append(
                pltpu.make_async_copy(
                    refs[operand].at[index + (pl.ds(start, rows),)],
                    buffer.at[pl.ds(base, rows), pl.ds(lane, LANES)],
                    sems.at[number],
                )
            )
        return out


class HeadWeights(Weights):
    def __init__(self, array, pieces, dp_size, owners, slots, cols):
        self.operands, self.pieces = [array], pieces
        self.shape, self.owners, self.slots = (dp_size, owners * slots, cols), owners, slots

    def scratch(self):
        return [pltpu.VMEM(self.shape, BF16), pltpu.SemaphoreType.DMA((len(self.pieces),))]

    def copies(self, refs, buffer, sems):
        return [
            pltpu.make_async_copy(
                refs[0].at[source], buffer.at[d, pl.ds(first, self.slots), pl.ds(column, width)], sems.at[number]
            )
            for number, (source, d, first, column, width) in enumerate(self.pieces)
        ]


def gathered_weights(array, start, rows):
    dp_size, owners = array.shape[:2]
    blocks = [(0, (d, o), start, rows, d * owners + o, 0) for d in range(dp_size) for o in range(owners)]
    return Weights([array], blocks, rows, dp_size, owners, False)


def relative_weights(pieces, rows, dp_size, owners):
    operands, blocks = [], []
    for arrays, masks, start, height, offset in pieces:
        for array, names in zip(arrays, masks):
            for index, mask in enumerate(names):
                blocks.append((len(operands), (index,), start, height, mask, offset))
            operands.append(array)
    return Weights(operands, blocks, rows, dp_size, owners, True)


class Gather:
    def __init__(self, block, order):
        self.values, self.masks, self.order = block[None], [0], list(order)

    def send(self):
        self.bit = self.order.pop(0)
        self.got = swap(self.values, self.bit)

    def join(self):
        more = [mask ^ (1 << self.bit) for mask in self.masks]
        if self.order:
            self.values, self.masks = jnp.concatenate([self.values, self.got], axis=0), self.masks + more
        else:
            self.values, self.masks = [self.values, self.got], [self.masks, more]


def meet(flows):
    got = lax.optimization_barrier([flow.got for flow in flows])
    for flow, values in zip(flows, got):
        flow.got = values
        flow.join()


def whole(shape):
    return pl.BlockSpec(shape, lambda *ids: (0,) * len(shape), pipeline_mode=pl.Buffered(1))


def strip(rows, width):
    return pl.BlockSpec((rows, width), lambda i: (i, 0))


ANYWHERE = pl.BlockSpec(memory_space=pl.ANY)
SCALAR = pl.BlockSpec(memory_space=pltpu.SMEM)


def launch(kernel, name, grid, operands, specs, outs, out_specs, scratch, flops):
    arrays, flat_specs, groups = [], [], []
    for operand, spec in zip(operands, specs):
        group = operand.operands if isinstance(operand, Weights) else [operand]
        groups.append(len(group) if isinstance(operand, Weights) else 0)
        arrays += group
        flat_specs += [spec] * len(group)

    def grouped(*refs):
        refs, firsts = list(refs), []
        for count in groups:
            if count:
                firsts.append(tuple(refs[:count]))
                refs = refs[count:]
            else:
                firsts.append(refs.pop(0))
        kernel(*firsts, *refs)

    moved = sum(math.prod(a.shape) * a.dtype.itemsize for a in jax.tree.leaves((arrays, outs)))
    return pl.pallas_call(
        grouped,
        name=name,
        grid=grid,
        in_specs=flat_specs,
        out_specs=out_specs,
        out_shape=outs,
        scratch_shapes=scratch,
        cost_estimate=pl.CostEstimate(flops=flops, bytes_accessed=min(moved, 2**25), transcendentals=0),
        compiler_params=pltpu.CompilerParams(
            vmem_limit_bytes=60 * 2**20, dimension_semantics=("arbitrary",) * len(grid)
        ),
    )(*arrays)


def out_of(shape, dtype):
    return jax.ShapeDtypeStruct(shape, dtype)


def block_rows(rows, parts):
    for count in range(parts, rows):
        if rows % count == 0 and (rows // count) % 16 == 0:
            return rows // count
    return rows


def dot_nn(left, right):
    return jnp.dot(left, right, preferred_element_type=F32)


def dot_nt(left, right):
    return lax.dot_general(left, right, (((1,), (1,)), ((), ())), preferred_element_type=F32)


def dot_tn(left, right):
    return lax.dot_general(left, right, (((0,), (0,)), ((), ())), preferred_element_type=F32)


def store_halves(kept_ref, sent_ref, place, values):
    even = (lax.axis_index("owner") & 1) == 0
    for pair in range(len(values) // 2):
        first, second = values[2 * pair], values[2 * pair + 1]
        kept_ref[(pair,) + place] = jnp.where(even, first, second).astype(BF16)
        sent_ref[(pair,) + place] = jnp.where(even, second, first).astype(BF16)


def first_reduce(images, masks, tallies, weights, devices):
    rows, wide = images.shape
    narrow = weights.width
    strip_rows = block_rows(rows, 3)
    steps = rows // strip_rows

    def kernel(x_ref, mask_ref, tally_ref, w_ref, h_ref, send_ref, buffer, sems, sums):
        step = pl.program_id(0)

        @pl.when(step == 0)
        def _():
            copies = weights.copies(w_ref, buffer, sems)
            for copy in copies:
                copy.start()
            sums[...] = jnp.zeros_like(sums)
            for copy in copies:
                copy.wait()

        hidden = dot_nn(x_ref[...], buffer[...])
        h_ref[...] = hidden
        kept = hidden * mask_ref[:, 0:1]
        sums[0:8] += fold_rows(kept)
        sums[8:16] += fold_rows(kept * hidden)

        @pl.when(step == steps - 1)
        def _():
            rows_here = [jnp.sum(sums[i * 8 : i * 8 + 8], axis=0, keepdims=True) for i in range(2)]
            send_rows(send_ref, rows_here + [tally_ref[i : i + 1] for i in range(8)])

    send = (devices, 2 * narrow // LANES + 8, LANES)
    return launch(
        kernel, "reduce_first", (steps,),
        (images, masks, tallies, weights),
        [strip(strip_rows, wide), strip(strip_rows, 2), whole(tallies.shape), ANYWHERE],
        (out_of((rows, narrow), F32), out_of(send, F32)),
        (strip(strip_rows, narrow), whole(send)),
        weights.scratch() + [pltpu.VMEM((16, narrow), F32)],
        2 * rows * wide * narrow,
    )


def store_shifted(shifted, place, values, zone, narrow):
    for offset in range(3):
        moved = values if offset == 1 else pltpu.roll(values, 1 if offset == 0 else zone - 1, 0)
        shifted[pl.ds(place, zone), offset * narrow : (offset + 1) * narrow] = moved.astype(BF16)


def clear_edges(shifted, rows, zone):
    edge = jnp.zeros((zone, shifted.shape[1]), BF16)
    shifted[0:zone] = edge
    shifted[zone + rows : 2 * zone + rows] = edge


def spatial_conv(hidden, parts, counts, norms, masks, weights, layer, zone, devices):
    rows, narrow = hidden.shape
    strip_rows = block_rows(rows, 3)
    steps = rows // strip_rows

    def kernel(
        h_ref, parts_ref, count_ref, norm_ref, mask_ref, w_ref,
        a_ref, out_ref, stat_ref, send_ref, buffer, sems, sums, shifted,
    ):
        step = pl.program_id(0)

        @pl.when(step == 0)
        def _():
            copies = weights.copies(w_ref, buffer, sems)
            for copy in copies:
                copy.start()
            sums[...] = jnp.zeros_like(sums)
            centre, inverse = norm_of(parts_ref, count_ref[0:1, 0:1], narrow)
            keep_norm(stat_ref, centre, inverse, norm_ref[0, layer : layer + 1, 0:narrow], norm_ref[1, layer : layer + 1, 0:narrow])
            clear_edges(shifted, rows, zone)

            def body(index, carry):
                start = pl.multiple_of(index * zone, zone)
                place = pl.ds(start, zone)
                value = silu(normed_of(h_ref[place, :], stat_ref)) * mask_ref[place, 1:2]
                a_ref[place, :] = value.astype(BF16)
                store_shifted(shifted, pl.multiple_of(start + zone, zone), value, zone, narrow)
                return carry

            lax.fori_loop(0, rows // zone, body, 0)
            for copy in copies:
                copy.wait()

        base = step * strip_rows
        total = None
        for tap in range(3):
            piece = shifted[pl.ds(pl.multiple_of(base + tap * zone, 16), strip_rows), :]
            part = dot_nn(piece, buffer[tap * 3 * narrow : (tap + 1) * 3 * narrow])
            total = part if total is None else total + part
        out_ref[...] = total
        kept = total * mask_ref[pl.ds(pl.multiple_of(base, 16), strip_rows), 0:1]
        sums[0:8] += fold_rows(kept)
        sums[8:16] += fold_rows(kept * total)

        @pl.when(step == steps - 1)
        def _():
            send_rows(send_ref, [jnp.sum(sums[i * 8 : i * 8 + 8], axis=0, keepdims=True) for i in range(2)])

    send = (devices, 2 * narrow // LANES, LANES)
    return launch(
        kernel, "spatial_conv", (steps,),
        (hidden, parts, counts, norms, masks, weights),
        [whole(hidden.shape), whole(parts.shape), whole(counts.shape), whole(norms.shape), whole(masks.shape), ANYWHERE],
        (out_of((rows, narrow), BF16), out_of((rows, narrow), F32), out_of((8, narrow), F32), out_of(send, F32)),
        (whole((rows, narrow)), strip(strip_rows, narrow), whole((8, narrow)), whole(send)),
        weights.scratch() + [pltpu.VMEM((16, narrow), F32), pltpu.VMEM((rows + 2 * zone, 3 * narrow), BF16)],
        2 * rows * 9 * narrow * narrow,
    )


def expand(hidden, parts, counts, norms, masks, weights, layer, devices):
    rows, narrow = hidden.shape
    wide = weights.depth
    strip_rows = block_rows(rows, 4)
    steps = rows // strip_rows

    def kernel(
        h_ref, parts_ref, count_ref, norm_ref, mask_ref, w_ref,
        a_ref, out_ref, stat_ref, send_ref, buffer, sems, sums,
    ):
        step = pl.program_id(0)

        @pl.when(step == 0)
        def _():
            copies = weights.copies(w_ref, buffer, sems)
            for copy in copies:
                copy.start()
            sums[...] = jnp.zeros_like(sums)
            centre, inverse = norm_of(parts_ref, count_ref[0:1, 0:1], narrow)
            span = slice(narrow, 2 * narrow)
            keep_norm(stat_ref, centre, inverse, norm_ref[0, layer : layer + 1, span], norm_ref[1, layer : layer + 1, span])
            for copy in copies:
                copy.wait()

        value = silu(normed_of(h_ref[...], stat_ref)).astype(BF16)
        a_ref[...] = value
        total = dot_nt(value, buffer[...])
        out_ref[...] = total.astype(BF16)
        kept = total * mask_ref[:, 0:1]
        sums[0:8] += fold_rows(kept)
        sums[8:16] += fold_rows(kept * total)

        @pl.when(step == steps - 1)
        def _():
            send_rows(send_ref, [jnp.sum(sums[i * 8 : i * 8 + 8], axis=0, keepdims=True) for i in range(2)])

    send = (devices, 2 * wide // LANES, LANES)
    return launch(
        kernel, "expand", (steps,),
        (hidden, parts, counts, norms, masks, weights),
        [strip(strip_rows, narrow), whole(parts.shape), whole(counts.shape), whole(norms.shape), strip(strip_rows, 2), ANYWHERE],
        (out_of((rows, narrow), BF16), out_of((rows, wide), BF16), out_of((8, narrow), F32), out_of(send, F32)),
        (strip(strip_rows, narrow), strip(strip_rows, wide), whole((8, narrow)), whole(send)),
        weights.scratch() + [pltpu.VMEM((16, wide), F32)],
        2 * rows * wide * narrow,
    )


def close_and_reduce(hidden, inputs, parts, counts, norms, masks, weights, layer, devices):
    rows, wide = hidden.shape
    narrow = weights.width
    strip_rows = block_rows(rows, 6)
    steps = rows // strip_rows

    def kernel(
        h_ref, x_ref, parts_ref, count_ref, norm_ref, mask_ref, w_ref,
        low_ref, out_ref, stat_ref, send_ref, buffer, sems, sums,
    ):
        step = pl.program_id(0)

        @pl.when(step == 0)
        def _():
            copies = weights.copies(w_ref, buffer, sems)
            for copy in copies:
                copy.start()
            sums[...] = jnp.zeros_like(sums)
            centre, inverse = norm_of(parts_ref, count_ref[0:1, 0:1], wide)
            span = slice(2 * narrow, None)
            keep_norm(stat_ref, centre, inverse, norm_ref[0, layer : layer + 1, span], norm_ref[1, layer : layer + 1, span])
            for copy in copies:
                copy.wait()

        value = silu(x_ref[...].astype(F32) + normed_of(h_ref[...].astype(F32), stat_ref))
        low = value.astype(BF16)
        low_ref[...] = low
        total = dot_nn(low, buffer[...])
        out_ref[...] = total
        kept = total * mask_ref[:, 0:1]
        sums[0:8] += fold_rows(kept)
        sums[8:16] += fold_rows(kept * total)

        @pl.when(step == steps - 1)
        def _():
            send_rows(send_ref, [jnp.sum(sums[i * 8 : i * 8 + 8], axis=0, keepdims=True) for i in range(2)])

    send = (devices, 2 * narrow // LANES, LANES)
    return launch(
        kernel, "close_and_reduce", (steps,),
        (hidden, inputs, parts, counts, norms, masks, weights),
        [strip(strip_rows, wide), strip(strip_rows, wide), whole(parts.shape), whole(counts.shape), whole(norms.shape), strip(strip_rows, 2), ANYWHERE],
        (out_of((rows, wide), BF16), out_of((rows, narrow), F32), out_of((8, wide), F32), out_of(send, F32)),
        (strip(strip_rows, wide), strip(strip_rows, narrow), whole((8, wide)), whole(send)),
        weights.scratch() + [pltpu.VMEM((16, narrow), F32)],
        2 * rows * wide * narrow,
    )


def head_step(hidden, inputs, parts, counts, norms, masks, head_weights, slot_bias, image_cols, layer, pixels, zone, devices):
    rows, wide = hidden.shape
    images = zone // SLOT
    dp_size, classes, cols = head_weights.shape
    owners, slots = head_weights.owners, head_weights.slots
    steps = rows // zone
    count_rows = classes // LANES + 8
    tile = LANES

    def kernel(
        h_ref, x_ref, parts_ref, count_ref, norm_ref, mask_ref, head_ref, bias_ref, image_ref,
        ds_ref, stat_ref, send_ref, kept_ref, sent_ref, head_buffer, sems, slopes, kept, piled, pooled, sums, extras,
    ):
        step = pl.program_id(0)

        @pl.when(step == 0)
        def _():
            for copy in head_weights.copies(head_ref, head_buffer, sems):
                copy.start()
            sums[...] = jnp.zeros_like(sums)
            piled[...] = jnp.zeros_like(piled)
            centre, inverse = norm_of(parts_ref, count_ref[0:1, 0:1], wide)
            span = slice(norm_ref.shape[2] - wide, None)
            keep_norm(stat_ref, centre, inverse, norm_ref[0, layer : layer + 1, span], norm_ref[1, layer : layer + 1, span])

        @pl.when(step < steps)
        def _():
            place = pl.ds(pl.multiple_of(step * zone, zone), zone)
            hidden_here = h_ref[...]
            kept[place, :] = hidden_here
            value = x_ref[...].astype(F32) + normed_of(hidden_here.astype(F32), stat_ref)
            half = 0.5 * value
            bend = jnp.tanh(half)
            piled[...] += (half * bend + half) * mask_ref[:, 1:2]
            slopes[place, :] = (0.5 * (1.0 + bend + half * (1.0 - bend * bend)) * mask_ref[:, 1:2]).astype(BF16)

        @pl.when(step == steps - 1)
        def _():
            for copy in head_weights.copies(head_ref, head_buffer, sems):
                copy.wait()
            low = (jnp.sum(piled[...].reshape(images, SLOT, wide), axis=1) * (1.0 / pixels)).astype(BF16)
            flipped = None
            for d in range(dp_size):
                part = dot_nt(head_buffer[d], low[:, d * cols : (d + 1) * cols])
                flipped = part if flipped is None else flipped + part
            logits = flipped.T + bias_ref[0:1, :]
            top = jnp.max(logits, axis=1, keepdims=True)
            shifted = jnp.exp(logits - top)
            mass = jnp.sum(shifted, axis=1, keepdims=True)
            log_total = jnp.log(mass) + top
            spots = lax.broadcasted_iota(jnp.int32, logits.shape, 1)
            onehot = (spots == image_ref[:, 0:1]).astype(F32)
            weight = image_ref[:, 1:2].astype(F32)
            picked = jnp.sum(logits * onehot, axis=1, keepdims=True)
            loss = jnp.sum(weight * (log_total - picked), axis=0, keepdims=True)
            residue = weight * (jnp.exp(logits - log_total) - onehot)
            loss = jnp.broadcast_to(loss, (1, LANES))
            loss_high = loss.astype(BF16).astype(F32)
            loss_middle = (loss - loss_high).astype(BF16).astype(F32)
            extras[0:1] = jnp.sum(residue, axis=0, keepdims=True)
            extras[1:2, 0:LANES] = loss_high
            extras[2:3, 0:LANES] = loss_middle
            extras[3:4, 0:LANES] = loss - loss_high - loss_middle
            exact = residue / count_ref[1:2, 0:1]
            grad, grad_flipped = exact.astype(BF16), exact.T.astype(BF16)
            for d in range(dp_size):
                back = dot_nn(grad, head_buffer[d])
                weight_part = dot_nn(grad_flipped, low[:, d * cols : (d + 1) * cols])
                for i in range(kept_ref.shape[2]):
                    parts = [weight_part[o * slots : (o + 1) * slots, i * tile : (i + 1) * tile] for o in range(owners)]
                    store_halves(kept_ref, sent_ref, (d, i), parts)
                pooled[:, d * cols : (d + 1) * cols] = back * (1.0 / pixels)

        @pl.when(step >= steps)
        def _():
            place = pl.ds(pl.multiple_of((step - steps) * zone, zone), zone)
            spread = jnp.broadcast_to(pooled[...][:, None, :], (images, SLOT, wide)).reshape(zone, wide)
            ds = spread * slopes[place, :].astype(F32)
            ds_ref[...] = ds.astype(BF16)
            sums[0:8] += fold_rows(ds)
            sums[8:16] += fold_rows(ds * kept[place, :].astype(F32))

        @pl.when(step == 2 * steps - 1)
        def _():
            more = [extras[0:1]] + [extras[i : i + 1, 0:LANES] for i in range(1, 4)] + [jnp.zeros((1, (count_rows - 3) * LANES - classes), F32)]
            send_back_sums(send_ref, sums, stat_ref, more)

    send = (devices, 2 * wide // LANES + count_rows, LANES)
    grads = (owners // 2, dp_size, cols // tile, slots, tile)
    once = pl.BlockSpec((zone, wide), lambda i: (jnp.minimum(i, steps - 1), 0))
    later = pl.BlockSpec((zone, wide), lambda i: (jnp.maximum(i - steps, 0), 0))
    return launch(
        kernel, "head_step", (2 * steps,),
        (hidden, inputs, parts, counts, norms, masks, head_weights, slot_bias, image_cols),
        [
            once, once, whole(parts.shape), whole(counts.shape), whole(norms.shape),
            pl.BlockSpec((zone, 2), lambda i: (lax.rem(i, steps), 0)),
            ANYWHERE, whole(slot_bias.shape), whole(image_cols.shape),
        ],
        (out_of((rows, wide), BF16), out_of((8, wide), F32), out_of(send, BF16), out_of(grads, BF16), out_of(grads, BF16)),
        (later, whole((8, wide)), whole(send), whole(grads), whole(grads)),
        head_weights.scratch()
        + [pltpu.VMEM((rows, wide), BF16), pltpu.VMEM((rows, wide), BF16), pltpu.VMEM((zone, wide), F32), pltpu.VMEM((images, wide), F32), pltpu.VMEM((16, wide), F32), pltpu.VMEM((8, classes), F32)],
        6 * images * classes * wide,
    )


def back_expand(ds, hidden, parts, stat_wide, counts, norms, masks, narrow_hidden, stat_narrow, weights, layer, devices):
    rows, wide = ds.shape
    narrow = weights.width
    strip_rows = block_rows(rows, 4)
    steps = rows // strip_rows

    def kernel(
        ds_ref, h_ref, parts_ref, stat_ref, count_ref, norm_ref, mask_ref, narrow_ref, narrow_stat, w_ref,
        low_ref, out_ref, send_ref, buffer, sems, sums, terms,
    ):
        step = pl.program_id(0)

        @pl.when(step == 0)
        def _():
            copies = weights.copies(w_ref, buffer, sems)
            for copy in copies:
                copy.start()
            sums[...] = jnp.zeros_like(sums)
            back_terms(terms, total_of(parts_ref), stat_ref, count_ref[0:1, 0:1], wide)
            for copy in copies:
                copy.wait()

        low = back_norm(ds_ref[...].astype(F32), h_ref[...].astype(F32), stat_ref, terms, mask_ref[:, 0:1]).astype(BF16)
        low_ref[...] = low
        total = dot_nn(low, buffer[...]) * silu_slope(normed_of(narrow_ref[...], narrow_stat))
        out_ref[...] = total
        sums[0:8] += fold_rows(total)
        sums[8:16] += fold_rows(total * narrow_ref[...])

        @pl.when(step == steps - 1)
        def _():
            send_back_sums(send_ref, sums, narrow_stat)

    send = (devices, 2 * narrow // LANES, LANES)
    return launch(
        kernel, "back_expand", (steps,),
        (ds, hidden, parts, stat_wide, counts, norms, masks, narrow_hidden, stat_narrow, weights),
        [
            strip(strip_rows, wide), strip(strip_rows, wide), whole(parts.shape), whole(stat_wide.shape), whole(counts.shape),
            whole(norms.shape), strip(strip_rows, 2), strip(strip_rows, narrow), whole(stat_narrow.shape), ANYWHERE,
        ],
        (out_of((rows, wide), BF16), out_of((rows, narrow), F32), out_of(send, F32)),
        (strip(strip_rows, wide), strip(strip_rows, narrow), whole(send)),
        weights.scratch() + [pltpu.VMEM((16, narrow), F32), pltpu.VMEM((8, wide), F32)],
        2 * rows * wide * narrow,
    )


def back_conv(dz, hidden, parts, stat_two, counts, norms, masks, first_hidden, stat_one, weights, layer, zone, devices):
    rows, narrow = dz.shape
    strip_rows = block_rows(rows, 3)
    steps = rows // strip_rows

    def kernel(
        dz_ref, h_ref, parts_ref, stat_ref, count_ref, norm_ref, mask_ref, first_ref, first_stat, w_ref,
        low_ref, out_ref, send_ref, buffer, sems, sums, terms, shifted,
    ):
        step = pl.program_id(0)

        @pl.when(step == 0)
        def _():
            copies = weights.copies(w_ref, buffer, sems)
            for copy in copies:
                copy.start()
            sums[...] = jnp.zeros_like(sums)
            back_terms(terms, total_of(parts_ref), stat_ref, count_ref[0:1, 0:1], narrow)
            clear_edges(shifted, rows, zone)

            def body(index, carry):
                start = pl.multiple_of(index * zone, zone)
                place = pl.ds(start, zone)
                value = back_norm(dz_ref[place, :], h_ref[place, :], stat_ref, terms, mask_ref[place, 0:1])
                low_ref[place, :] = value.astype(BF16)
                store_shifted(shifted, pl.multiple_of(start + zone, zone), value, zone, narrow)
                return carry

            lax.fori_loop(0, rows // zone, body, 0)
            for copy in copies:
                copy.wait()

        base = step * strip_rows
        total = None
        for tap_row in range(3):
            here = pl.ds(pl.multiple_of(base + (2 - tap_row) * zone, 16), strip_rows)
            for tap_col in range(3):
                tap = tap_row * 3 + tap_col
                piece = shifted[here, (2 - tap_col) * narrow : (3 - tap_col) * narrow]
                part = dot_nt(piece, buffer[tap * narrow : (tap + 1) * narrow])
                total = part if total is None else total + part
        place = pl.ds(pl.multiple_of(base, 16), strip_rows)
        total = total * silu_slope(normed_of(first_ref[...], first_stat)) * mask_ref[place, 1:2]
        out_ref[...] = total
        sums[0:8] += fold_rows(total)
        sums[8:16] += fold_rows(total * first_ref[...])

        @pl.when(step == steps - 1)
        def _():
            send_back_sums(send_ref, sums, first_stat)

    send = (devices, 2 * narrow // LANES, LANES)
    return launch(
        kernel, "back_conv", (steps,),
        (dz, hidden, parts, stat_two, counts, norms, masks, first_hidden, stat_one, weights),
        [
            whole(dz.shape), whole(hidden.shape), whole(parts.shape), whole(stat_two.shape), whole(counts.shape),
            whole(norms.shape), whole(masks.shape), strip(strip_rows, narrow), whole(stat_one.shape), ANYWHERE,
        ],
        (out_of((rows, narrow), BF16), out_of((rows, narrow), F32), out_of(send, F32)),
        (whole((rows, narrow)), strip(strip_rows, narrow), whole(send)),
        weights.scratch() + [pltpu.VMEM((16, narrow), F32), pltpu.VMEM((8, narrow), F32), pltpu.VMEM((rows + 2 * zone, 3 * narrow), BF16)],
        2 * rows * 9 * narrow * narrow,
    )


def back_reduce(dz, first_hidden, parts, stat_one, counts, norms, masks, ds, hidden, inputs, stat_wide, weights, layer, devices):
    rows, narrow = dz.shape
    wide = ds.shape[1]
    strip_rows = block_rows(rows, 6)
    steps = rows // strip_rows

    def kernel(
        dz_ref, first_ref, parts_ref, first_stat, count_ref, norm_ref, mask_ref, ds_ref, h_ref, x_ref, stat_ref, w_ref,
        low_ref, out_ref, send_ref, buffer, sems, sums, terms,
    ):
        step = pl.program_id(0)

        @pl.when(step == 0)
        def _():
            copies = weights.copies(w_ref, buffer, sems)
            for copy in copies:
                copy.start()
            sums[...] = jnp.zeros_like(sums)
            back_terms(terms, total_of(parts_ref), first_stat, count_ref[0:1, 0:1], narrow)
            for copy in copies:
                copy.wait()

        low = back_norm(dz_ref[...], first_ref[...], first_stat, terms, mask_ref[:, 0:1]).astype(BF16)
        low_ref[...] = low
        grad = dot_nt(low, buffer[...]) + ds_ref[...].astype(F32)
        hidden_here = h_ref[...].astype(F32)
        total = grad * silu_slope(x_ref[...].astype(F32) + normed_of(hidden_here, stat_ref))
        out_ref[...] = total.astype(BF16)
        sums[0:8] += fold_rows(total)
        sums[8:16] += fold_rows(total * hidden_here)

        @pl.when(step == steps - 1)
        def _():
            send_back_sums(send_ref, sums, stat_ref)

    send = (devices, 2 * wide // LANES, LANES)
    return launch(
        kernel, "back_reduce", (steps,),
        (dz, first_hidden, parts, stat_one, counts, norms, masks, ds, hidden, inputs, stat_wide, weights),
        [
            strip(strip_rows, narrow), strip(strip_rows, narrow), whole(parts.shape), whole(stat_one.shape), whole(counts.shape),
            whole(norms.shape), strip(strip_rows, 2), strip(strip_rows, wide), strip(strip_rows, wide), strip(strip_rows, wide),
            whole(stat_wide.shape), ANYWHERE,
        ],
        (out_of((rows, narrow), BF16), out_of((rows, wide), BF16), out_of(send, BF16)),
        (strip(strip_rows, narrow), strip(strip_rows, wide), whole(send)),
        weights.scratch() + [pltpu.VMEM((16, wide), F32), pltpu.VMEM((8, narrow), F32)],
        2 * rows * wide * narrow,
    )


def last_grad(inputs, dz, first_hidden, parts, stat_one, counts, masks, owners, zone):
    rows, depth = inputs.shape
    narrow = dz.shape[1]
    tile = min(depth, 512)

    def kernel(x_ref, dz_ref, h_ref, parts_ref, stat_ref, count_ref, mask_ref, kept_ref, sent_ref, terms, low):
        @pl.when(pl.program_id(0) == 0)
        def _():
            back_terms(terms, total_of(parts_ref), stat_ref, count_ref[0:1, 0:1], narrow)

            def body(index, carry):
                place = pl.ds(pl.multiple_of(index * zone, zone), zone)
                value = back_norm(dz_ref[place, :], h_ref[place, :], stat_ref, terms, mask_ref[place, 0:1])
                low[place, :] = value.astype(BF16)
                return carry

            lax.fori_loop(0, rows // zone, body, 0)

        total = dot_tn(x_ref[...], low[...])
        store_halves(kept_ref, sent_ref, (), [total[:, o * LANES : (o + 1) * LANES] for o in range(owners)])

    half = out_of((owners // 2, depth, LANES), BF16)
    half_spec = pl.BlockSpec((owners // 2, tile, LANES), lambda i: (0, i, 0))
    operands = (inputs, dz, first_hidden, parts, stat_one, counts, masks)
    return launch(
        kernel, "last_grad", (depth // tile,),
        operands,
        [pl.BlockSpec((rows, tile), lambda i: (0, i))] + [whole(a.shape) for a in operands[1:]],
        (half, half),
        (half_spec, half_spec),
        [pltpu.VMEM((8, narrow), F32), pltpu.VMEM((rows, narrow), BF16)],
        2 * rows * depth * narrow,
    )


def weight_grad(left, right, owners):
    rows, depth = left.shape
    narrow = right.shape[1]
    tile = min(depth, 512)

    def kernel(left_ref, right_ref, kept_ref, sent_ref):
        total = dot_tn(left_ref[...], right_ref[...])
        store_halves(kept_ref, sent_ref, (), [total[:, o * LANES : (o + 1) * LANES] for o in range(owners)])

    half = out_of((owners // 2, depth, LANES), BF16)
    half_spec = pl.BlockSpec((owners // 2, tile, LANES), lambda i: (0, i, 0))

    return launch(
        kernel, "weight_grad", (depth // tile,),
        (left, right),
        [pl.BlockSpec((rows, tile), lambda i: (0, i)), whole(right.shape)],
        (half, half),
        (half_spec, half_spec),
        [],
        2 * rows * depth * narrow,
    )


def spatial_grad(act, right, owners, zone):
    rows, narrow = act.shape

    def kernel(act_ref, right_ref, kept_ref, sent_ref, shifted):
        tap = pl.program_id(0)

        @pl.when(tap == 0)
        def _():
            clear_edges(shifted, rows, zone)

            def body(index, carry):
                start = pl.multiple_of(index * zone, zone)
                value = act_ref[pl.ds(start, zone), :].astype(F32)
                store_shifted(shifted, pl.multiple_of(start + zone, zone), value, zone, narrow)
                return carry

            lax.fori_loop(0, rows // zone, body, 0)

        for tap_col in range(3):
            piece = shifted[pl.ds(pl.multiple_of(tap * zone, zone), rows), tap_col * narrow : (tap_col + 1) * narrow]
            total = dot_tn(piece, right_ref[...])
            place = (slice(tap_col * narrow, (tap_col + 1) * narrow),)
            store_halves(kept_ref, sent_ref, place, [total[:, o * LANES : (o + 1) * LANES] for o in range(owners)])

    half = out_of((owners // 2, 9 * narrow, LANES), BF16)
    half_spec = pl.BlockSpec((owners // 2, 3 * narrow, LANES), lambda i: (0, i, 0))

    return launch(
        kernel, "spatial_grad", (3,),
        (act, right),
        [whole(act.shape), whole(right.shape)],
        (half, half),
        (half_spec, half_spec),
        [pltpu.VMEM((rows + 2 * zone, 3 * narrow), BF16)],
        2 * rows * 9 * narrow * narrow,
    )


def places_of(items):
    heights = [total.shape[0] + -total.shape[0] % 16 for _, _, total in items]
    return heights, [sum(heights[:i]) for i in range(len(heights))]


def low_momenta(items, olds, flipped):
    heights, starts = places_of(items)
    kinds = sorted({kind for _, kind, _ in items})

    def kernel(*refs):
        grads, sources, out_ref = refs[: len(items)], refs[len(items) : -1], refs[-1]
        for (layer, kind, total), grad, height, start in zip(items, grads, heights, starts):
            old, size = sources[kinds.index(kind)][layer], total.shape[0]
            value = MOMENTUM * (old if flipped[kind] else old.T) + grad[...].astype(F32)
            if height > size:
                value = jnp.concatenate([value, jnp.zeros((height - size, LANES), F32)], axis=0)
            out_ref[start : start + height] = value.astype(BF16)

    operands = [total for _, _, total in items] + [olds[kind] for kind in kinds]
    shape = (sum(heights), LANES)
    return launch(
        kernel, "momenta_low", (1,), operands, [whole(a.shape) for a in operands], out_of(shape, BF16), whole(shape), [],
        2**20,
    )


def new_momenta(items, olds, flipped):
    kinds = len(olds)

    def kernel(*refs):
        grads, sources, outs = refs[: len(items)], refs[len(items) : len(items) + kinds], refs[len(items) + kinds :]
        for (layer, kind, _), grad in zip(items, grads):
            value = grad[...].astype(F32)
            outs[kind][layer] = MOMENTUM * sources[kind][layer] + (value if flipped[kind] else value.T)

    operands = [total for _, _, total in items] + list(olds)
    return launch(
        kernel, "new_momenta", (1,), operands, [whole(a.shape) for a in operands],
        tuple(out_of(old.shape, F32) for old in olds), tuple(whole(old.shape) for old in olds), [], 2**20,
    )


def head_update(total, head, head_m, head_v, slots):
    classes, width = head.shape

    def kernel(total_ref, *refs):
        tiles = total_ref.shape[0] // slots
        grad = jnp.concatenate(
            [total_ref[i * slots : i * slots + slots, :].astype(F32)[:classes] for i in range(tiles)], axis=1
        )[:, :width]
        for out_ref, value in zip(refs[3:], adamw(refs[0][...], grad, refs[1][...], refs[2][...], LR_HEAD, DECAY_HEAD)):
            out_ref[...] = value

    operands = [total, head, head_m, head_v]
    return launch(
        kernel, "head_update", (1,), operands, [whole(a.shape) for a in operands],
        (out_of(head.shape, F32),) * 3, (whole(head.shape),) * 3, [], 2**20,
    )


def norm_update(parts, norms, norm_m, norm_v):
    layers, count = len(parts), len(parts[0])
    narrow = parts[0][0].shape[1] * LANES // 2
    widths = [narrow] * (count - 1) + [norms.shape[2] - narrow * (count - 1)]

    def kernel(*refs):
        tables, (p_ref, m_ref, v_ref), outs = refs[: layers * count], refs[layers * count : -3], refs[-3:]
        for layer in range(layers):
            begin = 0
            for number, width in enumerate(widths):
                table = total_of(tables[layer * count + number])
                span = slice(begin, begin + width)
                begin += width
                for row in range(2):
                    grad = row_of(table, (1 - row) * (width // LANES), width)
                    here = (row, slice(layer, layer + 1), span)
                    for out_ref, value in zip(outs, adamw(p_ref[here], grad, m_ref[here], v_ref[here], LR_VECTOR, 0.0)):
                        out_ref[here] = value

    operands = [part for group in parts for part in group] + [norms, norm_m, norm_v]
    return launch(
        kernel, "norm_update", (1,), operands, [whole(a.shape) for a in operands],
        (out_of(norms.shape, F32),) * 3, (whole(norms.shape),) * 3, [], 2**20,
    )


def upper_pairs(owners):
    return [(i, j) for i in range(owners) for j in range(i, owners)]


def own_grams(gathered, items):
    gathered, relative = zip(*gathered)
    owners = gathered[0].shape[0]
    pairs = upper_pairs(owners)
    share = len(pairs) * LANES // owners

    def kernel(*refs):
        sources, out_ref, packed = refs[: len(gathered)], refs[-2], refs[-1]
        me = lax.axis_index("owner")
        own = pl.multiple_of(me * share, 8)
        for number, (operand, start, size) in enumerate(items):
            for place, (i, j) in enumerate(pairs):
                if relative[operand]:
                    i, j = i ^ me, j ^ me
                packed[place * LANES : (place + 1) * LANES] = dot_tn(
                    sources[operand][i, start : start + size, :], sources[operand][j, start : start + size, :]
                )
            out_ref[number] = packed[pl.ds(own, share), :]
        for number in range(len(items), 4):
            out_ref[number] = jnp.zeros((share, LANES), F32)

    shape = (4, share, LANES)
    return launch(
        kernel, "own_grams", (1,), list(gathered), [whole(a.shape) for a in gathered], out_of(shape, F32), whole(shape),
        [pltpu.VMEM((len(pairs) * LANES, LANES), F32)], 2**27,
    )


def dp_bits():
    low = lax.axis_size("owner").bit_length() - 1
    return list(range(low, low + lax.axis_size("dp").bit_length() - 1))


def bit_of(bit):
    return (my_index() >> bit) & 1


def split_two(values):
    high = values.astype(BF16)
    return high, (values - high.astype(F32)).astype(BF16)


def dot_fine(left, right):
    return jnp.dot(left, right, precision=lax.Precision.HIGHEST, preferred_element_type=F32)


def dot_split(left, right):
    left_high, left_low = split_two(left)
    right_high, right_low = split_two(right)
    return dot_nn(left_high, right_high) + (dot_nn(left_high, right_low) + dot_nn(left_low, right_high))


def polynomial(packed, owners):
    side = owners * LANES
    pairs = upper_pairs(owners)

    def kernel(packed_ref, out_ref, gram, product):
        for place, (i, j) in enumerate(pairs):
            block = packed_ref[place * LANES : (place + 1) * LANES, :]
            gram[i * LANES : (i + 1) * LANES, j * LANES : (j + 1) * LANES] = block
            if i != j:
                gram[j * LANES : (j + 1) * LANES, i * LANES : (i + 1) * LANES] = block.T
        eye = (
            lax.broadcasted_iota(jnp.int32, (side, side), 0) == lax.broadcasted_iota(jnp.int32, (side, side), 1)
        ).astype(F32)
        trace = jnp.sum(jnp.sum(gram[...] * eye, axis=0, keepdims=True), axis=1, keepdims=True)
        factor = 1.0 / (jnp.sqrt(trace) + 1e-07)
        first = gram[...] * (factor * factor)
        poly = NS_A * eye + NS_B * first + NS_C * dot_fine(first, first)
        gram[...] = dot_fine(dot_fine(first, poly), poly)
        product[...] = poly * factor

        def body(index, carry):
            now = gram[...]
            poly = NS_A * eye + NS_B * now + NS_C * dot_split(now, now)
            gram[...] = dot_split(dot_split(now, poly), poly)
            product[...] = dot_split(product[...], poly)
            return carry

        lax.fori_loop(0, NS_STEPS - 2, body, 0)
        now = gram[...]
        poly = NS_A * eye + NS_B * now + NS_C * dot_split(now, now)
        own = pl.ds(pl.multiple_of(lax.axis_index("owner") * LANES, LANES), LANES)
        out_ref[...] = dot_split(product[own, :], poly).astype(BF16)

    return launch(
        kernel, "polynomial", (1,), (packed,), [whole(packed.shape)], out_of((LANES, side), BF16), whole((LANES, side)),
        [pltpu.VMEM((side, side), F32), pltpu.VMEM((side, side), F32)], 60 * 2 * side**3,
    )


def apply_polynomials(early, late, products, masters, flipped):
    sets = [list(zip(*arrays)) for arrays, _ in (early, late)]
    owners = sets[0][0][0].shape[0]
    y_bit, z_bit, turn_bit = dp_bits()[:3]
    shift = lax.axis_size("owner").bit_length() - 1
    kinds = len(masters)
    counts = [len(arrays) for arrays, _ in sets]

    def kernel(pair_ref, beside_ref, far_ref, *refs):
        arrays = [refs[: counts[0]], refs[counts[0] : sum(counts)]]
        sources, outs = refs[sum(counts) : sum(counts) + kinds], refs[sum(counts) + kinds :]
        place = lax.axis_index("dp")
        my_y, my_z, on_late = ((place >> (bit - shift)) & 1 for bit in (y_bit, z_bit, turn_bit))
        for turn, (_, items) in enumerate((early, late)):
            here = on_late ^ turn
            for number, (layer, kind, operand, start) in enumerate(items):
                y, z = number // 2, number % 2
                near = jnp.where(my_y == y, pair_ref[here].astype(F32), beside_ref[here].astype(F32))
                poly = jnp.where(my_z == z, near, far_ref[turn, y ^ my_y].astype(F32)).astype(BF16)
                size = sources[kind].shape[1 if flipped[kind] else 2]
                total = None
                me = lax.axis_index("owner") if sets[turn][1][operand] else 0
                for o in range(owners):
                    left, right = poly[:, o * LANES : (o + 1) * LANES], arrays[turn][operand][o ^ me, start : start + size, :]
                    part = dot_nt(right, left) if flipped[kind] else dot_nt(left, right)
                    total = part if total is None else total + part
                outs[kind][layer] = sources[kind][layer] * (1.0 - LR_MATRIX * DECAY_MATRIX) - LR_MATRIX * total

    operands = list(products) + list(sets[0][0]) + list(sets[1][0]) + list(masters)
    outs = tuple(out_of(master.shape, F32) for master in masters)
    return launch(
        kernel, "apply_polynomials", (1,), operands, [whole(a.shape) for a in operands], outs,
        tuple(whole(master.shape) for master in masters), [], 2**31,
    )


def newton_schulz(early, late, olds, masters, flipped, early_low, late_low):
    y_bit, z_bit, turn_bit = dp_bits()[:3]
    sets, grams, moments, first_got = [], [], None, None
    for groups, lows in ((early, early_low), (late, late_low)):
        arrays, items = [], []
        for group, low in zip(groups, lows):
            items += [(layer, kind, len(arrays), start) for (layer, kind, _), start in zip(group, places_of(group)[1])]
            if low is None:
                values, _ = lax.optimization_barrier((low_momenta(group, olds, flipped), first_got))
                low = lax.all_gather(values, "owner"), False
            arrays.append(low)
        sizes = [total.shape[0] for group in groups for _, _, total in group]
        sets.append((arrays, items))
        values = own_grams(arrays, [item[2:] + (size,) for item, size in zip(items, sizes)])
        for bit in dp_bits():
            if bit == turn_bit:
                continue
            if values.shape[0] > 1:
                halves = values.reshape((2, values.shape[0] // 2) + values.shape[1:])
                kept = lax.dynamic_index_in_dim(halves, bit_of(bit), 0, keepdims=False)
                sent = lax.dynamic_index_in_dim(halves, 1 - bit_of(bit), 0, keepdims=False)
            else:
                kept = sent = values
            sent = lax.optimization_barrier(sent)
            first_got = sent if first_got is None else first_got
            got = swap(sent, bit)
            if groups is late and moments is None:
                moments = new_momenta([item for group in early + late for item in group], olds, flipped)
                got, moments = lax.optimization_barrier((got, moments))
            values = kept + got
        grams.append(values[0])
    on_late = bit_of(turn_bit) == 1
    got = swap(jnp.where(on_late, grams[0], grams[1]), turn_bit)
    mine = jnp.where(on_late, grams[1], grams[0]) + got
    packed = lax.all_gather(mine, "owner", tiled=True)
    own = polynomial(packed, sets[0][0][0][0].shape[0])
    pair = jnp.stack([own, swap(own, turn_bit)])
    beside = swap(pair, y_bit)
    far = jnp.stack([pair, beside], axis=1)
    far = jnp.where(on_late, far[::-1], far)
    return apply_polynomials(sets[0], sets[1], (pair, beside, swap(far, z_bit)), masters, flipped), moments


def adamw(weight, grad, first, second, rate, decay):
    first = BETA_ONE * first + (1.0 - BETA_ONE) * grad
    second = BETA_TWO * second + (1.0 - BETA_TWO) * grad * grad
    first_hat = first / (1.0 - BETA_ONE**STEP)
    second_hat = second / (1.0 - BETA_TWO**STEP)
    weight = weight - rate * (first_hat / (jnp.sqrt(second_hat) + ADAM_EPS) + decay * weight)
    return (weight, first, second)


def per_device(
    images, valid_count, labels, loss_weight, w_reduce, w_spatial, w_expand, mom_reduce, mom_spatial, mom_expand,
    head, head_m, head_v, norm_params, norm_m, norm_v, head_bias, bias_m, bias_v,
):
    dp_size, owner_size = lax.axis_size("dp"), lax.axis_size("owner")
    devices = dp_size * owner_size
    count_img, side, _, wide = images.shape
    pixels = side * side
    narrow = w_reduce.shape[1] * owner_size
    zone = count_img * SLOT
    rows = side * zone

    valid = (jnp.arange(count_img, dtype=jnp.int32) < valid_count[0]).astype(jnp.int32)
    weight_img = valid * loss_weight
    tallies = jnp.stack([valid_count[0] * pixels, jnp.sum(weight_img)]).astype(F32)
    tallies = jnp.pad(tallies, (0, 6))[:, None]
    tallies = jnp.broadcast_to(tallies, (8, LANES))

    in_map = (jnp.arange(SLOT) < side).astype(F32)
    pad_mask = jnp.broadcast_to(in_map, (side, count_img, SLOT))
    masks = jnp.stack([pad_mask * valid.astype(F32)[:, None], pad_mask], axis=-1).reshape(rows, 2)
    arrange = lambda maps: jnp.pad(maps, ((0, 0), (0, 0), (0, SLOT - side), (0, 0))).transpose(1, 0, 2, 3).reshape(rows, wide)

    rows_of = (w_reduce.shape[2], w_spatial.shape[2], w_expand.shape[2])
    starts = (0, rows_of[0], rows_of[0] + rows_of[1])
    packs = [
        [part.T.astype(BF16) for part in (w_reduce[layer], w_spatial[layer], w_expand[layer])] for layer in range(LAYERS)
    ]
    mats = []
    if dp_size == 8 and owner_size == 4 and LAYERS == 2:
        first = Gather(packs[0][0], (4, 3, 2, 1, 0))
        first.send()
        first.join()
        first.send()
        half = rows_of[1] // 2
        sets = [packs[0][1][:half], packs[0][1][half:]]
        packed = jnp.concatenate([packs[0][2], packs[1][0]], axis=0)
        third = lax.all_gather(packed, AXES).reshape(dp_size, owner_size, packed.shape[0], LANES)
        first.got, sets, images = lax.optimization_barrier((first.got, sets, images))
        pixels_in = arrange(images)
        others = [Gather(sets[0], (4, 3, 1, 2, 0)), Gather(sets[1], (4, 2, 3, 1, 0))]
        first.join()
        first.send()
        for flow in others:
            flow.send()
        meet([first] + others)
        first.send()
        for flow in others:
            flow.send()
        meet([first] + others)
        first.values, pixels_in, masks, tallies = lax.optimization_barrier((first.values, pixels_in, masks, tallies))
        first.send()
        for flow in others:
            flow.send()
        first.join()
        mats.append(relative_weights([(first.values, first.masks, 0, rows_of[0], 0)], rows_of[0], dp_size, owner_size))
        h1_first, sums = first_reduce(pixels_in, masks, tallies, mats[0], devices)
        got, h1_first, packs[1] = lax.optimization_barrier(([flow.got for flow in others], h1_first, packs[1]))
        for flow, values in zip(others, got):
            flow.got = values
            flow.join()
        for flow in others:
            flow.send()
        first_parts = exchange(sums)
        got, first_parts = lax.optimization_barrier(([flow.got for flow in others], first_parts))
        for flow, values in zip(others, got):
            flow.got = values
            flow.join()
            flow.send()
        meet(others)
        pieces = [(others[i].values, others[i].masks, 0, half, i * half) for i in range(2)]
        mats.append(relative_weights(pieces, rows_of[1], dp_size, owner_size))
        mats.append(gathered_weights(third, 0, rows_of[2]))
    layers_done = len(mats) // 3
    classes = head.shape[0]
    slots = -(-classes // LANES) * LANES
    slack = slots - classes
    head_low = jnp.pad(head.astype(BF16), ((0, slack), (0, 0)))
    aligned = head.shape[1] % LANES == 0
    if layers_done:
        tiles = head.shape[1] // LANES
        head_tiles = [head_low[:, i * LANES : (i + 1) * LANES] for i in range(tiles)]
        packed = jnp.concatenate(packs[1][1:] + head_tiles, axis=0)
        gathered = lax.all_gather(packed, AXES).reshape(dp_size, owner_size, packed.shape[0], LANES)
        mats.append(gathered_weights(third, rows_of[2], rows_of[0]))
        mats.append(gathered_weights(gathered, 0, rows_of[1]))
        mats.append(gathered_weights(gathered, rows_of[1], rows_of[2]))
        begin = rows_of[1] + rows_of[2]
        pieces = [
            ((d, o, pl.ds(begin + i * slots, slots)), d, o * slots, i * LANES, LANES)
            for d in range(dp_size)
            for o in range(owner_size)
            for i in range(tiles)
        ]
        head_weights = HeadWeights(gathered, pieces, dp_size, owner_size, slots, head.shape[1])
    else:
        for layer in range(LAYERS):
            packed = jnp.concatenate(packs[layer], axis=0)
            gathered = lax.all_gather(packed, AXES).reshape(dp_size, owner_size, packed.shape[0], LANES)
            for kind in range(3):
                piece = gathered[:, :, starts[kind] : starts[kind] + rows_of[kind]]
                piece = piece.transpose(1, 0, 2, 3).reshape(1, owner_size, -1, LANES)
                mats.append(gathered_weights(piece, 0, piece.shape[2]))
        head_all = lax.all_gather(head_low, AXES).reshape(dp_size, owner_size, slots, head.shape[1])
        head_all = head_all.transpose(1, 2, 0, 3).reshape(owner_size, slots, wide)
        pieces = [((o,), 0, o * slots, 0, wide) for o in range(owner_size)]
        head_weights = HeadWeights(head_all, pieces, 1, owner_size, slots, wide)
    slot_bias = jnp.pad(head_bias.reshape(owner_size, classes), ((0, 0), (0, slack)), constant_values=-1e30)
    slot_bias = jnp.broadcast_to(slot_bias.reshape(1, -1), (8, owner_size * slots))
    slot_labels = (labels // classes) * slots + labels % classes
    image_cols = jnp.stack([slot_labels, weight_img], axis=1)

    norms = norm_params
    h1, h2, h3, a1, a2, stat1, stat2, stat3 = ([None] * LAYERS for _ in range(8))
    if not layers_done:
        pixels_in = arrange(images)
    inputs = [pixels_in] + [None] * (LAYERS - 1)
    if layers_done:
        h1[0] = h1_first
    else:
        h1[0], sums = first_reduce(pixels_in, masks, tallies, mats[0], devices)
    for layer in range(LAYERS):
        parts = first_parts if layer == 0 and layers_done else exchange(sums)
        if layer == 0:
            counts = jnp.sum(parts[:, parts.shape[1] - 8 :], axis=0)
            weight_total = counts[1, 0]
        a1[layer], h2[layer], stat1[layer], sums = spatial_conv(
            h1[layer], parts, counts, norms, masks, mats[3 * layer + 1], layer, zone, devices
        )
        a2[layer], h3[layer], stat2[layer], sums = expand(
            h2[layer], exchange(sums), counts, norms, masks, mats[3 * layer + 2], layer, devices
        )
        if layer < LAYERS - 1:
            inputs[layer + 1], h1[layer + 1], stat3[layer], sums = close_and_reduce(
                h3[layer], inputs[layer], exchange(sums), counts, norms, masks, mats[3 * layer + 3], layer, devices
            )
    last = LAYERS - 1
    ds, stat3[last], sums, *head_halves = head_step(
        h3[last], inputs[last], exchange(sums), counts, norms, masks, head_weights, slot_bias, image_cols, last, pixels, zone, devices
    )
    left = bits_of(dp_size, owner_size)
    rest = list(range(1, len(left)))
    turned = [[0] + rest[turn:] + rest[:turn] for turn in range(3)]
    if not layers_done:
        width = head.shape[1]
        head_halves = [
            jnp.pad(
                half.reshape(owner_size // 2, wide // LANES, slots, LANES // width, width).transpose(0, 1, 3, 2, 4),
                ((0, 0),) * 4 + ((0, LANES - width),),
            )
            for half in head_halves
        ]
    blocked = lambda halves: tuple(half.reshape(devices // 2, -1, LANES) for half in halves)
    head_flow = Flow([blocked(head_halves)], left, turned[0])
    flows = [head_flow]
    norm_sums, three_flow, two_flow = [], {}, {}
    wide_rows = 2 * wide // LANES
    for layer in reversed(range(LAYERS)):
        parts3 = exchange(sums)
        if layer == last:
            extra = parts3
        parts3 = advance(parts3, flows)
        dh3, dz2, sums = back_expand(
            ds, h3[layer], parts3, stat3[layer], counts, norms, masks, h2[layer], stat2[layer], mats[3 * layer + 2], layer, devices
        )
        sums = advance(sums, flows)
        grad_three = blocked(weight_grad(dh3, a2[layer], owner_size))
        three_flow[layer] = Flow([grad_three], left, turned[2] if layer > 0 else turned[0])
        flows.append(three_flow[layer])
        parts2 = exchange(sums)
        parts2 = advance(parts2, flows)
        dh2, dz1, sums = back_conv(
            dz2, h2[layer], parts2, stat2[layer], counts, norms, masks, h1[layer], stat1[layer], mats[3 * layer + 1], layer, zone, devices
        )
        sums = advance(sums, flows)
        grad_two = blocked(spatial_grad(a1[layer], dh2, owner_size, zone))
        two_flow[layer] = Fork(grad_two, left, 0, [turned[0 if layer > 0 else 2][1:], turned[1][1:]])
        flows.append(two_flow[layer])
        parts1 = exchange(sums)
        parts1 = advance(parts1, flows)
        if layer > 0:
            dh1, ds, sums = back_reduce(
                dz1, h1[layer], parts1, stat1[layer], counts, norms, masks, ds, h3[layer - 1], inputs[layer - 1], stat3[layer - 1],
                mats[3 * layer], layer, devices,
            )
            sums = advance(sums, flows)
        else:
            grad_one = blocked(
                last_grad(inputs[layer], dz1, h1[layer], parts1, stat1[layer], counts, masks, owner_size, zone)
            )
        if layer > 0:
            grad_one = blocked(weight_grad(inputs[layer], dh1, owner_size))
        if layer > 0:
            one_flow = Flow([grad_one], left, turned[0])
            flows.append(one_flow)
        norm_sums.insert(0, (parts1, parts2, parts3))
    extra = jnp.sum(extra[:, wide_rows:].astype(F32), axis=0)
    class_rows = owner_size * slots // LANES
    bias_raw = extra[:class_rows].reshape(owner_size, slots)[:, :classes].reshape(-1)
    loss_sum = extra[class_rows, 0] + (extra[class_rows + 1, 0] + extra[class_rows + 2, 0])
    grad_bias = bias_raw / weight_total
    last_flow = Flow([grad_one], left, turned[0])
    last_flow.sent = advance(last_flow.sent, [two_flow[0]], True)
    last_flow.send()
    advance([], [last_flow], True)
    flows.append(last_flow)
    high, low = LAYERS - 1, 0
    stored = lambda arrays: tuple(a if a.shape[2] % LANES == 0 else jnp.swapaxes(a, 1, 2) for a in arrays)
    flipped = [size % LANES != 0 for size in rows_of]
    olds = stored((mom_reduce, mom_spatial, mom_expand))
    results = {}
    turns = 0
    while turns < 4 or any(flow.got is not None for flow in flows):
        turns += 1
        if turns == 1:
            results["norm"] = norm_update(norm_sums, norm_params, norm_m, norm_v)
        if turns == 2:
            three_high, two_high, one_high = (flow.result() for flow in (three_flow[high], two_flow[high], one_flow))
            early = [[(high, 2, three_high), (high, 1, two_high), (high, 0, one_high)]]
            rows_all = Gather(low_momenta(early[0], olds, flipped), (0, 1))
            rows_all.send()
            results["early"] = rows_all.got
        if turns == 3:
            results["head"] = head_update(head_flow.result(), head, head_m, head_v, slots)
            rows_all.got = results["early"]
            rows_all.join()
            rows_all.send()
        if turns == 4:
            three_low = three_flow[low].result()
            results["third"] = lax.all_gather(low_momenta([(low, 2, three_low)], olds, flipped), "owner")
        if turns == 3:
            results.pop("early")
        results = advance(results, flows, True)
    rows_all = jnp.concatenate([rows_all.values, rows_all.got], axis=0)
    one_low, two_low = last_flow.result(), two_flow[low].result()
    late = [[(low, 2, three_low)], [(low, 1, two_low), (low, 0, one_low)]]
    outcomes = newton_schulz(
        early, late, olds, stored((w_reduce, w_spatial, w_expand)), flipped, [(rows_all, True)], [(results["third"], False), None]
    )
    updated, moments = (
        [jnp.swapaxes(a, 1, 2) if size % LANES else a for a, size in zip(arrays, rows_of)] for arrays in outcomes
    )
    (new_norm, new_norm_m, new_norm_v), (new_head, new_head_m, new_head_v) = results["norm"], results["head"]
    new_bias, new_bias_m, new_bias_v = adamw(head_bias, grad_bias, bias_m, bias_v, LR_VECTOR, 0.0)
    return (
        loss_sum,
        weight_total,
        updated[0],
        updated[1],
        updated[2],
        moments[0],
        moments[1],
        moments[2],
        new_head,
        new_head_m,
        new_head_v,
        new_norm,
        new_norm_m,
        new_norm_v,
        new_bias,
        new_bias_m,
        new_bias_v,
    )


def solution(mesh):
    return jax.shard_map(
        per_device,
        mesh=mesh,
        in_specs=(
            P(("dp", "owner"), None, None, None),
            P(("dp", "owner")),
            P(("dp", "owner")),
            P(("dp", "owner")),
            P(None, "owner", "dp"),
            P(None, "owner", "dp"),
            P(None, "owner", "dp"),
            P(None, "owner", "dp"),
            P(None, "owner", "dp"),
            P(None, "owner", "dp"),
            P("owner", "dp"),
            P("owner", "dp"),
            P("owner", "dp"),
            P(),
            P(),
            P(),
            P(),
            P(),
            P(),
        ),
        out_specs=(
            P(),
            P(),
            P(None, "owner", "dp"),
            P(None, "owner", "dp"),
            P(None, "owner", "dp"),
            P(None, "owner", "dp"),
            P(None, "owner", "dp"),
            P(None, "owner", "dp"),
            P("owner", "dp"),
            P("owner", "dp"),
            P("owner", "dp"),
            P(),
            P(),
            P(),
            P(),
            P(),
            P(),
        ),
        check_vma=False,
    )
```

```python
import functools
import math

import jax
import jax.numpy as jnp
from jax import lax
from jax.experimental import pallas as pl
from jax.experimental.pallas import tpu as pltpu
from jax.sharding import PartitionSpec as P

LAYERS = 2
NS_STEPS = 5
STEP = 10

AXES = ("dp", "owner")
EPS = 1e-05
NS_A = 3.4445
NS_B = -4.775
NS_C = 2.0315
MOMENTUM = 0.9
LR_MATRIX = 0.5
DECAY_MATRIX = 0.01
BETA_ONE = 0.9
BETA_TWO = 0.999
ADAM_EPS = 1e-08
LR_HEAD = 0.2
DECAY_HEAD = 0.01
LR_VECTOR = 0.4
LANES = 128
SLOT = 8
PATIENT = (2**18, 2**18 + 2**17)
F32 = jnp.float32
BF16 = jnp.bfloat16


def device_count():
    return lax.axis_size("dp") * lax.axis_size("owner")


def my_index():
    return lax.axis_index("dp") * lax.axis_size("owner") + lax.axis_index("owner")


def exchange(copies):
    return lax.all_to_all(copies, AXES, 0, 0, tiled=True)


def swap(values, bit):
    count = device_count()
    return lax.ppermute(values, AXES, [(src, src ^ (1 << bit)) for src in range(count)])


def half_of(values, place, side):
    split = values.reshape((2**place, 2, -1) + values.shape[1:])
    picked = lax.dynamic_index_in_dim(split, side, 1, keepdims=False)
    return picked.reshape((-1,) + values.shape[1:])


class Flow:
    def __init__(self, pairs, left, order):
        self.left, self.order = [bit for bit in left if bit != order[0]], list(order[1:])
        self.kept = [kept for kept, _ in pairs]
        self.sent = [sent for _, sent in pairs]
        self.bit = order[0]
        self.values = self.got = None
        self.wait = 1

    def send(self):
        self.got = [swap(sent, self.bit) for sent in self.sent]
        self.wait = 1 + sum(self.sent[0].size > most for most in PATIENT) if self.values is not None else 1
        self.sent = None

    def add(self):
        if self.values is None:
            parts = [kept + got for kept, got in zip(self.kept, self.got)]
            self.values = parts[0] if len(parts) == 1 else jnp.concatenate(parts, axis=1)
        else:
            self.values = half_of(self.values, self.place, self.own) + self.got[0]
        self.got = None

    def split(self):
        if self.order:
            self.bit = self.order.pop(0)
            self.place = self.left.index(self.bit)
            self.left.pop(self.place)
            self.own = (my_index() >> self.bit) & 1
            self.sent = [half_of(self.values, self.place, 1 - self.own)]

    def turn(self):
        if self.got is not None:
            self.add()
            self.split()
        if self.sent is not None:
            self.send()

    def result(self):
        while self.got is not None or self.sent is not None:
            self.turn()
        return self.values[0] if self.values.shape[0] == 1 else self.values


class Fork:
    def __init__(self, pair, left, first, orders):
        self.trunk, self.orders, self.branches = Flow([pair], left, [first]), orders, []
        self.wait = 1

    @property
    def parts(self):
        return self.branches or [self.trunk]

    def add(self):
        for part in self.parts:
            part.add()

    def split(self):
        if self.branches:
            for part in self.branches:
                part.split()
            return
        values, left, count = self.trunk.values, self.trunk.left, len(self.orders)
        step = values.shape[1] // count // 16 * 16
        for number, order in enumerate(self.orders):
            piece = values[:, number * step : (number + 1) * step if number < count - 1 else values.shape[1]]
            place = left.index(order[0])
            own = (my_index() >> order[0]) & 1
            self.branches.append(Flow([(half_of(piece, place, own), half_of(piece, place, 1 - own))], left, order))

    def send(self):
        for part in self.parts:
            if part.sent is not None:
                part.send()
        self.wait = max(part.wait for part in self.parts)

    @property
    def got(self):
        got = [part.got for part in self.parts]
        return None if all(values is None for values in got) else got

    @got.setter
    def got(self, values):
        for part, value in zip(self.parts, values or [None] * len(self.parts)):
            part.got = value

    @property
    def sent(self):
        sent = [part.sent for part in self.parts]
        return None if all(values is None for values in sent) else sent

    @sent.setter
    def sent(self, values):
        for part, value in zip(self.parts, values or [None] * len(self.parts)):
            part.sent = value

    def result(self):
        return jnp.concatenate([part.result() for part in self.branches], axis=0)


def advance(ahead, flows, eager=False):
    for flow in flows:
        flow.wait -= flow.got is not None
    moving = [flow for flow in flows if flow.got is not None and (eager or flow.wait <= 0)]
    ahead, got = lax.optimization_barrier((ahead, [flow.got for flow in moving]))
    for flow, values in zip(moving, got):
        flow.got = values
        flow.add()
        flow.split()
    moving = [flow for flow in flows if flow.sent is not None]
    ahead, sent = lax.optimization_barrier((ahead, [flow.sent for flow in moving]))
    for flow, values in zip(moving, sent):
        flow.sent = values
        flow.send()
    return ahead


def bits_of(dp_size, owner_size):
    low = owner_size.bit_length() - 1
    high = dp_size.bit_length() - 1
    return list(range(low - 1, -1, -1)) + list(range(low + high - 1, low - 1, -1))


def silu(values):
    half = 0.5 * values
    return half * jnp.tanh(half) + half


def silu_slope(values):
    half = 0.5 * values
    bend = jnp.tanh(half)
    return 0.5 * (1.0 + bend + half * (1.0 - bend * bend))


def total_of(parts_ref):
    return jnp.sum(parts_ref[...].astype(F32), axis=0)


def row_of(table, start, width):
    count = width // LANES
    return jnp.concatenate([table[start + i : start + i + 1, :] for i in range(count)], axis=1)


def send_rows(out_ref, rows):
    pieces = [row[:, i * LANES : (i + 1) * LANES] for row in rows for i in range(row.shape[1] // LANES)]
    block = jnp.concatenate(pieces, axis=0).astype(out_ref.dtype)
    out_ref[...] = jnp.broadcast_to(block[None], (out_ref.shape[0],) + block.shape)


def fold_rows(values):
    return jnp.sum(values.reshape(values.shape[0] // 8, 8, values.shape[1]), axis=0)


def norm_of(parts_ref, count, width):
    table = total_of(parts_ref)
    centre = row_of(table, 0, width) / count
    spread = row_of(table, width // LANES, width) / count - centre * centre
    return centre, lax.rsqrt(spread + EPS)


def keep_norm(stat_ref, centre, inverse, gain, bias):
    scale = inverse * gain
    rows = [centre, inverse, scale, bias - centre * scale]
    stat_ref[...] = jnp.concatenate(rows + [jnp.zeros_like(centre)] * 4, axis=0)


def normed_of(values, stat_ref):
    return values * stat_ref[2:3] + stat_ref[3:4]


def back_terms(terms, table, stat_ref, count, width):
    bias_sum, gain_sum = row_of(table, 0, width), row_of(table, width // LANES, width)
    centre, inverse, scale = stat_ref[0:1], stat_ref[1:2], stat_ref[2:3]
    terms[0:1] = scale * (bias_sum - centre * inverse * gain_sum) / count
    terms[1:2] = scale * inverse * gain_sum / count


def back_norm(grad, hidden, stat_ref, terms, mask):
    return grad * stat_ref[2:3] - mask * (terms[0:1] + hidden * terms[1:2])


def send_back_sums(send_ref, sums, stat_ref, more=()):
    bias_sum = jnp.sum(sums[0:8], axis=0, keepdims=True)
    cross = jnp.sum(sums[8:16], axis=0, keepdims=True)
    send_rows(send_ref, [bias_sum, (cross - stat_ref[0:1] * bias_sum) * stat_ref[1:2], *more])


class Weights:
    def __init__(self, operands, blocks, rows, dp_size, owners, masked):
        self.operands, self.blocks, self.rows, self.masked = operands, blocks, rows, masked
        self.owners = owners
        self.depth, self.width = dp_size * rows, owners * LANES

    def scratch(self):
        return [pltpu.VMEM((self.depth, self.width), BF16), pltpu.SemaphoreType.DMA((len(self.blocks),))]

    def copies(self, refs, buffer, sems):
        shift = self.owners.bit_length() - 1
        me = (lax.axis_index("dp") << shift) | lax.axis_index("owner") if self.masked else 0
        out = []
        for number, (operand, index, start, rows, device, offset) in enumerate(self.blocks):
            device = me ^ device
            base, lane = (device >> shift) * self.rows + offset, (device & (self.owners - 1)) * LANES
            if self.masked:
                base, lane = pl.multiple_of(base, 16), pl.multiple_of(lane, LANES)
            out.append(
                pltpu.make_async_copy(
                    refs[operand].at[index + (pl.ds(start, rows),)],
                    buffer.at[pl.ds(base, rows), pl.ds(lane, LANES)],
                    sems.at[number],
                )
            )
        return out


class HeadWeights(Weights):
    def __init__(self, array, pieces, dp_size, owners, slots, cols):
        self.operands, self.pieces = [array], pieces
        self.shape, self.owners, self.slots = (dp_size, owners * slots, cols), owners, slots

    def scratch(self):
        return [pltpu.VMEM(self.shape, BF16), pltpu.SemaphoreType.DMA((len(self.pieces),))]

    def copies(self, refs, buffer, sems):
        return [
            pltpu.make_async_copy(
                refs[0].at[source], buffer.at[d, pl.ds(first, self.slots), pl.ds(column, width)], sems.at[number]
            )
            for number, (source, d, first, column, width) in enumerate(self.pieces)
        ]


def gathered_weights(array, start, rows):
    dp_size, owners = array.shape[:2]
    blocks = [(0, (d, o), start, rows, d * owners + o, 0) for d in range(dp_size) for o in range(owners)]
    return Weights([array], blocks, rows, dp_size, owners, False)


def relative_weights(pieces, rows, dp_size, owners):
    operands, blocks = [], []
    for arrays, masks, start, height, offset in pieces:
        for array, names in zip(arrays, masks):
            for index, mask in enumerate(names):
                blocks.append((len(operands), (index,), start, height, mask, offset))
            operands.append(array)
    return Weights(operands, blocks, rows, dp_size, owners, True)


class Gather:
    def __init__(self, block, order):
        self.values, self.masks, self.order = block[None], [0], list(order)

    def send(self):
        self.bit = self.order.pop(0)
        self.got = swap(self.values, self.bit)

    def join(self):
        more = [mask ^ (1 << self.bit) for mask in self.masks]
        if self.order:
            self.values, self.masks = jnp.concatenate([self.values, self.got], axis=0), self.masks + more
        else:
            self.values, self.masks = [self.values, self.got], [self.masks, more]


def meet(flows):
    got = lax.optimization_barrier([flow.got for flow in flows])
    for flow, values in zip(flows, got):
        flow.got = values
        flow.join()


def whole(shape):
    return pl.BlockSpec(shape, lambda *ids: (0,) * len(shape), pipeline_mode=pl.Buffered(1))


def strip(rows, width):
    return pl.BlockSpec((rows, width), lambda i: (i, 0))


ANYWHERE = pl.BlockSpec(memory_space=pl.ANY)
SCALAR = pl.BlockSpec(memory_space=pltpu.SMEM)


def launch(kernel, name, grid, operands, specs, outs, out_specs, scratch, flops):
    arrays, flat_specs, groups = [], [], []
    for operand, spec in zip(operands, specs):
        group = operand.operands if isinstance(operand, Weights) else [operand]
        groups.append(len(group) if isinstance(operand, Weights) else 0)
        arrays += group
        flat_specs += [spec] * len(group)

    def grouped(*refs):
        refs, firsts = list(refs), []
        for count in groups:
            if count:
                firsts.append(tuple(refs[:count]))
                refs = refs[count:]
            else:
                firsts.append(refs.pop(0))
        kernel(*firsts, *refs)

    moved = sum(math.prod(a.shape) * a.dtype.itemsize for a in jax.tree.leaves((arrays, outs)))
    return pl.pallas_call(
        grouped,
        name=name,
        grid=grid,
        in_specs=flat_specs,
        out_specs=out_specs,
        out_shape=outs,
        scratch_shapes=scratch,
        cost_estimate=pl.CostEstimate(flops=flops, bytes_accessed=min(moved, 2**25), transcendentals=0),
        compiler_params=pltpu.CompilerParams(
            vmem_limit_bytes=60 * 2**20, dimension_semantics=("arbitrary",) * len(grid)
        ),
    )(*arrays)


def out_of(shape, dtype):
    return jax.ShapeDtypeStruct(shape, dtype)


def block_rows(rows, parts):
    for count in range(parts, rows):
        if rows % count == 0 and (rows // count) % 16 == 0:
            return rows // count
    return rows


def dot_nn(left, right):
    return jnp.dot(left, right, preferred_element_type=F32)


def dot_nt(left, right):
    return lax.dot_general(left, right, (((1,), (1,)), ((), ())), preferred_element_type=F32)


def dot_tn(left, right):
    return lax.dot_general(left, right, (((0,), (0,)), ((), ())), preferred_element_type=F32)


def store_halves(kept_ref, sent_ref, place, values):
    even = (lax.axis_index("owner") & 1) == 0
    for pair in range(len(values) // 2):
        first, second = values[2 * pair], values[2 * pair + 1]
        kept_ref[(pair,) + place] = jnp.where(even, first, second).astype(BF16)
        sent_ref[(pair,) + place] = jnp.where(even, second, first).astype(BF16)


def first_reduce(images, masks, tallies, weights, devices):
    rows, wide = images.shape
    narrow = weights.width
    strip_rows = block_rows(rows, 3)
    steps = rows // strip_rows

    def kernel(x_ref, mask_ref, tally_ref, w_ref, h_ref, send_ref, buffer, sems, sums):
        step = pl.program_id(0)

        @pl.when(step == 0)
        def _():
            copies = weights.copies(w_ref, buffer, sems)
            for copy in copies:
                copy.start()
            sums[...] = jnp.zeros_like(sums)
            for copy in copies:
                copy.wait()

        hidden = dot_nn(x_ref[...], buffer[...])
        h_ref[...] = hidden
        kept = hidden * mask_ref[:, 0:1]
        sums[0:8] += fold_rows(kept)
        sums[8:16] += fold_rows(kept * hidden)

        @pl.when(step == steps - 1)
        def _():
            rows_here = [jnp.sum(sums[i * 8 : i * 8 + 8], axis=0, keepdims=True) for i in range(2)]
            send_rows(send_ref, rows_here + [tally_ref[i : i + 1] for i in range(8)])

    send = (devices, 2 * narrow // LANES + 8, LANES)
    return launch(
        kernel, "reduce_first", (steps,),
        (images, masks, tallies, weights),
        [strip(strip_rows, wide), strip(strip_rows, 2), whole(tallies.shape), ANYWHERE],
        (out_of((rows, narrow), F32), out_of(send, F32)),
        (strip(strip_rows, narrow), whole(send)),
        weights.scratch() + [pltpu.VMEM((16, narrow), F32)],
        2 * rows * wide * narrow,
    )


def store_shifted(shifted, place, values, zone, narrow):
    for offset in range(3):
        moved = values if offset == 1 else pltpu.roll(values, 1 if offset == 0 else zone - 1, 0)
        shifted[pl.ds(place, zone), offset * narrow : (offset + 1) * narrow] = moved.astype(BF16)


def clear_edges(shifted, rows, zone):
    edge = jnp.zeros((zone, shifted.shape[1]), BF16)
    shifted[0:zone] = edge
    shifted[zone + rows : 2 * zone + rows] = edge


def spatial_conv(hidden, parts, counts, norms, masks, weights, layer, zone, devices):
    rows, narrow = hidden.shape
    strip_rows = block_rows(rows, 3)
    steps = rows // strip_rows

    def kernel(
        h_ref, parts_ref, count_ref, norm_ref, mask_ref, w_ref,
        a_ref, out_ref, stat_ref, send_ref, buffer, sems, sums, shifted,
    ):
        step = pl.program_id(0)

        @pl.when(step == 0)
        def _():
            copies = weights.copies(w_ref, buffer, sems)
            for copy in copies:
                copy.start()
            sums[...] = jnp.zeros_like(sums)
            centre, inverse = norm_of(parts_ref, count_ref[0:1, 0:1], narrow)
            keep_norm(stat_ref, centre, inverse, norm_ref[0, layer : layer + 1, 0:narrow], norm_ref[1, layer : layer + 1, 0:narrow])
            clear_edges(shifted, rows, zone)

            def body(index, carry):
                start = pl.multiple_of(index * zone, zone)
                place = pl.ds(start, zone)
                value = silu(normed_of(h_ref[place, :], stat_ref)) * mask_ref[place, 1:2]
                a_ref[place, :] = value.astype(BF16)
                store_shifted(shifted, pl.multiple_of(start + zone, zone), value, zone, narrow)
                return carry

            lax.fori_loop(0, rows // zone, body, 0)
            for copy in copies:
                copy.wait()

        base = step * strip_rows
        total = None
        for tap in range(3):
            piece = shifted[pl.ds(pl.multiple_of(base + tap * zone, 16), strip_rows), :]
            part = dot_nn(piece, buffer[tap * 3 * narrow : (tap + 1) * 3 * narrow])
            total = part if total is None else total + part
        out_ref[...] = total
        kept = total * mask_ref[pl.ds(pl.multiple_of(base, 16), strip_rows), 0:1]
        sums[0:8] += fold_rows(kept)
        sums[8:16] += fold_rows(kept * total)

        @pl.when(step == steps - 1)
        def _():
            send_rows(send_ref, [jnp.sum(sums[i * 8 : i * 8 + 8], axis=0, keepdims=True) for i in range(2)])

    send = (devices, 2 * narrow // LANES, LANES)
    return launch(
        kernel, "spatial_conv", (steps,),
        (hidden, parts, counts, norms, masks, weights),
        [whole(hidden.shape), whole(parts.shape), whole(counts.shape), whole(norms.shape), whole(masks.shape), ANYWHERE],
        (out_of((rows, narrow), BF16), out_of((rows, narrow), F32), out_of((8, narrow), F32), out_of(send, F32)),
        (whole((rows, narrow)), strip(strip_rows, narrow), whole((8, narrow)), whole(send)),
        weights.scratch() + [pltpu.VMEM((16, narrow), F32), pltpu.VMEM((rows + 2 * zone, 3 * narrow), BF16)],
        2 * rows * 9 * narrow * narrow,
    )


def expand(hidden, parts, counts, norms, masks, weights, layer, devices):
    rows, narrow = hidden.shape
    wide = weights.depth
    strip_rows = block_rows(rows, 4)
    steps = rows // strip_rows

    def kernel(
        h_ref, parts_ref, count_ref, norm_ref, mask_ref, w_ref,
        a_ref, out_ref, stat_ref, send_ref, buffer, sems, sums,
    ):
        step = pl.program_id(0)

        @pl.when(step == 0)
        def _():
            copies = weights.copies(w_ref, buffer, sems)
            for copy in copies:
                copy.start()
            sums[...] = jnp.zeros_like(sums)
            centre, inverse = norm_of(parts_ref, count_ref[0:1, 0:1], narrow)
            span = slice(narrow, 2 * narrow)
            keep_norm(stat_ref, centre, inverse, norm_ref[0, layer : layer + 1, span], norm_ref[1, layer : layer + 1, span])
            for copy in copies:
                copy.wait()

        value = silu(normed_of(h_ref[...], stat_ref)).astype(BF16)
        a_ref[...] = value
        total = dot_nt(value, buffer[...])
        out_ref[...] = total.astype(BF16)
        kept = total * mask_ref[:, 0:1]
        sums[0:8] += fold_rows(kept)
        sums[8:16] += fold_rows(kept * total)

        @pl.when(step == steps - 1)
        def _():
            send_rows(send_ref, [jnp.sum(sums[i * 8 : i * 8 + 8], axis=0, keepdims=True) for i in range(2)])

    send = (devices, 2 * wide // LANES, LANES)
    return launch(
        kernel, "expand", (steps,),
        (hidden, parts, counts, norms, masks, weights),
        [strip(strip_rows, narrow), whole(parts.shape), whole(counts.shape), whole(norms.shape), strip(strip_rows, 2), ANYWHERE],
        (out_of((rows, narrow), BF16), out_of((rows, wide), BF16), out_of((8, narrow), F32), out_of(send, F32)),
        (strip(strip_rows, narrow), strip(strip_rows, wide), whole((8, narrow)), whole(send)),
        weights.scratch() + [pltpu.VMEM((16, wide), F32)],
        2 * rows * wide * narrow,
    )


def close_and_reduce(hidden, inputs, parts, counts, norms, masks, weights, layer, devices):
    rows, wide = hidden.shape
    narrow = weights.width
    strip_rows = block_rows(rows, 6)
    steps = rows // strip_rows

    def kernel(
        h_ref, x_ref, parts_ref, count_ref, norm_ref, mask_ref, w_ref,
        low_ref, out_ref, stat_ref, send_ref, buffer, sems, sums,
    ):
        step = pl.program_id(0)

        @pl.when(step == 0)
        def _():
            copies = weights.copies(w_ref, buffer, sems)
            for copy in copies:
                copy.start()
            sums[...] = jnp.zeros_like(sums)
            centre, inverse = norm_of(parts_ref, count_ref[0:1, 0:1], wide)
            span = slice(2 * narrow, None)
            keep_norm(stat_ref, centre, inverse, norm_ref[0, layer : layer + 1, span], norm_ref[1, layer : layer + 1, span])
            for copy in copies:
                copy.wait()

        value = silu(x_ref[...].astype(F32) + normed_of(h_ref[...].astype(F32), stat_ref))
        low = value.astype(BF16)
        low_ref[...] = low
        total = dot_nn(low, buffer[...])
        out_ref[...] = total
        kept = total * mask_ref[:, 0:1]
        sums[0:8] += fold_rows(kept)
        sums[8:16] += fold_rows(kept * total)

        @pl.when(step == steps - 1)
        def _():
            send_rows(send_ref, [jnp.sum(sums[i * 8 : i * 8 + 8], axis=0, keepdims=True) for i in range(2)])

    send = (devices, 2 * narrow // LANES, LANES)
    return launch(
        kernel, "close_and_reduce", (steps,),
        (hidden, inputs, parts, counts, norms, masks, weights),
        [strip(strip_rows, wide), strip(strip_rows, wide), whole(parts.shape), whole(counts.shape), whole(norms.shape), strip(strip_rows, 2), ANYWHERE],
        (out_of((rows, wide), BF16), out_of((rows, narrow), F32), out_of((8, wide), F32), out_of(send, F32)),
        (strip(strip_rows, wide), strip(strip_rows, narrow), whole((8, wide)), whole(send)),
        weights.scratch() + [pltpu.VMEM((16, narrow), F32)],
        2 * rows * wide * narrow,
    )


def head_step(hidden, inputs, parts, counts, norms, masks, head_weights, slot_bias, image_cols, layer, pixels, zone, devices):
    rows, wide = hidden.shape
    images = zone // SLOT
    dp_size, classes, cols = head_weights.shape
    owners, slots = head_weights.owners, head_weights.slots
    steps = rows // zone
    count_rows = classes // LANES + 8
    tile = LANES

    def kernel(
        h_ref, x_ref, parts_ref, count_ref, norm_ref, mask_ref, head_ref, bias_ref, image_ref,
        ds_ref, stat_ref, send_ref, kept_ref, sent_ref, head_buffer, sems, slopes, kept, piled, pooled, sums, extras,
    ):
        step = pl.program_id(0)

        @pl.when(step == 0)
        def _():
            for copy in head_weights.copies(head_ref, head_buffer, sems):
                copy.start()
            sums[...] = jnp.zeros_like(sums)
            piled[...] = jnp.zeros_like(piled)
            centre, inverse = norm_of(parts_ref, count_ref[0:1, 0:1], wide)
            span = slice(norm_ref.shape[2] - wide, None)
            keep_norm(stat_ref, centre, inverse, norm_ref[0, layer : layer + 1, span], norm_ref[1, layer : layer + 1, span])

        @pl.when(step < steps)
        def _():
            place = pl.ds(pl.multiple_of(step * zone, zone), zone)
            hidden_here = h_ref[...]
            kept[place, :] = hidden_here
            value = x_ref[...].astype(F32) + normed_of(hidden_here.astype(F32), stat_ref)
            half = 0.5 * value
            bend = jnp.tanh(half)
            piled[...] += (half * bend + half) * mask_ref[:, 1:2]
            slopes[place, :] = (0.5 * (1.0 + bend + half * (1.0 - bend * bend)) * mask_ref[:, 1:2]).astype(BF16)

        @pl.when(step == steps - 1)
        def _():
            for copy in head_weights.copies(head_ref, head_buffer, sems):
                copy.wait()
            low = (jnp.sum(piled[...].reshape(images, SLOT, wide), axis=1) * (1.0 / pixels)).astype(BF16)
            flipped = None
            for d in range(dp_size):
                part = dot_nt(head_buffer[d], low[:, d * cols : (d + 1) * cols])
                flipped = part if flipped is None else flipped + part
            logits = flipped.T + bias_ref[0:1, :]
            top = jnp.max(logits, axis=1, keepdims=True)
            shifted = jnp.exp(logits - top)
            mass = jnp.sum(shifted, axis=1, keepdims=True)
            log_total = jnp.log(mass) + top
            spots = lax.broadcasted_iota(jnp.int32, logits.shape, 1)
            onehot = (spots == image_ref[:, 0:1]).astype(F32)
            weight = image_ref[:, 1:2].astype(F32)
            picked = jnp.sum(logits * onehot, axis=1, keepdims=True)
            loss = jnp.sum(weight * (log_total - picked), axis=0, keepdims=True)
            residue = weight * (jnp.exp(logits - log_total) - onehot)
            loss = jnp.broadcast_to(loss, (1, LANES))
            loss_high = loss.astype(BF16).astype(F32)
            loss_middle = (loss - loss_high).astype(BF16).astype(F32)
            extras[0:1] = jnp.sum(residue, axis=0, keepdims=True)
            extras[1:2, 0:LANES] = loss_high
            extras[2:3, 0:LANES] = loss_middle
            extras[3:4, 0:LANES] = loss - loss_high - loss_middle
            exact = residue / count_ref[1:2, 0:1]
            grad, grad_flipped = exact.astype(BF16), exact.T.astype(BF16)
            for d in range(dp_size):
                back = dot_nn(grad, head_buffer[d])
                weight_part = dot_nn(grad_flipped, low[:, d * cols : (d + 1) * cols])
                for i in range(kept_ref.shape[2]):
                    parts = [weight_part[o * slots : (o + 1) * slots, i * tile : (i + 1) * tile] for o in range(owners)]
                    store_halves(kept_ref, sent_ref, (d, i), parts)
                pooled[:, d * cols : (d + 1) * cols] = back * (1.0 / pixels)

        @pl.when(step >= steps)
        def _():
            place = pl.ds(pl.multiple_of((step - steps) * zone, zone), zone)
            spread = jnp.broadcast_to(pooled[...][:, None, :], (images, SLOT, wide)).reshape(zone, wide)
            ds = spread * slopes[place, :].astype(F32)
            ds_ref[...] = ds.astype(BF16)
            sums[0:8] += fold_rows(ds)
            sums[8:16] += fold_rows(ds * kept[place, :].astype(F32))

        @pl.when(step == 2 * steps - 1)
        def _():
            more = [extras[0:1]] + [extras[i : i + 1, 0:LANES] for i in range(1, 4)] + [jnp.zeros((1, (count_rows - 3) * LANES - classes), F32)]
            send_back_sums(send_ref, sums, stat_ref, more)

    send = (devices, 2 * wide // LANES + count_rows, LANES)
    grads = (owners // 2, dp_size, cols // tile, slots, tile)
    once = pl.BlockSpec((zone, wide), lambda i: (jnp.minimum(i, steps - 1), 0))
    later = pl.BlockSpec((zone, wide), lambda i: (jnp.maximum(i - steps, 0), 0))
    return launch(
        kernel, "head_step", (2 * steps,),
        (hidden, inputs, parts, counts, norms, masks, head_weights, slot_bias, image_cols),
        [
            once, once, whole(parts.shape), whole(counts.shape), whole(norms.shape),
            pl.BlockSpec((zone, 2), lambda i: (lax.rem(i, steps), 0)),
            ANYWHERE, whole(slot_bias.shape), whole(image_cols.shape),
        ],
        (out_of((rows, wide), BF16), out_of((8, wide), F32), out_of(send, BF16), out_of(grads, BF16), out_of(grads, BF16)),
        (later, whole((8, wide)), whole(send), whole(grads), whole(grads)),
        head_weights.scratch()
        + [pltpu.VMEM((rows, wide), BF16), pltpu.VMEM((rows, wide), BF16), pltpu.VMEM((zone, wide), F32), pltpu.VMEM((images, wide), F32), pltpu.VMEM((16, wide), F32), pltpu.VMEM((8, classes), F32)],
        6 * images * classes * wide,
    )


def back_expand(ds, hidden, parts, stat_wide, counts, norms, masks, narrow_hidden, stat_narrow, weights, layer, devices):
    rows, wide = ds.shape
    narrow = weights.width
    strip_rows = block_rows(rows, 4)
    steps = rows // strip_rows

    def kernel(
        ds_ref, h_ref, parts_ref, stat_ref, count_ref, norm_ref, mask_ref, narrow_ref, narrow_stat, w_ref,
        low_ref, out_ref, send_ref, buffer, sems, sums, terms,
    ):
        step = pl.program_id(0)

        @pl.when(step == 0)
        def _():
            copies = weights.copies(w_ref, buffer, sems)
            for copy in copies:
                copy.start()
            sums[...] = jnp.zeros_like(sums)
            back_terms(terms, total_of(parts_ref), stat_ref, count_ref[0:1, 0:1], wide)
            for copy in copies:
                copy.wait()

        low = back_norm(ds_ref[...].astype(F32), h_ref[...].astype(F32), stat_ref, terms, mask_ref[:, 0:1]).astype(BF16)
        low_ref[...] = low
        total = dot_nn(low, buffer[...]) * silu_slope(normed_of(narrow_ref[...], narrow_stat))
        out_ref[...] = total
        sums[0:8] += fold_rows(total)
        sums[8:16] += fold_rows(total * narrow_ref[...])

        @pl.when(step == steps - 1)
        def _():
            send_back_sums(send_ref, sums, narrow_stat)

    send = (devices, 2 * narrow // LANES, LANES)
    return launch(
        kernel, "back_expand", (steps,),
        (ds, hidden, parts, stat_wide, counts, norms, masks, narrow_hidden, stat_narrow, weights),
        [
            strip(strip_rows, wide), strip(strip_rows, wide), whole(parts.shape), whole(stat_wide.shape), whole(counts.shape),
            whole(norms.shape), strip(strip_rows, 2), strip(strip_rows, narrow), whole(stat_narrow.shape), ANYWHERE,
        ],
        (out_of((rows, wide), BF16), out_of((rows, narrow), F32), out_of(send, F32)),
        (strip(strip_rows, wide), strip(strip_rows, narrow), whole(send)),
        weights.scratch() + [pltpu.VMEM((16, narrow), F32), pltpu.VMEM((8, wide), F32)],
        2 * rows * wide * narrow,
    )


def back_conv(dz, hidden, parts, stat_two, counts, norms, masks, first_hidden, stat_one, weights, layer, zone, devices):
    rows, narrow = dz.shape
    strip_rows = block_rows(rows, 3)
    steps = rows // strip_rows

    def kernel(
        dz_ref, h_ref, parts_ref, stat_ref, count_ref, norm_ref, mask_ref, first_ref, first_stat, w_ref,
        low_ref, out_ref, send_ref, buffer, sems, sums, terms, shifted,
    ):
        step = pl.program_id(0)

        @pl.when(step == 0)
        def _():
            copies = weights.copies(w_ref, buffer, sems)
            for copy in copies:
                copy.start()
            sums[...] = jnp.zeros_like(sums)
            back_terms(terms, total_of(parts_ref), stat_ref, count_ref[0:1, 0:1], narrow)
            clear_edges(shifted, rows, zone)

            def body(index, carry):
                start = pl.multiple_of(index * zone, zone)
                place = pl.ds(start, zone)
                value = back_norm(dz_ref[place, :], h_ref[place, :], stat_ref, terms, mask_ref[place, 0:1])
                low_ref[place, :] = value.astype(BF16)
                store_shifted(shifted, pl.multiple_of(start + zone, zone), value, zone, narrow)
                return carry

            lax.fori_loop(0, rows // zone, body, 0)
            for copy in copies:
                copy.wait()

        base = step * strip_rows
        total = None
        for tap_row in range(3):
            here = pl.ds(pl.multiple_of(base + (2 - tap_row) * zone, 16), strip_rows)
            for tap_col in range(3):
                tap = tap_row * 3 + tap_col
                piece = shifted[here, (2 - tap_col) * narrow : (3 - tap_col) * narrow]
                part = dot_nt(piece, buffer[tap * narrow : (tap + 1) * narrow])
                total = part if total is None else total + part
        place = pl.ds(pl.multiple_of(base, 16), strip_rows)
        total = total * silu_slope(normed_of(first_ref[...], first_stat)) * mask_ref[place, 1:2]
        out_ref[...] = total
        sums[0:8] += fold_rows(total)
        sums[8:16] += fold_rows(total * first_ref[...])

        @pl.when(step == steps - 1)
        def _():
            send_back_sums(send_ref, sums, first_stat)

    send = (devices, 2 * narrow // LANES, LANES)
    return launch(
        kernel, "back_conv", (steps,),
        (dz, hidden, parts, stat_two, counts, norms, masks, first_hidden, stat_one, weights),
        [
            whole(dz.shape), whole(hidden.shape), whole(parts.shape), whole(stat_two.shape), whole(counts.shape),
            whole(norms.shape), whole(masks.shape), strip(strip_rows, narrow), whole(stat_one.shape), ANYWHERE,
        ],
        (out_of((rows, narrow), BF16), out_of((rows, narrow), F32), out_of(send, F32)),
        (whole((rows, narrow)), strip(strip_rows, narrow), whole(send)),
        weights.scratch() + [pltpu.VMEM((16, narrow), F32), pltpu.VMEM((8, narrow), F32), pltpu.VMEM((rows + 2 * zone, 3 * narrow), BF16)],
        2 * rows * 9 * narrow * narrow,
    )


def back_reduce(dz, first_hidden, parts, stat_one, counts, norms, masks, ds, hidden, inputs, stat_wide, weights, layer, devices):
    rows, narrow = dz.shape
    wide = ds.shape[1]
    strip_rows = block_rows(rows, 6)
    steps = rows // strip_rows

    def kernel(
        dz_ref, first_ref, parts_ref, first_stat, count_ref, norm_ref, mask_ref, ds_ref, h_ref, x_ref, stat_ref, w_ref,
        low_ref, out_ref, send_ref, buffer, sems, sums, terms,
    ):
        step = pl.program_id(0)

        @pl.when(step == 0)
        def _():
            copies = weights.copies(w_ref, buffer, sems)
            for copy in copies:
                copy.start()
            sums[...] = jnp.zeros_like(sums)
            back_terms(terms, total_of(parts_ref), first_stat, count_ref[0:1, 0:1], narrow)
            for copy in copies:
                copy.wait()

        low = back_norm(dz_ref[...], first_ref[...], first_stat, terms, mask_ref[:, 0:1]).astype(BF16)
        low_ref[...] = low
        grad = dot_nt(low, buffer[...]) + ds_ref[...].astype(F32)
        hidden_here = h_ref[...].astype(F32)
        total = grad * silu_slope(x_ref[...].astype(F32) + normed_of(hidden_here, stat_ref))
        out_ref[...] = total.astype(BF16)
        sums[0:8] += fold_rows(total)
        sums[8:16] += fold_rows(total * hidden_here)

        @pl.when(step == steps - 1)
        def _():
            send_back_sums(send_ref, sums, stat_ref)

    send = (devices, 2 * wide // LANES, LANES)
    return launch(
        kernel, "back_reduce", (steps,),
        (dz, first_hidden, parts, stat_one, counts, norms, masks, ds, hidden, inputs, stat_wide, weights),
        [
            strip(strip_rows, narrow), strip(strip_rows, narrow), whole(parts.shape), whole(stat_one.shape), whole(counts.shape),
            whole(norms.shape), strip(strip_rows, 2), strip(strip_rows, wide), strip(strip_rows, wide), strip(strip_rows, wide),
            whole(stat_wide.shape), ANYWHERE,
        ],
        (out_of((rows, narrow), BF16), out_of((rows, wide), BF16), out_of(send, BF16)),
        (strip(strip_rows, narrow), strip(strip_rows, wide), whole(send)),
        weights.scratch() + [pltpu.VMEM((16, wide), F32), pltpu.VMEM((8, narrow), F32)],
        2 * rows * wide * narrow,
    )


def last_grad(inputs, dz, first_hidden, parts, stat_one, counts, masks, owners, zone):
    rows, depth = inputs.shape
    narrow = dz.shape[1]
    tile = min(depth, 512)

    def kernel(x_ref, dz_ref, h_ref, parts_ref, stat_ref, count_ref, mask_ref, kept_ref, sent_ref, terms, low):
        @pl.when(pl.program_id(0) == 0)
        def _():
            back_terms(terms, total_of(parts_ref), stat_ref, count_ref[0:1, 0:1], narrow)

            def body(index, carry):
                place = pl.ds(pl.multiple_of(index * zone, zone), zone)
                value = back_norm(dz_ref[place, :], h_ref[place, :], stat_ref, terms, mask_ref[place, 0:1])
                low[place, :] = value.astype(BF16)
                return carry

            lax.fori_loop(0, rows // zone, body, 0)

        total = dot_tn(x_ref[...], low[...])
        store_halves(kept_ref, sent_ref, (), [total[:, o * LANES : (o + 1) * LANES] for o in range(owners)])

    half = out_of((owners // 2, depth, LANES), BF16)
    half_spec = pl.BlockSpec((owners // 2, tile, LANES), lambda i: (0, i, 0))
    operands = (inputs, dz, first_hidden, parts, stat_one, counts, masks)
    return launch(
        kernel, "last_grad", (depth // tile,),
        operands,
        [pl.BlockSpec((rows, tile), lambda i: (0, i))] + [whole(a.shape) for a in operands[1:]],
        (half, half),
        (half_spec, half_spec),
        [pltpu.VMEM((8, narrow), F32), pltpu.VMEM((rows, narrow), BF16)],
        2 * rows * depth * narrow,
    )


def weight_grad(left, right, owners):
    rows, depth = left.shape
    narrow = right.shape[1]
    tile = min(depth, 512)

    def kernel(left_ref, right_ref, kept_ref, sent_ref):
        total = dot_tn(left_ref[...], right_ref[...])
        store_halves(kept_ref, sent_ref, (), [total[:, o * LANES : (o + 1) * LANES] for o in range(owners)])

    half = out_of((owners // 2, depth, LANES), BF16)
    half_spec = pl.BlockSpec((owners // 2, tile, LANES), lambda i: (0, i, 0))

    return launch(
        kernel, "weight_grad", (depth // tile,),
        (left, right),
        [pl.BlockSpec((rows, tile), lambda i: (0, i)), whole(right.shape)],
        (half, half),
        (half_spec, half_spec),
        [],
        2 * rows * depth * narrow,
    )


def spatial_grad(act, right, owners, zone):
    rows, narrow = act.shape

    def kernel(act_ref, right_ref, kept_ref, sent_ref, shifted):
        tap = pl.program_id(0)

        @pl.when(tap == 0)
        def _():
            clear_edges(shifted, rows, zone)

            def body(index, carry):
                start = pl.multiple_of(index * zone, zone)
                value = act_ref[pl.ds(start, zone), :].astype(F32)
                store_shifted(shifted, pl.multiple_of(start + zone, zone), value, zone, narrow)
                return carry

            lax.fori_loop(0, rows // zone, body, 0)

        for tap_col in range(3):
            piece = shifted[pl.ds(pl.multiple_of(tap * zone, zone), rows), tap_col * narrow : (tap_col + 1) * narrow]
            total = dot_tn(piece, right_ref[...])
            place = (slice(tap_col * narrow, (tap_col + 1) * narrow),)
            store_halves(kept_ref, sent_ref, place, [total[:, o * LANES : (o + 1) * LANES] for o in range(owners)])

    half = out_of((owners // 2, 9 * narrow, LANES), BF16)
    half_spec = pl.BlockSpec((owners // 2, 3 * narrow, LANES), lambda i: (0, i, 0))

    return launch(
        kernel, "spatial_grad", (3,),
        (act, right),
        [whole(act.shape), whole(right.shape)],
        (half, half),
        (half_spec, half_spec),
        [pltpu.VMEM((rows + 2 * zone, 3 * narrow), BF16)],
        2 * rows * 9 * narrow * narrow,
    )


def places_of(items):
    heights = [total.shape[0] + -total.shape[0] % 16 for _, _, total in items]
    return heights, [sum(heights[:i]) for i in range(len(heights))]


def low_momenta(items, olds, flipped):
    heights, starts = places_of(items)
    kinds = sorted({kind for _, kind, _ in items})

    def kernel(*refs):
        grads, sources, out_ref = refs[: len(items)], refs[len(items) : -1], refs[-1]
        for (layer, kind, total), grad, height, start in zip(items, grads, heights, starts):
            old, size = sources[kinds.index(kind)][layer], total.shape[0]
            value = MOMENTUM * (old if flipped[kind] else old.T) + grad[...].astype(F32)
            if height > size:
                value = jnp.concatenate([value, jnp.zeros((height - size, LANES), F32)], axis=0)
            out_ref[start : start + height] = value.astype(BF16)

    operands = [total for _, _, total in items] + [olds[kind] for kind in kinds]
    shape = (sum(heights), LANES)
    return launch(
        kernel, "momenta_low", (1,), operands, [whole(a.shape) for a in operands], out_of(shape, BF16), whole(shape), [],
        2**20,
    )


def new_momenta(items, olds, flipped):
    kinds = len(olds)

    def kernel(*refs):
        grads, sources, outs = refs[: len(items)], refs[len(items) : len(items) + kinds], refs[len(items) + kinds :]
        for (layer, kind, _), grad in zip(items, grads):
            value = grad[...].astype(F32)
            outs[kind][layer] = MOMENTUM * sources[kind][layer] + (value if flipped[kind] else value.T)

    operands = [total for _, _, total in items] + list(olds)
    return launch(
        kernel, "new_momenta", (1,), operands, [whole(a.shape) for a in operands],
        tuple(out_of(old.shape, F32) for old in olds), tuple(whole(old.shape) for old in olds), [], 2**20,
    )


def head_update(total, head, head_m, head_v, slots):
    classes, width = head.shape

    def kernel(total_ref, *refs):
        tiles = total_ref.shape[0] // slots
        grad = jnp.concatenate(
            [total_ref[i * slots : i * slots + slots, :].astype(F32)[:classes] for i in range(tiles)], axis=1
        )[:, :width]
        for out_ref, value in zip(refs[3:], adamw(refs[0][...], grad, refs[1][...], refs[2][...], LR_HEAD, DECAY_HEAD)):
            out_ref[...] = value

    operands = [total, head, head_m, head_v]
    return launch(
        kernel, "head_update", (1,), operands, [whole(a.shape) for a in operands],
        (out_of(head.shape, F32),) * 3, (whole(head.shape),) * 3, [], 2**20,
    )


def norm_update(parts, norms, norm_m, norm_v):
    layers, count = len(parts), len(parts[0])
    narrow = parts[0][0].shape[1] * LANES // 2
    widths = [narrow] * (count - 1) + [norms.shape[2] - narrow * (count - 1)]

    def kernel(*refs):
        tables, (p_ref, m_ref, v_ref), outs = refs[: layers * count], refs[layers * count : -3], refs[-3:]
        for layer in range(layers):
            begin = 0
            for number, width in enumerate(widths):
                table = total_of(tables[layer * count + number])
                span = slice(begin, begin + width)
                begin += width
                for row in range(2):
                    grad = row_of(table, (1 - row) * (width // LANES), width)
                    here = (row, slice(layer, layer + 1), span)
                    for out_ref, value in zip(outs, adamw(p_ref[here], grad, m_ref[here], v_ref[here], LR_VECTOR, 0.0)):
                        out_ref[here] = value

    operands = [part for group in parts for part in group] + [norms, norm_m, norm_v]
    return launch(
        kernel, "norm_update", (1,), operands, [whole(a.shape) for a in operands],
        (out_of(norms.shape, F32),) * 3, (whole(norms.shape),) * 3, [], 2**20,
    )


def upper_pairs(owners):
    return [(i, j) for i in range(owners) for j in range(i, owners)]


def own_grams(gathered, items):
    gathered, relative = zip(*gathered)
    owners = gathered[0].shape[0]
    pairs = upper_pairs(owners)
    share = len(pairs) * LANES // owners

    def kernel(*refs):
        sources, out_ref, packed = refs[: len(gathered)], refs[-2], refs[-1]
        me = lax.axis_index("owner")
        own = pl.multiple_of(me * share, 8)
        for number, (operand, start, size) in enumerate(items):
            for place, (i, j) in enumerate(pairs):
                if relative[operand]:
                    i, j = i ^ me, j ^ me
                packed[place * LANES : (place + 1) * LANES] = dot_tn(
                    sources[operand][i, start : start + size, :], sources[operand][j, start : start + size, :]
                )
            out_ref[number] = packed[pl.ds(own, share), :]
        for number in range(len(items), 4):
            out_ref[number] = jnp.zeros((share, LANES), F32)

    shape = (4, share, LANES)
    return launch(
        kernel, "own_grams", (1,), list(gathered), [whole(a.shape) for a in gathered], out_of(shape, F32), whole(shape),
        [pltpu.VMEM((len(pairs) * LANES, LANES), F32)], 2**27,
    )


def dp_bits():
    low = lax.axis_size("owner").bit_length() - 1
    return list(range(low, low + lax.axis_size("dp").bit_length() - 1))


def bit_of(bit):
    return (my_index() >> bit) & 1


def split_two(values):
    high = values.astype(BF16)
    return high, (values - high.astype(F32)).astype(BF16)


def dot_fine(left, right):
    return jnp.dot(left, right, precision=lax.Precision.HIGHEST, preferred_element_type=F32)


def dot_split(left, right):
    left_high, left_low = split_two(left)
    right_high, right_low = split_two(right)
    return dot_nn(left_high, right_high) + (dot_nn(left_high, right_low) + dot_nn(left_low, right_high))


def polynomial(packed, owners):
    side = owners * LANES
    pairs = upper_pairs(owners)

    def kernel(packed_ref, out_ref, gram, product):
        for place, (i, j) in enumerate(pairs):
            block = packed_ref[place * LANES : (place + 1) * LANES, :]
            gram[i * LANES : (i + 1) * LANES, j * LANES : (j + 1) * LANES] = block
            if i != j:
                gram[j * LANES : (j + 1) * LANES, i * LANES : (i + 1) * LANES] = block.T
        eye = (
            lax.broadcasted_iota(jnp.int32, (side, side), 0) == lax.broadcasted_iota(jnp.int32, (side, side), 1)
        ).astype(F32)
        trace = jnp.sum(jnp.sum(gram[...] * eye, axis=0, keepdims=True), axis=1, keepdims=True)
        factor = 1.0 / (jnp.sqrt(trace) + 1e-07)
        first = gram[...] * (factor * factor)
        poly = NS_A * eye + NS_B * first + NS_C * dot_fine(first, first)
        gram[...] = dot_fine(dot_fine(first, poly), poly)
        product[...] = poly * factor

        def body(index, carry):
            now = gram[...]
            poly = NS_A * eye + NS_B * now + NS_C * dot_split(now, now)
            gram[...] = dot_split(dot_split(now, poly), poly)
            product[...] = dot_split(product[...], poly)
            return carry

        lax.fori_loop(0, NS_STEPS - 2, body, 0)
        now = gram[...]
        poly = NS_A * eye + NS_B * now + NS_C * dot_split(now, now)
        own = pl.ds(pl.multiple_of(lax.axis_index("owner") * LANES, LANES), LANES)
        out_ref[...] = dot_split(product[own, :], poly).astype(BF16)

    return launch(
        kernel, "polynomial", (1,), (packed,), [whole(packed.shape)], out_of((LANES, side), BF16), whole((LANES, side)),
        [pltpu.VMEM((side, side), F32), pltpu.VMEM((side, side), F32)], 60 * 2 * side**3,
    )


def apply_polynomials(early, late, products, masters, flipped):
    sets = [list(zip(*arrays)) for arrays, _ in (early, late)]
    owners = sets[0][0][0].shape[0]
    y_bit, z_bit, turn_bit = dp_bits()[:3]
    shift = lax.axis_size("owner").bit_length() - 1
    kinds = len(masters)
    counts = [len(arrays) for arrays, _ in sets]

    def kernel(upper_ref, upper_far, lower_ref, lower_far, *refs):
        arrays = [refs[: counts[0]], refs[counts[0] : sum(counts)]]
        sources, outs = refs[sum(counts) : sum(counts) + kinds], refs[sum(counts) + kinds :]
        place = lax.axis_index("dp")
        my_y, my_z, on_late = ((place >> (bit - shift)) & 1 for bit in (y_bit, z_bit, turn_bit))
        for turn, (_, items) in enumerate((early, late)):
            here = on_late ^ turn
            for number, (layer, kind, operand, start) in enumerate(items):
                y, z = number // 2, number % 2
                turn_y, turn_z = y ^ my_y, z ^ my_z
                halves = (
                    jnp.where(turn_z == 0, upper_ref[turn_y, here].astype(F32), upper_far[turn_y, here].astype(F32)),
                    jnp.where(turn_y == 0, lower_ref[turn_z, here].astype(F32), lower_far[turn_z, here].astype(F32)),
                )
                poly = jnp.concatenate(halves, axis=0).astype(BF16)
                size = sources[kind].shape[1 if flipped[kind] else 2]
                total = None
                me = lax.axis_index("owner") if sets[turn][1][operand] else 0
                for o in range(owners):
                    left, right = poly[:, o * LANES : (o + 1) * LANES], arrays[turn][operand][o ^ me, start : start + size, :]
                    part = dot_nt(right, left) if flipped[kind] else dot_nt(left, right)
                    total = part if total is None else total + part
                outs[kind][layer] = sources[kind][layer] * (1.0 - LR_MATRIX * DECAY_MATRIX) - LR_MATRIX * total

    operands = list(products) + list(sets[0][0]) + list(sets[1][0]) + list(masters)
    outs = tuple(out_of(master.shape, F32) for master in masters)
    return launch(
        kernel, "apply_polynomials", (1,), operands, [whole(a.shape) for a in operands], outs,
        tuple(whole(master.shape) for master in masters), [], 2**31,
    )


def newton_schulz(early, late, olds, masters, flipped, early_low, late_low):
    y_bit, z_bit, turn_bit = dp_bits()[:3]
    sets, grams, moments, first_got = [], [], None, None
    for groups, lows in ((early, early_low), (late, late_low)):
        arrays, items = [], []
        for group, low in zip(groups, lows):
            items += [(layer, kind, len(arrays), start) for (layer, kind, _), start in zip(group, places_of(group)[1])]
            if low is None:
                values, _ = lax.optimization_barrier((low_momenta(group, olds, flipped), first_got))
                low = lax.all_gather(values, "owner"), False
            arrays.append(low)
        sizes = [total.shape[0] for group in groups for _, _, total in group]
        sets.append((arrays, items))
        values = own_grams(arrays, [item[2:] + (size,) for item, size in zip(items, sizes)])
        for bit in dp_bits():
            if bit == turn_bit:
                continue
            if values.shape[0] > 1:
                halves = values.reshape((2, values.shape[0] // 2) + values.shape[1:])
                kept = lax.dynamic_index_in_dim(halves, bit_of(bit), 0, keepdims=False)
                sent = lax.dynamic_index_in_dim(halves, 1 - bit_of(bit), 0, keepdims=False)
            else:
                kept = sent = values
            sent = lax.optimization_barrier(sent)
            first_got = sent if first_got is None else first_got
            got = swap(sent, bit)
            if groups is late and moments is None:
                every = [item for group in early + late for item in group]
                totals, _ = lax.optimization_barrier(([item[2] for item in every], sent))
                moments = new_momenta([item[:2] + (total,) for item, total in zip(every, totals)], olds, flipped)
                got, moments = lax.optimization_barrier((got, moments))
            values = kept + got
        grams.append(values[0])
    on_late = bit_of(turn_bit) == 1
    got = swap(jnp.where(on_late, grams[0], grams[1]), turn_bit)
    mine = jnp.where(on_late, grams[1], grams[0]) + got
    packed = lax.all_gather(mine, "owner", tiled=True)
    own = polynomial(packed, sets[0][0][0][0].shape[0])
    pair = jnp.stack([own, swap(own, turn_bit)])
    middle = own.shape[0] // 2
    upper, lower = pair[:, :middle], pair[:, middle:]
    upper, lower = jnp.stack([upper, swap(upper, y_bit)]), jnp.stack([lower, swap(lower, z_bit)])
    products = (upper, swap(upper, z_bit), lower, swap(lower, y_bit))
    return apply_polynomials(sets[0], sets[1], products, masters, flipped), moments


def adamw(weight, grad, first, second, rate, decay):
    first = BETA_ONE * first + (1.0 - BETA_ONE) * grad
    second = BETA_TWO * second + (1.0 - BETA_TWO) * grad * grad
    first_hat = first / (1.0 - BETA_ONE**STEP)
    second_hat = second / (1.0 - BETA_TWO**STEP)
    weight = weight - rate * (first_hat / (jnp.sqrt(second_hat) + ADAM_EPS) + decay * weight)
    return (weight, first, second)


def per_device(
    images, valid_count, labels, loss_weight, w_reduce, w_spatial, w_expand, mom_reduce, mom_spatial, mom_expand,
    head, head_m, head_v, norm_params, norm_m, norm_v, head_bias, bias_m, bias_v,
):
    dp_size, owner_size = lax.axis_size("dp"), lax.axis_size("owner")
    devices = dp_size * owner_size
    count_img, side, _, wide = images.shape
    pixels = side * side
    narrow = w_reduce.shape[1] * owner_size
    zone = count_img * SLOT
    rows = side * zone

    valid = (jnp.arange(count_img, dtype=jnp.int32) < valid_count[0]).astype(jnp.int32)
    weight_img = valid * loss_weight
    tallies = jnp.stack([valid_count[0] * pixels, jnp.sum(weight_img)]).astype(F32)
    tallies = jnp.pad(tallies, (0, 6))[:, None]
    tallies = jnp.broadcast_to(tallies, (8, LANES))

    in_map = (jnp.arange(SLOT) < side).astype(F32)
    pad_mask = jnp.broadcast_to(in_map, (side, count_img, SLOT))
    masks = jnp.stack([pad_mask * valid.astype(F32)[:, None], pad_mask], axis=-1).reshape(rows, 2)
    arrange = lambda maps: jnp.pad(maps, ((0, 0), (0, 0), (0, SLOT - side), (0, 0))).transpose(1, 0, 2, 3).reshape(rows, wide)

    rows_of = (w_reduce.shape[2], w_spatial.shape[2], w_expand.shape[2])
    starts = (0, rows_of[0], rows_of[0] + rows_of[1])
    packs = [
        [part.T.astype(BF16) for part in (w_reduce[layer], w_spatial[layer], w_expand[layer])] for layer in range(LAYERS)
    ]
    mats = []
    if dp_size == 8 and owner_size == 4 and LAYERS == 2:
        first = Gather(packs[0][0], (4, 3, 2, 1, 0))
        first.send()
        first.join()
        first.send()
        half = rows_of[1] // 2
        sets = [packs[0][1][:half], packs[0][1][half:]]
        packed = jnp.concatenate([packs[0][2], packs[1][0]], axis=0)
        third = lax.all_gather(packed, AXES).reshape(dp_size, owner_size, packed.shape[0], LANES)
        first.got, sets, images = lax.optimization_barrier((first.got, sets, images))
        pixels_in = arrange(images)
        others = [Gather(sets[0], (4, 3, 1, 2, 0)), Gather(sets[1], (4, 2, 3, 1, 0))]
        first.join()
        first.send()
        for flow in others:
            flow.send()
        meet([first] + others)
        first.send()
        for flow in others:
            flow.send()
        meet([first] + others)
        first.values, pixels_in, masks, tallies = lax.optimization_barrier((first.values, pixels_in, masks, tallies))
        first.send()
        for flow in others:
            flow.send()
        first.join()
        mats.append(relative_weights([(first.values, first.masks, 0, rows_of[0], 0)], rows_of[0], dp_size, owner_size))
        h1_first, sums = first_reduce(pixels_in, masks, tallies, mats[0], devices)
        got, h1_first, packs[1] = lax.optimization_barrier(([flow.got for flow in others], h1_first, packs[1]))
        for flow, values in zip(others, got):
            flow.got = values
            flow.join()
        for flow in others:
            flow.send()
        first_parts = exchange(sums)
        got, first_parts = lax.optimization_barrier(([flow.got for flow in others], first_parts))
        for flow, values in zip(others, got):
            flow.got = values
            flow.join()
            flow.send()
        meet(others)
        pieces = [(others[i].values, others[i].masks, 0, half, i * half) for i in range(2)]
        mats.append(relative_weights(pieces, rows_of[1], dp_size, owner_size))
        mats.append(gathered_weights(third, 0, rows_of[2]))
    layers_done = len(mats) // 3
    classes = head.shape[0]
    slots = -(-classes // LANES) * LANES
    slack = slots - classes
    head_low = jnp.pad(head.astype(BF16), ((0, slack), (0, 0)))
    aligned = head.shape[1] % LANES == 0
    if layers_done:
        tiles = head.shape[1] // LANES
        head_tiles = [head_low[:, i * LANES : (i + 1) * LANES] for i in range(tiles)]
        packed = jnp.concatenate(packs[1][1:] + head_tiles, axis=0)
        gathered = lax.all_gather(packed, AXES).reshape(dp_size, owner_size, packed.shape[0], LANES)
        mats.append(gathered_weights(third, rows_of[2], rows_of[0]))
        mats.append(gathered_weights(gathered, 0, rows_of[1]))
        mats.append(gathered_weights(gathered, rows_of[1], rows_of[2]))
        begin = rows_of[1] + rows_of[2]
        pieces = [
            ((d, o, pl.ds(begin + i * slots, slots)), d, o * slots, i * LANES, LANES)
            for d in range(dp_size)
            for o in range(owner_size)
            for i in range(tiles)
        ]
        head_weights = HeadWeights(gathered, pieces, dp_size, owner_size, slots, head.shape[1])
    else:
        for layer in range(LAYERS):
            packed = jnp.concatenate(packs[layer], axis=0)
            gathered = lax.all_gather(packed, AXES).reshape(dp_size, owner_size, packed.shape[0], LANES)
            for kind in range(3):
                piece = gathered[:, :, starts[kind] : starts[kind] + rows_of[kind]]
                piece = piece.transpose(1, 0, 2, 3).reshape(1, owner_size, -1, LANES)
                mats.append(gathered_weights(piece, 0, piece.shape[2]))
        head_all = lax.all_gather(head_low, AXES).reshape(dp_size, owner_size, slots, head.shape[1])
        head_all = head_all.transpose(1, 2, 0, 3).reshape(owner_size, slots, wide)
        pieces = [((o,), 0, o * slots, 0, wide) for o in range(owner_size)]
        head_weights = HeadWeights(head_all, pieces, 1, owner_size, slots, wide)
    slot_bias = jnp.pad(head_bias.reshape(owner_size, classes), ((0, 0), (0, slack)), constant_values=-1e30)
    slot_bias = jnp.broadcast_to(slot_bias.reshape(1, -1), (8, owner_size * slots))
    slot_labels = (labels // classes) * slots + labels % classes
    image_cols = jnp.stack([slot_labels, weight_img], axis=1)

    norms = norm_params
    h1, h2, h3, a1, a2, stat1, stat2, stat3 = ([None] * LAYERS for _ in range(8))
    if not layers_done:
        pixels_in = arrange(images)
    inputs = [pixels_in] + [None] * (LAYERS - 1)
    if layers_done:
        h1[0] = h1_first
    else:
        h1[0], sums = first_reduce(pixels_in, masks, tallies, mats[0], devices)
    for layer in range(LAYERS):
        parts = first_parts if layer == 0 and layers_done else exchange(sums)
        if layer == 0:
            counts = jnp.sum(parts[:, parts.shape[1] - 8 :], axis=0)
            weight_total = counts[1, 0]
        a1[layer], h2[layer], stat1[layer], sums = spatial_conv(
            h1[layer], parts, counts, norms, masks, mats[3 * layer + 1], layer, zone, devices
        )
        a2[layer], h3[layer], stat2[layer], sums = expand(
            h2[layer], exchange(sums), counts, norms, masks, mats[3 * layer + 2], layer, devices
        )
        if layer < LAYERS - 1:
            inputs[layer + 1], h1[layer + 1], stat3[layer], sums = close_and_reduce(
                h3[layer], inputs[layer], exchange(sums), counts, norms, masks, mats[3 * layer + 3], layer, devices
            )
    last = LAYERS - 1
    ds, stat3[last], sums, *head_halves = head_step(
        h3[last], inputs[last], exchange(sums), counts, norms, masks, head_weights, slot_bias, image_cols, last, pixels, zone, devices
    )
    left = bits_of(dp_size, owner_size)
    rest = list(range(1, len(left)))
    turned = [[0] + rest[turn:] + rest[:turn] for turn in range(3)]
    if not layers_done:
        width = head.shape[1]
        head_halves = [
            jnp.pad(
                half.reshape(owner_size // 2, wide // LANES, slots, LANES // width, width).transpose(0, 1, 3, 2, 4),
                ((0, 0),) * 4 + ((0, LANES - width),),
            )
            for half in head_halves
        ]
    blocked = lambda halves: tuple(half.reshape(devices // 2, -1, LANES) for half in halves)
    head_flow = Flow([blocked(head_halves)], left, turned[0])
    flows = [head_flow]
    norm_sums, three_flow, two_flow = [], {}, {}
    wide_rows = 2 * wide // LANES
    for layer in reversed(range(LAYERS)):
        parts3 = exchange(sums)
        if layer == last:
            extra = parts3
        parts3 = advance(parts3, flows)
        dh3, dz2, sums = back_expand(
            ds, h3[layer], parts3, stat3[layer], counts, norms, masks, h2[layer], stat2[layer], mats[3 * layer + 2], layer, devices
        )
        sums = advance(sums, flows)
        grad_three = blocked(weight_grad(dh3, a2[layer], owner_size))
        three_flow[layer] = Flow([grad_three], left, turned[2] if layer > 0 else turned[0])
        flows.append(three_flow[layer])
        parts2 = exchange(sums)
        parts2 = advance(parts2, flows)
        dh2, dz1, sums = back_conv(
            dz2, h2[layer], parts2, stat2[layer], counts, norms, masks, h1[layer], stat1[layer], mats[3 * layer + 1], layer, zone, devices
        )
        sums = advance(sums, flows)
        grad_two = blocked(spatial_grad(a1[layer], dh2, owner_size, zone))
        two_flow[layer] = Fork(grad_two, left, 0, [turned[0 if layer > 0 else 2][1:], turned[1][1:]])
        flows.append(two_flow[layer])
        parts1 = exchange(sums)
        parts1 = advance(parts1, flows)
        if layer > 0:
            dh1, ds, sums = back_reduce(
                dz1, h1[layer], parts1, stat1[layer], counts, norms, masks, ds, h3[layer - 1], inputs[layer - 1], stat3[layer - 1],
                mats[3 * layer], layer, devices,
            )
            sums = advance(sums, flows)
        else:
            grad_one = blocked(
                last_grad(inputs[layer], dz1, h1[layer], parts1, stat1[layer], counts, masks, owner_size, zone)
            )
        if layer > 0:
            grad_one = blocked(weight_grad(inputs[layer], dh1, owner_size))
        if layer > 0:
            one_flow = Flow([grad_one], left, turned[0])
            flows.append(one_flow)
        norm_sums.insert(0, (parts1, parts2, parts3))
    extra = jnp.sum(extra[:, wide_rows:].astype(F32), axis=0)
    class_rows = owner_size * slots // LANES
    bias_raw = extra[:class_rows].reshape(owner_size, slots)[:, :classes].reshape(-1)
    loss_sum = extra[class_rows, 0] + (extra[class_rows + 1, 0] + extra[class_rows + 2, 0])
    grad_bias = bias_raw / weight_total
    last_flow = Flow([grad_one], left, turned[0])
    last_flow.send()
    advance([], [two_flow[0], last_flow], True)
    flows.append(last_flow)
    high, low = LAYERS - 1, 0
    stored = lambda arrays: tuple(a if a.shape[2] % LANES == 0 else jnp.swapaxes(a, 1, 2) for a in arrays)
    flipped = [size % LANES != 0 for size in rows_of]
    olds = stored((mom_reduce, mom_spatial, mom_expand))
    results = {}
    turns = 0
    while turns < 4 or any(flow.got is not None for flow in flows):
        turns += 1
        if turns == 1:
            results["norm"] = norm_update(norm_sums, norm_params, norm_m, norm_v)
        if turns == 2:
            three_high, two_high, one_high = (flow.result() for flow in (three_flow[high], two_flow[high], one_flow))
            early = [[(high, 2, three_high), (high, 1, two_high), (high, 0, one_high)]]
            rows_all = Gather(low_momenta(early[0], olds, flipped), (0, 1))
            rows_all.send()
            results["early"] = rows_all.got
        if turns == 3:
            results["head"] = head_update(head_flow.result(), head, head_m, head_v, slots)
            rows_all.got = results["early"]
            rows_all.join()
            rows_all.send()
        if turns == 4:
            three_low = three_flow[low].result()
            results["third"] = lax.all_gather(low_momenta([(low, 2, three_low)], olds, flipped), "owner")
        if turns == 3:
            results.pop("early")
        results = advance(results, flows, True)
    rows_all = jnp.concatenate([rows_all.values, rows_all.got], axis=0)
    one_low, two_low = last_flow.result(), two_flow[low].result()
    late = [[(low, 2, three_low)], [(low, 1, two_low), (low, 0, one_low)]]
    outcomes = newton_schulz(
        early, late, olds, stored((w_reduce, w_spatial, w_expand)), flipped, [(rows_all, True)], [(results["third"], False), None]
    )
    updated, moments = (
        [jnp.swapaxes(a, 1, 2) if size % LANES else a for a, size in zip(arrays, rows_of)] for arrays in outcomes
    )
    (new_norm, new_norm_m, new_norm_v), (new_head, new_head_m, new_head_v) = results["norm"], results["head"]
    new_bias, new_bias_m, new_bias_v = adamw(head_bias, grad_bias, bias_m, bias_v, LR_VECTOR, 0.0)
    return (
        loss_sum,
        weight_total,
        updated[0],
        updated[1],
        updated[2],
        moments[0],
        moments[1],
        moments[2],
        new_head,
        new_head_m,
        new_head_v,
        new_norm,
        new_norm_m,
        new_norm_v,
        new_bias,
        new_bias_m,
        new_bias_v,
    )


def solution(mesh):
    return jax.shard_map(
        per_device,
        mesh=mesh,
        in_specs=(
            P(("dp", "owner"), None, None, None),
            P(("dp", "owner")),
            P(("dp", "owner")),
            P(("dp", "owner")),
            P(None, "owner", "dp"),
            P(None, "owner", "dp"),
            P(None, "owner", "dp"),
            P(None, "owner", "dp"),
            P(None, "owner", "dp"),
            P(None, "owner", "dp"),
            P("owner", "dp"),
            P("owner", "dp"),
            P("owner", "dp"),
            P(),
            P(),
            P(),
            P(),
            P(),
            P(),
        ),
        out_specs=(
            P(),
            P(),
            P(None, "owner", "dp"),
            P(None, "owner", "dp"),
            P(None, "owner", "dp"),
            P(None, "owner", "dp"),
            P(None, "owner", "dp"),
            P(None, "owner", "dp"),
            P("owner", "dp"),
            P("owner", "dp"),
            P("owner", "dp"),
            P(),
            P(),
            P(),
            P(),
            P(),
            P(),
        ),
        check_vma=False,
    )
```

```python
import functools
import math

import jax
import jax.numpy as jnp
from jax import lax
from jax.experimental import pallas as pl
from jax.experimental.pallas import tpu as pltpu
from jax.sharding import PartitionSpec as P

LAYERS = 2
NS_STEPS = 5
STEP = 10

AXES = ("dp", "owner")
EPS = 1e-05
NS_A = 3.4445
NS_B = -4.775
NS_C = 2.0315
MOMENTUM = 0.9
LR_MATRIX = 0.5
DECAY_MATRIX = 0.01
BETA_ONE = 0.9
BETA_TWO = 0.999
ADAM_EPS = 1e-08
LR_HEAD = 0.2
DECAY_HEAD = 0.01
LR_VECTOR = 0.4
LANES = 128
SLOT = 8
PATIENT = (2**18, 2**18 + 2**17)
F32 = jnp.float32
BF16 = jnp.bfloat16


def device_count():
    return lax.axis_size("dp") * lax.axis_size("owner")


def my_index():
    return lax.axis_index("dp") * lax.axis_size("owner") + lax.axis_index("owner")


def exchange(copies):
    return lax.all_to_all(copies, AXES, 0, 0, tiled=True)


def swap(values, bit):
    count = device_count()
    return lax.ppermute(values, AXES, [(src, src ^ (1 << bit)) for src in range(count)])


def half_of(values, place, side):
    split = values.reshape((2**place, 2, -1) + values.shape[1:])
    picked = lax.dynamic_index_in_dim(split, side, 1, keepdims=False)
    return picked.reshape((-1,) + values.shape[1:])


class Flow:
    def __init__(self, pairs, left, order):
        self.left, self.order = [bit for bit in left if bit != order[0]], list(order[1:])
        self.kept = [kept for kept, _ in pairs]
        self.sent = [sent for _, sent in pairs]
        self.bit = order[0]
        self.values = self.got = None
        self.wait = 1

    def send(self):
        self.got = [swap(sent, self.bit) for sent in self.sent]
        self.wait = 1 + sum(self.sent[0].size > most for most in PATIENT) if self.values is not None else 1
        self.sent = None

    def add(self):
        if self.values is None:
            parts = [kept + got for kept, got in zip(self.kept, self.got)]
            self.values = parts[0] if len(parts) == 1 else jnp.concatenate(parts, axis=1)
        else:
            self.values = half_of(self.values, self.place, self.own) + self.got[0]
        self.got = None

    def split(self):
        if self.order:
            self.bit = self.order.pop(0)
            self.place = self.left.index(self.bit)
            self.left.pop(self.place)
            self.own = (my_index() >> self.bit) & 1
            self.sent = [half_of(self.values, self.place, 1 - self.own)]

    def turn(self):
        if self.got is not None:
            self.add()
            self.split()
        if self.sent is not None:
            self.send()

    def result(self):
        while self.got is not None or self.sent is not None:
            self.turn()
        return self.values[0] if self.values.shape[0] == 1 else self.values


class Fork:
    def __init__(self, pair, left, first, orders):
        self.trunk, self.orders, self.branches = Flow([pair], left, [first]), orders, []
        self.wait = 1

    @property
    def parts(self):
        return self.branches or [self.trunk]

    def add(self):
        for part in self.parts:
            part.add()

    def split(self):
        if self.branches:
            for part in self.branches:
                part.split()
            return
        values, left, count = self.trunk.values, self.trunk.left, len(self.orders)
        step = values.shape[1] // count // 16 * 16
        for number, order in enumerate(self.orders):
            piece = values[:, number * step : (number + 1) * step if number < count - 1 else values.shape[1]]
            place = left.index(order[0])
            own = (my_index() >> order[0]) & 1
            self.branches.append(Flow([(half_of(piece, place, own), half_of(piece, place, 1 - own))], left, order))

    def send(self):
        for part in self.parts:
            if part.sent is not None:
                part.send()
        self.wait = max(part.wait for part in self.parts)

    @property
    def got(self):
        got = [part.got for part in self.parts]
        return None if all(values is None for values in got) else got

    @got.setter
    def got(self, values):
        for part, value in zip(self.parts, values or [None] * len(self.parts)):
            part.got = value

    @property
    def sent(self):
        sent = [part.sent for part in self.parts]
        return None if all(values is None for values in sent) else sent

    @sent.setter
    def sent(self, values):
        for part, value in zip(self.parts, values or [None] * len(self.parts)):
            part.sent = value

    def result(self):
        return jnp.concatenate([part.result() for part in self.branches], axis=0)


def advance(ahead, flows, eager=False):
    for flow in flows:
        flow.wait -= flow.got is not None
    moving = [flow for flow in flows if flow.got is not None and (eager or flow.wait <= 0)]
    ahead, got = lax.optimization_barrier((ahead, [flow.got for flow in moving]))
    for flow, values in zip(moving, got):
        flow.got = values
        flow.add()
        flow.split()
    moving = [flow for flow in flows if flow.sent is not None]
    ahead, sent = lax.optimization_barrier((ahead, [flow.sent for flow in moving]))
    for flow, values in zip(moving, sent):
        flow.sent = values
        flow.send()
    return ahead


def bits_of(dp_size, owner_size):
    low = owner_size.bit_length() - 1
    high = dp_size.bit_length() - 1
    return list(range(low - 1, -1, -1)) + list(range(low + high - 1, low - 1, -1))


def silu(values):
    half = 0.5 * values
    return half * jnp.tanh(half) + half


def silu_slope(values):
    half = 0.5 * values
    bend = jnp.tanh(half)
    return 0.5 * (1.0 + bend + half * (1.0 - bend * bend))


def total_of(parts_ref):
    return jnp.sum(parts_ref[...].astype(F32), axis=0)


def row_of(table, start, width):
    count = width // LANES
    return jnp.concatenate([table[start + i : start + i + 1, :] for i in range(count)], axis=1)


def send_rows(out_ref, rows):
    pieces = [row[:, i * LANES : (i + 1) * LANES] for row in rows for i in range(row.shape[1] // LANES)]
    block = jnp.concatenate(pieces, axis=0).astype(out_ref.dtype)
    out_ref[...] = jnp.broadcast_to(block[None], (out_ref.shape[0],) + block.shape)


def fold_rows(values):
    return jnp.sum(values.reshape(values.shape[0] // 8, 8, values.shape[1]), axis=0)


def norm_of(parts_ref, count, width):
    table = total_of(parts_ref)
    centre = row_of(table, 0, width) / count
    spread = row_of(table, width // LANES, width) / count - centre * centre
    return centre, lax.rsqrt(spread + EPS)


def keep_norm(stat_ref, centre, inverse, gain, bias):
    scale = inverse * gain
    rows = [centre, inverse, scale, bias - centre * scale]
    stat_ref[...] = jnp.concatenate(rows + [jnp.zeros_like(centre)] * 4, axis=0)


def normed_of(values, stat_ref):
    return values * stat_ref[2:3] + stat_ref[3:4]


def back_terms(terms, table, stat_ref, count, width):
    bias_sum, gain_sum = row_of(table, 0, width), row_of(table, width // LANES, width)
    centre, inverse, scale = stat_ref[0:1], stat_ref[1:2], stat_ref[2:3]
    terms[0:1] = scale * (bias_sum - centre * inverse * gain_sum) / count
    terms[1:2] = scale * inverse * gain_sum / count


def back_norm(grad, hidden, stat_ref, terms, mask):
    return grad * stat_ref[2:3] - mask * (terms[0:1] + hidden * terms[1:2])


def send_back_sums(send_ref, sums, stat_ref, more=()):
    bias_sum = jnp.sum(sums[0:8], axis=0, keepdims=True)
    cross = jnp.sum(sums[8:16], axis=0, keepdims=True)
    send_rows(send_ref, [bias_sum, (cross - stat_ref[0:1] * bias_sum) * stat_ref[1:2], *more])


class Weights:
    def __init__(self, operands, blocks, rows, dp_size, owners, masked):
        self.operands, self.blocks, self.rows, self.masked = operands, blocks, rows, masked
        self.owners = owners
        self.depth, self.width = dp_size * rows, owners * LANES

    def scratch(self):
        return [pltpu.VMEM((self.depth, self.width), BF16), pltpu.SemaphoreType.DMA((len(self.blocks),))]

    def copies(self, refs, buffer, sems):
        shift = self.owners.bit_length() - 1
        me = (lax.axis_index("dp") << shift) | lax.axis_index("owner") if self.masked else 0
        out = []
        for number, (operand, index, start, rows, device, offset) in enumerate(self.blocks):
            device = me ^ device
            base, lane = (device >> shift) * self.rows + offset, (device & (self.owners - 1)) * LANES
            if self.masked:
                base, lane = pl.multiple_of(base, 16), pl.multiple_of(lane, LANES)
            out.append(
                pltpu.make_async_copy(
                    refs[operand].at[index + (pl.ds(start, rows),)],
                    buffer.at[pl.ds(base, rows), pl.ds(lane, LANES)],
                    sems.at[number],
                )
            )
        return out


class HeadWeights(Weights):
    def __init__(self, array, pieces, dp_size, owners, slots, cols):
        self.operands, self.pieces = [array], pieces
        self.shape, self.owners, self.slots = (dp_size, owners * slots, cols), owners, slots

    def scratch(self):
        return [pltpu.VMEM(self.shape, BF16), pltpu.SemaphoreType.DMA((len(self.pieces),))]

    def copies(self, refs, buffer, sems):
        return [
            pltpu.make_async_copy(
                refs[0].at[source], buffer.at[d, pl.ds(first, self.slots), pl.ds(column, width)], sems.at[number]
            )
            for number, (source, d, first, column, width) in enumerate(self.pieces)
        ]


def gathered_weights(array, start, rows):
    dp_size, owners = array.shape[:2]
    blocks = [(0, (d, o), start, rows, d * owners + o, 0) for d in range(dp_size) for o in range(owners)]
    return Weights([array], blocks, rows, dp_size, owners, False)


def relative_weights(pieces, rows, dp_size, owners):
    operands, blocks = [], []
    for arrays, masks, start, height, offset in pieces:
        for array, names in zip(arrays, masks):
            for index, mask in enumerate(names):
                blocks.append((len(operands), (index,), start, height, mask, offset))
            operands.append(array)
    return Weights(operands, blocks, rows, dp_size, owners, True)


class Gather:
    def __init__(self, block, order):
        self.values, self.masks, self.order = block[None], [0], list(order)

    def send(self):
        self.bit = self.order.pop(0)
        self.got = swap(self.values, self.bit)

    def join(self):
        more = [mask ^ (1 << self.bit) for mask in self.masks]
        if self.order:
            self.values, self.masks = jnp.concatenate([self.values, self.got], axis=0), self.masks + more
        else:
            self.values, self.masks = [self.values, self.got], [self.masks, more]


def meet(flows):
    got = lax.optimization_barrier([flow.got for flow in flows])
    for flow, values in zip(flows, got):
        flow.got = values
        flow.join()


def whole(shape):
    return pl.BlockSpec(shape, lambda *ids: (0,) * len(shape), pipeline_mode=pl.Buffered(1))


def strip(rows, width):
    return pl.BlockSpec((rows, width), lambda i: (i, 0))


ANYWHERE = pl.BlockSpec(memory_space=pl.ANY)
SCALAR = pl.BlockSpec(memory_space=pltpu.SMEM)


def launch(kernel, name, grid, operands, specs, outs, out_specs, scratch, flops):
    arrays, flat_specs, groups = [], [], []
    for operand, spec in zip(operands, specs):
        group = operand.operands if isinstance(operand, Weights) else [operand]
        groups.append(len(group) if isinstance(operand, Weights) else 0)
        arrays += group
        flat_specs += [spec] * len(group)

    def grouped(*refs):
        refs, firsts = list(refs), []
        for count in groups:
            if count:
                firsts.append(tuple(refs[:count]))
                refs = refs[count:]
            else:
                firsts.append(refs.pop(0))
        kernel(*firsts, *refs)

    moved = sum(math.prod(a.shape) * a.dtype.itemsize for a in jax.tree.leaves((arrays, outs)))
    return pl.pallas_call(
        grouped,
        name=name,
        grid=grid,
        in_specs=flat_specs,
        out_specs=out_specs,
        out_shape=outs,
        scratch_shapes=scratch,
        cost_estimate=pl.CostEstimate(flops=flops, bytes_accessed=min(moved, 2**25), transcendentals=0),
        compiler_params=pltpu.CompilerParams(
            vmem_limit_bytes=60 * 2**20, dimension_semantics=("arbitrary",) * len(grid)
        ),
    )(*arrays)


def out_of(shape, dtype):
    return jax.ShapeDtypeStruct(shape, dtype)


def block_rows(rows, parts):
    for count in range(parts, rows):
        if rows % count == 0 and (rows // count) % 16 == 0:
            return rows // count
    return rows


def dot_nn(left, right):
    return jnp.dot(left, right, preferred_element_type=F32)


def dot_nt(left, right):
    return lax.dot_general(left, right, (((1,), (1,)), ((), ())), preferred_element_type=F32)


def dot_tn(left, right):
    return lax.dot_general(left, right, (((0,), (0,)), ((), ())), preferred_element_type=F32)


def store_halves(kept_ref, sent_ref, place, values):
    even = (lax.axis_index("owner") & 1) == 0
    for pair in range(len(values) // 2):
        first, second = values[2 * pair], values[2 * pair + 1]
        kept_ref[(pair,) + place] = jnp.where(even, first, second).astype(BF16)
        sent_ref[(pair,) + place] = jnp.where(even, second, first).astype(BF16)


def first_reduce(images, masks, tallies, weights, devices):
    rows, wide = images.shape
    narrow = weights.width
    strip_rows = block_rows(rows, 3)
    steps = rows // strip_rows

    def kernel(x_ref, mask_ref, tally_ref, w_ref, h_ref, send_ref, buffer, sems, sums):
        step = pl.program_id(0)

        @pl.when(step == 0)
        def _():
            copies = weights.copies(w_ref, buffer, sems)
            for copy in copies:
                copy.start()
            sums[...] = jnp.zeros_like(sums)
            for copy in copies:
                copy.wait()

        hidden = dot_nn(x_ref[...], buffer[...])
        h_ref[...] = hidden
        kept = hidden * mask_ref[:, 0:1]
        sums[0:8] += fold_rows(kept)
        sums[8:16] += fold_rows(kept * hidden)

        @pl.when(step == steps - 1)
        def _():
            rows_here = [jnp.sum(sums[i * 8 : i * 8 + 8], axis=0, keepdims=True) for i in range(2)]
            send_rows(send_ref, rows_here + [tally_ref[i : i + 1] for i in range(8)])

    send = (devices, 2 * narrow // LANES + 8, LANES)
    return launch(
        kernel, "reduce_first", (steps,),
        (images, masks, tallies, weights),
        [strip(strip_rows, wide), strip(strip_rows, 2), whole(tallies.shape), ANYWHERE],
        (out_of((rows, narrow), F32), out_of(send, F32)),
        (strip(strip_rows, narrow), whole(send)),
        weights.scratch() + [pltpu.VMEM((16, narrow), F32)],
        2 * rows * wide * narrow,
    )


def store_shifted(shifted, place, values, zone, narrow):
    for offset in range(3):
        moved = values if offset == 1 else pltpu.roll(values, 1 if offset == 0 else zone - 1, 0)
        shifted[pl.ds(place, zone), offset * narrow : (offset + 1) * narrow] = moved.astype(BF16)


def clear_edges(shifted, rows, zone):
    edge = jnp.zeros((zone, shifted.shape[1]), BF16)
    shifted[0:zone] = edge
    shifted[zone + rows : 2 * zone + rows] = edge


def spatial_conv(hidden, parts, counts, norms, masks, weights, layer, zone, devices):
    rows, narrow = hidden.shape
    strip_rows = block_rows(rows, 3)
    steps = rows // strip_rows

    def kernel(
        h_ref, parts_ref, count_ref, norm_ref, mask_ref, w_ref,
        a_ref, out_ref, stat_ref, send_ref, buffer, sems, sums, shifted,
    ):
        step = pl.program_id(0)

        @pl.when(step == 0)
        def _():
            copies = weights.copies(w_ref, buffer, sems)
            for copy in copies:
                copy.start()
            sums[...] = jnp.zeros_like(sums)
            centre, inverse = norm_of(parts_ref, count_ref[0:1, 0:1], narrow)
            keep_norm(stat_ref, centre, inverse, norm_ref[0, layer : layer + 1, 0:narrow], norm_ref[1, layer : layer + 1, 0:narrow])
            clear_edges(shifted, rows, zone)

            def body(index, carry):
                start = pl.multiple_of(index * zone, zone)
                place = pl.ds(start, zone)
                value = silu(normed_of(h_ref[place, :], stat_ref)) * mask_ref[place, 1:2]
                a_ref[place, :] = value.astype(BF16)
                store_shifted(shifted, pl.multiple_of(start + zone, zone), value, zone, narrow)
                return carry

            lax.fori_loop(0, rows // zone, body, 0)
            for copy in copies:
                copy.wait()

        base = step * strip_rows
        total = None
        for tap in range(3):
            piece = shifted[pl.ds(pl.multiple_of(base + tap * zone, 16), strip_rows), :]
            part = dot_nn(piece, buffer[tap * 3 * narrow : (tap + 1) * 3 * narrow])
            total = part if total is None else total + part
        out_ref[...] = total
        kept = total * mask_ref[pl.ds(pl.multiple_of(base, 16), strip_rows), 0:1]
        sums[0:8] += fold_rows(kept)
        sums[8:16] += fold_rows(kept * total)

        @pl.when(step == steps - 1)
        def _():
            send_rows(send_ref, [jnp.sum(sums[i * 8 : i * 8 + 8], axis=0, keepdims=True) for i in range(2)])

    send = (devices, 2 * narrow // LANES, LANES)
    return launch(
        kernel, "spatial_conv", (steps,),
        (hidden, parts, counts, norms, masks, weights),
        [whole(hidden.shape), whole(parts.shape), whole(counts.shape), whole(norms.shape), whole(masks.shape), ANYWHERE],
        (out_of((rows, narrow), BF16), out_of((rows, narrow), F32), out_of((8, narrow), F32), out_of(send, F32)),
        (whole((rows, narrow)), strip(strip_rows, narrow), whole((8, narrow)), whole(send)),
        weights.scratch() + [pltpu.VMEM((16, narrow), F32), pltpu.VMEM((rows + 2 * zone, 3 * narrow), BF16)],
        2 * rows * 9 * narrow * narrow,
    )


def expand(hidden, parts, counts, norms, masks, weights, layer, devices):
    rows, narrow = hidden.shape
    wide = weights.depth
    strip_rows = block_rows(rows, 4)
    steps = rows // strip_rows

    def kernel(
        h_ref, parts_ref, count_ref, norm_ref, mask_ref, w_ref,
        a_ref, out_ref, stat_ref, send_ref, buffer, sems, sums,
    ):
        step = pl.program_id(0)

        @pl.when(step == 0)
        def _():
            copies = weights.copies(w_ref, buffer, sems)
            for copy in copies:
                copy.start()
            sums[...] = jnp.zeros_like(sums)
            centre, inverse = norm_of(parts_ref, count_ref[0:1, 0:1], narrow)
            span = slice(narrow, 2 * narrow)
            keep_norm(stat_ref, centre, inverse, norm_ref[0, layer : layer + 1, span], norm_ref[1, layer : layer + 1, span])
            for copy in copies:
                copy.wait()

        value = silu(normed_of(h_ref[...], stat_ref)).astype(BF16)
        a_ref[...] = value
        total = dot_nt(value, buffer[...])
        out_ref[...] = total.astype(BF16)
        kept = total * mask_ref[:, 0:1]
        sums[0:8] += fold_rows(kept)
        sums[8:16] += fold_rows(kept * total)

        @pl.when(step == steps - 1)
        def _():
            send_rows(send_ref, [jnp.sum(sums[i * 8 : i * 8 + 8], axis=0, keepdims=True) for i in range(2)])

    send = (devices, 2 * wide // LANES, LANES)
    return launch(
        kernel, "expand", (steps,),
        (hidden, parts, counts, norms, masks, weights),
        [strip(strip_rows, narrow), whole(parts.shape), whole(counts.shape), whole(norms.shape), strip(strip_rows, 2), ANYWHERE],
        (out_of((rows, narrow), BF16), out_of((rows, wide), BF16), out_of((8, narrow), F32), out_of(send, F32)),
        (strip(strip_rows, narrow), strip(strip_rows, wide), whole((8, narrow)), whole(send)),
        weights.scratch() + [pltpu.VMEM((16, wide), F32)],
        2 * rows * wide * narrow,
    )


def close_and_reduce(hidden, inputs, parts, counts, norms, masks, weights, layer, devices):
    rows, wide = hidden.shape
    narrow = weights.width
    strip_rows = block_rows(rows, 4)
    steps = rows // strip_rows

    def kernel(
        h_ref, x_ref, parts_ref, count_ref, norm_ref, mask_ref, w_ref,
        low_ref, out_ref, stat_ref, send_ref, buffer, sems, sums,
    ):
        step = pl.program_id(0)

        @pl.when(step == 0)
        def _():
            copies = weights.copies(w_ref, buffer, sems)
            for copy in copies:
                copy.start()
            sums[...] = jnp.zeros_like(sums)
            centre, inverse = norm_of(parts_ref, count_ref[0:1, 0:1], wide)
            span = slice(2 * narrow, None)
            keep_norm(stat_ref, centre, inverse, norm_ref[0, layer : layer + 1, span], norm_ref[1, layer : layer + 1, span])
            for copy in copies:
                copy.wait()

        value = silu(x_ref[...].astype(F32) + normed_of(h_ref[...].astype(F32), stat_ref))
        low = value.astype(BF16)
        low_ref[...] = low
        total = dot_nn(low, buffer[...])
        out_ref[...] = total
        kept = total * mask_ref[:, 0:1]
        sums[0:8] += fold_rows(kept)
        sums[8:16] += fold_rows(kept * total)

        @pl.when(step == steps - 1)
        def _():
            send_rows(send_ref, [jnp.sum(sums[i * 8 : i * 8 + 8], axis=0, keepdims=True) for i in range(2)])

    send = (devices, 2 * narrow // LANES, LANES)
    return launch(
        kernel, "close_and_reduce", (steps,),
        (hidden, inputs, parts, counts, norms, masks, weights),
        [strip(strip_rows, wide), strip(strip_rows, wide), whole(parts.shape), whole(counts.shape), whole(norms.shape), strip(strip_rows, 2), ANYWHERE],
        (out_of((rows, wide), BF16), out_of((rows, narrow), F32), out_of((8, wide), F32), out_of(send, F32)),
        (strip(strip_rows, wide), strip(strip_rows, narrow), whole((8, wide)), whole(send)),
        weights.scratch() + [pltpu.VMEM((16, narrow), F32)],
        2 * rows * wide * narrow,
    )


def head_step(hidden, inputs, parts, counts, norms, masks, head_weights, slot_bias, image_cols, layer, pixels, zone, devices):
    rows, wide = hidden.shape
    images = zone // SLOT
    dp_size, classes, cols = head_weights.shape
    owners, slots = head_weights.owners, head_weights.slots
    steps = rows // zone
    count_rows = classes // LANES + 8
    tile = LANES

    def kernel(
        h_ref, x_ref, parts_ref, count_ref, norm_ref, mask_ref, head_ref, bias_ref, image_ref,
        ds_ref, stat_ref, send_ref, kept_ref, sent_ref, head_buffer, sems, slopes, kept, piled, pooled, sums, extras,
    ):
        step = pl.program_id(0)

        @pl.when(step == 0)
        def _():
            for copy in head_weights.copies(head_ref, head_buffer, sems):
                copy.start()
            sums[...] = jnp.zeros_like(sums)
            piled[...] = jnp.zeros_like(piled)
            centre, inverse = norm_of(parts_ref, count_ref[0:1, 0:1], wide)
            span = slice(norm_ref.shape[2] - wide, None)
            keep_norm(stat_ref, centre, inverse, norm_ref[0, layer : layer + 1, span], norm_ref[1, layer : layer + 1, span])

        @pl.when(step < steps)
        def _():
            place = pl.ds(pl.multiple_of(step * zone, zone), zone)
            hidden_here = h_ref[...]
            kept[place, :] = hidden_here
            value = x_ref[...].astype(F32) + normed_of(hidden_here.astype(F32), stat_ref)
            half = 0.5 * value
            bend = jnp.tanh(half)
            piled[...] += (half * bend + half) * mask_ref[:, 1:2]
            slopes[place, :] = (0.5 * (1.0 + bend + half * (1.0 - bend * bend)) * mask_ref[:, 1:2]).astype(BF16)

        @pl.when(step == steps - 1)
        def _():
            for copy in head_weights.copies(head_ref, head_buffer, sems):
                copy.wait()
            low = (jnp.sum(piled[...].reshape(images, SLOT, wide), axis=1) * (1.0 / pixels)).astype(BF16)
            flipped = None
            for d in range(dp_size):
                part = dot_nt(head_buffer[d], low[:, d * cols : (d + 1) * cols])
                flipped = part if flipped is None else flipped + part
            logits = flipped.T + bias_ref[0:1, :]
            top = jnp.max(logits, axis=1, keepdims=True)
            shifted = jnp.exp(logits - top)
            mass = jnp.sum(shifted, axis=1, keepdims=True)
            log_total = jnp.log(mass) + top
            spots = lax.broadcasted_iota(jnp.int32, logits.shape, 1)
            onehot = (spots == image_ref[:, 0:1]).astype(F32)
            weight = image_ref[:, 1:2].astype(F32)
            picked = jnp.sum(logits * onehot, axis=1, keepdims=True)
            loss = jnp.sum(weight * (log_total - picked), axis=0, keepdims=True)
            residue = weight * (jnp.exp(logits - log_total) - onehot)
            loss = jnp.broadcast_to(loss, (1, LANES))
            loss_high = loss.astype(BF16).astype(F32)
            loss_middle = (loss - loss_high).astype(BF16).astype(F32)
            extras[0:1] = jnp.sum(residue, axis=0, keepdims=True)
            extras[1:2, 0:LANES] = loss_high
            extras[2:3, 0:LANES] = loss_middle
            extras[3:4, 0:LANES] = loss - loss_high - loss_middle
            exact = residue / count_ref[1:2, 0:1]
            grad, grad_flipped = exact.astype(BF16), exact.T.astype(BF16)
            for d in range(dp_size):
                back = dot_nn(grad, head_buffer[d])
                weight_part = dot_nn(grad_flipped, low[:, d * cols : (d + 1) * cols])
                for i in range(kept_ref.shape[2]):
                    parts = [weight_part[o * slots : (o + 1) * slots, i * tile : (i + 1) * tile] for o in range(owners)]
                    store_halves(kept_ref, sent_ref, (d, i), parts)
                pooled[:, d * cols : (d + 1) * cols] = back * (1.0 / pixels)

        @pl.when(step >= steps)
        def _():
            place = pl.ds(pl.multiple_of((step - steps) * zone, zone), zone)
            spread = jnp.broadcast_to(pooled[...][:, None, :], (images, SLOT, wide)).reshape(zone, wide)
            ds = spread * slopes[place, :].astype(F32)
            ds_ref[...] = ds.astype(BF16)
            sums[0:8] += fold_rows(ds)
            sums[8:16] += fold_rows(ds * kept[place, :].astype(F32))

        @pl.when(step == 2 * steps - 1)
        def _():
            more = [extras[0:1]] + [extras[i : i + 1, 0:LANES] for i in range(1, 4)] + [jnp.zeros((1, (count_rows - 3) * LANES - classes), F32)]
            send_back_sums(send_ref, sums, stat_ref, more)

    send = (devices, 2 * wide // LANES + count_rows, LANES)
    grads = (owners // 2, dp_size, cols // tile, slots, tile)
    once = pl.BlockSpec((zone, wide), lambda i: (jnp.minimum(i, steps - 1), 0))
    later = pl.BlockSpec((zone, wide), lambda i: (jnp.maximum(i - steps, 0), 0))
    return launch(
        kernel, "head_step", (2 * steps,),
        (hidden, inputs, parts, counts, norms, masks, head_weights, slot_bias, image_cols),
        [
            once, once, whole(parts.shape), whole(counts.shape), whole(norms.shape),
            pl.BlockSpec((zone, 2), lambda i: (lax.rem(i, steps), 0)),
            ANYWHERE, whole(slot_bias.shape), whole(image_cols.shape),
        ],
        (out_of((rows, wide), BF16), out_of((8, wide), F32), out_of(send, BF16), out_of(grads, BF16), out_of(grads, BF16)),
        (later, whole((8, wide)), whole(send), whole(grads), whole(grads)),
        head_weights.scratch()
        + [pltpu.VMEM((rows, wide), BF16), pltpu.VMEM((rows, wide), BF16), pltpu.VMEM((zone, wide), F32), pltpu.VMEM((images, wide), F32), pltpu.VMEM((16, wide), F32), pltpu.VMEM((8, classes), F32)],
        6 * images * classes * wide,
    )


def back_expand(ds, hidden, parts, stat_wide, counts, norms, masks, narrow_hidden, stat_narrow, weights, layer, devices):
    rows, wide = ds.shape
    narrow = weights.width
    strip_rows = block_rows(rows, 4)
    steps = rows // strip_rows

    def kernel(
        ds_ref, h_ref, parts_ref, stat_ref, count_ref, norm_ref, mask_ref, narrow_ref, narrow_stat, w_ref,
        low_ref, out_ref, send_ref, buffer, sems, sums, terms,
    ):
        step = pl.program_id(0)

        @pl.when(step == 0)
        def _():
            copies = weights.copies(w_ref, buffer, sems)
            for copy in copies:
                copy.start()
            sums[...] = jnp.zeros_like(sums)
            back_terms(terms, total_of(parts_ref), stat_ref, count_ref[0:1, 0:1], wide)
            for copy in copies:
                copy.wait()

        low = back_norm(ds_ref[...].astype(F32), h_ref[...].astype(F32), stat_ref, terms, mask_ref[:, 0:1]).astype(BF16)
        low_ref[...] = low
        total = dot_nn(low, buffer[...]) * silu_slope(normed_of(narrow_ref[...], narrow_stat))
        out_ref[...] = total
        sums[0:8] += fold_rows(total)
        sums[8:16] += fold_rows(total * narrow_ref[...])

        @pl.when(step == steps - 1)
        def _():
            send_back_sums(send_ref, sums, narrow_stat)

    send = (devices, 2 * narrow // LANES, LANES)
    return launch(
        kernel, "back_expand", (steps,),
        (ds, hidden, parts, stat_wide, counts, norms, masks, narrow_hidden, stat_narrow, weights),
        [
            strip(strip_rows, wide), strip(strip_rows, wide), whole(parts.shape), whole(stat_wide.shape), whole(counts.shape),
            whole(norms.shape), strip(strip_rows, 2), strip(strip_rows, narrow), whole(stat_narrow.shape), ANYWHERE,
        ],
        (out_of((rows, wide), BF16), out_of((rows, narrow), F32), out_of(send, F32)),
        (strip(strip_rows, wide), strip(strip_rows, narrow), whole(send)),
        weights.scratch() + [pltpu.VMEM((16, narrow), F32), pltpu.VMEM((8, wide), F32)],
        2 * rows * wide * narrow,
    )


def back_conv(dz, hidden, parts, stat_two, counts, norms, masks, first_hidden, stat_one, weights, layer, zone, devices):
    rows, narrow = dz.shape
    strip_rows = block_rows(rows, 3)
    steps = rows // strip_rows

    def kernel(
        dz_ref, h_ref, parts_ref, stat_ref, count_ref, norm_ref, mask_ref, first_ref, first_stat, w_ref,
        low_ref, out_ref, send_ref, buffer, sems, sums, terms, shifted,
    ):
        step = pl.program_id(0)

        @pl.when(step == 0)
        def _():
            copies = weights.copies(w_ref, buffer, sems)
            for copy in copies:
                copy.start()
            sums[...] = jnp.zeros_like(sums)
            back_terms(terms, total_of(parts_ref), stat_ref, count_ref[0:1, 0:1], narrow)
            clear_edges(shifted, rows, zone)

            def body(index, carry):
                start = pl.multiple_of(index * zone, zone)
                place = pl.ds(start, zone)
                value = back_norm(dz_ref[place, :], h_ref[place, :], stat_ref, terms, mask_ref[place, 0:1])
                low_ref[place, :] = value.astype(BF16)
                store_shifted(shifted, pl.multiple_of(start + zone, zone), value, zone, narrow)
                return carry

            lax.fori_loop(0, rows // zone, body, 0)
            for copy in copies:
                copy.wait()

        base = step * strip_rows
        total = None
        for tap_row in range(3):
            here = pl.ds(pl.multiple_of(base + (2 - tap_row) * zone, 16), strip_rows)
            for tap_col in range(3):
                tap = tap_row * 3 + tap_col
                piece = shifted[here, (2 - tap_col) * narrow : (3 - tap_col) * narrow]
                part = dot_nt(piece, buffer[tap * narrow : (tap + 1) * narrow])
                total = part if total is None else total + part
        place = pl.ds(pl.multiple_of(base, 16), strip_rows)
        total = total * silu_slope(normed_of(first_ref[...], first_stat)) * mask_ref[place, 1:2]
        out_ref[...] = total
        sums[0:8] += fold_rows(total)
        sums[8:16] += fold_rows(total * first_ref[...])

        @pl.when(step == steps - 1)
        def _():
            send_back_sums(send_ref, sums, first_stat)

    send = (devices, 2 * narrow // LANES, LANES)
    return launch(
        kernel, "back_conv", (steps,),
        (dz, hidden, parts, stat_two, counts, norms, masks, first_hidden, stat_one, weights),
        [
            whole(dz.shape), whole(hidden.shape), whole(parts.shape), whole(stat_two.shape), whole(counts.shape),
            whole(norms.shape), whole(masks.shape), strip(strip_rows, narrow), whole(stat_one.shape), ANYWHERE,
        ],
        (out_of((rows, narrow), BF16), out_of((rows, narrow), F32), out_of(send, F32)),
        (whole((rows, narrow)), strip(strip_rows, narrow), whole(send)),
        weights.scratch() + [pltpu.VMEM((16, narrow), F32), pltpu.VMEM((8, narrow), F32), pltpu.VMEM((rows + 2 * zone, 3 * narrow), BF16)],
        2 * rows * 9 * narrow * narrow,
    )


def back_reduce(dz, first_hidden, parts, stat_one, counts, norms, masks, ds, hidden, inputs, stat_wide, weights, layer, devices):
    rows, narrow = dz.shape
    wide = ds.shape[1]
    strip_rows = block_rows(rows, 4)
    steps = rows // strip_rows

    def kernel(
        dz_ref, first_ref, parts_ref, first_stat, count_ref, norm_ref, mask_ref, ds_ref, h_ref, x_ref, stat_ref, w_ref,
        low_ref, out_ref, send_ref, buffer, sems, sums, terms,
    ):
        step = pl.program_id(0)

        @pl.when(step == 0)
        def _():
            copies = weights.copies(w_ref, buffer, sems)
            for copy in copies:
                copy.start()
            sums[...] = jnp.zeros_like(sums)
            back_terms(terms, total_of(parts_ref), first_stat, count_ref[0:1, 0:1], narrow)
            for copy in copies:
                copy.wait()

        low = back_norm(dz_ref[...], first_ref[...], first_stat, terms, mask_ref[:, 0:1]).astype(BF16)
        low_ref[...] = low
        grad = dot_nt(low, buffer[...]) + ds_ref[...].astype(F32)
        hidden_here = h_ref[...].astype(F32)
        total = grad * silu_slope(x_ref[...].astype(F32) + normed_of(hidden_here, stat_ref))
        out_ref[...] = total.astype(BF16)
        sums[0:8] += fold_rows(total)
        sums[8:16] += fold_rows(total * hidden_here)

        @pl.when(step == steps - 1)
        def _():
            send_back_sums(send_ref, sums, stat_ref)

    send = (devices, 2 * wide // LANES, LANES)
    return launch(
        kernel, "back_reduce", (steps,),
        (dz, first_hidden, parts, stat_one, counts, norms, masks, ds, hidden, inputs, stat_wide, weights),
        [
            strip(strip_rows, narrow), strip(strip_rows, narrow), whole(parts.shape), whole(stat_one.shape), whole(counts.shape),
            whole(norms.shape), strip(strip_rows, 2), strip(strip_rows, wide), strip(strip_rows, wide), strip(strip_rows, wide),
            whole(stat_wide.shape), ANYWHERE,
        ],
        (out_of((rows, narrow), BF16), out_of((rows, wide), BF16), out_of(send, BF16)),
        (strip(strip_rows, narrow), strip(strip_rows, wide), whole(send)),
        weights.scratch() + [pltpu.VMEM((16, wide), F32), pltpu.VMEM((8, narrow), F32)],
        2 * rows * wide * narrow,
    )


def last_grad(inputs, dz, first_hidden, parts, stat_one, counts, masks, owners, zone):
    rows, depth = inputs.shape
    narrow = dz.shape[1]
    tile = min(depth, 512)

    def kernel(x_ref, dz_ref, h_ref, parts_ref, stat_ref, count_ref, mask_ref, kept_ref, sent_ref, terms, low):
        @pl.when(pl.program_id(0) == 0)
        def _():
            back_terms(terms, total_of(parts_ref), stat_ref, count_ref[0:1, 0:1], narrow)

            def body(index, carry):
                place = pl.ds(pl.multiple_of(index * zone, zone), zone)
                value = back_norm(dz_ref[place, :], h_ref[place, :], stat_ref, terms, mask_ref[place, 0:1])
                low[place, :] = value.astype(BF16)
                return carry

            lax.fori_loop(0, rows // zone, body, 0)

        total = dot_tn(x_ref[...], low[...])
        store_halves(kept_ref, sent_ref, (), [total[:, o * LANES : (o + 1) * LANES] for o in range(owners)])

    half = out_of((owners // 2, depth, LANES), BF16)
    half_spec = pl.BlockSpec((owners // 2, tile, LANES), lambda i: (0, i, 0))
    operands = (inputs, dz, first_hidden, parts, stat_one, counts, masks)
    return launch(
        kernel, "last_grad", (depth // tile,),
        operands,
        [pl.BlockSpec((rows, tile), lambda i: (0, i))] + [whole(a.shape) for a in operands[1:]],
        (half, half),
        (half_spec, half_spec),
        [pltpu.VMEM((8, narrow), F32), pltpu.VMEM((rows, narrow), BF16)],
        2 * rows * depth * narrow,
    )


def weight_grad(left, right, owners):
    rows, depth = left.shape
    narrow = right.shape[1]
    tile = min(depth, 512)

    def kernel(left_ref, right_ref, kept_ref, sent_ref):
        total = dot_tn(left_ref[...], right_ref[...])
        store_halves(kept_ref, sent_ref, (), [total[:, o * LANES : (o + 1) * LANES] for o in range(owners)])

    half = out_of((owners // 2, depth, LANES), BF16)
    half_spec = pl.BlockSpec((owners // 2, tile, LANES), lambda i: (0, i, 0))

    return launch(
        kernel, "weight_grad", (depth // tile,),
        (left, right),
        [pl.BlockSpec((rows, tile), lambda i: (0, i)), whole(right.shape)],
        (half, half),
        (half_spec, half_spec),
        [],
        2 * rows * depth * narrow,
    )


def spatial_grad(act, right, owners, zone):
    rows, narrow = act.shape

    def kernel(act_ref, right_ref, kept_ref, sent_ref, shifted):
        tap = pl.program_id(0)

        @pl.when(tap == 0)
        def _():
            clear_edges(shifted, rows, zone)

            def body(index, carry):
                start = pl.multiple_of(index * zone, zone)
                value = act_ref[pl.ds(start, zone), :].astype(F32)
                store_shifted(shifted, pl.multiple_of(start + zone, zone), value, zone, narrow)
                return carry

            lax.fori_loop(0, rows // zone, body, 0)

        for tap_col in range(3):
            piece = shifted[pl.ds(pl.multiple_of(tap * zone, zone), rows), tap_col * narrow : (tap_col + 1) * narrow]
            total = dot_tn(piece, right_ref[...])
            place = (slice(tap_col * narrow, (tap_col + 1) * narrow),)
            store_halves(kept_ref, sent_ref, place, [total[:, o * LANES : (o + 1) * LANES] for o in range(owners)])

    half = out_of((owners // 2, 9 * narrow, LANES), BF16)
    half_spec = pl.BlockSpec((owners // 2, 3 * narrow, LANES), lambda i: (0, i, 0))

    return launch(
        kernel, "spatial_grad", (3,),
        (act, right),
        [whole(act.shape), whole(right.shape)],
        (half, half),
        (half_spec, half_spec),
        [pltpu.VMEM((rows + 2 * zone, 3 * narrow), BF16)],
        2 * rows * 9 * narrow * narrow,
    )


def places_of(items):
    heights = [total.shape[0] + -total.shape[0] % 16 for _, _, total in items]
    return heights, [sum(heights[:i]) for i in range(len(heights))]


def low_momenta(items, olds, flipped):
    heights, starts = places_of(items)
    kinds = sorted({kind for _, kind, _ in items})

    def kernel(*refs):
        grads, sources, out_ref = refs[: len(items)], refs[len(items) : -1], refs[-1]
        for (layer, kind, total), grad, height, start in zip(items, grads, heights, starts):
            old, size = sources[kinds.index(kind)][layer], total.shape[0]
            value = MOMENTUM * (old if flipped[kind] else old.T) + grad[...].astype(F32)
            if height > size:
                value = jnp.concatenate([value, jnp.zeros((height - size, LANES), F32)], axis=0)
            out_ref[start : start + height] = value.astype(BF16)

    operands = [total for _, _, total in items] + [olds[kind] for kind in kinds]
    shape = (sum(heights), LANES)
    return launch(
        kernel, "momenta_low", (1,), operands, [whole(a.shape) for a in operands], out_of(shape, BF16), whole(shape), [],
        2**20,
    )


def new_momenta(items, olds, flipped):
    kinds = len(olds)

    def kernel(*refs):
        grads, sources, outs = refs[: len(items)], refs[len(items) : len(items) + kinds], refs[len(items) + kinds :]
        for (layer, kind, _), grad in zip(items, grads):
            value = grad[...].astype(F32)
            outs[kind][layer] = MOMENTUM * sources[kind][layer] + (value if flipped[kind] else value.T)

    operands = [total for _, _, total in items] + list(olds)
    return launch(
        kernel, "new_momenta", (1,), operands, [whole(a.shape) for a in operands],
        tuple(out_of(old.shape, F32) for old in olds), tuple(whole(old.shape) for old in olds), [], 2**20,
    )


def head_update(total, head, head_m, head_v, slots):
    classes, width = head.shape

    def kernel(total_ref, *refs):
        tiles = total_ref.shape[0] // slots
        grad = jnp.concatenate(
            [total_ref[i * slots : i * slots + slots, :].astype(F32)[:classes] for i in range(tiles)], axis=1
        )[:, :width]
        for out_ref, value in zip(refs[3:], adamw(refs[0][...], grad, refs[1][...], refs[2][...], LR_HEAD, DECAY_HEAD)):
            out_ref[...] = value

    operands = [total, head, head_m, head_v]
    return launch(
        kernel, "head_update", (1,), operands, [whole(a.shape) for a in operands],
        (out_of(head.shape, F32),) * 3, (whole(head.shape),) * 3, [], 2**20,
    )


def norm_update(parts, norms, norm_m, norm_v):
    layers, count = len(parts), len(parts[0])
    narrow = parts[0][0].shape[1] * LANES // 2
    widths = [narrow] * (count - 1) + [norms.shape[2] - narrow * (count - 1)]

    def kernel(*refs):
        tables, (p_ref, m_ref, v_ref), outs = refs[: layers * count], refs[layers * count : -3], refs[-3:]
        for layer in range(layers):
            begin = 0
            for number, width in enumerate(widths):
                table = total_of(tables[layer * count + number])
                span = slice(begin, begin + width)
                begin += width
                for row in range(2):
                    grad = row_of(table, (1 - row) * (width // LANES), width)
                    here = (row, slice(layer, layer + 1), span)
                    for out_ref, value in zip(outs, adamw(p_ref[here], grad, m_ref[here], v_ref[here], LR_VECTOR, 0.0)):
                        out_ref[here] = value

    operands = [part for group in parts for part in group] + [norms, norm_m, norm_v]
    return launch(
        kernel, "norm_update", (1,), operands, [whole(a.shape) for a in operands],
        (out_of(norms.shape, F32),) * 3, (whole(norms.shape),) * 3, [], 2**20,
    )


def upper_pairs(owners):
    return [(i, j) for i in range(owners) for j in range(i, owners)]


def own_grams(gathered, items):
    gathered, relative = zip(*gathered)
    owners = gathered[0].shape[0]
    pairs = upper_pairs(owners)
    share = len(pairs) * LANES // owners

    def kernel(*refs):
        sources, out_ref, packed = refs[: len(gathered)], refs[-2], refs[-1]
        me = lax.axis_index("owner")
        own = pl.multiple_of(me * share, 8)
        for number, (operand, start, size) in enumerate(items):
            for place, (i, j) in enumerate(pairs):
                if relative[operand]:
                    i, j = i ^ me, j ^ me
                packed[place * LANES : (place + 1) * LANES] = dot_tn(
                    sources[operand][i, start : start + size, :], sources[operand][j, start : start + size, :]
                )
            out_ref[number] = packed[pl.ds(own, share), :]
        for number in range(len(items), 4):
            out_ref[number] = jnp.zeros((share, LANES), F32)

    shape = (4, share, LANES)
    return launch(
        kernel, "own_grams", (1,), list(gathered), [whole(a.shape) for a in gathered], out_of(shape, F32), whole(shape),
        [pltpu.VMEM((len(pairs) * LANES, LANES), F32)], 2**27,
    )


def dp_bits():
    low = lax.axis_size("owner").bit_length() - 1
    return list(range(low, low + lax.axis_size("dp").bit_length() - 1))


def bit_of(bit):
    return (my_index() >> bit) & 1


def split_two(values):
    high = values.astype(BF16)
    return high, (values - high.astype(F32)).astype(BF16)


def dot_fine(left, right):
    return jnp.dot(left, right, precision=lax.Precision.HIGHEST, preferred_element_type=F32)


def dot_split(left, right):
    left_high, left_low = split_two(left)
    right_high, right_low = split_two(right)
    return dot_nn(left_high, right_high) + (dot_nn(left_high, right_low) + dot_nn(left_low, right_high))


def polynomial(packed, owners):
    side = owners * LANES
    pairs = upper_pairs(owners)

    def kernel(packed_ref, out_ref, gram, product):
        for place, (i, j) in enumerate(pairs):
            block = packed_ref[place * LANES : (place + 1) * LANES, :]
            gram[i * LANES : (i + 1) * LANES, j * LANES : (j + 1) * LANES] = block
            if i != j:
                gram[j * LANES : (j + 1) * LANES, i * LANES : (i + 1) * LANES] = block.T
        eye = (
            lax.broadcasted_iota(jnp.int32, (side, side), 0) == lax.broadcasted_iota(jnp.int32, (side, side), 1)
        ).astype(F32)
        trace = jnp.sum(jnp.sum(gram[...] * eye, axis=0, keepdims=True), axis=1, keepdims=True)
        factor = 1.0 / (jnp.sqrt(trace) + 1e-07)
        first = gram[...] * (factor * factor)
        poly = NS_A * eye + NS_B * first + NS_C * dot_fine(first, first)
        gram[...] = dot_fine(dot_fine(first, poly), poly)
        product[...] = poly * factor

        def body(index, carry):
            now = gram[...]
            poly = NS_A * eye + NS_B * now + NS_C * dot_split(now, now)
            gram[...] = dot_split(dot_split(now, poly), poly)
            product[...] = dot_split(product[...], poly)
            return carry

        lax.fori_loop(0, NS_STEPS - 2, body, 0)
        now = gram[...]
        poly = NS_A * eye + NS_B * now + NS_C * dot_split(now, now)
        own = pl.ds(pl.multiple_of(lax.axis_index("owner") * LANES, LANES), LANES)
        out_ref[...] = dot_split(product[own, :], poly).astype(BF16)

    return launch(
        kernel, "polynomial", (1,), (packed,), [whole(packed.shape)], out_of((LANES, side), BF16), whole((LANES, side)),
        [pltpu.VMEM((side, side), F32), pltpu.VMEM((side, side), F32)], 60 * 2 * side**3,
    )


def apply_polynomials(early, late, products, masters, flipped):
    sets = [list(zip(*arrays)) for arrays, _ in (early, late)]
    owners = sets[0][0][0].shape[0]
    y_bit, z_bit, turn_bit = dp_bits()[:3]
    shift = lax.axis_size("owner").bit_length() - 1
    kinds = len(masters)
    counts = [len(arrays) for arrays, _ in sets]

    def kernel(upper_ref, upper_far, lower_ref, lower_far, *refs):
        arrays = [refs[: counts[0]], refs[counts[0] : sum(counts)]]
        sources, outs = refs[sum(counts) : sum(counts) + kinds], refs[sum(counts) + kinds :]
        place = lax.axis_index("dp")
        my_y, my_z, on_late = ((place >> (bit - shift)) & 1 for bit in (y_bit, z_bit, turn_bit))
        for turn, (_, items) in enumerate((early, late)):
            here = on_late ^ turn
            for number, (layer, kind, operand, start) in enumerate(items):
                y, z = number // 2, number % 2
                turn_y, turn_z = y ^ my_y, z ^ my_z
                halves = (
                    jnp.where(turn_z == 0, upper_ref[turn_y, here].astype(F32), upper_far[turn_y, here].astype(F32)),
                    jnp.where(turn_y == 0, lower_ref[turn_z, here].astype(F32), lower_far[turn_z, here].astype(F32)),
                )
                poly = jnp.concatenate(halves, axis=0).astype(BF16)
                size = sources[kind].shape[1 if flipped[kind] else 2]
                total = None
                me = lax.axis_index("owner") if sets[turn][1][operand] else 0
                for o in range(owners):
                    left, right = poly[:, o * LANES : (o + 1) * LANES], arrays[turn][operand][o ^ me, start : start + size, :]
                    part = dot_nt(right, left) if flipped[kind] else dot_nt(left, right)
                    total = part if total is None else total + part
                outs[kind][layer] = sources[kind][layer] * (1.0 - LR_MATRIX * DECAY_MATRIX) - LR_MATRIX * total

    operands = list(products) + list(sets[0][0]) + list(sets[1][0]) + list(masters)
    outs = tuple(out_of(master.shape, F32) for master in masters)
    return launch(
        kernel, "apply_polynomials", (1,), operands, [whole(a.shape) for a in operands], outs,
        tuple(whole(master.shape) for master in masters), [], 2**31,
    )


def newton_schulz(early, late, olds, masters, flipped, early_low, late_low):
    y_bit, z_bit, turn_bit = dp_bits()[:3]
    sets, grams, moments, first_got = [], [], None, None
    for groups, lows in ((early, early_low), (late, late_low)):
        arrays, items = [], []
        for group, low in zip(groups, lows):
            items += [(layer, kind, len(arrays), start) for (layer, kind, _), start in zip(group, places_of(group)[1])]
            if low is None:
                values, _ = lax.optimization_barrier((low_momenta(group, olds, flipped), first_got))
                low = lax.all_gather(values, "owner"), False
            arrays.append(low)
        sizes = [total.shape[0] for group in groups for _, _, total in group]
        sets.append((arrays, items))
        values = own_grams(arrays, [item[2:] + (size,) for item, size in zip(items, sizes)])
        for bit in dp_bits():
            if bit == turn_bit:
                continue
            if values.shape[0] > 1:
                halves = values.reshape((2, values.shape[0] // 2) + values.shape[1:])
                kept = lax.dynamic_index_in_dim(halves, bit_of(bit), 0, keepdims=False)
                sent = lax.dynamic_index_in_dim(halves, 1 - bit_of(bit), 0, keepdims=False)
            else:
                kept = sent = values
            sent = lax.optimization_barrier(sent)
            first_got = sent if first_got is None else first_got
            got = swap(sent, bit)
            if groups is late and moments is None:
                every = [item for group in early + late for item in group]
                totals, _ = lax.optimization_barrier(([item[2] for item in every], sent))
                moments = new_momenta([item[:2] + (total,) for item, total in zip(every, totals)], olds, flipped)
                got, moments = lax.optimization_barrier((got, moments))
            values = kept + got
        grams.append(values[0])
    on_late = bit_of(turn_bit) == 1
    got = swap(jnp.where(on_late, grams[0], grams[1]), turn_bit)
    mine = jnp.where(on_late, grams[1], grams[0]) + got
    packed = lax.all_gather(mine, "owner", tiled=True)
    own = polynomial(packed, sets[0][0][0][0].shape[0])
    pair = jnp.stack([own, swap(own, turn_bit)])
    middle = own.shape[0] // 2
    upper, lower = pair[:, :middle], pair[:, middle:]
    upper, lower = jnp.stack([upper, swap(upper, y_bit)]), jnp.stack([lower, swap(lower, z_bit)])
    products = (upper, swap(upper, z_bit), lower, swap(lower, y_bit))
    return apply_polynomials(sets[0], sets[1], products, masters, flipped), moments


def adamw(weight, grad, first, second, rate, decay):
    first = BETA_ONE * first + (1.0 - BETA_ONE) * grad
    second = BETA_TWO * second + (1.0 - BETA_TWO) * grad * grad
    first_hat = first / (1.0 - BETA_ONE**STEP)
    second_hat = second / (1.0 - BETA_TWO**STEP)
    weight = weight - rate * (first_hat / (jnp.sqrt(second_hat) + ADAM_EPS) + decay * weight)
    return (weight, first, second)


def per_device(
    images, valid_count, labels, loss_weight, w_reduce, w_spatial, w_expand, mom_reduce, mom_spatial, mom_expand,
    head, head_m, head_v, norm_params, norm_m, norm_v, head_bias, bias_m, bias_v,
):
    dp_size, owner_size = lax.axis_size("dp"), lax.axis_size("owner")
    devices = dp_size * owner_size
    count_img, side, _, wide = images.shape
    pixels = side * side
    narrow = w_reduce.shape[1] * owner_size
    zone = count_img * SLOT
    rows = side * zone

    valid = (jnp.arange(count_img, dtype=jnp.int32) < valid_count[0]).astype(jnp.int32)
    weight_img = valid * loss_weight
    tallies = jnp.stack([valid_count[0] * pixels, jnp.sum(weight_img)]).astype(F32)
    tallies = jnp.pad(tallies, (0, 6))[:, None]
    tallies = jnp.broadcast_to(tallies, (8, LANES))

    in_map = (jnp.arange(SLOT) < side).astype(F32)
    pad_mask = jnp.broadcast_to(in_map, (side, count_img, SLOT))
    masks = jnp.stack([pad_mask * valid.astype(F32)[:, None], pad_mask], axis=-1).reshape(rows, 2)
    arrange = lambda maps: jnp.pad(maps, ((0, 0), (0, 0), (0, SLOT - side), (0, 0))).transpose(1, 0, 2, 3).reshape(rows, wide)

    rows_of = (w_reduce.shape[2], w_spatial.shape[2], w_expand.shape[2])
    starts = (0, rows_of[0], rows_of[0] + rows_of[1])
    packs = [
        [part.T.astype(BF16) for part in (w_reduce[layer], w_spatial[layer], w_expand[layer])] for layer in range(LAYERS)
    ]
    mats = []
    if dp_size == 8 and owner_size == 4 and LAYERS == 2:
        first = Gather(packs[0][0], (4, 3, 2, 1, 0))
        first.send()
        first.join()
        first.send()
        half = rows_of[1] // 2
        sets = [packs[0][1][:half], packs[0][1][half:]]
        packed = jnp.concatenate([packs[0][2], packs[1][0]], axis=0)
        third = lax.all_gather(packed, AXES).reshape(dp_size, owner_size, packed.shape[0], LANES)
        first.got, sets, images = lax.optimization_barrier((first.got, sets, images))
        pixels_in = arrange(images)
        others = [Gather(sets[0], (4, 3, 1, 2, 0)), Gather(sets[1], (4, 2, 3, 1, 0))]
        first.join()
        first.send()
        for flow in others:
            flow.send()
        meet([first] + others)
        first.send()
        for flow in others:
            flow.send()
        meet([first] + others)
        first.values, pixels_in, masks, tallies = lax.optimization_barrier((first.values, pixels_in, masks, tallies))
        first.send()
        for flow in others:
            flow.send()
        first.join()
        mats.append(relative_weights([(first.values, first.masks, 0, rows_of[0], 0)], rows_of[0], dp_size, owner_size))
        h1_first, sums = first_reduce(pixels_in, masks, tallies, mats[0], devices)
        got, h1_first, packs[1] = lax.optimization_barrier(([flow.got for flow in others], h1_first, packs[1]))
        for flow, values in zip(others, got):
            flow.got = values
            flow.join()
        for flow in others:
            flow.send()
        first_parts = exchange(sums)
        got, first_parts = lax.optimization_barrier(([flow.got for flow in others], first_parts))
        for flow, values in zip(others, got):
            flow.got = values
            flow.join()
            flow.send()
        meet(others)
        pieces = [(others[i].values, others[i].masks, 0, half, i * half) for i in range(2)]
        mats.append(relative_weights(pieces, rows_of[1], dp_size, owner_size))
        mats.append(gathered_weights(third, 0, rows_of[2]))
    layers_done = len(mats) // 3
    classes = head.shape[0]
    slots = -(-classes // LANES) * LANES
    slack = slots - classes
    head_low = jnp.pad(head.astype(BF16), ((0, slack), (0, 0)))
    aligned = head.shape[1] % LANES == 0
    if layers_done:
        tiles = head.shape[1] // LANES
        head_tiles = [head_low[:, i * LANES : (i + 1) * LANES] for i in range(tiles)]
        packed = jnp.concatenate(packs[1][1:] + head_tiles, axis=0)
        gathered = lax.all_gather(packed, AXES).reshape(dp_size, owner_size, packed.shape[0], LANES)
        mats.append(gathered_weights(third, rows_of[2], rows_of[0]))
        mats.append(gathered_weights(gathered, 0, rows_of[1]))
        mats.append(gathered_weights(gathered, rows_of[1], rows_of[2]))
        begin = rows_of[1] + rows_of[2]
        pieces = [
            ((d, o, pl.ds(begin + i * slots, slots)), d, o * slots, i * LANES, LANES)
            for d in range(dp_size)
            for o in range(owner_size)
            for i in range(tiles)
        ]
        head_weights = HeadWeights(gathered, pieces, dp_size, owner_size, slots, head.shape[1])
    else:
        for layer in range(LAYERS):
            packed = jnp.concatenate(packs[layer], axis=0)
            gathered = lax.all_gather(packed, AXES).reshape(dp_size, owner_size, packed.shape[0], LANES)
            for kind in range(3):
                piece = gathered[:, :, starts[kind] : starts[kind] + rows_of[kind]]
                piece = piece.transpose(1, 0, 2, 3).reshape(1, owner_size, -1, LANES)
                mats.append(gathered_weights(piece, 0, piece.shape[2]))
        head_all = lax.all_gather(head_low, AXES).reshape(dp_size, owner_size, slots, head.shape[1])
        head_all = head_all.transpose(1, 2, 0, 3).reshape(owner_size, slots, wide)
        pieces = [((o,), 0, o * slots, 0, wide) for o in range(owner_size)]
        head_weights = HeadWeights(head_all, pieces, 1, owner_size, slots, wide)
    slot_bias = jnp.pad(head_bias.reshape(owner_size, classes), ((0, 0), (0, slack)), constant_values=-1e30)
    slot_bias = jnp.broadcast_to(slot_bias.reshape(1, -1), (8, owner_size * slots))
    slot_labels = (labels // classes) * slots + labels % classes
    image_cols = jnp.stack([slot_labels, weight_img], axis=1)

    norms = norm_params
    h1, h2, h3, a1, a2, stat1, stat2, stat3 = ([None] * LAYERS for _ in range(8))
    if not layers_done:
        pixels_in = arrange(images)
    inputs = [pixels_in] + [None] * (LAYERS - 1)
    if layers_done:
        h1[0] = h1_first
    else:
        h1[0], sums = first_reduce(pixels_in, masks, tallies, mats[0], devices)
    for layer in range(LAYERS):
        parts = first_parts if layer == 0 and layers_done else exchange(sums)
        if layer == 0:
            counts = jnp.sum(parts[:, parts.shape[1] - 8 :], axis=0)
            weight_total = counts[1, 0]
        a1[layer], h2[layer], stat1[layer], sums = spatial_conv(
            h1[layer], parts, counts, norms, masks, mats[3 * layer + 1], layer, zone, devices
        )
        a2[layer], h3[layer], stat2[layer], sums = expand(
            h2[layer], exchange(sums), counts, norms, masks, mats[3 * layer + 2], layer, devices
        )
        if layer < LAYERS - 1:
            inputs[layer + 1], h1[layer + 1], stat3[layer], sums = close_and_reduce(
                h3[layer], inputs[layer], exchange(sums), counts, norms, masks, mats[3 * layer + 3], layer, devices
            )
    last = LAYERS - 1
    ds, stat3[last], sums, *head_halves = head_step(
        h3[last], inputs[last], exchange(sums), counts, norms, masks, head_weights, slot_bias, image_cols, last, pixels, zone, devices
    )
    left = bits_of(dp_size, owner_size)
    rest = list(range(1, len(left)))
    turned = [[0] + rest[turn:] + rest[:turn] for turn in range(3)]
    if not layers_done:
        width = head.shape[1]
        head_halves = [
            jnp.pad(
                half.reshape(owner_size // 2, wide // LANES, slots, LANES // width, width).transpose(0, 1, 3, 2, 4),
                ((0, 0),) * 4 + ((0, LANES - width),),
            )
            for half in head_halves
        ]
    blocked = lambda halves: tuple(half.reshape(devices // 2, -1, LANES) for half in halves)
    head_flow = Flow([blocked(head_halves)], left, turned[0])
    flows = [head_flow]
    norm_sums, three_flow, two_flow = [], {}, {}
    wide_rows = 2 * wide // LANES
    for layer in reversed(range(LAYERS)):
        parts3 = exchange(sums)
        if layer == last:
            extra = parts3
        parts3 = advance(parts3, flows)
        dh3, dz2, sums = back_expand(
            ds, h3[layer], parts3, stat3[layer], counts, norms, masks, h2[layer], stat2[layer], mats[3 * layer + 2], layer, devices
        )
        sums = advance(sums, flows)
        grad_three = blocked(weight_grad(dh3, a2[layer], owner_size))
        three_flow[layer] = Flow([grad_three], left, turned[2] if layer > 0 else turned[0])
        flows.append(three_flow[layer])
        parts2 = exchange(sums)
        parts2 = advance(parts2, flows)
        dh2, dz1, sums = back_conv(
            dz2, h2[layer], parts2, stat2[layer], counts, norms, masks, h1[layer], stat1[layer], mats[3 * layer + 1], layer, zone, devices
        )
        sums = advance(sums, flows)
        grad_two = blocked(spatial_grad(a1[layer], dh2, owner_size, zone))
        two_flow[layer] = Fork(grad_two, left, 0, [turned[0 if layer > 0 else 2][1:], turned[1][1:]])
        flows.append(two_flow[layer])
        parts1 = exchange(sums)
        parts1 = advance(parts1, flows)
        if layer > 0:
            dh1, ds, sums = back_reduce(
                dz1, h1[layer], parts1, stat1[layer], counts, norms, masks, ds, h3[layer - 1], inputs[layer - 1], stat3[layer - 1],
                mats[3 * layer], layer, devices,
            )
            sums = advance(sums, flows)
        else:
            grad_one = blocked(
                last_grad(inputs[layer], dz1, h1[layer], parts1, stat1[layer], counts, masks, owner_size, zone)
            )
        if layer > 0:
            grad_one = blocked(weight_grad(inputs[layer], dh1, owner_size))
        if layer > 0:
            one_flow = Flow([grad_one], left, turned[0])
            flows.append(one_flow)
        norm_sums.insert(0, (parts1, parts2, parts3))
    extra = jnp.sum(extra[:, wide_rows:].astype(F32), axis=0)
    class_rows = owner_size * slots // LANES
    bias_raw = extra[:class_rows].reshape(owner_size, slots)[:, :classes].reshape(-1)
    loss_sum = extra[class_rows, 0] + (extra[class_rows + 1, 0] + extra[class_rows + 2, 0])
    grad_bias = bias_raw / weight_total
    last_flow = Flow([grad_one], left, turned[0])
    last_flow.send()
    advance([], [two_flow[0], last_flow], True)
    flows.append(last_flow)
    high, low = LAYERS - 1, 0
    stored = lambda arrays: tuple(a if a.shape[2] % LANES == 0 else jnp.swapaxes(a, 1, 2) for a in arrays)
    flipped = [size % LANES != 0 for size in rows_of]
    olds = stored((mom_reduce, mom_spatial, mom_expand))
    results = {}
    turns = 0
    while turns < 4 or any(flow.got is not None for flow in flows):
        turns += 1
        if turns == 1:
            results["norm"] = norm_update(norm_sums, norm_params, norm_m, norm_v)
        if turns == 2:
            three_high, two_high, one_high = (flow.result() for flow in (three_flow[high], two_flow[high], one_flow))
            early = [[(high, 2, three_high), (high, 1, two_high), (high, 0, one_high)]]
            rows_all = Gather(low_momenta(early[0], olds, flipped), (0, 1))
            rows_all.send()
            results["early"] = rows_all.got
        if turns == 3:
            results["head"] = head_update(head_flow.result(), head, head_m, head_v, slots)
            rows_all.got = results["early"]
            rows_all.join()
            rows_all.send()
        if turns == 4:
            three_low = three_flow[low].result()
            results["third"] = lax.all_gather(low_momenta([(low, 2, three_low)], olds, flipped), "owner")
        if turns == 3:
            results.pop("early")
        results = advance(results, flows, True)
    rows_all = jnp.concatenate([rows_all.values, rows_all.got], axis=0)
    one_low, two_low = last_flow.result(), two_flow[low].result()
    late = [[(low, 2, three_low)], [(low, 1, two_low), (low, 0, one_low)]]
    outcomes = newton_schulz(
        early, late, olds, stored((w_reduce, w_spatial, w_expand)), flipped, [(rows_all, True)], [(results["third"], False), None]
    )
    updated, moments = (
        [jnp.swapaxes(a, 1, 2) if size % LANES else a for a, size in zip(arrays, rows_of)] for arrays in outcomes
    )
    (new_norm, new_norm_m, new_norm_v), (new_head, new_head_m, new_head_v) = results["norm"], results["head"]
    new_bias, new_bias_m, new_bias_v = adamw(head_bias, grad_bias, bias_m, bias_v, LR_VECTOR, 0.0)
    return (
        loss_sum,
        weight_total,
        updated[0],
        updated[1],
        updated[2],
        moments[0],
        moments[1],
        moments[2],
        new_head,
        new_head_m,
        new_head_v,
        new_norm,
        new_norm_m,
        new_norm_v,
        new_bias,
        new_bias_m,
        new_bias_v,
    )


def solution(mesh):
    return jax.shard_map(
        per_device,
        mesh=mesh,
        in_specs=(
            P(("dp", "owner"), None, None, None),
            P(("dp", "owner")),
            P(("dp", "owner")),
            P(("dp", "owner")),
            P(None, "owner", "dp"),
            P(None, "owner", "dp"),
            P(None, "owner", "dp"),
            P(None, "owner", "dp"),
            P(None, "owner", "dp"),
            P(None, "owner", "dp"),
            P("owner", "dp"),
            P("owner", "dp"),
            P("owner", "dp"),
            P(),
            P(),
            P(),
            P(),
            P(),
            P(),
        ),
        out_specs=(
            P(),
            P(),
            P(None, "owner", "dp"),
            P(None, "owner", "dp"),
            P(None, "owner", "dp"),
            P(None, "owner", "dp"),
            P(None, "owner", "dp"),
            P(None, "owner", "dp"),
            P("owner", "dp"),
            P("owner", "dp"),
            P("owner", "dp"),
            P(),
            P(),
            P(),
            P(),
            P(),
            P(),
        ),
        check_vma=False,
    )
```
